32 devices in a mesh: dp: 16 (over z, y, x), group: 2 (over core).
Axes of the slice: x: 2, y: 2, z: 4, core: 2. Of those that a mesh axis runs over, the one named last changes fastest.
Arguments:
- tokens: bfloat16 [32, 512, 768], P('group', 'dp'), may hold values from -6 to 6
- memory: bfloat16 [32, 512, 768], P('group', 'dp'), may hold values from -6 to 6
- segments: int32 [32, 512], P('group', 'dp'), may hold values from 0 to 3, never falling along the last dimension, each value on 1 to 256 neighbouring positions
- memory_segments: int32 [32, 512], P('group', 'dp'), may hold values from 0 to 3, never falling along the last dimension, each value on 1 to 256 neighbouring positions
- row_source: int32 [32], replicated, may hold values from 0 to 31, as said below
- denoiser_modes: int32 [32], replicated, may hold values from 0 to 2, as said below
- sentinel: int32 [32, 512], P(('dp', 'group')), may hold values 0 or 1
- cotangent: bfloat16 [32, 512, 768], P(('dp', 'group')), may hold values from -6 to 6
- w_in: float32 [768, 8704], P(None, ('dp', 'group')), may hold values from -0.21875 to 0.21875
- w_out: float32 [3584, 768], P(('dp', 'group')), may hold values from -0.625 to 0.625
- norm_gains: float32 [3, 768], replicated, may hold values from 0.5 to 1.5
- rel_bias: float32 [3, 32, 12], replicated, may hold values from -4 to 4
- rows_in: float32 [3, 768], replicated, may hold values from 1024 to 16384
- cols_in: float32 [8704], P(('dp', 'group')), may hold values from 1024 to 16384
- rows_out: float32 [3584], P(('dp', 'group')), may hold values from 1024 to 16384
- cols_out: float32 [3, 768], replicated, may hold values from 1024 to 16384
- sq_gains: float32 [3, 768], replicated, may hold values from 1024 to 16384
- sq_rel: float32 [3, 32, 12], replicated, may hold values from 1024 to 16384
Outputs:
- mixed: bfloat16 [32, 512, 768], P(('dp', 'group'))
- d_tokens: bfloat16 [32, 512, 768], P('group', 'dp')
- d_memory: bfloat16 [32, 512, 768], P('group', 'dp')
- grad_in: float32 [768, 8704], P(None, ('dp', 'group'))
- grad_out: float32 [3584, 768], P(('dp', 'group'))
- grad_gains: float32 [3, 768], replicated
- grad_rel: float32 [3, 32, 12], replicated
- new_in: float32 [768, 8704], P(None, ('dp', 'group'))
- new_out: float32 [3584, 768], P(('dp', 'group'))
- new_gains: float32 [3, 768], replicated
- new_rel: float32 [3, 32, 12], replicated
- rows_in_new: float32 [3, 768], replicated
- cols_in_new: float32 [8704], P(('dp', 'group'))
- rows_out_new: float32 [3584], P(('dp', 'group'))
- cols_out_new: float32 [3, 768], replicated
- sq_gains_new: float32 [3, 768], replicated
- sq_rel_new: float32 [3, 32, 12], replicated
The draws below stay inside these ranges and needn't reach their ends.
Inputs may be any that keep to these rules, and one draw needn't show every extreme that they name: row_source is a permutation of the rows; its entry at q = (i * 2 + g) + k, for index i of dp, g of group and k below 1, is a row of half g, from g * 16 to (g + 1) * 16 - 1. `denoiser_modes`: the rows that row_source places at one index i of dp, for both indices of group, share one mode. `segments`: every row holds each number 0 to 3, never falling along the row. `memory_segments`: every row holds each number 0 to 3, never falling along the row.
All inputs are finite; a program needn't handle non-finite values. No bound on the sum of `sentinel` on one device may be relied on, other than what follows from the above.
Results may differ from the reference program's by a relative error of at most 0.02.
Values may be sent and summed in bfloat16 or wider, within the bound.
A program may use at most 320 MiB of HBM per device.

```python
import math
import jax
import jax.numpy as jnp
import numpy as np
from jax import lax

D = 768
HEADS = 12
HSIZE = 64
FF = 2048
BUCKETS = 32
MODES = 3
SEQ = 512
SEGS = 4
ROWS_DEV = 1
NIN = 8704
NOUT = 3584
ROWS = 32


def regroup_table(key):
    half_rows = ROWS // 2
    indices = ROWS // (2 * ROWS_DEV)
    subkeys = jax.random.split(key, 3)
    index_mode = jax.random.permutation(subkeys[0], indices) % 3
    first_half = jax.random.permutation(subkeys[1], half_rows)
    second_half = jax.random.permutation(subkeys[2], half_rows) + half_rows
    source = jnp.stack([first_half, second_half], axis=1).reshape(indices, ROWS_DEV, 2)
    source = jnp.transpose(source, (0, 2, 1)).reshape(ROWS)
    slot_mode = jnp.repeat(index_mode, ROWS_DEV)
    mode_rows = jnp.zeros((ROWS,), jnp.int32).at[first_half].set(slot_mode).at[second_half].set(slot_mode)
    return (source.astype(jnp.int32), mode_rows.astype(jnp.int32))


def draw_row_source(key, part):
    return regroup_table(key)[0]


def draw_denoiser_modes(key, part):
    return regroup_table(key)[1]


def plant(entries, rng, low, largest):
    longest = entries.shape.index(max(entries.shape))
    spots = []
    for shift in (0, 1):
        where = [jax.random.randint(jax.random.fold_in(rng, axis), (), 0, length) for axis, length in enumerate(entries.shape)]
        where[longest] = (where[longest] + shift) % entries.shape[longest]
        spots.append(tuple(where))
    return entries.at[spots[0]].set(low).at[spots[1]].set(largest)


def block_levels(own_key, dims, shards, smallest, largest):
    def one(position, parts):
        steps = jax.random.uniform(jax.random.fold_in(jax.random.fold_in(own_key, 6), position), (parts,), jnp.float32, smallest / len(shards), largest / len(shards))
        return jnp.repeat(jnp.exp(steps), dims[position] // parts).reshape((-1,) + (1,) * (len(dims) - position - 1))

    level = one(*shards[0])
    for cut in shards[1:]:
        level = level * one(*cut)
    return level


def split_up(number_of, total, bound, lean):
    portions = [(1 << 20) // math.isqrt(grade ** lean) + 1 for grade in range(2, number_of + 1)]
    spare, counts = total - bound - (number_of - 1), [1] * (number_of - 1)
    while spare > 0:
        movable = [i for i in range(number_of - 1) if counts[i] < bound]
        mass, remaining = sum([portions[i] for i in movable]), spare
        for i in movable:
            more = min(bound - counts[i], max(1, remaining * portions[i] // mass), spare)
            counts[i] = counts[i] + more
            spare = spare - more
    return np.array([bound] + counts)


def ragged(stream_key, number_of, total, most, slope):
    if number_of == 2:
        one = jax.random.randint(stream_key, (), max(1, total - most), min(most, total - 1) + 1)
        return jnp.stack([one, total - one])
    sizes = jnp.asarray(split_up(number_of, total, most, slope), jnp.int32)
    twos = (number_of - 1) // 2
    source_of, sink = sizes[1:1 + 2 * twos:2], sizes[2:2 + 2 * twos:2]
    slack = jnp.minimum(source_of - 1, most - sink)
    moved = jax.random.randint(jax.random.fold_in(stream_key, 1), (twos,), 0, 1 << 20) % (slack + 1)
    sizes = sizes.at[1:1 + 2 * twos:2].set(source_of - moved).at[2:2 + 2 * twos:2].set(sink + moved)
    return sizes[jax.random.permutation(jax.random.fold_in(stream_key, 2), number_of)]


def centred(own_key, extent, deviation, limit, cuts=(), held_as=jnp.bfloat16):
    values = jax.random.normal(own_key, extent, jnp.float32) * deviation
    if len(cuts) > 0:
        values = block_levels(own_key, extent, cuts, -0.22, 0.18) * values
    return jnp.clip(values, min=-limit, max=limit).astype(held_as)


def setup_inputs(seed: int = 0) -> dict:
    key_list = jax.random.split(jax.random.key(seed), 19)
    return {
        "tokens": centred(key_list[0], (ROWS, SEQ, D), 1.0, 6.0, ((0, 2), (1, 16))),
        "memory": centred(key_list[1], (ROWS, SEQ, D), 1.0, 6.0, ((0, 2), (1, 16))),
        "segments": jax.vmap(lambda own: jnp.searchsorted(jnp.cumsum(ragged(own, SEGS, SEQ, SEQ // 2, 0)), jnp.arange(SEQ), side="right"))(jax.random.split(key_list[2], ROWS)).reshape((ROWS, SEQ)).astype(jnp.int32),
        "memory_segments": jax.vmap(lambda own: jnp.searchsorted(jnp.cumsum(ragged(own, SEGS, SEQ, SEQ // 2, 0)), jnp.arange(SEQ), side="right"))(jax.random.split(key_list[3], ROWS)).reshape((ROWS, SEQ)).astype(jnp.int32),
        "row_source": draw_row_source(jax.random.fold_in(key_list[18], 71), 0),
        "denoiser_modes": draw_denoiser_modes(jax.random.fold_in(key_list[18], 71), 0),
        "sentinel": plant((jax.random.randint(key_list[6], (ROWS, SEQ), 0, 8) < 1).astype(jnp.int32), jax.random.fold_in(key_list[6], 1), 0, 1),
        "cotangent": centred(key_list[7], (ROWS, SEQ, D), 1.0, 6.0, ((0, 32),)),
        "w_in": centred(key_list[8], (D, NIN), D ** -0.5, 0.21875, ((1, 32),), jnp.float32),
        "w_out": centred(key_list[9], (NOUT, D), (D // 8) ** -0.5, 0.625, ((0, 32),), jnp.float32),
        "norm_gains": jnp.clip(1.0 + 0.1 * jax.random.normal(key_list[10], (3, D), jnp.float32), 0.5, 1.5),
        "rel_bias": centred(key_list[11], (MODES, BUCKETS, HEADS), 1.0, 4.0, (), jnp.float32),
        "rows_in": jnp.clip(jnp.exp(jax.random.uniform(key_list[12], (3, D), jnp.float32, math.log(1024.0), math.log(16384.0))), 1024.0, 16384.0),
        "cols_in": jnp.clip(jnp.exp(math.log(16384.0) - 2.7725887 * jax.random.uniform(key_list[13], (NIN,), jnp.float32) ** block_levels(key_list[13], (NIN,), ((0, 32),), -0.2, 0.2)), 1024.0, 16384.0),
        "rows_out": jnp.clip(jnp.exp(math.log(16384.0) - 2.7725887 * jax.random.uniform(key_list[14], (NOUT,), jnp.float32) ** block_levels(key_list[14], (NOUT,), ((0, 32),), -0.2, 0.2)), 1024.0, 16384.0),
        "cols_out": jnp.clip(jnp.exp(jax.random.uniform(key_list[15], (3, D), jnp.float32, math.log(1024.0), math.log(16384.0))), 1024.0, 16384.0),
        "sq_gains": jnp.clip(jnp.exp(jax.random.uniform(key_list[16], (3, D), jnp.float32, math.log(1024.0), math.log(16384.0))), 1024.0, 16384.0),
        "sq_rel": jnp.clip(jnp.exp(jax.random.uniform(key_list[17], (MODES, BUCKETS, HEADS), jnp.float32, math.log(1024.0), math.log(16384.0))), 1024.0, 16384.0),
    }


EPSILON = 1e-06
MASKED = -1e+30
DECAY_RATE = 0.9
STEP_SIZE = 0.01
PLAIN_STEP = 0.15
PRECISE = lax.Precision.HIGHEST

@jax.custom_vjp
def low(v):
    return lax.optimization_barrier(v.astype(jnp.bfloat16)).astype(jnp.float32)

@jax.custom_vjp
def low_back(v):
    return v

def low_keep(v):
    return (low(v), None)

def low_pass(kept, grad):
    return (grad,)

def back_keep(v):
    return (v, None)

def back_low(kept, grad):
    return (low(grad),)
low.defvjp(low_keep, low_pass)
low_back.defvjp(back_keep, back_low)

def bucket_table(length, buckets):
    exact_span = buckets // 2
    distances = np.arange(length)
    safe_spans = np.maximum(distances, 1)
    logged = np.floor(np.log(safe_spans / exact_span) / np.log(128.0 / exact_span) * (buckets - exact_span))
    far_bucket = np.minimum(exact_span + logged, buckets - 1)
    return np.where(distances < exact_span, distances, far_bucket).astype(np.int32)

def distance_index(length):
    places = np.arange(length)
    return np.maximum(places[:, None] - places[None, :], 0)

def rms_norm(values, gain_vec):
    return values * lax.rsqrt(lax.optimization_barrier(jnp.mean(values * values, axis=-1, keepdims=True)) + EPSILON) * gain_vec

def softmax_rows(scores):
    row_top = lax.optimization_barrier(jnp.max(scores, axis=-1, keepdims=True))
    raised = jnp.exp(scores - row_top)
    return raised / lax.optimization_barrier(jnp.sum(raised, axis=-1, keepdims=True))

def attend(query, key_part, value_part, allowed, bias_rows):
    scores = jnp.einsum('qhe,khe->hqk', query, key_part, precision=PRECISE) * HSIZE ** (-0.5) + bias_rows
    scores = jnp.where(allowed[None], low_back(scores), MASKED)
    weights = low(softmax_rows(scores))
    return jnp.einsum('hqk,khe->qhe', weights, value_part, precision=PRECISE)

def project(values, matrix):
    return jnp.einsum('rlk,kn->rln', values, matrix, precision=PRECISE)

def layer(tokens, memory, w_in, w_out, norm_gains, rel_bias, segments, memory_segments, denoiser_modes, row_source):
    head_cols = HEADS * HSIZE
    tok_rows = tokens[row_source]
    mem_rows = memory[row_source]
    seg_rows = segments[row_source]
    mseg_rows = memory_segments[row_source]
    mode_rows = denoiser_modes[row_source]
    w_in_low = low(w_in)
    w_out_low = low(w_out)
    bucket_of = jnp.asarray(bucket_table(SEQ, BUCKETS)[distance_index(SEQ)])
    causal = jnp.asarray(np.tril(np.ones((SEQ, SEQ), dtype=bool)))
    h_one = low(rms_norm(tok_rows, norm_gains[0]))
    qkv_rows = low(low_back(project(h_one, w_in_low[:, :3 * head_cols]))).reshape(ROWS, SEQ, 3, HEADS, HSIZE)

    def self_row(packed):
        qkv_row, seg_row, mode_row = packed
        mode_table = jnp.take(rel_bias, mode_row, axis=0)
        bias_rows = jnp.transpose(jnp.take(mode_table, bucket_of, axis=0), (2, 0, 1))
        allowed = causal & (seg_row[:, None] == seg_row[None, :])
        return attend(qkv_row[:, 0], qkv_row[:, 1], qkv_row[:, 2], allowed, bias_rows).reshape(SEQ, head_cols)
    att_one = low(low_back(lax.map(jax.checkpoint(self_row), (qkv_rows, seg_rows, mode_rows))))
    x_one = tok_rows + low_back(project(att_one, w_out_low[:head_cols]))
    h_two = low(rms_norm(x_one, norm_gains[1]))
    q_cross = low(low_back(project(h_two, w_in_low[:, 3 * head_cols:4 * head_cols]))).reshape(ROWS, SEQ, HEADS, HSIZE)
    kv_cross = low(low_back(project(mem_rows, w_in_low[:, 4 * head_cols:6 * head_cols]))).reshape(ROWS, SEQ, 2, HEADS, HSIZE)

    def cross_row(packed):
        query, kv_row, seg_row, mseg_row = packed
        allowed = seg_row[:, None] == mseg_row[None, :]
        return attend(query, kv_row[:, 0], kv_row[:, 1], allowed, 0.0).reshape(SEQ, head_cols)
    att_two = low(low_back(lax.map(jax.checkpoint(cross_row), (q_cross, kv_cross, seg_rows, mseg_rows))))
    x_two = x_one + low_back(project(att_two, w_out_low[head_cols:2 * head_cols]))
    h_three = low(rms_norm(x_two, norm_gains[2]))
    gate_up = low_back(project(h_three, w_in_low[:, 6 * head_cols:]))
    hidden = low(jax.nn.gelu(gate_up[..., :FF], approximate=True) * gate_up[..., FF:])
    return x_two + low_back(project(hidden, w_out_low[2 * head_cols:]))

def update_in(weight, grad_full, rows_old, cols_old):
    head_cols = HEADS * HSIZE
    bounds = [0, 3 * head_cols, 6 * head_cols, NIN]
    squares = grad_full * grad_full
    cols_next = DECAY_RATE * cols_old + (1 - DECAY_RATE) * lax.optimization_barrier(jnp.mean(squares, axis=0))
    row_list = []
    block_list = []
    for block_id in range(3):
        start_col = bounds[block_id]
        stop_col = bounds[block_id + 1]
        row_next = DECAY_RATE * rows_old[block_id] + (1 - DECAY_RATE) * lax.optimization_barrier(jnp.mean(squares[:, start_col:stop_col], axis=1))
        scaled = row_next[:, None] * cols_next[None, start_col:stop_col] / jnp.mean(row_next)
        block_list.append(weight[:, start_col:stop_col] - STEP_SIZE * grad_full[:, start_col:stop_col] * lax.rsqrt(scaled))
        row_list.append(row_next)
    return (jnp.concatenate(block_list, axis=1), jnp.stack(row_list, axis=0), cols_next)

def update_out(weight, grad_full, rows_old, cols_old):
    head_cols = HEADS * HSIZE
    bounds = [0, head_cols, 2 * head_cols, NOUT]
    squares = grad_full * grad_full
    rows_next = DECAY_RATE * rows_old + (1 - DECAY_RATE) * lax.optimization_barrier(jnp.mean(squares, axis=1))
    col_list = []
    block_list = []
    for block_id in range(3):
        start_row = bounds[block_id]
        stop_row = bounds[block_id + 1]
        col_next = DECAY_RATE * cols_old[block_id] + (1 - DECAY_RATE) * lax.optimization_barrier(jnp.mean(squares[start_row:stop_row], axis=0))
        row_part = rows_next[start_row:stop_row]
        scaled = row_part[:, None] * col_next[None, :] / jnp.mean(row_part)
        block_list.append(weight[start_row:stop_row] - STEP_SIZE * grad_full[start_row:stop_row] * lax.rsqrt(scaled))
        col_list.append(col_next)
    return (jnp.concatenate(block_list, axis=0), rows_next, jnp.stack(col_list, axis=0))

def update_plain(weight, grad_full, squares_old):
    squares_next = DECAY_RATE * squares_old + (1 - DECAY_RATE) * grad_full * grad_full
    return (weight - PLAIN_STEP * grad_full * lax.rsqrt(squares_next), squares_next)

def reference(tokens, memory, segments, memory_segments, row_source, denoiser_modes, sentinel, cotangent, w_in, w_out, norm_gains, rel_bias, rows_in, cols_in, rows_out, cols_out, sq_gains, sq_rel):

    def forward(tok_f, mem_f, w_in_f, w_out_f, gains_f, rel_f):
        return layer(tok_f, mem_f, w_in_f, w_out_f, gains_f, rel_f, segments, memory_segments, denoiser_modes, row_source)
    mixed, pull = jax.vjp(forward, tokens.astype(jnp.float32), memory.astype(jnp.float32), w_in, w_out, norm_gains, rel_bias)
    kept = (1 - sentinel).astype(jnp.float32)
    d_tokens, d_memory, grad_in, grad_out, grad_gains, grad_rel = pull(cotangent.astype(jnp.float32) * kept[:, :, None])
    new_in, rows_in_new, cols_in_new = update_in(w_in, grad_in, rows_in, cols_in)
    new_out, rows_out_new, cols_out_new = update_out(w_out, grad_out, rows_out, cols_out)
    new_gains, sq_gains_new = update_plain(norm_gains, grad_gains, sq_gains)
    new_rel, sq_rel_new = update_plain(rel_bias, grad_rel, sq_rel)
    return (mixed.astype(jnp.bfloat16), d_tokens.astype(jnp.bfloat16), d_memory.astype(jnp.bfloat16), grad_in, grad_out, grad_gains, grad_rel, new_in, new_out, new_gains, new_rel, rows_in_new, cols_in_new, rows_out_new, cols_out_new, sq_gains_new, sq_rel_new)
```

```python
import functools

import jax
import jax.numpy as jnp
import numpy as np
from jax import lax
from jax.experimental import pallas as pl
from jax.experimental.pallas import tpu as pltpu
from jax.sharding import PartitionSpec as P

HEADS = 12
HSIZE = 64
FF = 2048
BUCKETS = 32
MODES = 3
SEGS = 4
SEQ = 512
WIDTH = 768
EPSILON = 1e-06
MASKED = -1e30
DECAY_RATE = 0.9
STEP_SIZE = 0.01
PLAIN_STEP = 0.15
GELU_SCALE = 0.7978845608028654
PRECISE = lax.Precision.HIGHEST
MESH = pl.DeviceIdType.MESH
VMEM_BYTES = 60 << 20


def bucket_table(length, buckets):
    exact_span = buckets // 2
    distances = np.arange(length)
    safe_spans = np.maximum(distances, 1)
    logged = np.floor(
        np.log(safe_spans / exact_span) / np.log(128.0 / exact_span) * (buckets - exact_span)
    )
    far_bucket = np.minimum(exact_span + logged, buckets - 1)
    return np.where(distances < exact_span, distances, far_bucket).astype(np.int32)


def nt(a, b):
    return lax.dot_general(a, b, (((1,), (1,)), ((), ())), preferred_element_type=jnp.float32)


def nn(a, b):
    return lax.dot_general(a, b, (((1,), (0,)), ((), ())), preferred_element_type=jnp.float32)


def tn(a, b):
    return lax.dot_general(a, b, (((0,), (0,)), ((), ())), preferred_element_type=jnp.float32)


def inv_rms(values):
    return lax.rsqrt(jnp.mean(values * values, axis=-1, keepdims=True) + EPSILON)


def rms_back(values, gain, grad):
    inv = inv_rms(values)
    scaled = grad * gain
    along = jnp.mean(scaled * values, axis=-1, keepdims=True)
    return inv * scaled - values * (inv * inv * inv * along), jnp.sum(
        grad * (values * inv), axis=0, keepdims=True
    )


def lane_of(shape):
    return lax.broadcasted_iota(jnp.int32, shape, 1)


def ext_masks(aux, first):
    lane = lane_of(aux.shape)
    spot = lane & 63
    documents = (spot >= first) & (spot < first + SEGS)
    hot = jnp.where(documents, aux.astype(jnp.float32), 0.0)
    against = jnp.where(documents, (1.0 - aux.astype(jnp.float32)) * MASKED, 0.0)
    return hot, against


def halves(tile, ext, even):
    lane = lane_of(tile.shape)
    return jnp.where((lane < HSIZE) if even else (lane >= HSIZE), tile, ext)


def pick(first, second, lane):
    return jnp.where(lane < HSIZE, first, second)


def tile_cols(p, base=0):
    return pl.ds(pl.multiple_of(p * 128 + base, 128), 128)


def attend_pair(p, q_tile, k_tile, v_tile, k_ext, q_ext, att_ref, lse_ref, bias_of):
    lane = lane_of((128, 128))
    ones = jnp.ones((SEQ, 128), jnp.bfloat16)
    sides = []
    for even in (True, False):
        sides.append(
            (
                halves(q_tile, q_ext, even),
                halves(k_tile, k_ext, even),
                halves(v_tile, ones, even),
                None if bias_of is None else bias_of(2 * p + (0 if even else 1)),
            )
        )
    for i in range(SEQ // 128):
        lo = 0 if bias_of is None else max(0, i - 2) * 128
        hi = SEQ if bias_of is None else (i + 1) * 128
        outs, tops = [], []
        for qe, ke, ve, bias in sides:
            s = nt(qe[i * 128 : (i + 1) * 128], ke[lo:hi])
            if bias is not None:
                near, far = bias
                parts = [near[:, 128:]] if i == 0 else [near] if i == 1 else [far, near]
                s = s + (parts[0] if len(parts) == 1 else jnp.concatenate(parts, axis=1))
            top = jnp.max(s, axis=1, keepdims=True)
            e = jnp.exp(s - top).astype(jnp.bfloat16)
            outs.append(nn(e, ve[lo:hi]))
            tops.append(top)
        att = pick(outs[0], outs[1], lane)
        total = pltpu.roll(pick(outs[1], outs[0], lane), HSIZE, 1)
        rows = pl.ds(i * 128, 128)
        att_ref[rows, tile_cols(p)] = (att / total).astype(jnp.bfloat16)
        lse = pick(tops[0], tops[1], lane) + jnp.log(total)
        kept = lse_ref[rows, :]
        first = jnp.sum(jnp.where(lane == 0, lse, 0.0), axis=1, keepdims=True)
        second = jnp.sum(jnp.where(lane == HSIZE, lse, 0.0), axis=1, keepdims=True)
        lse_ref[rows, :] = jnp.where(
            lane == 2 * p, first, jnp.where(lane == 2 * p + 1, second, kept)
        )


def forward_bias(table_ref):
    def bias_of(h):
        row = table_ref[pl.ds(h, 1), :]
        near = pltpu.roll(jnp.broadcast_to(row, (128, 256)), 0, 1, stride=1, stride_axis=0)
        lane = lax.broadcasted_iota(jnp.int32, (128, 256), 1)
        sub = lax.broadcasted_iota(jnp.int32, (128, 256), 0)
        near = jnp.where(lane - 128 > sub, MASKED, near)
        far = jnp.broadcast_to(row[:, :1], (128, 128))
        return near, far

    return bias_of


def back_bias(table_ref):
    def bias_of(h):
        row = table_ref[pl.ds(h, 1), :]
        near = pltpu.roll(jnp.broadcast_to(row, (128, 256)), 0, 1, stride=1, stride_axis=0)
        lane = lax.broadcasted_iota(jnp.int32, (128, 256), 1)
        sub = lax.broadcasted_iota(jnp.int32, (128, 256), 0)
        near = jnp.where(lane < sub, MASKED, near)
        far = jnp.broadcast_to(row[:, 128:129], (128, 128))
        return near, far

    return bias_of


def by_distance(near):
    rows = 64
    while rows >= 8:
        near = near[:rows] + pltpu.roll(near[rows:], 256 - rows, 1)
        rows //= 2
    sub = lax.broadcasted_iota(jnp.int32, (8, 256), 0)
    for bit in (4, 2, 1):
        near = jnp.where((sub & bit) != 0, pltpu.roll(near, 256 - bit, 1), near)
    return near


def split_cols(values, base, lane, count):
    rest, out = values, jnp.zeros((values.shape[0], 128), jnp.float32)
    for k in range(count):
        part = rest.astype(jnp.bfloat16).astype(jnp.float32)
        out = jnp.where((lane & 63) == base + k, part, out)
        rest = rest - part
    return out


def back_pair(
    p, q_tile, k_tile, v_tile, do_tile, att_tile, lse_all, hot, against, bias_of, dq_acc, rel_acc, dist_ref
):
    lane = lane_of((SEQ, 128))
    lane1 = lane_of((128, 128))
    spot = lane & 63
    ones3 = jnp.where((spot >= 8) & (spot < 11), 1.0, 0.0)
    k_ext = (hot + ones3).astype(jnp.bfloat16)
    v_ext = jnp.where((spot >= 0) & (spot < 2), 1.0, 0.0).astype(jnp.bfloat16)
    product = do_tile.astype(jnp.float32) * att_tile.astype(jnp.float32)
    sides = []
    for even in (True, False):
        h = 2 * p + (0 if even else 1)
        lse = jnp.sum(jnp.where(lane == h, lse_all, 0.0), axis=1, keepdims=True)
        own = (lane < HSIZE) if even else (lane >= HSIZE)
        delta = jnp.sum(jnp.where(own, product, 0.0), axis=1, keepdims=True)
        q_ext = (against + split_cols(-lse, 8, lane, 3)).astype(jnp.bfloat16)
        d_ext = split_cols(-delta, 0, lane, 2).astype(jnp.bfloat16)
        sides.append(
            (
                halves(q_tile, q_ext, even),
                halves(k_tile, k_ext, even),
                halves(v_tile, v_ext, even),
                halves(do_tile, d_ext, even),
                None if bias_of is None else bias_of(h),
            )
        )
    dks, dvs = [], []
    dq_acc[...] = jnp.zeros_like(dq_acc)
    if bias_of is not None:
        rel_acc[...] = jnp.zeros_like(rel_acc)
    for j in range(SEQ // 128):
        lo = 0 if bias_of is None else j * 128
        hi = SEQ if bias_of is None else min(SEQ, (j + 3) * 128)
        dk2, dv2 = [], []
        for n, (qe, ke, ve, de, bias) in enumerate(sides):
            s = nt(ke[j * 128 : (j + 1) * 128], qe[lo:hi])
            if bias is not None:
                near, far = bias
                s = s + (
                    near[:, :128] if hi - lo == 128 else near if hi - lo == 256
                    else jnp.concatenate([near, far], axis=1)
                )
            w = jnp.exp(s)
            dv2.append(nn(w.astype(jnp.bfloat16), do_tile[lo:hi]))
            ds = w * nt(ve[j * 128 : (j + 1) * 128], de[lo:hi])
            if bias is not None:
                rel_acc[n, :, : hi - lo] += ds
            ds = ds.astype(jnp.bfloat16)
            dk2.append(nn(ds, q_tile[lo:hi]))
            dq_acc[n, :, lo:hi] += tn(k_tile[j * 128 : (j + 1) * 128], ds)
        dks.append(pick(dk2[0], dk2[1], lane1))
        dvs.append(pick(dv2[0], dv2[1], lane1))
    if bias_of is not None:
        for n in range(2):
            near = by_distance(rel_acc[n, :, :256])
            dist_ref[pl.ds(2 * p + n, 1), :] = jnp.concatenate(
                [
                    jnp.sum(near, axis=0, keepdims=True),
                    jnp.sum(rel_acc[n, :, 256:], axis=0, keepdims=True),
                ],
                axis=1,
            )
    sub = lax.broadcasted_iota(jnp.int32, (128, SEQ), 0)
    dq = jnp.where(sub < HSIZE, dq_acc[0], dq_acc[1]).T * HSIZE**-0.5
    return dq, jnp.concatenate(dks, axis=0), jnp.concatenate(dvs, axis=0)


HEAD_COLS = HEADS * HSIZE


def attention_forward(
    tok, mem, aux, win, wout, gains, table, qkv, att1, lse1, x1, qc, kvc, att2, lse2, x2, step
):
    x0 = tok[...].astype(jnp.float32)
    a1 = (x0 * inv_rms(x0) * gains[0:1, :]).astype(jnp.bfloat16)
    for k in range(3):
        cols = slice(k * HEAD_COLS, (k + 1) * HEAD_COLS)
        got = nt(a1, win[cols, :])
        if k == 0:
            got = got.astype(jnp.bfloat16).astype(jnp.float32) * HSIZE**-0.5
        qkv[:, cols] = got.astype(jnp.bfloat16)
    lse1[...] = jnp.zeros_like(lse1)
    lse2[...] = jnp.zeros_like(lse2)

    @pl.loop(0, HEADS // 2)
    def _(p):
        hot, against = ext_masks(aux[...], 0)
        attend_pair(
            p, qkv[:, tile_cols(p)], qkv[:, tile_cols(p, HEAD_COLS)], qkv[:, tile_cols(p, 2 * HEAD_COLS)],
            hot.astype(jnp.bfloat16), against.astype(jnp.bfloat16), att1, lse1, forward_bias(table),
        )
        step("self", p)

    x1[...] = tok[...].astype(jnp.float32) + nn(att1[...], wout[0:HEAD_COLS, :])
    a2 = (x1[...] * inv_rms(x1[...]) * gains[1:2, :]).astype(jnp.bfloat16)
    got = nt(a2, win[3 * HEAD_COLS : 4 * HEAD_COLS, :])
    qc[...] = (got.astype(jnp.bfloat16).astype(jnp.float32) * HSIZE**-0.5).astype(jnp.bfloat16)
    for k in range(2):
        kvc[:, k * HEAD_COLS : (k + 1) * HEAD_COLS] = nt(
            mem[...], win[(4 + k) * HEAD_COLS : (5 + k) * HEAD_COLS, :]
        ).astype(jnp.bfloat16)

    @pl.loop(0, HEADS // 2)
    def _(p):
        _, against = ext_masks(aux[...], 0)
        hot = pltpu.roll(ext_masks(aux[...], SEGS)[0], 128 - SEGS, 1)
        attend_pair(
            p, qc[:, tile_cols(p)], kvc[:, tile_cols(p)], kvc[:, tile_cols(p, HEAD_COLS)],
            hot.astype(jnp.bfloat16), against.astype(jnp.bfloat16), att2, lse2, None,
        )
        step("cross", p)

    x2[...] = x1[...] + nn(att2[...], wout[HEAD_COLS : 2 * HEAD_COLS, :])


def ff_kernel(
    x2, cot, keep, gains, w_gate, w_up, w_down, mixed, g2, d_gain, g_win, g_wout, a3, e3, acc, da3, held, sem
):
    c = pl.program_id(0)
    slot = lax.rem(c, 2)
    rows = w_gate.shape[0]
    first = pl.multiple_of(c * rows, rows)
    puts = [
        pltpu.make_async_copy(held.at[slot, 0], g_win.at[pl.ds(6 * HEAD_COLS + first, rows)], sem.at[slot, 0]),
        pltpu.make_async_copy(held.at[slot, 1], g_win.at[pl.ds(6 * HEAD_COLS + FF + first, rows)], sem.at[slot, 1]),
        pltpu.make_async_copy(held.at[slot, 2], g_wout.at[pl.ds(2 * HEAD_COLS + first, rows)], sem.at[slot, 2]),
    ]

    @pl.when(c >= 2)
    def _():
        for put in puts:
            put.wait()

    @pl.when(c == 0)
    def _():
        a3[...] = (x2[...] * inv_rms(x2[...]) * gains[2:3, :]).astype(jnp.bfloat16)
        e3[...] = (cot[...].astype(jnp.float32) * keep[:, 0:1]).astype(jnp.bfloat16)
        acc[...] = x2[...]
        da3[...] = jnp.zeros_like(da3)

    gate = nt(a3[...], w_gate[...])
    up = nt(a3[...], w_up[...])
    dh = nt(e3[...], w_down[...])
    cube = 0.044715 * gate * gate
    inner = jnp.tanh(GELU_SCALE * gate * (1.0 + cube))
    half = 0.5 * (1.0 + inner)
    gelu = gate * half
    slope = half + 0.5 * gate * (1.0 - inner * inner) * (GELU_SCALE * (1.0 + 3.0 * cube))
    hidden = (gelu * up).astype(jnp.bfloat16)
    d_gate = (dh * up * slope).astype(jnp.bfloat16)
    d_up = (dh * gelu).astype(jnp.bfloat16)
    acc[...] += nn(hidden, w_down[...])
    held[slot, 0] = tn(d_gate, a3[...]).astype(jnp.bfloat16)
    held[slot, 1] = tn(d_up, a3[...]).astype(jnp.bfloat16)
    held[slot, 2] = tn(hidden, e3[...]).astype(jnp.bfloat16)
    for put in puts:
        put.start()
    da3[...] += nn(d_gate, w_gate[...]) + nn(d_up, w_up[...])

    @pl.when(c == pl.num_programs(0) - 1)
    def _():
        mixed[...] = acc[...].astype(jnp.bfloat16)
        part, gain = rms_back(x2[...], gains[2:3, :], da3[...])
        g2[...] = cot[...].astype(jnp.float32) * keep[:, 0:1] + part
        d_gain[...] = gain
        for k in range(3):
            for other in range(2):
                pltpu.make_async_copy(held.at[other, k], g_wout.at[0:rows], sem.at[other, k]).wait()


def attention_backward(
    tok, mem, aux, win, wout, gains, table, qkv, att1, lse1, x1, qc, kvc, att2, lse2, g2,
    d_mem, d_tok, d_gains, dist, do, dqkv, dq_acc, rel_acc, emit, step,
):
    e2 = g2[...].astype(jnp.bfloat16)
    do[...] = nt(e2, wout[HEAD_COLS : 2 * HEAD_COLS, :]).astype(jnp.bfloat16)
    emit(7, tn(att2[...], e2))

    @pl.loop(0, HEADS // 2)
    def _(p):
        _, against = ext_masks(aux[...], 0)
        hot = pltpu.roll(ext_masks(aux[...], SEGS)[0], 128 - SEGS, 1)
        dq, dk, dv = back_pair(
            p, qc[:, tile_cols(p)], kvc[:, tile_cols(p)], kvc[:, tile_cols(p, HEAD_COLS)], do[:, tile_cols(p)],
            att2[:, tile_cols(p)], lse2[...], hot, against, None, dq_acc, rel_acc, dist,
        )
        dqkv[:, tile_cols(p)] = dq.astype(jnp.bfloat16)
        dqkv[:, tile_cols(p, HEAD_COLS)] = dk.astype(jnp.bfloat16)
        dqkv[:, tile_cols(p, 2 * HEAD_COLS)] = dv.astype(jnp.bfloat16)
        step("cross", p)

    a2 = (x1[...] * inv_rms(x1[...]) * gains[1:2, :]).astype(jnp.bfloat16)
    for k in range(3):
        cols = slice(k * HEAD_COLS, (k + 1) * HEAD_COLS)
        emit(3 + k, tn(dqkv[:, cols], a2 if k == 0 else mem[...]))
    d_mem[...] = nn(
        dqkv[:, HEAD_COLS : 3 * HEAD_COLS], win[4 * HEAD_COLS : 6 * HEAD_COLS, :]
    ).astype(jnp.bfloat16)
    da2 = nn(dqkv[:, 0:HEAD_COLS], win[3 * HEAD_COLS : 4 * HEAD_COLS, :])
    part, gain = rms_back(x1[...], gains[1:2, :], da2)
    d_gains[1:2, :] = gain
    g2[...] += part
    e1 = g2[...].astype(jnp.bfloat16)
    do[...] = nt(e1, wout[0:HEAD_COLS, :]).astype(jnp.bfloat16)
    emit(6, tn(att1[...], e1))
    step("middle", 0)

    @pl.loop(0, HEADS // 2)
    def _(p):
        hot, against = ext_masks(aux[...], 0)
        dq, dk, dv = back_pair(
            p, qkv[:, tile_cols(p)], qkv[:, tile_cols(p, HEAD_COLS)], qkv[:, tile_cols(p, 2 * HEAD_COLS)],
            do[:, tile_cols(p)], att1[:, tile_cols(p)], lse1[...], hot, against, back_bias(table), dq_acc, rel_acc, dist,
        )
        dqkv[:, tile_cols(p)] = dq.astype(jnp.bfloat16)
        dqkv[:, tile_cols(p, HEAD_COLS)] = dk.astype(jnp.bfloat16)
        dqkv[:, tile_cols(p, 2 * HEAD_COLS)] = dv.astype(jnp.bfloat16)
        step("self", p)

    x0 = tok[...].astype(jnp.float32)
    a1 = (x0 * inv_rms(x0) * gains[0:1, :]).astype(jnp.bfloat16)
    for k in range(3):
        cols = slice(k * HEAD_COLS, (k + 1) * HEAD_COLS)
        emit(k, tn(dqkv[:, cols], a1))
    da1 = nn(dqkv[...], win[0 : 3 * HEAD_COLS, :])
    part, gain = rms_back(x0, gains[0:1, :], da1)
    d_gains[0:1, :] = gain
    d_tok[...] = (g2[...] + part).astype(jnp.bfloat16)


SHARE = {"i": 272, "o": 112}
PIECES = (
    ("i", 0, 64, 32), ("i", 64, 64, 32), ("i", 128, 64, 32), ("i", 192, 80, 48),
    ("o", 0, 64, 32), ("o", 64, 48, 16),
)


def place():
    dp = lax.axis_index("dp")
    return dp // 4, (dp // 2) % 2, dp % 2, lax.axis_index("group")


def dev(z, y, x, g):
    return ((z * 2 + y) * 2 + x, g)


def rows_of(ref, kind, zz, yy, xx, gg, lo, n):
    share = ((zz * 2 + yy) * 2 + xx) * 2 + gg
    return ref.at[pl.ds(pl.multiple_of(share * SHARE[kind] + lo, 16), n)]


class Links:
    def __init__(self, send_sem, recv_sem):
        self.send_sem, self.recv_sem, self.count, self.sent = send_sem, recv_sem, 0, []

    def reserve(self, n):
        self.count += n
        return self.count - n

    def copy(self, src, dst, device, sem=None):
        k = self.reserve(1) if sem is None else sem
        return pltpu.make_async_remote_copy(
            src_ref=src, dst_ref=dst, send_sem=self.send_sem.at[k], recv_sem=self.recv_sem.at[k],
            device_id=device, device_id_type=MESH,
        )

    def start(self, copy, cond=None):
        if cond is None:
            copy.start()
        else:
            pl.when(cond)(copy.start)
        self.sent.append((copy, cond))

    def drain(self):
        for copy, cond in self.sent:
            if cond is None:
                copy.wait_send()
            else:
                pl.when(cond)(copy.wait_send)
        self.sent = []


def greet(peers):
    barrier = pltpu.get_barrier_semaphore()
    total = 0
    for device, cond in peers:
        if cond is None:
            pl.semaphore_signal(barrier, inc=1, device_id=device, device_id_type=MESH)
            total = total + 1
        else:

            @pl.when(cond)
            def _(device=device):
                pl.semaphore_signal(barrier, inc=1, device_id=device, device_id_type=MESH)

            total = total + cond.astype(jnp.int32)
    pl.semaphore_wait(barrier, total)


def near_peers():
    z, y, x, g = place()
    return [
        (dev(z, y, 1 - x, g), None), (dev(z, 1 - y, x, g), None), (dev(z, y, x, 1 - g), None),
        (dev(jnp.minimum(z + 1, 3), y, x, g), z < 3), (dev(jnp.maximum(z - 1, 0), y, x, g), z > 0),
    ]


def all_peers():
    z, y, x, g = place()
    me = lax.axis_index("dp")
    return [((lax.rem(me + k, 16), g), None) for k in range(1, 16)] + [(dev(z, y, x, 1 - g), None)]


def gather_steps(links, arrays, low, lag1=2, lag2=4):
    z, y, x, g = place()
    items = []
    nearest = jnp.clip(z, low, low + 1)
    bases = [(links.reserve(2), links.reserve(2)) for _ in PIECES]
    for zz in (nearest, 2 * low + 1 - nearest):
        for (kind, lo, n, half), (b_up, b_down) in zip(PIECES, bases):

            def here(yy, xx, first, count, zz=zz, kind=kind):
                return rows_of(arrays[kind], kind, zz, yy, xx, g, first, count)

            c = {"zz": zz}

            def add(name, ref, device, sem=None, c=c):
                c[name] = links.copy(ref, ref, device, sem)

            own = here(y, x, lo, n)
            add("up", own, dev(jnp.minimum(z + 1, 3), y, x, g), b_up + zz - low)
            add("down", own, dev(jnp.maximum(z - 1, 0), y, x, g), b_down + zz - low)
            add("x", own, dev(z, y, 1 - x, g))
            add("y", own, dev(z, 1 - y, x, g))
            add("p", own, dev(z, y, x, 1 - g))
            add("a", here(y, 1 - x, lo, half), dev(z, 1 - y, x, g))
            add("b", here(1 - y, x, lo + half, n - half), dev(z, y, 1 - x, g))
            add("px", here(y, 1 - x, lo, n), dev(z, y, x, 1 - g))
            add("py", here(1 - y, x, lo, n), dev(z, y, x, 1 - g))
            add("pa", here(1 - y, 1 - x, lo, half), dev(z, y, x, 1 - g))
            add("pb", here(1 - y, 1 - x, lo + half, n - half), dev(z, y, x, 1 - g))
            items.append(c)

    def first(c):
        zz = c["zz"]
        pl.when(z > zz)(c["up"].wait_recv)
        pl.when(z < zz)(c["down"].wait_recv)
        links.start(c["up"], (z >= zz) & (z < 3))
        links.start(c["down"], (z <= zz) & (z > 0))
        for k in ("x", "y", "p"):
            links.start(c[k])

    def second(c):
        c["x"].wait_recv()
        links.start(c["a"])
        links.start(c["px"])
        c["y"].wait_recv()
        links.start(c["b"])
        links.start(c["py"])

    def third(c):
        c["a"].wait_recv()
        links.start(c["pa"])
        c["b"].wait_recv()
        links.start(c["pb"])

    n = len(items)
    steps = []
    for t in range(n + lag2):

        def step(t=t):
            if t < n:
                first(items[t])
            if 0 <= t - lag1 < n:
                second(items[t - lag1])
            if 0 <= t - lag2 < n:
                third(items[t - lag2])

        steps.append(step)

    def end():
        for c in items:
            for k in ("p", "px", "py", "pa", "pb"):
                c[k].wait_recv()

    return steps, end


def gather_kernel(win_sh, wout_sh, tok_s, mem_s, aux_s, win, wout, tok, mem, aux, ss, rs, ls):
    z, y, x, g = place()
    me = lax.axis_index("dp")
    links = Links(ss, rs)
    near = [
        pltpu.make_async_copy(win_sh, rows_of(win, "i", z, y, x, g, 0, 272), ls.at[0]),
        pltpu.make_async_copy(wout_sh, rows_of(wout, "o", z, y, x, g, 0, 112), ls.at[1]),
    ]
    moves = ((tok_s, tok), (aux_s, aux), (mem_s, mem))
    own = [pltpu.make_async_copy(s.at[me], t.at[me], ls.at[2 + k]) for k, (s, t) in enumerate(moves)]
    for c in near + own:
        c.start()
    greet(all_peers())
    for c in near:
        c.wait()
    queue = []
    for s, t in moves:
        for k in range(1, 16):
            to = lax.rem(me + k, 16)
            queue.append(links.copy(s.at[to], t.at[me], (to, g)))
    steps, ends = [], []
    for low in (0, 2):
        more, end = gather_steps(links, {"i": win, "o": wout}, low)
        steps += more
        ends.append(end)
    per = -(-len(queue) // len(steps))
    for k, step in enumerate(steps):
        step()
        for c in queue[k * per : (k + 1) * per]:
            links.start(c)
    for c in queue:
        c.wait_recv()
    for end in ends:
        end()
    for c in own:
        c.wait()
    links.drain()


def sums_kernel(win_g, wout_g, dtok, dmem, part_in, part_out, btok, bmem, own, got, gx, gy, fin, gz, final, ss, rs, ls):
    z, y, x, g = place()
    me = lax.axis_index("dp")
    links = Links(ss, rs)
    moves = ((dmem, bmem), (dtok, btok))
    mine = [pltpu.make_async_copy(s.at[me], t.at[me], ls.at[k]) for k, (s, t) in enumerate(moves)]
    for c in mine:
        c.start()
    greet(all_peers())
    queue = []
    for s, t in moves:
        for k in range(1, 16):
            to = lax.rem(me + k, 16)
            queue.append(links.copy(s.at[to], t.at[me], (to, g)))
    arrays = {"i": win_g, "o": wout_g}
    order = [(zz, k) for zz in (3, 0, 2, 1) for k in range(len(PIECES))]
    cols = ((y, x), (y, 1 - x), (1 - y, x), (1 - y, 1 - x))
    tot = sum(p[2] for p in PIECES)
    items = []
    for zz, k in order:
        kind, lo, n, half = PIECES[k]
        base = zz * tot + sum(p[2] for p in PIECES[:k])
        at = lambda ref, c, off, m, base=base: ref.at[c, pl.ds(base + off, m)]
        it = {"zz": zz, "n": n, "half": half, "base": base, "kind": kind, "lo": lo}
        it["load"], it["pair"] = [], []
        for c, (yy, xx) in enumerate(cols):
            it["load"].append(
                pltpu.make_async_copy(
                    rows_of(arrays[kind], kind, zz, yy, xx, g, lo, n), at(own, c, 0, n), ls.at[2 + 4 * len(items) + c]
                )
            )
            it["pair"].append(
                links.copy(
                    rows_of(arrays[kind], kind, zz, yy, xx, 1 - g, lo, n), at(got, c, 0, n), dev(z, y, x, 1 - g)
                )
            )
        nx, ny = dev(z, y, 1 - x, g), dev(z, 1 - y, x, g)
        it["x1"] = [links.copy(at(own, c, 0, half), at(gx, s, 0, half), nx) for s, c in ((0, 1), (1, 3))]
        it["y1"] = [links.copy(at(own, c, half, n - half), at(gy, s, half, n - half), ny) for s, c in ((0, 2), (1, 3))]
        it["y2"] = links.copy(at(own, 2, 0, half), at(fin, 0, 0, half), ny)
        it["x2"] = links.copy(at(own, 1, half, n - half), at(fin, 0, half, n - half), nx)
        whole = at(own, 0, 0, n)
        it["up"] = links.copy(whole, at(gz, 0, 0, n), dev(jnp.minimum(z + 1, 3), y, x, g))
        it["down"] = links.copy(whole, at(gz, 1, 0, n), dev(jnp.maximum(z - 1, 0), y, x, g))
        items.append(it)

    def add(dst, c, src, s, it, off, m):
        rows = pl.ds(it["base"] + off, m)
        dst[c, rows, :] = (dst[c, rows, :].astype(jnp.float32) + src[s, rows, :].astype(jnp.float32)).astype(jnp.bfloat16)

    def stage0(it):
        for c in it["load"]:
            c.start()
        for c in it["pair"]:
            links.start(c)

    def stage1(it):
        for c in (3, 1, 2, 0):
            it["load"][c].wait()
            it["pair"][c].wait_recv()
            add(own, c, got, c, it, 0, it["n"])
            if c == 3:
                links.start(it["x1"][1])
                links.start(it["y1"][1])
            if c == 1:
                links.start(it["x1"][0])
            if c == 2:
                links.start(it["y1"][0])

    def stage2(it):
        half, rest = it["half"], it["n"] - it["half"]
        it["x1"][1].wait_recv()
        add(own, 2, gx, 1, it, 0, half)
        links.start(it["y2"])
        it["y1"][1].wait_recv()
        add(own, 1, gy, 1, it, half, rest)
        links.start(it["x2"])
        it["x1"][0].wait_recv()
        add(own, 0, gx, 0, it, 0, half)
        it["y1"][0].wait_recv()
        add(own, 0, gy, 0, it, half, rest)

    def stage3(it):
        zz, n, half = it["zz"], it["n"], it["half"]
        it["y2"].wait_recv()
        it["x2"].wait_recv()
        add(own, 0, fin, 0, it, 0, n)

        @pl.when(z < zz)
        def _():
            @pl.when(z > 0)
            def _():
                it["up"].wait_recv()
                add(own, 0, gz, 0, it, 0, n)

            it["up"].start()

        @pl.when(z > zz)
        def _():
            @pl.when(z < 3)
            def _():
                it["down"].wait_recv()
                add(own, 0, gz, 1, it, 0, n)

            it["down"].start()

        links.sent.append((it["up"], z < zz))
        links.sent.append((it["down"], z > zz))

        @pl.when(z == zz)
        def _():
            rows = pl.ds(it["base"], n)
            total = own[0, rows, :].astype(jnp.float32)
            if zz > 0:
                it["up"].wait_recv()
                total += gz[0, rows, :].astype(jnp.float32)
            if zz < 3:
                it["down"].wait_recv()
                total += gz[1, rows, :].astype(jnp.float32)
            into = part_in if it["kind"] == "i" else part_out
            into[it["lo"] : it["lo"] + n, :] = total

    lags = (0, 2, 4, 6)
    stages = (stage0, stage1, stage2, stage3)
    n = len(items)
    per = -(-len(queue) // n)
    for t in range(n + lags[-1]):
        for lag, stage in zip(lags, stages):
            if 0 <= t - lag < n:
                stage(items[t - lag])
        for c in queue[t * per : (t + 1) * per]:
            links.start(c)
    for c in queue:
        c.wait_recv()
    for c in mine:
        c.wait()
    links.drain()


def vmem_call(kernel, out_shape, scratch, **kw):
    return pl.pallas_call(
        kernel,
        out_shape=out_shape,
        scratch_shapes=scratch,
        compiler_params=pltpu.CompilerParams(vmem_limit_bytes=VMEM_BYTES),
        **kw,
    )


def sds(shape, dtype=jnp.bfloat16):
    return jax.ShapeDtypeStruct(shape, dtype)


WEIGHTS = [
    pltpu.VMEM((6 * HEAD_COLS, WIDTH), jnp.bfloat16), pltpu.VMEM((2 * HEAD_COLS, WIDTH), jnp.bfloat16),
    pltpu.SemaphoreType.DMA((2,)),
]


def load_weights(win, wout, win_v, wout_v, sem):
    copies = [
        pltpu.make_async_copy(win.at[0 : 6 * HEAD_COLS], win_v, sem.at[0]),
        pltpu.make_async_copy(wout.at[0 : 2 * HEAD_COLS], wout_v, sem.at[1]),
    ]
    for c in copies:
        c.start()
    return copies


def anywhere():
    return pl.BlockSpec(memory_space=pl.ANY)


def whole():
    return pl.BlockSpec(memory_space=pltpu.VMEM)


def gather_all(win_sh, wout_sh, tok_s, mem_s, aux_s):
    any_ = pl.BlockSpec(memory_space=pl.ANY)
    sems = 45 + 2 * 22 * len(PIECES)
    return pl.pallas_call(
        gather_kernel,
        out_shape=(
            sds((32 * win_sh.shape[0], WIDTH)), sds((32 * wout_sh.shape[0], WIDTH)),
            sds(tok_s.shape), sds(mem_s.shape), sds(aux_s.shape),
        ),
        in_specs=[whole(), whole(), any_, any_, any_],
        out_specs=(any_,) * 5,
        scratch_shapes=[
            pltpu.SemaphoreType.DMA((sems,)), pltpu.SemaphoreType.DMA((sems,)), pltpu.SemaphoreType.DMA((5,)),
        ],
        compiler_params=pltpu.CompilerParams(
            collective_id=1, has_side_effects=True, vmem_limit_bytes=VMEM_BYTES
        ),
    )(win_sh, wout_sh, tok_s, mem_s, aux_s)


def sum_all(g_win, g_wout, d_tok, d_mem):
    any_ = pl.BlockSpec(memory_space=pl.ANY)
    tot = 4 * sum(p[2] for p in PIECES)
    items = 4 * len(PIECES)
    sems = 30 + 12 * items
    vm = lambda k: pltpu.VMEM((k, tot, WIDTH), jnp.bfloat16)
    return pl.pallas_call(
        sums_kernel,
        out_shape=(
            sds((272, WIDTH), jnp.float32), sds((112, WIDTH), jnp.float32), sds(d_tok.shape), sds(d_mem.shape),
        ),
        in_specs=[any_] * 4,
        out_specs=(whole(), whole(), any_, any_),
        scratch_shapes=[
            vm(4), vm(4), vm(2), vm(2), vm(1), vm(2), pltpu.VMEM((8, 128), jnp.float32),
            pltpu.SemaphoreType.DMA((sems,)), pltpu.SemaphoreType.DMA((sems,)),
            pltpu.SemaphoreType.DMA((2 + 4 * items,)),
        ],
        compiler_params=pltpu.CompilerParams(
            collective_id=2, has_side_effects=True, vmem_limit_bytes=VMEM_BYTES
        ),
    )(g_win, g_wout, d_tok, d_mem)


def forward_call(tok, mem, aux, win, wout, gains, table):
    f32 = jnp.float32

    def kernel(tok, mem, aux, win, wout, *refs):
        win_v, wout_v, sem = refs[-3:]
        loads = load_weights(win, wout, win_v, wout_v, sem)
        for c in loads:
            c.wait()
        attention_forward(tok, mem, aux, win_v, wout_v, *refs[:-3], step=lambda name, p: None)

    return vmem_call(
        kernel,
        (
            sds((SEQ, 3 * HEAD_COLS)), sds((SEQ, HEAD_COLS)), sds((SEQ, 128), f32), sds((SEQ, WIDTH), f32),
            sds((SEQ, HEAD_COLS)), sds((SEQ, 2 * HEAD_COLS)), sds((SEQ, HEAD_COLS)), sds((SEQ, 128), f32),
            sds((SEQ, WIDTH), f32),
        ),
        WEIGHTS,
        in_specs=[whole(), whole(), whole(), anywhere(), anywhere(), whole(), whole()],
    )(tok, mem, aux, win, wout, gains, table)


def ff_call(x2, cot, keep, gains, win, wout):
    f32 = jnp.float32
    step = 256
    n = FF // step
    at = lambda block, first: pl.BlockSpec((step, WIDTH), lambda c: (first + c, 0))
    full = lambda rows, cols: pl.BlockSpec((rows, cols), lambda c: (0, 0))
    gate0, down0 = 6 * HEAD_COLS // step, 2 * HEAD_COLS // step
    return vmem_call(
        ff_kernel,
        (
            sds((SEQ, WIDTH)), sds((SEQ, WIDTH), f32), sds((1, WIDTH), f32), sds(win.shape), sds(wout.shape),
        ),
        [
            pltpu.VMEM((SEQ, WIDTH), jnp.bfloat16), pltpu.VMEM((SEQ, WIDTH), jnp.bfloat16),
            pltpu.VMEM((SEQ, WIDTH), f32), pltpu.VMEM((SEQ, WIDTH), f32),
            pltpu.VMEM((2, 3, step, WIDTH), jnp.bfloat16), pltpu.SemaphoreType.DMA((2, 3)),
        ],
        grid=(n,),
        in_specs=[
            full(SEQ, WIDTH), full(SEQ, WIDTH), full(SEQ, 128), full(3, WIDTH),
            at(step, gate0), at(step, gate0 + n), at(step, down0),
        ],
        out_specs=(full(SEQ, WIDTH), full(SEQ, WIDTH), full(1, WIDTH), anywhere(), anywhere()),
    )(x2, cot, keep, gains, win, win, wout)


def backward_call(tok, mem, aux, win, wout, gains, table, kept, g2, g_win, g_wout):
    f32 = jnp.float32

    def kernel(_, __, tok, mem, aux, win, wout, *refs):
        ins, (g_win, g_wout), outs = refs[:11], refs[11:13], refs[13:17]
        scratch, (held, put_sem, win_v, wout_v, sem) = refs[17:21], refs[21:]
        loads = load_weights(win, wout, win_v, wout_v, sem)
        puts = []

        def emit(block, value):
            held[block] = value.astype(jnp.bfloat16)
            into, first = (g_win, block) if block < 6 else (g_wout, block - 6)
            rows = pl.ds(first * HEAD_COLS, HEAD_COLS)
            puts.append(pltpu.make_async_copy(held.at[block], into.at[rows], put_sem.at[block]))
            puts[-1].start()

        for c in loads:
            c.wait()
        attention_backward(
            tok, mem, aux, win_v, wout_v, *ins, *outs, *scratch, emit=emit, step=lambda name, p: None
        )
        for c in puts:
            c.wait()

    return vmem_call(
        kernel,
        (
            sds(g_win.shape), sds(g_wout.shape), sds((SEQ, WIDTH)), sds((SEQ, WIDTH)),
            sds((2, WIDTH), f32), sds((16, 384), f32),
        ),
        [
            pltpu.VMEM((SEQ, HEAD_COLS), jnp.bfloat16), pltpu.VMEM((SEQ, 3 * HEAD_COLS), jnp.bfloat16),
            pltpu.VMEM((2, 128, SEQ), f32), pltpu.VMEM((2, 128, 384), f32),
            pltpu.VMEM((8, HEAD_COLS, WIDTH), jnp.bfloat16), pltpu.SemaphoreType.DMA((8,)),
        ]
        + WEIGHTS,
        in_specs=[anywhere()] * 2 + [whole()] * 3 + [anywhere()] * 2 + [whole()] * 11,
        out_specs=(anywhere(), anywhere()) + (whole(),) * 4,
        input_output_aliases={0: 0, 1: 1},
    )(g_win, g_wout, tok, mem, aux, win, wout, gains, table, *kept, g2)


def body(
    tokens, memory, segments, memory_segments, row_source, denoiser_modes, sentinel, cotangent, w_in, w_out,
    norm_gains, rel_bias, rows_in, cols_in, rows_out, cols_out, sq_gains, sq_rel,
):
    n_index = lax.axis_size("dp")
    n_group = lax.axis_size("group")
    my_group = lax.axis_index("group")
    my_place = lax.axis_index(("dp", "group"))
    half_rows = tokens.shape[0]
    rows_dev = cotangent.shape[0]
    assert rows_dev == 1
    boxed = n_index == 16 and n_group == 2
    slot_table = row_source.reshape(n_index, n_group)
    sources = lax.dynamic_index_in_dim(slot_table, my_group, 1, keepdims=False) - my_group * half_rows
    own_row = lax.dynamic_index_in_dim(row_source, my_place, 0, keepdims=False)
    own_mode = lax.dynamic_index_in_dim(denoiser_modes, own_row, 0, keepdims=False)

    spot = jnp.arange(128) % HSIZE
    both = jnp.where(spot < SEGS, segments[sources][:, :, None], memory_segments[sources][:, :, None])
    aux_s = ((both == spot % SEGS) & (spot < 2 * SEGS)).astype(jnp.bfloat16)
    win_sh = w_in.T.astype(jnp.bfloat16)
    wout_sh = w_out.astype(jnp.bfloat16)
    tok_s, mem_s = tokens[sources], memory[sources]
    if boxed:
        win, wout, tok, mem, aux = gather_all(win_sh, wout_sh, tok_s, mem_s, aux_s)
    else:
        win = lax.all_gather(win_sh, ("dp", "group"), axis=0, tiled=True)
        wout = lax.all_gather(wout_sh, ("dp", "group"), axis=0, tiled=True)
        tok, mem, aux = (
            lax.all_to_all(v, "dp", split_axis=0, concat_axis=0, tiled=True) for v in (tok_s, mem_s, aux_s)
        )
    tok, mem, aux = tok.reshape(SEQ, WIDTH), mem.reshape(SEQ, WIDTH), aux.reshape(SEQ, 128)

    buckets = bucket_table(SEQ, BUCKETS)
    hot = (buckets[:256, None] == np.arange(BUCKETS)[None, :]).astype(np.float32)
    lane = np.arange(256)
    dist_f = np.where(lane <= 128, 128 - lane, 384 - lane)
    hot_f = hot[dist_f]
    rel_row = lax.dynamic_index_in_dim(rel_bias, own_mode, 0, keepdims=False)
    rel_pad = jnp.pad(rel_row.T, ((0, 4), (0, 0)))
    tables = jnp.dot(rel_pad, np.concatenate([hot_f, hot], axis=0).T, precision=PRECISE)
    table_f, table_b = tables[:, :256], tables[:, 256:]

    kept = forward_call(tok, mem, aux, win, wout, norm_gains, table_f)
    x2 = kept[8]
    keep = jnp.broadcast_to((1 - sentinel).astype(jnp.float32).reshape(SEQ, 1), (SEQ, 128))
    mixed, g2, d_gain_three, g_win, g_wout = ff_call(
        x2, cotangent.reshape(SEQ, WIDTH), keep, norm_gains, win, wout
    )
    g_win, g_wout, d_mem, d_tok, d_gains, dist = backward_call(
        tok, mem, aux, win, wout, norm_gains, table_b, kept[:8], g2, g_win, g_wout
    )
    d_tok, d_mem = d_tok.reshape(tok_s.shape), d_mem.reshape(mem_s.shape)
    if boxed:
        part_in_t, part_out, back_tok, back_mem = sum_all(g_win, g_wout, d_tok, d_mem)
    else:
        back_tok, back_mem = (
            lax.all_to_all(v, "dp", split_axis=0, concat_axis=0, tiled=True) for v in (d_tok, d_mem)
        )
        part_in_t, part_out = (
            lax.psum_scatter(v.astype(jnp.float32), ("dp", "group"), scatter_dimension=0, tiled=True)
            for v in (g_win, g_wout)
        )
    part_in = part_in_t.T
    inverse = jnp.argsort(sources)
    merge = lambda v: v.reshape(n_index, SEQ // n_index, WIDTH)[inverse]
    d_tokens_out, d_memory_out = merge(back_tok), merge(back_mem)
    hot_dist = np.concatenate([hot, np.repeat(np.eye(BUCKETS, dtype=np.float32)[-1:], 128, axis=0)], axis=0)
    d_rel_row = jnp.dot(dist[:HEADS], hot_dist, precision=PRECISE).T
    mode_hot = (own_mode == jnp.arange(MODES)).astype(jnp.float32)
    d_rel = mode_hot[:, None, None] * d_rel_row[None]

    col_count = part_in.shape[1]
    col_ids = my_place * col_count + jnp.arange(col_count)
    col_hot = jnp.stack(
        [
            col_ids < 3 * HEAD_COLS,
            (col_ids >= 3 * HEAD_COLS) & (col_ids < 6 * HEAD_COLS),
            col_ids >= 6 * HEAD_COLS,
        ],
        axis=0,
    ).astype(jnp.float32)
    sq_in = part_in * part_in
    row_terms = jnp.einsum("mc,dc->md", col_hot, sq_in, precision=PRECISE)
    row_count = part_out.shape[0]
    row_ids = my_place * row_count + jnp.arange(row_count)
    row_hot = jnp.stack(
        [
            row_ids < HEAD_COLS,
            (row_ids >= HEAD_COLS) & (row_ids < 2 * HEAD_COLS),
            row_ids >= 2 * HEAD_COLS,
        ],
        axis=0,
    ).astype(jnp.float32)
    sq_out = part_out * part_out
    rows_out_new = DECAY_RATE * rows_out + (1 - DECAY_RATE) * jnp.mean(sq_out, axis=1)
    col_terms = jnp.einsum("mr,rd->md", row_hot, sq_out, precision=PRECISE)
    row_totals = jnp.dot(row_hot, rows_out_new, precision=PRECISE)
    gain_grads = jnp.concatenate([d_gains, d_gain_three], axis=0)
    row_sums, col_sums, total_sums, g_gains, g_rel = lax.psum(
        (row_terms, col_terms, row_totals, gain_grads, d_rel), ("dp", "group")
    )
    in_counts = jnp.array([3 * HEAD_COLS, 3 * HEAD_COLS, 2 * FF], jnp.float32)
    out_counts = jnp.array([HEAD_COLS, HEAD_COLS, FF], jnp.float32)
    rows_in_new = DECAY_RATE * rows_in + (1 - DECAY_RATE) * row_sums / in_counts[:, None]
    cols_in_new = DECAY_RATE * cols_in + (1 - DECAY_RATE) * jnp.mean(sq_in, axis=0)
    row_scaled = rows_in_new / jnp.mean(rows_in_new, axis=1, keepdims=True)
    in_scale = jnp.einsum("mc,md->dc", col_hot, row_scaled, precision=PRECISE) * cols_in_new[None, :]
    new_in = w_in - STEP_SIZE * part_in * lax.rsqrt(in_scale)
    cols_out_new = DECAY_RATE * cols_out + (1 - DECAY_RATE) * col_sums / out_counts[:, None]
    row_mean = jnp.dot(row_hot.T, total_sums / out_counts, precision=PRECISE)
    col_pick = jnp.einsum("mr,md->rd", row_hot, cols_out_new, precision=PRECISE)
    new_out = w_out - STEP_SIZE * part_out * lax.rsqrt((rows_out_new / row_mean)[:, None] * col_pick)
    sq_gains_new = DECAY_RATE * sq_gains + (1 - DECAY_RATE) * g_gains * g_gains
    new_gains = norm_gains - PLAIN_STEP * g_gains * lax.rsqrt(sq_gains_new)
    sq_rel_new = DECAY_RATE * sq_rel + (1 - DECAY_RATE) * g_rel * g_rel
    new_rel = rel_bias - PLAIN_STEP * g_rel * lax.rsqrt(sq_rel_new)
    return (
        mixed[None], d_tokens_out, d_memory_out, part_in, part_out, g_gains, g_rel, new_in, new_out, new_gains,
        new_rel, rows_in_new, cols_in_new, rows_out_new, cols_out_new, sq_gains_new, sq_rel_new,
    )


def solution(mesh):
    both = ("dp", "group")
    row_in = P("group", "dp", None)
    seg_in = P("group", "dp")
    return jax.shard_map(
        body,
        mesh=mesh,
        in_specs=(
            row_in, row_in, seg_in, seg_in, P(), P(), P(both, None), P(both, None, None), P(None, both),
            P(both, None), P(), P(), P(), P(both), P(both), P(), P(), P(),
        ),
        out_specs=(
            P(both, None, None), row_in, row_in, P(None, both), P(both, None), P(), P(), P(None, both),
            P(both, None), P(), P(), P(), P(both), P(both), P(), P(), P(),
        ),
        check_vma=False,
    )
```

```python
import functools

import jax
import jax.numpy as jnp
import numpy as np
from jax import lax
from jax.experimental import pallas as pl
from jax.experimental.pallas import tpu as pltpu
from jax.sharding import PartitionSpec as P

HEADS = 12
HSIZE = 64
FF = 2048
BUCKETS = 32
MODES = 3
SEGS = 4
SEQ = 512
WIDTH = 768
EPSILON = 1e-06
MASKED = -1e30
DECAY_RATE = 0.9
STEP_SIZE = 0.01
PLAIN_STEP = 0.15
GELU_SCALE = 0.7978845608028654
PRECISE = lax.Precision.HIGHEST
MESH = pl.DeviceIdType.MESH
VMEM_BYTES = 60 << 20


def bucket_table(length, buckets):
    exact_span = buckets // 2
    distances = np.arange(length)
    safe_spans = np.maximum(distances, 1)
    logged = np.floor(
        np.log(safe_spans / exact_span) / np.log(128.0 / exact_span) * (buckets - exact_span)
    )
    far_bucket = np.minimum(exact_span + logged, buckets - 1)
    return np.where(distances < exact_span, distances, far_bucket).astype(np.int32)


def nt(a, b):
    return lax.dot_general(a, b, (((1,), (1,)), ((), ())), preferred_element_type=jnp.float32)


def nn(a, b):
    return lax.dot_general(a, b, (((1,), (0,)), ((), ())), preferred_element_type=jnp.float32)


def tn(a, b):
    return lax.dot_general(a, b, (((0,), (0,)), ((), ())), preferred_element_type=jnp.float32)


def inv_rms(values):
    return lax.rsqrt(jnp.mean(values * values, axis=-1, keepdims=True) + EPSILON)


def rms_back(values, gain, grad):
    inv = inv_rms(values)
    scaled = grad * gain
    along = jnp.mean(scaled * values, axis=-1, keepdims=True)
    return inv * scaled - values * (inv * inv * inv * along), jnp.sum(
        grad * (values * inv), axis=0, keepdims=True
    )


def lane_of(shape):
    return lax.broadcasted_iota(jnp.int32, shape, 1)


def ext_masks(aux, first):
    lane = lane_of(aux.shape)
    spot = lane & 63
    documents = (spot >= first) & (spot < first + SEGS)
    hot = jnp.where(documents, aux.astype(jnp.float32), 0.0)
    against = jnp.where(documents, (1.0 - aux.astype(jnp.float32)) * MASKED, 0.0)
    return hot, against


def halves(tile, ext, even):
    lane = lane_of(tile.shape)
    return jnp.where((lane < HSIZE) if even else (lane >= HSIZE), tile, ext)


def pick(first, second, lane):
    return jnp.where(lane < HSIZE, first, second)


def tile_cols(p, base=0):
    return pl.ds(pl.multiple_of(p * 128 + base, 128), 128)


def attend_pair(p, q_tile, k_tile, v_tile, k_ext, q_ext, att_ref, lse_ref, bias_of):
    lane = lane_of((128, 128))
    ones = jnp.ones((SEQ, 128), jnp.bfloat16)
    sides = []
    for even in (True, False):
        sides.append(
            (
                halves(q_tile, q_ext, even),
                halves(k_tile, k_ext, even),
                halves(v_tile, ones, even),
                None if bias_of is None else bias_of(2 * p + (0 if even else 1)),
            )
        )
    for i in range(SEQ // 128):
        lo = 0 if bias_of is None else max(0, i - 2) * 128
        hi = SEQ if bias_of is None else (i + 1) * 128
        outs, tops = [], []
        for qe, ke, ve, bias in sides:
            s = nt(qe[i * 128 : (i + 1) * 128], ke[lo:hi])
            if bias is not None:
                near, far = bias
                parts = [near[:, 128:]] if i == 0 else [near] if i == 1 else [far, near]
                s = s + (parts[0] if len(parts) == 1 else jnp.concatenate(parts, axis=1))
            top = jnp.max(s, axis=1, keepdims=True)
            e = jnp.exp(s - top).astype(jnp.bfloat16)
            outs.append(nn(e, ve[lo:hi]))
            tops.append(top)
        att = pick(outs[0], outs[1], lane)
        total = pltpu.roll(pick(outs[1], outs[0], lane), HSIZE, 1)
        rows = pl.ds(i * 128, 128)
        att_ref[rows, tile_cols(p)] = (att / total).astype(jnp.bfloat16)
        lse = pick(tops[0], tops[1], lane) + jnp.log(total)
        kept = lse_ref[rows, :]
        first = jnp.sum(jnp.where(lane == 0, lse, 0.0), axis=1, keepdims=True)
        second = jnp.sum(jnp.where(lane == HSIZE, lse, 0.0), axis=1, keepdims=True)
        lse_ref[rows, :] = jnp.where(
            lane == 2 * p, first, jnp.where(lane == 2 * p + 1, second, kept)
        )


def forward_bias(table_ref):
    def bias_of(h):
        row = table_ref[pl.ds(h, 1), :]
        near = pltpu.roll(jnp.broadcast_to(row, (128, 256)), 0, 1, stride=1, stride_axis=0)
        lane = lax.broadcasted_iota(jnp.int32, (128, 256), 1)
        sub = lax.broadcasted_iota(jnp.int32, (128, 256), 0)
        near = jnp.where(lane - 128 > sub, MASKED, near)
        far = jnp.broadcast_to(row[:, :1], (128, 128))
        return near, far

    return bias_of


def back_bias(table_ref):
    def bias_of(h):
        row = table_ref[pl.ds(h, 1), :]
        near = pltpu.roll(jnp.broadcast_to(row, (128, 256)), 0, 1, stride=1, stride_axis=0)
        lane = lax.broadcasted_iota(jnp.int32, (128, 256), 1)
        sub = lax.broadcasted_iota(jnp.int32, (128, 256), 0)
        near = jnp.where(lane < sub, MASKED, near)
        far = jnp.broadcast_to(row[:, 128:129], (128, 128))
        return near, far

    return bias_of


def by_distance(near):
    rows = 64
    while rows >= 8:
        near = near[:rows] + pltpu.roll(near[rows:], 256 - rows, 1)
        rows //= 2
    sub = lax.broadcasted_iota(jnp.int32, (8, 256), 0)
    for bit in (4, 2, 1):
        near = jnp.where((sub & bit) != 0, pltpu.roll(near, 256 - bit, 1), near)
    return near


def split_cols(values, base, lane, count):
    rest, out = values, jnp.zeros((values.shape[0], 128), jnp.float32)
    for k in range(count):
        part = rest.astype(jnp.bfloat16).astype(jnp.float32)
        out = jnp.where((lane & 63) == base + k, part, out)
        rest = rest - part
    return out


def back_pair(
    p, q_tile, k_tile, v_tile, do_tile, att_tile, lse_all, hot, against, bias_of, dq_acc, rel_acc, dist_ref
):
    lane = lane_of((SEQ, 128))
    lane1 = lane_of((128, 128))
    spot = lane & 63
    ones3 = jnp.where((spot >= 8) & (spot < 11), 1.0, 0.0)
    k_ext = (hot + ones3).astype(jnp.bfloat16)
    v_ext = jnp.where((spot >= 0) & (spot < 2), 1.0, 0.0).astype(jnp.bfloat16)
    product = do_tile.astype(jnp.float32) * att_tile.astype(jnp.float32)
    sides = []
    for even in (True, False):
        h = 2 * p + (0 if even else 1)
        lse = jnp.sum(jnp.where(lane == h, lse_all, 0.0), axis=1, keepdims=True)
        own = (lane < HSIZE) if even else (lane >= HSIZE)
        delta = jnp.sum(jnp.where(own, product, 0.0), axis=1, keepdims=True)
        q_ext = (against + split_cols(-lse, 8, lane, 3)).astype(jnp.bfloat16)
        d_ext = split_cols(-delta, 0, lane, 2).astype(jnp.bfloat16)
        sides.append(
            (
                halves(q_tile, q_ext, even),
                halves(k_tile, k_ext, even),
                halves(v_tile, v_ext, even),
                halves(do_tile, d_ext, even),
                None if bias_of is None else bias_of(h),
            )
        )
    dks, dvs = [], []
    dq_acc[...] = jnp.zeros_like(dq_acc)
    if bias_of is not None:
        rel_acc[...] = jnp.zeros_like(rel_acc)
    for j in range(SEQ // 128):
        lo = 0 if bias_of is None else j * 128
        hi = SEQ if bias_of is None else min(SEQ, (j + 3) * 128)
        dk2, dv2 = [], []
        for n, (qe, ke, ve, de, bias) in enumerate(sides):
            s = nt(ke[j * 128 : (j + 1) * 128], qe[lo:hi])
            if bias is not None:
                near, far = bias
                s = s + (
                    near[:, :128] if hi - lo == 128 else near if hi - lo == 256
                    else jnp.concatenate([near, far], axis=1)
                )
            w = jnp.exp(s)
            dv2.append(nn(w.astype(jnp.bfloat16), do_tile[lo:hi]))
            ds = w * nt(ve[j * 128 : (j + 1) * 128], de[lo:hi])
            if bias is not None:
                rel_acc[n, :, : hi - lo] += ds
            ds = ds.astype(jnp.bfloat16)
            dk2.append(nn(ds, q_tile[lo:hi]))
            dq_acc[n, :, lo:hi] += tn(k_tile[j * 128 : (j + 1) * 128], ds)
        dks.append(pick(dk2[0], dk2[1], lane1))
        dvs.append(pick(dv2[0], dv2[1], lane1))
    if bias_of is not None:
        for n in range(2):
            near = by_distance(rel_acc[n, :, :256])
            dist_ref[pl.ds(2 * p + n, 1), :] = jnp.concatenate(
                [
                    jnp.sum(near, axis=0, keepdims=True),
                    jnp.sum(rel_acc[n, :, 256:], axis=0, keepdims=True),
                ],
                axis=1,
            )
    sub = lax.broadcasted_iota(jnp.int32, (128, SEQ), 0)
    dq = jnp.where(sub < HSIZE, dq_acc[0], dq_acc[1]).T * HSIZE**-0.5
    return dq, jnp.concatenate(dks, axis=0), jnp.concatenate(dvs, axis=0)


HEAD_COLS = HEADS * HSIZE


def attention_forward(
    tok, mem, aux, win, wout, gains, table, qkv, att1, lse1, x1, qc, kvc, att2, lse2, x2, step
):
    x0 = tok[...].astype(jnp.float32)
    a1 = (x0 * inv_rms(x0) * gains[0:1, :]).astype(jnp.bfloat16)
    for k in range(3):
        cols = slice(k * HEAD_COLS, (k + 1) * HEAD_COLS)
        got = nt(a1, win[cols, :])
        if k == 0:
            got = got.astype(jnp.bfloat16).astype(jnp.float32) * HSIZE**-0.5
        qkv[:, cols] = got.astype(jnp.bfloat16)
    lse1[...] = jnp.zeros_like(lse1)
    lse2[...] = jnp.zeros_like(lse2)

    @pl.loop(0, HEADS // 2)
    def _(p):
        hot, against = ext_masks(aux[...], 0)
        attend_pair(
            p, qkv[:, tile_cols(p)], qkv[:, tile_cols(p, HEAD_COLS)], qkv[:, tile_cols(p, 2 * HEAD_COLS)],
            hot.astype(jnp.bfloat16), against.astype(jnp.bfloat16), att1, lse1, forward_bias(table),
        )
        step("self", p)

    x1[...] = tok[...].astype(jnp.float32) + nn(att1[...], wout[0:HEAD_COLS, :])
    a2 = (x1[...] * inv_rms(x1[...]) * gains[1:2, :]).astype(jnp.bfloat16)
    got = nt(a2, win[3 * HEAD_COLS : 4 * HEAD_COLS, :])
    qc[...] = (got.astype(jnp.bfloat16).astype(jnp.float32) * HSIZE**-0.5).astype(jnp.bfloat16)
    for k in range(2):
        kvc[:, k * HEAD_COLS : (k + 1) * HEAD_COLS] = nt(
            mem[...], win[(4 + k) * HEAD_COLS : (5 + k) * HEAD_COLS, :]
        ).astype(jnp.bfloat16)

    @pl.loop(0, HEADS // 2)
    def _(p):
        _, against = ext_masks(aux[...], 0)
        hot = pltpu.roll(ext_masks(aux[...], SEGS)[0], 128 - SEGS, 1)
        attend_pair(
            p, qc[:, tile_cols(p)], kvc[:, tile_cols(p)], kvc[:, tile_cols(p, HEAD_COLS)],
            hot.astype(jnp.bfloat16), against.astype(jnp.bfloat16), att2, lse2, None,
        )
        step("cross", p)

    x2[...] = x1[...] + nn(att2[...], wout[HEAD_COLS : 2 * HEAD_COLS, :])


def ff_kernel(
    x2, cot, keep, gains, w_gate, w_up, w_down, mixed, g2, d_gain, g_win, g_wout, a3, e3, acc, da3, held, sem
):
    c = pl.program_id(0)
    slot = lax.rem(c, 2)
    rows = w_gate.shape[0]
    first = pl.multiple_of(c * rows, rows)
    puts = [
        pltpu.make_async_copy(held.at[slot, 0], g_win.at[pl.ds(6 * HEAD_COLS + first, rows)], sem.at[slot, 0]),
        pltpu.make_async_copy(held.at[slot, 1], g_win.at[pl.ds(6 * HEAD_COLS + FF + first, rows)], sem.at[slot, 1]),
        pltpu.make_async_copy(held.at[slot, 2], g_wout.at[pl.ds(2 * HEAD_COLS + first, rows)], sem.at[slot, 2]),
    ]

    @pl.when(c >= 2)
    def _():
        for put in puts:
            put.wait()

    @pl.when(c == 0)
    def _():
        a3[...] = (x2[...] * inv_rms(x2[...]) * gains[2:3, :]).astype(jnp.bfloat16)
        e3[...] = (cot[...].astype(jnp.float32) * keep[:, 0:1]).astype(jnp.bfloat16)
        acc[...] = x2[...]
        da3[...] = jnp.zeros_like(da3)

    gate = nt(a3[...], w_gate[...])
    up = nt(a3[...], w_up[...])
    dh = nt(e3[...], w_down[...])
    cube = 0.044715 * gate * gate
    inner = jnp.tanh(GELU_SCALE * gate * (1.0 + cube))
    half = 0.5 * (1.0 + inner)
    gelu = gate * half
    slope = half + 0.5 * gate * (1.0 - inner * inner) * (GELU_SCALE * (1.0 + 3.0 * cube))
    hidden = (gelu * up).astype(jnp.bfloat16)
    d_gate = (dh * up * slope).astype(jnp.bfloat16)
    d_up = (dh * gelu).astype(jnp.bfloat16)
    acc[...] += nn(hidden, w_down[...])
    held[slot, 0] = tn(d_gate, a3[...]).astype(jnp.bfloat16)
    held[slot, 1] = tn(d_up, a3[...]).astype(jnp.bfloat16)
    held[slot, 2] = tn(hidden, e3[...]).astype(jnp.bfloat16)
    for put in puts:
        put.start()
    da3[...] += nn(d_gate, w_gate[...]) + nn(d_up, w_up[...])

    @pl.when(c == pl.num_programs(0) - 1)
    def _():
        mixed[...] = acc[...].astype(jnp.bfloat16)
        part, gain = rms_back(x2[...], gains[2:3, :], da3[...])
        g2[...] = cot[...].astype(jnp.float32) * keep[:, 0:1] + part
        d_gain[...] = gain
        for k in range(3):
            for other in range(2):
                pltpu.make_async_copy(held.at[other, k], g_wout.at[0:rows], sem.at[other, k]).wait()


def attention_backward(
    tok, mem, aux, win, wout, gains, table, qkv, att1, lse1, x1, qc, kvc, att2, lse2, g2,
    d_mem, d_tok, d_gains, dist, do, dqkv, dq_acc, rel_acc, emit, step,
):
    e2 = g2[...].astype(jnp.bfloat16)
    do[...] = nt(e2, wout[HEAD_COLS : 2 * HEAD_COLS, :]).astype(jnp.bfloat16)
    emit(7, tn(att2[...], e2))

    @pl.loop(0, HEADS // 2)
    def _(p):
        _, against = ext_masks(aux[...], 0)
        hot = pltpu.roll(ext_masks(aux[...], SEGS)[0], 128 - SEGS, 1)
        dq, dk, dv = back_pair(
            p, qc[:, tile_cols(p)], kvc[:, tile_cols(p)], kvc[:, tile_cols(p, HEAD_COLS)], do[:, tile_cols(p)],
            att2[:, tile_cols(p)], lse2[...], hot, against, None, dq_acc, rel_acc, dist,
        )
        dqkv[:, tile_cols(p)] = dq.astype(jnp.bfloat16)
        dqkv[:, tile_cols(p, HEAD_COLS)] = dk.astype(jnp.bfloat16)
        dqkv[:, tile_cols(p, 2 * HEAD_COLS)] = dv.astype(jnp.bfloat16)
        step("cross", p)

    a2 = (x1[...] * inv_rms(x1[...]) * gains[1:2, :]).astype(jnp.bfloat16)
    for k in range(3):
        cols = slice(k * HEAD_COLS, (k + 1) * HEAD_COLS)
        emit(3 + k, tn(dqkv[:, cols], a2 if k == 0 else mem[...]))
    d_mem[...] = nn(
        dqkv[:, HEAD_COLS : 3 * HEAD_COLS], win[4 * HEAD_COLS : 6 * HEAD_COLS, :]
    ).astype(jnp.bfloat16)
    da2 = nn(dqkv[:, 0:HEAD_COLS], win[3 * HEAD_COLS : 4 * HEAD_COLS, :])
    part, gain = rms_back(x1[...], gains[1:2, :], da2)
    d_gains[1:2, :] = gain
    g2[...] += part
    e1 = g2[...].astype(jnp.bfloat16)
    do[...] = nt(e1, wout[0:HEAD_COLS, :]).astype(jnp.bfloat16)
    emit(6, tn(att1[...], e1))
    step("middle", 0)

    @pl.loop(0, HEADS // 2)
    def _(p):
        hot, against = ext_masks(aux[...], 0)
        dq, dk, dv = back_pair(
            p, qkv[:, tile_cols(p)], qkv[:, tile_cols(p, HEAD_COLS)], qkv[:, tile_cols(p, 2 * HEAD_COLS)],
            do[:, tile_cols(p)], att1[:, tile_cols(p)], lse1[...], hot, against, back_bias(table), dq_acc, rel_acc, dist,
        )
        dqkv[:, tile_cols(p)] = dq.astype(jnp.bfloat16)
        dqkv[:, tile_cols(p, HEAD_COLS)] = dk.astype(jnp.bfloat16)
        dqkv[:, tile_cols(p, 2 * HEAD_COLS)] = dv.astype(jnp.bfloat16)
        step("self", p)

    x0 = tok[...].astype(jnp.float32)
    a1 = (x0 * inv_rms(x0) * gains[0:1, :]).astype(jnp.bfloat16)
    for k in range(3):
        cols = slice(k * HEAD_COLS, (k + 1) * HEAD_COLS)
        emit(k, tn(dqkv[:, cols], a1))
    da1 = nn(dqkv[...], win[0 : 3 * HEAD_COLS, :])
    part, gain = rms_back(x0, gains[0:1, :], da1)
    d_gains[0:1, :] = gain
    d_tok[...] = (g2[...] + part).astype(jnp.bfloat16)


SHARE = {"i": 272, "o": 112}
PIECES = (
    ("i", 0, 64, 32), ("i", 64, 64, 32), ("i", 128, 64, 32), ("i", 192, 80, 48),
    ("o", 0, 64, 32), ("o", 64, 48, 16),
)


REGION = 400


def place():
    dp = lax.axis_index("dp")
    return dp // 4, (dp // 2) % 2, dp % 2, lax.axis_index("group")


def dev(z, y, x, g):
    return ((z * 2 + y) * 2 + x, g)


def rows_of(ref, kind, zz, yy, xx, gg, lo, n):
    share = ((zz * 2 + yy) * 2 + xx) * 2 + gg
    return ref.at[pl.ds(pl.multiple_of(share * SHARE[kind] + lo, 16), n)]


class Links:
    def __init__(self, send_sem, recv_sem, count=0):
        self.send_sem, self.recv_sem, self.count, self.sent = send_sem, recv_sem, count, []

    def reserve(self, n):
        self.count += n
        return self.count - n

    def copy(self, src, dst, device, sem=None):
        k = self.reserve(1) if sem is None else sem
        return pltpu.make_async_remote_copy(
            src_ref=src, dst_ref=dst, send_sem=self.send_sem.at[k], recv_sem=self.recv_sem.at[k],
            device_id=device, device_id_type=MESH,
        )

    def start(self, copy, cond=None):
        if cond is None:
            copy.start()
        else:
            pl.when(cond)(copy.start)
        self.sent.append((copy, cond))

    def drain(self):
        for copy, cond in self.sent:
            if cond is None:
                copy.wait_send()
            else:
                pl.when(cond)(copy.wait_send)
        self.sent = []


def greet(peers):
    barrier = pltpu.get_barrier_semaphore()
    total = 0
    for device, cond in peers:
        if cond is None:
            pl.semaphore_signal(barrier, inc=1, device_id=device, device_id_type=MESH)
            total = total + 1
        else:

            @pl.when(cond)
            def _(device=device):
                pl.semaphore_signal(barrier, inc=1, device_id=device, device_id_type=MESH)

            total = total + cond.astype(jnp.int32)
    pl.semaphore_wait(barrier, total)


def near_peers():
    z, y, x, g = place()
    return [
        (dev(z, y, 1 - x, g), None), (dev(z, 1 - y, x, g), None), (dev(z, y, x, 1 - g), None),
        (dev(jnp.minimum(z + 1, 3), y, x, g), z < 3), (dev(jnp.maximum(z - 1, 0), y, x, g), z > 0),
    ]


def all_peers():
    z, y, x, g = place()
    me = lax.axis_index("dp")
    return [((lax.rem(me + k, 16), g), None) for k in range(1, 16)] + [(dev(z, y, x, 1 - g), None)]


def gather_steps(links, arrays, low, lag1=2, lag2=4):
    z, y, x, g = place()
    items = []
    nearest = jnp.clip(z, low, low + 1)
    bases = [(links.reserve(2), links.reserve(2)) for _ in PIECES]
    for zz in (nearest, 2 * low + 1 - nearest):
        for (kind, lo, n, half), (b_up, b_down) in zip(PIECES, bases):

            def here(yy, xx, first, count, zz=zz, kind=kind):
                return rows_of(arrays[kind], kind, zz, yy, xx, g, first, count)

            c = {"zz": zz, "go_up": (z >= zz) & (z < 3), "go_down": (z <= zz) & (z > 0)}
            c["from_below"], c["from_above"] = z > zz, z < zz

            def add(name, ref, device, sem=None, c=c):
                c[name] = links.copy(ref, ref, device, sem)

            own = here(y, x, lo, n)
            add("up", own, dev(jnp.minimum(z + 1, 3), y, x, g), b_up + zz - low)
            add("down", own, dev(jnp.maximum(z - 1, 0), y, x, g), b_down + zz - low)
            add("x", own, dev(z, y, 1 - x, g))
            add("y", own, dev(z, 1 - y, x, g))
            add("p", own, dev(z, y, x, 1 - g))
            add("a", here(y, 1 - x, lo, half), dev(z, 1 - y, x, g))
            add("b", here(1 - y, x, lo + half, n - half), dev(z, y, 1 - x, g))
            add("px", here(y, 1 - x, lo, n), dev(z, y, x, 1 - g))
            add("py", here(1 - y, x, lo, n), dev(z, y, x, 1 - g))
            add("pa", here(1 - y, 1 - x, lo, half), dev(z, y, x, 1 - g))
            add("pb", here(1 - y, 1 - x, lo + half, n - half), dev(z, y, x, 1 - g))
            items.append(c)

    def first(c):
        pl.when(c["from_below"])(c["up"].wait_recv)
        pl.when(c["from_above"])(c["down"].wait_recv)
        links.start(c["up"], c["go_up"])
        links.start(c["down"], c["go_down"])
        for k in ("x", "y", "p"):
            links.start(c[k])

    def second(c):
        c["x"].wait_recv()
        links.start(c["a"])
        links.start(c["px"])
        c["y"].wait_recv()
        links.start(c["b"])
        links.start(c["py"])

    def third(c):
        c["a"].wait_recv()
        links.start(c["pa"])
        c["b"].wait_recv()
        links.start(c["pb"])

    n = len(items)
    steps = []
    for t in range(n + lag2):

        def step(t=t):
            if t < n:
                first(items[t])
            if 0 <= t - lag1 < n:
                second(items[t - lag1])
            if 0 <= t - lag2 < n:
                third(items[t - lag2])

        steps.append(step)

    def end():
        for c in items:
            for k in ("p", "px", "py", "pa", "pb"):
                c[k].wait_recv()

    return steps, end


def gather_kernel(win_sh, wout_sh, tok_s, mem_s, aux_s, win, wout, tok, mem, aux, ss, rs, ls):
    z, y, x, g = place()
    me = lax.axis_index("dp")
    links = Links(ss, rs)
    near = [
        pltpu.make_async_copy(win_sh, rows_of(win, "i", z, y, x, g, 0, 272), ls.at[0]),
        pltpu.make_async_copy(wout_sh, rows_of(wout, "o", z, y, x, g, 0, 112), ls.at[1]),
    ]
    moves = ((tok_s, tok), (aux_s, aux), (mem_s, mem))
    own = [pltpu.make_async_copy(s.at[me], t.at[me], ls.at[2 + k]) for k, (s, t) in enumerate(moves)]
    for c in near + own:
        c.start()
    greet(all_peers())
    for c in near:
        c.wait()
    queue = []
    for s, t in moves:
        for k in range(1, 16):
            to = lax.rem(me + k, 16)
            queue.append(links.copy(s.at[to], t.at[me], (to, g)))
    steps, ends = [], []
    for low in (0, 2):
        more, end = gather_steps(links, {"i": win, "o": wout}, low)
        steps += more
        ends.append(end)
    per = -(-len(queue) // len(steps))
    for k, step in enumerate(steps):
        step()
        for c in queue[k * per : (k + 1) * per]:
            links.start(c)
    for c in queue:
        c.wait_recv()
    for end in ends:
        end()
    for c in own:
        c.wait()
    links.drain()


class Sums:
    def __init__(self, win_g, wout_g, own, got, plane, fin, line, part_in, part_out, load_sem):
        self.arrays = {"i": win_g, "o": wout_g}
        self.own, self.got, self.plane, self.fin, self.line = own, got, plane, fin, line
        self.part_in, self.part_out, self.load_sem = part_in, part_out, load_sem
        self.loads, self.line_rows = 0, 0

    def batch(self, links, region, members):
        z, y, x, g = place()
        base = region * REGION
        items = []
        for zz, k in members:
            kind, lo, n, half = PIECES[k]
            at = lambda ref, c, off, m, base=base: ref.at[c, pl.ds(base + off, m)]
            it = {"zz": zz, "n": n, "half": half, "base": base, "kind": kind, "lo": lo, "line": self.line_rows}
            it["links"] = links
            it["below"], it["above"], it["z"] = z < zz, z > zz, z
            it["load"], it["pair"] = [], []
            for c, (yy, xx) in enumerate(((y, x), (y, 1 - x), (1 - y, x), (1 - y, 1 - x))):
                ref = self.arrays[kind]
                it["load"].append(
                    pltpu.make_async_copy(
                        rows_of(ref, kind, zz, yy, xx, g, lo, n), at(self.own, c, 0, n), self.load_sem.at[self.loads]
                    )
                )
                self.loads += 1
                it["pair"].append(
                    links.copy(
                        rows_of(ref, kind, zz, yy, xx, 1 - g, lo, n), at(self.got, c, 0, n), dev(z, y, x, 1 - g)
                    )
                )
            nx, ny, rest = dev(z, y, 1 - x, g), dev(z, 1 - y, x, g), n - half
            own, plane, fin = self.own, self.plane, self.fin
            it["x1"] = [links.copy(at(own, c, 0, half), at(plane, s, 0, half), nx) for s, c in ((0, 1), (1, 3))]
            it["y1"] = [links.copy(at(own, c, half, rest), at(plane, s, half, rest), ny) for s, c in ((0, 2), (1, 3))]
            it["y2"] = links.copy(at(own, 2, 0, half), at(fin, 0, 0, half), ny)
            it["x2"] = links.copy(at(own, 1, half, rest), at(fin, 0, half, rest), nx)
            there = lambda s: self.line.at[s, pl.ds(it["line"], n)]
            it["up"] = links.copy(at(own, 0, 0, n), there(0), dev(jnp.minimum(z + 1, 3), y, x, g))
            it["down"] = links.copy(at(own, 0, 0, n), there(1), dev(jnp.maximum(z - 1, 0), y, x, g))
            items.append(it)
            base += n
            self.line_rows += n
        assert base <= (region + 1) * REGION
        n = len(items)
        lag2, lag3 = 2, 4
        steps = []

        def begin():
            for it in items:
                for c in it["load"]:
                    c.start()
                for c in (3, 1, 2, 0):
                    links.start(it["pair"][c])

        steps.append(begin)
        for t in range(n + lag3):

            def step(t=t):
                if t < n:
                    self.to_core(items[t])
                if 0 <= t - lag2 < n:
                    self.to_plane(items[t - lag2])
                if 0 <= t - lag3 < n:
                    self.to_line(items[t - lag3])

            steps.append(step)
        return steps

    @staticmethod
    def add(dst, c, first, src, s, start, m):
        rows = pl.ds(first, m)
        more = src[s, pl.ds(start, m), :].astype(jnp.float32)
        dst[c, rows, :] = (dst[c, rows, :].astype(jnp.float32) + more).astype(jnp.bfloat16)

    def to_core(self, it):
        for c in (3, 1, 2, 0):
            it["load"][c].wait()
            it["pair"][c].wait_recv()
            self.add(self.own, c, it["base"], self.got, c, it["base"], it["n"])
            if c == 3:
                it["links"].start(it["x1"][1])
                it["links"].start(it["y1"][1])
            if c == 1:
                it["links"].start(it["x1"][0])
            if c == 2:
                it["links"].start(it["y1"][0])

    def to_plane(self, it):
        half, rest, base = it["half"], it["n"] - it["half"], it["base"]
        low = base + half
        it["x1"][1].wait_recv()
        self.add(self.own, 2, base, self.plane, 1, base, half)
        it["links"].start(it["y2"])
        it["y1"][1].wait_recv()
        self.add(self.own, 1, low, self.plane, 1, low, rest)
        it["links"].start(it["x2"])
        it["x1"][0].wait_recv()
        self.add(self.own, 0, base, self.plane, 0, base, half)
        it["y1"][0].wait_recv()
        self.add(self.own, 0, low, self.plane, 0, low, rest)

    def to_line(self, it):
        z, below, above = it["z"], it["below"], it["above"]
        zz, n, base, line = it["zz"], it["n"], it["base"], it["line"]
        it["y2"].wait_recv()
        it["x2"].wait_recv()
        self.add(self.own, 0, base, self.fin, 0, base, n)
        up, down = it["up"], it["down"]
        if zz > 0:

            @pl.when(below)
            def _():
                @pl.when(z > 0)
                def _():
                    up.wait_recv()
                    self.add(self.own, 0, base, self.line, 0, line, n)

                up.start()

            it["links"].sent.append((up, below))
        if zz < 3:

            @pl.when(above)
            def _():
                @pl.when(z < 3)
                def _():
                    down.wait_recv()
                    self.add(self.own, 0, base, self.line, 1, line, n)

                down.start()

            it["links"].sent.append((down, above))

        @pl.when(z == zz)
        def _():
            total = self.own[0, pl.ds(base, n), :].astype(jnp.float32)
            if zz > 0:
                up.wait_recv()
                total += self.line[0, pl.ds(line, n), :].astype(jnp.float32)
            if zz < 3:
                down.wait_recv()
                total += self.line[1, pl.ds(line, n), :].astype(jnp.float32)
            into = self.part_in if it["kind"] == "i" else self.part_out
            into[it["lo"] : it["lo"] + n, :] = total


def total_steps(links, ref, room):
    z, y, x, g = place()
    hops = [dev(z, y, x, 1 - g), dev(z, y, 1 - x, g), dev(z, 1 - y, x, g)]
    copies = [links.copy(ref, room.at[k], to) for k, to in enumerate(hops)]
    over = [links.copy(ref, room.at[2 + k], dev(lax.rem(z + k, 4), y, x, g)) for k in (1, 2, 3)]

    def hop(k):
        def step():
            if k > 0:
                copies[k - 1].wait()
                ref[...] = ref[...] + room[k - 1]
            copies[k].start()

        return step

    def spread():
        copies[2].wait()
        ref[...] = ref[...] + room[2]
        for c in over:
            c.start()

    def finish():
        for c in over:
            c.wait()
        mine = ref[...]
        total = jnp.zeros_like(mine)
        for plane in range(4):
            back = lax.rem(z - plane + 4, 4)
            term = jnp.where(back == 0, mine, jnp.zeros_like(mine))
            for k in (1, 2, 3):
                term = jnp.where(back == k, room[2 + k], term)
            total = total + term
        ref[...] = total

    return [hop(0), hop(1), hop(2), spread, finish]


def vmem_call(kernel, out_shape, scratch, **kw):
    return pl.pallas_call(
        kernel,
        out_shape=out_shape,
        scratch_shapes=scratch,
        compiler_params=pltpu.CompilerParams(vmem_limit_bytes=VMEM_BYTES),
        **kw,
    )


def sds(shape, dtype=jnp.bfloat16):
    return jax.ShapeDtypeStruct(shape, dtype)


WEIGHTS = [
    pltpu.VMEM((6 * HEAD_COLS, WIDTH), jnp.bfloat16), pltpu.VMEM((2 * HEAD_COLS, WIDTH), jnp.bfloat16),
    pltpu.SemaphoreType.DMA((2,)),
]


def load_weights(win, wout, win_v, wout_v, sem):
    copies = [
        pltpu.make_async_copy(win.at[0 : 6 * HEAD_COLS], win_v, sem.at[0]),
        pltpu.make_async_copy(wout.at[0 : 2 * HEAD_COLS], wout_v, sem.at[1]),
    ]
    for c in copies:
        c.start()
    return copies


def anywhere():
    return pl.BlockSpec(memory_space=pl.ANY)


def whole():
    return pl.BlockSpec(memory_space=pltpu.VMEM)


def gather_all(win_sh, wout_sh, tok_s, mem_s, aux_s):
    any_ = pl.BlockSpec(memory_space=pl.ANY)
    sems = 45 + 2 * 22 * len(PIECES)
    return pl.pallas_call(
        gather_kernel,
        out_shape=(
            sds((32 * win_sh.shape[0], WIDTH)), sds((32 * wout_sh.shape[0], WIDTH)),
            sds(tok_s.shape), sds(mem_s.shape), sds(aux_s.shape),
        ),
        in_specs=[whole(), whole(), any_, any_, any_],
        out_specs=(any_,) * 5,
        scratch_shapes=[
            pltpu.SemaphoreType.DMA((sems,)), pltpu.SemaphoreType.DMA((sems,)), pltpu.SemaphoreType.DMA((5,)),
        ],
        compiler_params=pltpu.CompilerParams(
            collective_id=1, has_side_effects=True, vmem_limit_bytes=VMEM_BYTES
        ),
    )(win_sh, wout_sh, tok_s, mem_s, aux_s)


def spread_steps(calls, steps):
    out, done = [], 0
    for k in range(calls):
        upto = -(-len(steps) * (k + 1) // calls)
        out.append(steps[done:upto])
        done = upto
    return out


def run(steps):
    for s in steps:
        s()


def block_of(ids, edges):
    return (ids >= edges[0]).astype(jnp.int32) + (ids >= edges[1]).astype(jnp.int32)


IN_EDGES = (3 * HEAD_COLS, 6 * HEAD_COLS)
OUT_EDGES = (HEAD_COLS, 2 * HEAD_COLS)


def block_sums(part_in_t, part_out, rows_out, first_in, first_out):
    sq_in, sq_out = part_in_t * part_in_t, part_out * part_out
    block_in = block_of(first_in + lax.broadcasted_iota(jnp.int32, (sq_in.shape[0], 1), 0), IN_EDGES)
    block_out = block_of(first_out + lax.broadcasted_iota(jnp.int32, (sq_out.shape[0], 1), 0), OUT_EDGES)
    rows_new = DECAY_RATE * rows_out + (1 - DECAY_RATE) * jnp.mean(sq_out, axis=1, keepdims=True)
    lane = lax.broadcasted_iota(jnp.int32, (1, WIDTH), 1)
    lines = [jnp.sum(jnp.where(block_in == k, sq_in, 0.0), axis=0, keepdims=True) for k in range(3)]
    lines += [jnp.sum(jnp.where(block_out == k, sq_out, 0.0), axis=0, keepdims=True) for k in range(3)]
    totals = jnp.zeros((1, WIDTH), jnp.float32)
    for k in range(3):
        total = jnp.sum(jnp.where(block_out == k, rows_new, 0.0), axis=0, keepdims=True)
        totals = jnp.where(lane == k, total, totals)
    return jnp.concatenate(lines + [totals, jnp.zeros((1, WIDTH), jnp.float32)], axis=0)


def prep_kernel(
    ids, row_source, modes, tokens, memory, segments, msegments, w_in, w_out, rel_bias, hot, sentinel,
    tok_s, mem_s, aux_s, win_sh, wout_sh, tables, keep, flip, seg_t, mseg_t,
):
    half_rows, length = tokens.shape[0], tokens.shape[1]
    groups, group, where = ids[0], ids[1], ids[2]
    flip[:, 0 : w_in.shape[1]] = w_in[...]
    win_sh[...] = flip[...].T[0 : w_in.shape[1], :].astype(jnp.bfloat16)
    wout_sh[...] = w_out[...].astype(jnp.bfloat16)
    for source, out in ((segments, seg_t), (msegments, mseg_t)):
        out[0:half_rows, 0:length] = source[...].astype(jnp.float32)
        out[...] = out[...].T
    lane = lax.broadcasted_iota(jnp.int32, (length, 128), 1)
    spot = (lane & (HSIZE - 1)).astype(jnp.float32)

    @pl.loop(0, half_rows)
    def _(i):
        source = row_source[i * groups + group] - group * half_rows
        tok_s[i] = tokens[source]
        mem_s[i] = memory[source]
        col = jnp.sum(jnp.where(lane == source, seg_t[0:length, :], 0.0), axis=1, keepdims=True)
        mcol = jnp.sum(jnp.where(lane == source, mseg_t[0:length, :], 0.0), axis=1, keepdims=True)
        same = ((spot < SEGS) & (spot == col)) | ((spot >= SEGS) & (spot < 2 * SEGS) & (spot - SEGS == mcol))
        aux_s[i] = jnp.where(same, 1.0, 0.0).astype(jnp.bfloat16)

    mode = modes[row_source[where]]
    tables[...] = jnp.zeros_like(tables)
    tables[0:HEADS, :] = lax.dot_general(
        rel_bias[mode], hot[...], (((0,), (0,)), ((), ())), precision=PRECISE, preferred_element_type=jnp.float32
    )
    kept = (1 - sentinel[...]).astype(jnp.float32)
    keep[...] = jnp.broadcast_to(kept, (128, SEQ)).T


def prep_call(ids, row_source, modes, tokens, memory, segments, msegments, w_in, w_out, rel_bias, hot, sentinel):
    f32 = jnp.float32
    scalars = pl.BlockSpec(memory_space=pltpu.SMEM)
    half_rows, length = tokens.shape[0], tokens.shape[1]
    padded = -(-w_in.shape[1] // 128) * 128
    return vmem_call(
        prep_kernel,
        (
            sds(tokens.shape), sds(memory.shape), sds((half_rows, length, 128)), sds((w_in.shape[1], WIDTH)),
            sds(w_out.shape), sds((16, 512), f32), sds((SEQ, 128), f32),
        ),
        [pltpu.VMEM((WIDTH, padded), f32), pltpu.VMEM((128, 128), f32), pltpu.VMEM((128, 128), f32)],
        in_specs=[scalars] * 3 + [whole()] * 9,
    )(ids, row_source, modes, tokens, memory, segments, msegments, w_in, w_out, rel_bias, hot, sentinel)


def update_kernel(
    ids, row_source, part_in_t, part_out, sums, early, back_tok, back_mem, w_in, w_out, gains, rel_bias, rows_in,
    cols_in, rows_out, cols_out, sq_gains, sq_rel,
    d_tokens, d_memory, grad_in, grad_out, grad_gains, grad_rel, new_in, new_out, new_gains, new_rel, rows_in_new,
    cols_in_new, rows_out_new, cols_out_new, sq_gains_new, sq_rel_new, flip,
):
    half_rows = back_tok.shape[0]
    groups, group, where = ids[0], ids[1], ids[2]

    @pl.loop(0, half_rows)
    def _(i):
        source = row_source[i * groups + group] - group * half_rows
        d_tokens[source] = back_tok[i]
        d_memory[source] = back_mem[i]

    n_in, n_out = w_in.shape[1], w_out.shape[0]
    flip[0:n_in, :] = part_in_t[...]
    part_in = flip[...].T[:, 0:n_in]
    grad_in[...] = part_in
    cols_new = DECAY_RATE * cols_in[...] + (1 - DECAY_RATE) * jnp.mean(part_in * part_in, axis=0, keepdims=True)
    cols_in_new[...] = cols_new
    rows_new, scaled = [], []
    for k, count in enumerate((3 * HEAD_COLS, 3 * HEAD_COLS, 2 * FF)):
        row = DECAY_RATE * rows_in[k : k + 1, :] + (1 - DECAY_RATE) * (sums[k : k + 1, :] / count)
        rows_in_new[k : k + 1, :] = row
        scaled.append(row / jnp.mean(row, axis=1, keepdims=True))
    upright = jnp.concatenate(scaled + [jnp.zeros((128 - 3, WIDTH), jnp.float32)], axis=0).T
    block_in = block_of(where * n_in + lax.broadcasted_iota(jnp.int32, (1, n_in), 1), IN_EDGES)
    spread = jnp.where(block_in == 0, upright[:, 0:1], jnp.where(block_in == 1, upright[:, 1:2], upright[:, 2:3]))
    new_in[...] = w_in[...] - STEP_SIZE * part_in * lax.rsqrt(spread * cols_new)

    p_out = part_out[...]
    grad_out[...] = p_out
    out_rows = DECAY_RATE * rows_out[...] + (1 - DECAY_RATE) * jnp.mean(p_out * p_out, axis=1, keepdims=True)
    rows_out_new[...] = out_rows
    block_out = block_of(where * n_out + lax.broadcasted_iota(jnp.int32, (n_out, 1), 0), OUT_EDGES)
    scale = jnp.zeros((n_out, WIDTH), jnp.float32)
    for k, count in enumerate((HEAD_COLS, HEAD_COLS, FF)):
        col = DECAY_RATE * cols_out[k : k + 1, :] + (1 - DECAY_RATE) * (sums[3 + k : 4 + k, :] / count)
        cols_out_new[k : k + 1, :] = col
        mean = sums[6:7, k : k + 1] / count
        scale = jnp.where(block_out == k, (out_rows / mean) * col, scale)
    new_out[...] = w_out[...] - STEP_SIZE * p_out * lax.rsqrt(scale)

    g = early[0:3, :]
    grad_gains[...] = g
    sq = DECAY_RATE * sq_gains[...] + (1 - DECAY_RATE) * g * g
    sq_gains_new[...] = sq
    new_gains[...] = gains[...] - PLAIN_STEP * g * lax.rsqrt(sq)
    for k in range(MODES):
        both = jnp.concatenate([early[8:24, k * 128 : (k + 1) * 128], jnp.zeros((112, 128), jnp.float32)], axis=0)
        g = both.T[0:BUCKETS, 0:HEADS]
        grad_rel[k] = g
        sq = DECAY_RATE * sq_rel[k] + (1 - DECAY_RATE) * g * g
        sq_rel_new[k] = sq
        new_rel[k] = rel_bias[k] - PLAIN_STEP * g * lax.rsqrt(sq)


def update_call(ids, row_source, *arrays):
    f32 = jnp.float32
    scalars = pl.BlockSpec(memory_space=pltpu.SMEM)
    (part_in_t, part_out, sums, early, back_tok, back_mem, w_in, w_out, gains, rel_bias) = arrays[:10]
    n_in, n_out = w_in.shape[1], w_out.shape[0]
    three = sds((3, WIDTH), f32)
    rel = sds(rel_bias.shape, f32)
    return vmem_call(
        update_kernel,
        (
            sds(back_tok.shape), sds(back_mem.shape), sds(w_in.shape, f32), sds(w_out.shape, f32), three, rel,
            sds(w_in.shape, f32), sds(w_out.shape, f32), three, rel, three, sds((1, n_in), f32), sds((n_out, 1), f32),
            three, three, rel,
        ),
        [pltpu.VMEM((-(-n_in // 128) * 128, WIDTH), f32)],
        in_specs=[scalars] * 2 + [whole()] * len(arrays),
    )(ids, row_source, *arrays)


def forward_call(tok, mem, aux, win, wout, gains, table):
    f32 = jnp.float32

    def kernel(tok, mem, aux, win, wout, *refs):
        win_v, wout_v, sem = refs[-3:]
        loads = load_weights(win, wout, win_v, wout_v, sem)
        for c in loads:
            c.wait()
        attention_forward(tok, mem, aux, win_v, wout_v, *refs[:-3], step=lambda name, p: None)

    return vmem_call(
        kernel,
        (
            sds((SEQ, 3 * HEAD_COLS)), sds((SEQ, HEAD_COLS)), sds((SEQ, 128), f32), sds((SEQ, WIDTH), f32),
            sds((SEQ, HEAD_COLS)), sds((SEQ, 2 * HEAD_COLS)), sds((SEQ, HEAD_COLS)), sds((SEQ, 128), f32),
            sds((SEQ, WIDTH), f32),
        ),
        WEIGHTS,
        in_specs=[whole(), whole(), whole(), anywhere(), anywhere(), whole(), whole()],
    )(tok, mem, aux, win, wout, gains, table)


def ff_call(x2, cot, keep, gains, win, wout):
    f32 = jnp.float32
    step = 256
    n = FF // step
    at = lambda block, first: pl.BlockSpec((step, WIDTH), lambda c: (first + c, 0))
    full = lambda rows, cols: pl.BlockSpec((rows, cols), lambda c: (0, 0))
    gate0, down0 = 6 * HEAD_COLS // step, 2 * HEAD_COLS // step
    return vmem_call(
        ff_kernel,
        (
            sds((SEQ, WIDTH)), sds((SEQ, WIDTH), f32), sds((1, WIDTH), f32), sds(win.shape), sds(wout.shape),
        ),
        [
            pltpu.VMEM((SEQ, WIDTH), jnp.bfloat16), pltpu.VMEM((SEQ, WIDTH), jnp.bfloat16),
            pltpu.VMEM((SEQ, WIDTH), f32), pltpu.VMEM((SEQ, WIDTH), f32),
            pltpu.VMEM((2, 3, step, WIDTH), jnp.bfloat16), pltpu.SemaphoreType.DMA((2, 3)),
        ],
        grid=(n,),
        in_specs=[
            full(SEQ, WIDTH), full(SEQ, WIDTH), full(SEQ, 128), full(3, WIDTH),
            at(step, gate0), at(step, gate0 + n), at(step, down0),
        ],
        out_specs=(full(SEQ, WIDTH), full(SEQ, WIDTH), full(1, WIDTH), anywhere(), anywhere()),
    )(x2, cot, keep, gains, win, win, wout)


def rel_sums(dist, hot_dist, mode_rows):
    by_bucket = jnp.dot(dist, hot_dist, precision=PRECISE, preferred_element_type=jnp.float32)
    return jnp.concatenate([by_bucket * mode_rows[k : k + 1, :] for k in range(MODES)], axis=1)


def backward_kernel(boxed, _, __, tok, mem, aux, win, wout, *refs):
    ins, (hot_dist, mode_rows, gain_three, rows_out) = refs[:11], refs[11:15]
    refs = refs[15:]
    if boxed:
        (g_win, g_wout, part_in, part_out, sums, early, btok, bmem), refs = refs[:8], refs[8:]
        (d_mem, d_tok, d_gains, dist), refs = refs[:4], refs[4:]
    else:
        (g_win, g_wout, d_mem, d_tok, early), refs = refs[:5], refs[5:]
        (d_gains, dist), refs = refs[:2], refs[2:]
    scratch, (held, put_sem, win_v, wout_v, sem), refs = refs[:4], refs[4:9], refs[9:]
    loads = load_weights(win, wout, win_v, wout_v, sem)
    puts, settled = [], []

    def settle(upto):
        while len(settled) < upto:
            puts[len(settled)].wait()
            settled.append(True)

    def emit(block, value):
        k = len(puts)
        settle(k - 2)
        held[k % 3] = value.astype(jnp.bfloat16)
        into, first = (g_win, block) if block < 6 else (g_wout, block - 6)
        puts.append(
            pltpu.make_async_copy(
                held.at[k % 3], into.at[pl.ds(first * HEAD_COLS, HEAD_COLS)], put_sem.at[k]
            )
        )
        puts[k].start()

    dist[...] = jnp.zeros_like(dist)
    step = lambda name, p: None
    if boxed:
        own, got, plane, fin, line, room, early_room, ss, rs, load_sem = refs
        z, y, x, g = place()
        me = lax.axis_index("dp")
        pos = SEQ // 16
        greet(all_peers())
        work = Sums(g_win, g_wout, own, got, plane, fin, line, part_in, part_out, load_sem)
        n = len(PIECES)
        groups = (
            (0, [(3, k) for k in range(n)]),
            (1, [(2, k) for k in range(n)]),
            (0, [(1, k) for k in range(2, n)] + [(0, k) for k in range(4, n)]),
            (1, [(0, k) for k in range(4)] + [(1, k) for k in range(2)]),
        )
        links, batches = [Links(ss, rs)], []
        for region, members in groups:
            batches.append(work.batch(links[-1], region, members))
            links.append(Links(ss, rs, links[-1].count))
        back = links[-1]

        def row_copies(src, dst):
            copies = []
            for k in range(1, 16):
                to = lax.rem(me + k, 16)
                here = src.at[pl.ds(pl.multiple_of(to * pos, 16), pos)]
                copies.append(back.copy(here, dst.at[me], (to, g)))
            return copies

        def keep_rows(src, dst, k):
            return pltpu.make_async_copy(src.at[pl.ds(pl.multiple_of(me * pos, 16), pos)], dst.at[me], sem.at[2 + k])

        mem_copies, tok_copies = row_copies(d_mem, bmem), row_copies(d_tok, btok)
        kept_mem, kept_tok = keep_rows(d_mem, bmem, 0), keep_rows(d_tok, btok, 1)

        def begin_third():
            links[0].drain()
            batches[2][0]()

        first = spread_steps(6, batches[0][1:])
        second = spread_steps(6, batches[1][1:] + [begin_third] + batches[2][1:6])
        rest = batches[2][6:]
        batches[0][0]()

        def step(name, p):
            if name == "middle":
                kept_mem.start()
                settle(len(puts))
                batches[1][0]()
                return
            for k, part in enumerate(first if name == "cross" else second):

                @pl.when(p == k)
                def _(part=part, k=k):
                    if name == "self":
                        for c in mem_copies[3 * k : 3 * k + 3]:
                            back.start(c)
                    run(part)

    for c in loads:
        c.wait()
    attention_backward(
        tok, mem, aux, win_v, wout_v, *ins, d_mem, d_tok, d_gains, dist, *scratch, emit=emit, step=step
    )
    early[...] = jnp.zeros_like(early)
    early[0:2, :] = d_gains[0:2, :]
    early[2:3, :] = gain_three[...]
    early[8:24, 0:384] = rel_sums(dist[...], hot_dist[...], mode_rows[...])
    settle(len(puts))
    if not boxed:
        return
    kept_tok.start()
    links[1].drain()
    batches[3][0]()
    run(rest)
    turns = total_steps(back, early, early_room)
    last = batches[3][1:]
    for k, part in enumerate(last):
        part()
        if k < len(turns):
            turns[k]()
        for c in tok_copies[3 * k : 3 * k + 3]:
            back.start(c)
    where = me * 2 + g
    sums[...] = block_sums(part_in[...], part_out[...], rows_out[...], where * 272, where * 112)
    run(total_steps(back, sums, room))
    for c in mem_copies + tok_copies:
        c.wait_recv()
    kept_mem.wait()
    kept_tok.wait()
    for k in range(2, 5):
        links[k].drain()


def backward_call(boxed, tok, mem, aux, win, wout, gains, table, kept, g2, g_win, g_wout, *more):
    f32, bf16 = jnp.float32, jnp.bfloat16
    vm, dma = pltpu.VMEM, pltpu.SemaphoreType.DMA
    row = sds((SEQ, WIDTH))
    rows = [vm((SEQ, WIDTH), bf16), vm((SEQ, WIDTH), bf16)]
    scratch = [vm((8, WIDTH), f32), vm((16, 384), f32)]
    scratch += [
        vm((SEQ, HEAD_COLS), bf16), vm((SEQ, 3 * HEAD_COLS), bf16), vm((2, 128, SEQ), f32), vm((2, 128, 384), f32),
        vm((3, HEAD_COLS, WIDTH), bf16), dma((8,)),
    ]
    scratch += WEIGHTS[:2] + [dma((4,))]
    outs = [sds(g_win.shape), sds(g_wout.shape)]
    if boxed:
        items, both = 4 * len(PIECES), 2 * REGION
        chunks = sds((16, SEQ // 16, WIDTH))
        outs += [sds((272, WIDTH), f32), sds((112, WIDTH), f32), sds((8, WIDTH), f32), sds((24, WIDTH), f32), chunks, chunks]
        specs = (anywhere(),) * 2 + (whole(),) * 4 + (anywhere(),) * 2
        scratch = rows + scratch
        scratch += [
            vm((4, both, WIDTH), bf16), vm((4, both, WIDTH), bf16), vm((2, both, WIDTH), bf16),
            vm((1, both, WIDTH), bf16), vm((2, 4 * 384, WIDTH), bf16), vm((6, 8, WIDTH), f32), vm((6, 24, WIDTH), f32),
            dma((12 * items + 48,)), dma((12 * items + 48,)), dma((4 * items,)),
        ]
    else:
        outs += [row, row, sds((24, WIDTH), f32)]
        specs = (anywhere(),) * 2 + (whole(),) * 3
    extra = dict(collective_id=2, has_side_effects=True) if boxed else {}
    return pl.pallas_call(
        functools.partial(backward_kernel, boxed),
        out_shape=tuple(outs),
        scratch_shapes=scratch,
        in_specs=[anywhere()] * 2 + [whole()] * 3 + [anywhere()] * 2 + [whole()] * 15,
        out_specs=specs,
        input_output_aliases={0: 0, 1: 1},
        compiler_params=pltpu.CompilerParams(vmem_limit_bytes=VMEM_BYTES, **extra),
    )(g_win, g_wout, tok, mem, aux, win, wout, gains, table, *kept, g2, *more)


def body(
    tokens, memory, segments, memory_segments, row_source, denoiser_modes, sentinel, cotangent, w_in, w_out,
    norm_gains, rel_bias, rows_in, cols_in, rows_out, cols_out, sq_gains, sq_rel,
):
    n_index = lax.axis_size("dp")
    n_group = lax.axis_size("group")
    my_group = lax.axis_index("group")
    my_place = lax.axis_index(("dp", "group"))
    half_rows = tokens.shape[0]
    rows_dev = cotangent.shape[0]
    assert rows_dev == 1
    boxed = n_index == 16 and n_group == 2
    ids = jnp.stack([jnp.int32(n_group), my_group, my_place])
    buckets = bucket_table(SEQ, BUCKETS)
    hot = (buckets[:256, None] == np.arange(BUCKETS)[None, :]).astype(np.float32)
    lane = np.arange(256)
    dist_f = np.where(lane <= 128, 128 - lane, 384 - lane)
    hot_t = jnp.asarray(np.concatenate([hot[dist_f], hot], axis=0).T)
    tok_s, mem_s, aux_s, win_sh, wout_sh, tables, keep = prep_call(
        ids, row_source, denoiser_modes, tokens, memory, segments, memory_segments, w_in, w_out, rel_bias, hot_t, sentinel
    )
    if boxed:
        win, wout, tok, mem, aux = gather_all(win_sh, wout_sh, tok_s, mem_s, aux_s)
    else:
        win = lax.all_gather(win_sh, ("dp", "group"), axis=0, tiled=True)
        wout = lax.all_gather(wout_sh, ("dp", "group"), axis=0, tiled=True)
        tok, mem, aux = (
            lax.all_to_all(v, "dp", split_axis=0, concat_axis=0, tiled=True) for v in (tok_s, mem_s, aux_s)
        )
    tok, mem, aux = tok.reshape(SEQ, WIDTH), mem.reshape(SEQ, WIDTH), aux.reshape(SEQ, 128)

    table_f, table_b = tables[:, :256], tables[:, 256:]
    kept = forward_call(tok, mem, aux, win, wout, norm_gains, table_f)
    x2 = kept[8]
    mixed, g2, d_gain_three, g_win, g_wout = ff_call(
        x2, cotangent.reshape(SEQ, WIDTH), keep, norm_gains, win, wout
    )
    hot_dist = np.concatenate([hot, np.repeat(np.eye(BUCKETS, dtype=np.float32)[-1:], 128, axis=0)], axis=0)
    hot_dist = jnp.asarray(np.pad(hot_dist, ((0, 0), (0, 128 - BUCKETS))))
    own_mode = denoiser_modes[row_source[my_place]]
    mode_rows = jnp.broadcast_to((own_mode == jnp.arange(8)).astype(jnp.float32)[:, None], (8, 128))
    rows_out_up = rows_out.reshape(-1, 1)
    result = backward_call(
        boxed, tok, mem, aux, win, wout, norm_gains, table_b, kept[:8], g2, g_win, g_wout,
        hot_dist, mode_rows, d_gain_three, rows_out_up,
    )
    if boxed:
        _, _, part_in_t, part_out, sums, early, back_tok, back_mem = result
    else:
        g_win, g_wout, d_mem, d_tok, early = result
        back_tok, back_mem = (
            lax.all_to_all(v.reshape(tok_s.shape), "dp", split_axis=0, concat_axis=0, tiled=True)
            for v in (d_tok, d_mem)
        )
        part_in_t, part_out = (
            lax.psum_scatter(v.astype(jnp.float32), ("dp", "group"), scatter_dimension=0, tiled=True)
            for v in (g_win, g_wout)
        )
        sums = block_sums(
            part_in_t, part_out, rows_out_up, my_place * part_in_t.shape[0], my_place * part_out.shape[0]
        )
        sums, early = lax.psum((sums, early), ("dp", "group"))
    (
        d_tokens, d_memory, grad_in, grad_out, grad_gains, grad_rel, new_in, new_out, new_gains, new_rel,
        rows_in_new, cols_in_new, rows_out_new, cols_out_new, sq_gains_new, sq_rel_new,
    ) = update_call(
        ids, row_source, part_in_t, part_out, sums, early, back_tok, back_mem, w_in, w_out, norm_gains, rel_bias,
        rows_in, cols_in.reshape(1, -1), rows_out_up, cols_out, sq_gains, sq_rel,
    )
    return (
        mixed[None], d_tokens, d_memory, grad_in, grad_out, grad_gains, grad_rel, new_in, new_out, new_gains,
        new_rel, rows_in_new, cols_in_new.reshape(-1), rows_out_new.reshape(-1), cols_out_new, sq_gains_new,
        sq_rel_new,
    )


def solution(mesh):
    both = ("dp", "group")
    row_in = P("group", "dp", None)
    seg_in = P("group", "dp")
    return jax.shard_map(
        body,
        mesh=mesh,
        in_specs=(
            row_in, row_in, seg_in, seg_in, P(), P(), P(both, None), P(both, None, None), P(None, both),
            P(both, None), P(), P(), P(), P(both), P(both), P(), P(), P(),
        ),
        out_specs=(
            P(both, None, None), row_in, row_in, P(None, both), P(both, None), P(), P(), P(None, both),
            P(both, None), P(), P(), P(), P(both), P(both), P(), P(), P(),
        ),
        check_vma=False,
    )
```

```python
import functools

import jax
import jax.numpy as jnp
import numpy as np
from jax import lax
from jax.experimental import pallas as pl
from jax.experimental.pallas import tpu as pltpu
from jax.sharding import PartitionSpec as P

HEADS = 12
HSIZE = 64
FF = 2048
BUCKETS = 32
MODES = 3
SEGS = 4
SEQ = 512
WIDTH = 768
EPSILON = 1e-06
MASKED = -1e30
DECAY_RATE = 0.9
STEP_SIZE = 0.01
PLAIN_STEP = 0.15
GELU_SCALE = 0.7978845608028654
PRECISE = lax.Precision.HIGHEST
MESH = pl.DeviceIdType.MESH
VMEM_BYTES = 60 << 20


def bucket_table(length, buckets):
    exact_span = buckets // 2
    distances = np.arange(length)
    safe_spans = np.maximum(distances, 1)
    logged = np.floor(
        np.log(safe_spans / exact_span) / np.log(128.0 / exact_span) * (buckets - exact_span)
    )
    far_bucket = np.minimum(exact_span + logged, buckets - 1)
    return np.where(distances < exact_span, distances, far_bucket).astype(np.int32)


def nt(a, b):
    return lax.dot_general(a, b, (((1,), (1,)), ((), ())), preferred_element_type=jnp.float32)


def nn(a, b):
    return lax.dot_general(a, b, (((1,), (0,)), ((), ())), preferred_element_type=jnp.float32)


def tn(a, b):
    return lax.dot_general(a, b, (((0,), (0,)), ((), ())), preferred_element_type=jnp.float32)


def inv_rms(values):
    return lax.rsqrt(jnp.mean(values * values, axis=-1, keepdims=True) + EPSILON)


def rms_back(values, gain, grad):
    inv = inv_rms(values)
    scaled = grad * gain
    along = jnp.mean(scaled * values, axis=-1, keepdims=True)
    return inv * scaled - values * (inv * inv * inv * along), jnp.sum(
        grad * (values * inv), axis=0, keepdims=True
    )


def lane_of(shape):
    return lax.broadcasted_iota(jnp.int32, shape, 1)


def ext_masks(aux, first):
    lane = lane_of(aux.shape)
    spot = lane & 63
    documents = (spot >= first) & (spot < first + SEGS)
    hot = jnp.where(documents, aux.astype(jnp.float32), 0.0)
    against = jnp.where(documents, (1.0 - aux.astype(jnp.float32)) * MASKED, 0.0)
    return hot, against


def halves(tile, ext, even):
    lane = lane_of(tile.shape)
    return jnp.where((lane < HSIZE) if even else (lane >= HSIZE), tile, ext)


def pick(first, second, lane):
    return jnp.where(lane < HSIZE, first, second)


def tile_cols(p, base=0):
    return pl.ds(pl.multiple_of(p * 128 + base, 128), 128)


def attend_pair(p, q_tile, k_tile, v_tile, k_ext, q_ext, att_ref, lse_ref, bias_of):
    lane = lane_of((128, 128))
    ones = jnp.ones((SEQ, 128), jnp.bfloat16)
    sides = []
    for even in (True, False):
        sides.append(
            (
                halves(q_tile, q_ext, even),
                halves(k_tile, k_ext, even),
                halves(v_tile, ones, even),
                None if bias_of is None else bias_of(2 * p + (0 if even else 1)),
            )
        )
    for i in range(SEQ // 128):
        lo = 0 if bias_of is None else max(0, i - 2) * 128
        hi = SEQ if bias_of is None else (i + 1) * 128
        outs, tops = [], []
        for qe, ke, ve, bias in sides:
            s = nt(qe[i * 128 : (i + 1) * 128], ke[lo:hi])
            if bias is not None:
                near, far = bias
                parts = [near[:, 128:]] if i == 0 else [near] if i == 1 else [far, near]
                s = s + (parts[0] if len(parts) == 1 else jnp.concatenate(parts, axis=1))
            top = jnp.max(s, axis=1, keepdims=True)
            e = jnp.exp(s - top).astype(jnp.bfloat16)
            outs.append(nn(e, ve[lo:hi]))
            tops.append(top)
        att = pick(outs[0], outs[1], lane)
        total = pltpu.roll(pick(outs[1], outs[0], lane), HSIZE, 1)
        rows = pl.ds(i * 128, 128)
        att_ref[rows, tile_cols(p)] = (att / total).astype(jnp.bfloat16)
        lse = pick(tops[0], tops[1], lane) + jnp.log(total)
        kept = lse_ref[rows, :]
        first = jnp.sum(jnp.where(lane == 0, lse, 0.0), axis=1, keepdims=True)
        second = jnp.sum(jnp.where(lane == HSIZE, lse, 0.0), axis=1, keepdims=True)
        lse_ref[rows, :] = jnp.where(
            lane == 2 * p, first, jnp.where(lane == 2 * p + 1, second, kept)
        )


def forward_bias(table_ref):
    def bias_of(h):
        row = table_ref[pl.ds(h, 1), :]
        near = pltpu.roll(jnp.broadcast_to(row, (128, 256)), 0, 1, stride=1, stride_axis=0)
        lane = lax.broadcasted_iota(jnp.int32, (128, 256), 1)
        sub = lax.broadcasted_iota(jnp.int32, (128, 256), 0)
        near = jnp.where(lane - 128 > sub, MASKED, near)
        far = jnp.broadcast_to(row[:, :1], (128, 128))
        return near, far

    return bias_of


def back_bias(table_ref):
    def bias_of(h):
        row = table_ref[pl.ds(h, 1), :]
        near = pltpu.roll(jnp.broadcast_to(row, (128, 256)), 0, 1, stride=1, stride_axis=0)
        lane = lax.broadcasted_iota(jnp.int32, (128, 256), 1)
        sub = lax.broadcasted_iota(jnp.int32, (128, 256), 0)
        near = jnp.where(lane < sub, MASKED, near)
        far = jnp.broadcast_to(row[:, 128:129], (128, 128))
        return near, far

    return bias_of


def by_distance(near):
    rows = 64
    while rows >= 8:
        near = near[:rows] + pltpu.roll(near[rows:], 256 - rows, 1)
        rows //= 2
    sub = lax.broadcasted_iota(jnp.int32, (8, 256), 0)
    for bit in (4, 2, 1):
        near = jnp.where((sub & bit) != 0, pltpu.roll(near, 256 - bit, 1), near)
    return near


def split_cols(values, base, lane, count):
    rest, out = values, jnp.zeros((values.shape[0], 128), jnp.float32)
    for k in range(count):
        part = rest.astype(jnp.bfloat16).astype(jnp.float32)
        out = jnp.where((lane & 63) == base + k, part, out)
        rest = rest - part
    return out


def back_pair(
    p, q_tile, k_tile, v_tile, do_tile, att_tile, lse_all, hot, against, bias_of, dq_acc, rel_acc, dist_ref
):
    lane = lane_of((SEQ, 128))
    lane1 = lane_of((128, 128))
    spot = lane & 63
    ones3 = jnp.where((spot >= 8) & (spot < 11), 1.0, 0.0)
    k_ext = (hot + ones3).astype(jnp.bfloat16)
    v_ext = jnp.where((spot >= 0) & (spot < 2), 1.0, 0.0).astype(jnp.bfloat16)
    product = do_tile.astype(jnp.float32) * att_tile.astype(jnp.float32)
    sides = []
    for even in (True, False):
        h = 2 * p + (0 if even else 1)
        lse = jnp.sum(jnp.where(lane == h, lse_all, 0.0), axis=1, keepdims=True)
        own = (lane < HSIZE) if even else (lane >= HSIZE)
        delta = jnp.sum(jnp.where(own, product, 0.0), axis=1, keepdims=True)
        q_ext = (against + split_cols(-lse, 8, lane, 3)).astype(jnp.bfloat16)
        d_ext = split_cols(-delta, 0, lane, 2).astype(jnp.bfloat16)
        sides.append(
            (
                halves(q_tile, q_ext, even),
                halves(k_tile, k_ext, even),
                halves(v_tile, v_ext, even),
                halves(do_tile, d_ext, even),
                None if bias_of is None else bias_of(h),
            )
        )
    dks, dvs = [], []
    dq_acc[...] = jnp.zeros_like(dq_acc)
    if bias_of is not None:
        rel_acc[...] = jnp.zeros_like(rel_acc)
    for j in range(SEQ // 128):
        lo = 0 if bias_of is None else j * 128
        hi = SEQ if bias_of is None else min(SEQ, (j + 3) * 128)
        dk2, dv2 = [], []
        for n, (qe, ke, ve, de, bias) in enumerate(sides):
            s = nt(ke[j * 128 : (j + 1) * 128], qe[lo:hi])
            if bias is not None:
                near, far = bias
                s = s + (
                    near[:, :128] if hi - lo == 128 else near if hi - lo == 256
                    else jnp.concatenate([near, far], axis=1)
                )
            w = jnp.exp(s)
            dv2.append(nn(w.astype(jnp.bfloat16), do_tile[lo:hi]))
            ds = w * nt(ve[j * 128 : (j + 1) * 128], de[lo:hi])
            if bias is not None:
                rel_acc[n, :, : hi - lo] += ds
            ds = ds.astype(jnp.bfloat16)
            dk2.append(nn(ds, q_tile[lo:hi]))
            dq_acc[n, :, lo:hi] += tn(k_tile[j * 128 : (j + 1) * 128], ds)
        dks.append(pick(dk2[0], dk2[1], lane1))
        dvs.append(pick(dv2[0], dv2[1], lane1))
    if bias_of is not None:
        for n in range(2):
            near = by_distance(rel_acc[n, :, :256])
            dist_ref[pl.ds(2 * p + n, 1), :] = jnp.concatenate(
                [
                    jnp.sum(near, axis=0, keepdims=True),
                    jnp.sum(rel_acc[n, :, 256:], axis=0, keepdims=True),
                ],
                axis=1,
            )
    sub = lax.broadcasted_iota(jnp.int32, (128, SEQ), 0)
    dq = jnp.where(sub < HSIZE, dq_acc[0], dq_acc[1]).T * HSIZE**-0.5
    return dq, jnp.concatenate(dks, axis=0), jnp.concatenate(dvs, axis=0)


HEAD_COLS = HEADS * HSIZE


def attention_forward(
    tok, mem, aux, win, wout, gains, table, qkv, att1, lse1, x1, qc, kvc, att2, lse2, x2, step
):
    x0 = tok[...].astype(jnp.float32)
    a1 = (x0 * inv_rms(x0) * gains[0:1, :]).astype(jnp.bfloat16)
    for k in range(3):
        cols = slice(k * HEAD_COLS, (k + 1) * HEAD_COLS)
        got = nt(a1, win[cols, :])
        if k == 0:
            got = got.astype(jnp.bfloat16).astype(jnp.float32) * HSIZE**-0.5
        qkv[:, cols] = got.astype(jnp.bfloat16)
    step("projected", 0)
    lse1[...] = jnp.zeros_like(lse1)
    lse2[...] = jnp.zeros_like(lse2)

    @pl.loop(0, HEADS // 2)
    def _(p):
        hot, against = ext_masks(aux[...], 0)
        attend_pair(
            p, qkv[:, tile_cols(p)], qkv[:, tile_cols(p, HEAD_COLS)], qkv[:, tile_cols(p, 2 * HEAD_COLS)],
            hot.astype(jnp.bfloat16), against.astype(jnp.bfloat16), att1, lse1, forward_bias(table),
        )
        step("self", p)

    x1[...] = tok[...].astype(jnp.float32) + nn(att1[...], wout[0:HEAD_COLS, :])
    step("middle", 0)
    a2 = (x1[...] * inv_rms(x1[...]) * gains[1:2, :]).astype(jnp.bfloat16)
    got = nt(a2, win[3 * HEAD_COLS : 4 * HEAD_COLS, :])
    qc[...] = (got.astype(jnp.bfloat16).astype(jnp.float32) * HSIZE**-0.5).astype(jnp.bfloat16)
    for k in range(2):
        kvc[:, k * HEAD_COLS : (k + 1) * HEAD_COLS] = nt(
            mem[...], win[(4 + k) * HEAD_COLS : (5 + k) * HEAD_COLS, :]
        ).astype(jnp.bfloat16)
    step("crossed", 0)

    @pl.loop(0, HEADS // 2)
    def _(p):
        _, against = ext_masks(aux[...], 0)
        hot = pltpu.roll(ext_masks(aux[...], SEGS)[0], 128 - SEGS, 1)
        attend_pair(
            p, qc[:, tile_cols(p)], kvc[:, tile_cols(p)], kvc[:, tile_cols(p, HEAD_COLS)],
            hot.astype(jnp.bfloat16), against.astype(jnp.bfloat16), att2, lse2, None,
        )
        step("cross", p)

    step("attended", 0)
    x2[...] = x1[...] + nn(att2[...], wout[HEAD_COLS : 2 * HEAD_COLS, :])
    step("end", 0)


def ff_kernel(
    x2, cot, keep, gains, w_gate, w_up, w_down, mixed, g2, d_gain, g_win, g_wout, a3, e3, acc, da3, held, sem
):
    c = pl.program_id(0)
    slot = lax.rem(c, 2)
    rows = w_gate.shape[0]
    first = pl.multiple_of(c * rows, rows)
    puts = [
        pltpu.make_async_copy(held.at[slot, 0], g_win.at[pl.ds(6 * HEAD_COLS + first, rows)], sem.at[slot, 0]),
        pltpu.make_async_copy(held.at[slot, 1], g_win.at[pl.ds(6 * HEAD_COLS + FF + first, rows)], sem.at[slot, 1]),
        pltpu.make_async_copy(held.at[slot, 2], g_wout.at[pl.ds(2 * HEAD_COLS + first, rows)], sem.at[slot, 2]),
    ]

    @pl.when(c >= 2)
    def _():
        for put in puts:
            put.wait()

    @pl.when(c == 0)
    def _():
        a3[...] = (x2[...] * inv_rms(x2[...]) * gains[2:3, :]).astype(jnp.bfloat16)
        e3[...] = (cot[...].astype(jnp.float32) * keep[:, 0:1]).astype(jnp.bfloat16)
        acc[...] = x2[...]
        da3[...] = jnp.zeros_like(da3)

    gate = nt(a3[...], w_gate[...])
    up = nt(a3[...], w_up[...])
    dh = nt(e3[...], w_down[...])
    cube = 0.044715 * gate * gate
    inner = jnp.tanh(GELU_SCALE * gate * (1.0 + cube))
    half = 0.5 * (1.0 + inner)
    gelu = gate * half
    slope = half + 0.5 * gate * (1.0 - inner * inner) * (GELU_SCALE * (1.0 + 3.0 * cube))
    hidden = (gelu * up).astype(jnp.bfloat16)
    d_gate = (dh * up * slope).astype(jnp.bfloat16)
    d_up = (dh * gelu).astype(jnp.bfloat16)
    acc[...] += nn(hidden, w_down[...])
    held[slot, 0] = tn(d_gate, a3[...]).astype(jnp.bfloat16)
    held[slot, 1] = tn(d_up, a3[...]).astype(jnp.bfloat16)
    held[slot, 2] = tn(hidden, e3[...]).astype(jnp.bfloat16)
    for put in puts:
        put.start()
    da3[...] += nn(d_gate, w_gate[...]) + nn(d_up, w_up[...])

    @pl.when(c == pl.num_programs(0) - 1)
    def _():
        mixed[...] = acc[...].astype(jnp.bfloat16)
        part, gain = rms_back(x2[...], gains[2:3, :], da3[...])
        g2[...] = cot[...].astype(jnp.float32) * keep[:, 0:1] + part
        d_gain[...] = gain
        for k in range(3):
            for other in range(2):
                pltpu.make_async_copy(held.at[other, k], g_wout.at[0:rows], sem.at[other, k]).wait()


LATE = 4


BACK_BLOCKS = (("o", 1), ("i", 4), ("i", 5), ("i", 3), ("o", 0), ("i", 0), ("i", 1), ("i", 2))


def attention_backward(
    tok, mem, aux, gains, table, qkv, att1, lse1, x1, qc, kvc, att2, lse2, g2,
    d_mem, d_tok, d_gains, dist, do, dqkv, dq_acc, rel_acc, weight, need, emit, step,
):
    need(1)
    e2 = g2[...].astype(jnp.bfloat16)
    do[...] = weight(0, lambda w: nt(e2, w)).astype(jnp.bfloat16)
    need(8)

    def cross_pairs(first, last):
        @pl.loop(first, last)
        def _(p):
            _, against = ext_masks(aux[...], 0)
            hot = pltpu.roll(ext_masks(aux[...], SEGS)[0], 128 - SEGS, 1)
            dq, dk, dv = back_pair(
                p, qc[:, tile_cols(p)], kvc[:, tile_cols(p)], kvc[:, tile_cols(p, HEAD_COLS)], do[:, tile_cols(p)],
                att2[:, tile_cols(p)], lse2[...], hot, against, None, dq_acc, rel_acc, dist,
            )
            dqkv[:, tile_cols(p)] = dq.astype(jnp.bfloat16)
            dqkv[:, tile_cols(p, HEAD_COLS)] = dk.astype(jnp.bfloat16)
            dqkv[:, tile_cols(p, 2 * HEAD_COLS)] = dv.astype(jnp.bfloat16)
            step("cross", p, first, last)

    late = 2 * HEAD_COLS + LATE * 128
    cross_pairs(LATE, HEADS // 2)
    emit("i", 3 * HEAD_COLS + late, tn(dqkv[:, late:], mem[...]))
    step("late", None, 0, 0)
    cross_pairs(0, LATE)
    need(12)
    a2 = (x1[...] * inv_rms(x1[...]) * gains[1:2, :]).astype(jnp.bfloat16)
    emit("o", HEAD_COLS, tn(att2[...], e2))
    emit("i", 3 * HEAD_COLS, tn(dqkv[:, 0:HEAD_COLS], a2))
    emit("i", 4 * HEAD_COLS, tn(dqkv[:, HEAD_COLS : 2 * HEAD_COLS], mem[...]))
    emit("i", 5 * HEAD_COLS, tn(dqkv[:, 2 * HEAD_COLS : late], mem[...]))
    d_rows = weight(1, lambda w: nn(dqkv[:, HEAD_COLS : 2 * HEAD_COLS], w))
    d_rows += weight(2, lambda w: nn(dqkv[:, 2 * HEAD_COLS : 3 * HEAD_COLS], w))
    d_mem[...] = d_rows.astype(jnp.bfloat16)
    da2 = weight(3, lambda w: nn(dqkv[:, 0:HEAD_COLS], w))
    part, gain = rms_back(x1[...], gains[1:2, :], da2)
    d_gains[1:2, :] = gain
    g2[...] += part
    e1 = g2[...].astype(jnp.bfloat16)
    do[...] = weight(4, lambda w: nt(e1, w)).astype(jnp.bfloat16)
    emit("o", 0, tn(att1[...], e1))
    step("middle", None, 0, 0)

    @pl.loop(0, HEADS // 2)
    def _(p):
        hot, against = ext_masks(aux[...], 0)
        dq, dk, dv = back_pair(
            p, qkv[:, tile_cols(p)], qkv[:, tile_cols(p, HEAD_COLS)], qkv[:, tile_cols(p, 2 * HEAD_COLS)],
            do[:, tile_cols(p)], att1[:, tile_cols(p)], lse1[...], hot, against, back_bias(table), dq_acc, rel_acc, dist,
        )
        dqkv[:, tile_cols(p)] = dq.astype(jnp.bfloat16)
        dqkv[:, tile_cols(p, HEAD_COLS)] = dk.astype(jnp.bfloat16)
        dqkv[:, tile_cols(p, 2 * HEAD_COLS)] = dv.astype(jnp.bfloat16)
        step("self", p, 0, HEADS // 2)

    x0 = tok[...].astype(jnp.float32)
    a1 = (x0 * inv_rms(x0) * gains[0:1, :]).astype(jnp.bfloat16)
    for k in range(3):
        emit("i", k * HEAD_COLS, tn(dqkv[:, k * HEAD_COLS : (k + 1) * HEAD_COLS], a1))
    step("last", None, 0, 0)
    da1 = weight(5, lambda w: nn(dqkv[:, 0:HEAD_COLS], w))
    for k in (1, 2):
        da1 += weight(5 + k, lambda w: nn(dqkv[:, k * HEAD_COLS : (k + 1) * HEAD_COLS], w))
    part, gain = rms_back(x0, gains[0:1, :], da1)
    d_gains[0:1, :] = gain
    d_tok[...] = (g2[...] + part).astype(jnp.bfloat16)


SHARE = {"i": 272, "o": 112}
PIECES = (
    ("i", 0, 64, 32), ("i", 64, 64, 32), ("i", 128, 64, 32), ("i", 192, 80, 48),
    ("o", 0, 64, 32), ("o", 64, 48, 16),
)


def place():
    dp = lax.axis_index("dp")
    return dp // 4, (dp // 2) % 2, dp % 2, lax.axis_index("group")


def dev(z, y, x, g):
    return ((z * 2 + y) * 2 + x, g)


def rows_of(ref, kind, zz, yy, xx, gg, lo, n):
    share = ((zz * 2 + yy) * 2 + xx) * 2 + gg
    return ref.at[pl.ds(pl.multiple_of(share * SHARE[kind] + lo, 16), n)]


class Links:
    def __init__(self, send_sem, recv_sem, count=0):
        self.send_sem, self.recv_sem, self.count, self.sent = send_sem, recv_sem, count, []

    def reserve(self, n):
        self.count += n
        return self.count - n

    def copy(self, src, dst, device, sem=None):
        k = self.reserve(1) if sem is None else sem
        return pltpu.make_async_remote_copy(
            src_ref=src, dst_ref=dst, send_sem=self.send_sem.at[k], recv_sem=self.recv_sem.at[k],
            device_id=device, device_id_type=MESH,
        )

    def start(self, copy, cond=None):
        if cond is None:
            copy.start()
        else:
            pl.when(cond)(copy.start)
        self.sent.append((copy, cond))

    def drain(self):
        for copy, cond in self.sent:
            if cond is None:
                copy.wait_send()
            else:
                pl.when(cond)(copy.wait_send)
        self.sent = []


def greet(peers):
    barrier = pltpu.get_barrier_semaphore()
    total = 0
    for device, cond in peers:
        if cond is None:
            pl.semaphore_signal(barrier, inc=1, device_id=device, device_id_type=MESH)
            total = total + 1
        else:

            @pl.when(cond)
            def _(device=device):
                pl.semaphore_signal(barrier, inc=1, device_id=device, device_id_type=MESH)

            total = total + cond.astype(jnp.int32)
    pl.semaphore_wait(barrier, total)


def near_peers():
    z, y, x, g = place()
    return [
        (dev(z, y, 1 - x, g), None), (dev(z, 1 - y, x, g), None), (dev(z, y, x, 1 - g), None),
        (dev(jnp.minimum(z + 1, 3), y, x, g), z < 3), (dev(jnp.maximum(z - 1, 0), y, x, g), z > 0),
    ]


def all_peers():
    z, y, x, g = place()
    me = lax.axis_index("dp")
    return [((lax.rem(me + k, 16), g), None) for k in range(1, 16)] + [(dev(z, y, x, 1 - g), None)]


class Gather:
    def __init__(self, links, arrays):
        z, y, x, g = place()
        self.links, self.items = links, []
        for low in (0, 2):
            nearest = jnp.clip(z, 0, 1) if low == 0 else low
            bases = [(links.reserve(2), links.reserve(2)) for _ in PIECES]
            for zz in (nearest, 2 * low + 1 - nearest):
                for (kind, lo, n, half), (b_up, b_down) in zip(PIECES, bases):

                    def here(yy, xx, first, count, zz=zz, kind=kind):
                        return rows_of(arrays[kind], kind, zz, yy, xx, g, first, count)

                    c = {"go_up": (z >= zz) & (z < 3), "go_down": (z <= zz) & (z > 0)}
                    c["from_below"], c["from_above"] = z > zz, z < zz
                    c["hops"] = jnp.abs(z - zz)

                    def add(name, ref, device, sem=None, c=c):
                        c[name] = links.copy(ref, ref, device, sem)

                    own = here(y, x, lo, n)
                    add("up", own, dev(jnp.minimum(z + 1, 3), y, x, g), b_up + zz - low)
                    add("down", own, dev(jnp.maximum(z - 1, 0), y, x, g), b_down + zz - low)
                    add("x", own, dev(z, y, 1 - x, g))
                    add("y", own, dev(z, 1 - y, x, g))
                    add("p", own, dev(z, y, x, 1 - g))
                    add("a", here(y, 1 - x, lo, half), dev(z, 1 - y, x, g))
                    add("b", here(1 - y, x, lo + half, n - half), dev(z, y, 1 - x, g))
                    add("px", here(y, 1 - x, lo, n), dev(z, y, x, 1 - g))
                    add("py", here(1 - y, x, lo, n), dev(z, y, x, 1 - g))
                    add("pa", here(1 - y, 1 - x, lo, half), dev(z, y, x, 1 - g))
                    add("pb", here(1 - y, 1 - x, lo + half, n - half), dev(z, y, x, 1 - g))
                    self.items.append(c)

    def along(self, c):
        pl.when(c["from_below"])(c["up"].wait_recv)
        pl.when(c["from_above"])(c["down"].wait_recv)
        self.links.start(c["up"], c["go_up"])
        self.links.start(c["down"], c["go_down"])

    def near(self, c):
        for k in ("x", "y", "p"):
            self.links.start(c[k])

    def second(self, c):
        c["x"].wait_recv()
        self.links.start(c["a"])
        self.links.start(c["px"])
        c["y"].wait_recv()
        self.links.start(c["b"])
        self.links.start(c["py"])

    def third(self, c):
        c["a"].wait_recv()
        self.links.start(c["pa"])
        c["b"].wait_recv()
        self.links.start(c["pb"])

    def arrived(self, first, last):
        for c in self.items[first:last]:
            for k in ("p", "px", "py", "pa", "pb"):
                c[k].wait_recv()

    def slots(self):
        n = len(self.items)
        half = n // 2
        lead = half // 2
        out = [[] for _ in range(n + 6)]
        for t, c in enumerate(self.items):
            if t < half:
                out[t].append(functools.partial(self.along, c))
            else:
                for h in range(4):

                    def hop(c=c, h=h):
                        @pl.when(c["hops"] == h)
                        def _():
                            pl.when(c["from_below"])(c["up"].wait_recv)
                            pl.when(c["from_above"])(c["down"].wait_recv)
                            pl.when(c["go_up"])(c["up"].start)
                            pl.when(c["go_down"])(c["down"].start)

                    out[t - lead + h].append(hop)
                self.links.sent += [(c["up"], c["go_up"]), (c["down"], c["go_down"])]
        for t, c in enumerate(self.items):
            out[t].append(functools.partial(self.near, c))
            out[t + 3].append(functools.partial(self.second, c))
            out[t + 6].append(functools.partial(self.third, c))
        return out


def row_exchange(links, sources, targets, rows):
    me, g = lax.axis_index("dp"), lax.axis_index("group")
    copies = []
    for src, dst in zip(sources, targets):
        for k in range(1, 16):
            to = lax.rem(me + k, 16)
            there = dst.at[pl.ds(pl.multiple_of(me * rows, 16), rows)]
            copies.append(links.copy(src.at[pl.ds(pl.multiple_of(to * rows, 16), rows)], there, (to, g)))
    return copies


def own_rows(src, dst, rows, sem):
    here = pl.ds(pl.multiple_of(lax.axis_index("dp") * rows, 16), rows)
    return pltpu.make_async_copy(src.at[here], dst.at[here], sem)


class Sums:
    def __init__(self, win_g, wout_g, own, got, plane, fin, line, part_in, part_out, load_sem):
        self.arrays = {"i": win_g, "o": wout_g}
        self.own, self.got, self.plane, self.fin, self.line = own, got, plane, fin, line
        self.part_in, self.part_out, self.load_sem = part_in, part_out, load_sem
        self.loads, self.rows, self.line_rows = 0, 0, 0

    def batch(self, links, members):
        z, y, x, g = place()
        items = []
        for zz, k in members:
            kind, lo, n, half = PIECES[k]
            base = self.rows
            at = lambda ref, c, off, m, base=base: ref.at[c, pl.ds(base + off, m)]
            it = {"zz": zz, "n": n, "half": half, "base": base, "kind": kind, "lo": lo}
            it["links"] = links
            it["below"], it["above"], it["z"] = z < zz, z > zz, z
            it["load"], it["pair"] = [], []
            for c, (yy, xx) in enumerate(((y, x), (y, 1 - x), (1 - y, x), (1 - y, 1 - x))):
                ref = self.arrays[kind]
                it["load"].append(
                    pltpu.make_async_copy(
                        rows_of(ref, kind, zz, yy, xx, g, lo, n), at(self.own, c, 0, n), self.load_sem.at[self.loads]
                    )
                )
                self.loads += 1
                it["pair"].append(
                    links.copy(
                        rows_of(ref, kind, zz, yy, xx, 1 - g, lo, n), at(self.got, c, 0, n), dev(z, y, x, 1 - g)
                    )
                )
            nx, ny, rest = dev(z, y, 1 - x, g), dev(z, 1 - y, x, g), n - half
            own, plane, fin = self.own, self.plane, self.fin
            it["x1"] = [links.copy(at(own, c, 0, half), at(plane, s, 0, half), nx) for s, c in ((0, 1), (1, 3))]
            it["y1"] = [links.copy(at(own, c, half, rest), at(plane, s, half, rest), ny) for s, c in ((0, 2), (1, 3))]
            it["y2"] = links.copy(at(own, 2, 0, half), at(fin, 0, 0, half), ny)
            it["x2"] = links.copy(at(own, 1, half, rest), at(fin, 0, half, rest), nx)
            for way, needed in (("from_below", zz > 0), ("from_above", zz < 3)):
                if needed:
                    it[way] = pl.ds(self.line_rows, n)
                    self.line_rows += n
            if zz > 0:
                it["up"] = links.copy(at(own, 0, 0, n), self.line.at[it["from_below"]], dev(jnp.minimum(z + 1, 3), y, x, g))
            if zz < 3:
                it["down"] = links.copy(at(own, 0, 0, n), self.line.at[it["from_above"]], dev(jnp.maximum(z - 1, 0), y, x, g))
            items.append(it)
            self.rows += n
        return items

    def begin(self, items):
        for it in items:
            for c in it["load"]:
                c.start()
            for c in (3, 1, 2, 0):
                it["links"].start(it["pair"][c])

    def place_in(self, slots, first, items):
        for k, it in enumerate(items):
            t = first + k
            slots[t].append((2, self.to_core, it))
            slots[t + 3].append((1, self.to_plane, it))
            slots[t + 6].append((0, self.to_line, it))
            for h in range(1, max(it["zz"], 3 - it["zz"]) + 1):
                slots[t + 6 + 2 * h].append((-h, functools.partial(self.hop, h), it))

    @staticmethod
    def add(dst, c, first, src, s, start, m):
        rows = pl.ds(first, m)
        more = src[s, pl.ds(start, m), :].astype(jnp.float32)
        dst[c, rows, :] = (dst[c, rows, :].astype(jnp.float32) + more).astype(jnp.bfloat16)

    def add_line(self, it, way):
        rows = pl.ds(it["base"], it["n"])
        more = self.line[it[way], :].astype(jnp.float32)
        self.own[0, rows, :] = (self.own[0, rows, :].astype(jnp.float32) + more).astype(jnp.bfloat16)

    def to_core(self, it):
        for c in (3, 1, 2, 0):
            it["load"][c].wait()
            it["pair"][c].wait_recv()
            self.add(self.own, c, it["base"], self.got, c, it["base"], it["n"])
            if c == 3:
                it["links"].start(it["x1"][1])
                it["links"].start(it["y1"][1])
            if c == 1:
                it["links"].start(it["x1"][0])
            if c == 2:
                it["links"].start(it["y1"][0])

    def to_plane(self, it):
        half, rest, base = it["half"], it["n"] - it["half"], it["base"]
        low = base + half
        it["x1"][1].wait_recv()
        self.add(self.own, 2, base, self.plane, 1, base, half)
        it["links"].start(it["y2"])
        it["y1"][1].wait_recv()
        self.add(self.own, 1, low, self.plane, 1, low, rest)
        it["links"].start(it["x2"])
        it["x1"][0].wait_recv()
        self.add(self.own, 0, base, self.plane, 0, base, half)
        it["y1"][0].wait_recv()
        self.add(self.own, 0, low, self.plane, 0, low, rest)

    def to_line(self, it):
        it["y2"].wait_recv()
        it["x2"].wait_recv()
        self.add(self.own, 0, it["base"], self.fin, 0, it["base"], it["n"])
        z, zz = it["z"], it["zz"]
        if zz > 0:
            pl.when(z == 0)(it["up"].start)
            it["links"].sent.append((it["up"], it["below"]))
        if zz < 3:
            pl.when(z == 3)(it["down"].start)
            it["links"].sent.append((it["down"], it["above"]))

    def hop(self, h, it):
        z, zz, n, base = it["z"], it["zz"], it["n"], it["base"]
        if h < zz:

            @pl.when(z == h)
            def _():
                it["up"].wait_recv()
                self.add_line(it, "from_below")
                it["up"].start()

        if h < 3 - zz:

            @pl.when(z == 3 - h)
            def _():
                it["down"].wait_recv()
                self.add_line(it, "from_above")
                it["down"].start()

        if h == max(zz, 3 - zz):

            @pl.when(z == zz)
            def _():
                total = self.own[0, pl.ds(base, n), :].astype(jnp.float32)
                if zz > 0:
                    it["up"].wait_recv()
                    total += self.line[it["from_below"], :].astype(jnp.float32)
                if zz < 3:
                    it["down"].wait_recv()
                    total += self.line[it["from_above"], :].astype(jnp.float32)
                into = self.part_in if it["kind"] == "i" else self.part_out
                into[it["lo"] : it["lo"] + n, :] = total


def run_slot(slot):
    for _, step, it in sorted(slot, key=lambda entry: entry[0]):
        step(it)


def total_steps(links, ref, room):
    z, y, x, g = place()
    hops = [dev(z, y, x, 1 - g), dev(z, y, 1 - x, g), dev(z, 1 - y, x, g)]
    copies = [links.copy(ref, room.at[k], to) for k, to in enumerate(hops)]
    over = [links.copy(ref, room.at[2 + k], dev(lax.rem(z + k, 4), y, x, g)) for k in (1, 2, 3)]

    def hop(k):
        def step():
            if k > 0:
                copies[k - 1].wait()
                ref[...] = ref[...] + room[k - 1]
            copies[k].start()

        return step

    def spread():
        copies[2].wait()
        ref[...] = ref[...] + room[2]
        for c in over:
            c.start()

    def finish():
        for c in over:
            c.wait()
        mine = ref[...]
        total = jnp.zeros_like(mine)
        for plane in range(4):
            back = lax.rem(z - plane + 4, 4)
            term = jnp.where(back == 0, mine, jnp.zeros_like(mine))
            for k in (1, 2, 3):
                term = jnp.where(back == k, room[2 + k], term)
            total = total + term
        ref[...] = total

    return [hop(0), hop(1), hop(2), spread, finish]


def vmem_call(kernel, out_shape, scratch, **kw):
    return pl.pallas_call(
        kernel,
        out_shape=out_shape,
        scratch_shapes=scratch,
        compiler_params=pltpu.CompilerParams(vmem_limit_bytes=VMEM_BYTES),
        **kw,
    )


def sds(shape, dtype=jnp.bfloat16):
    return jax.ShapeDtypeStruct(shape, dtype)


WEIGHTS = [pltpu.VMEM((6 * HEAD_COLS, WIDTH), jnp.bfloat16), pltpu.VMEM((2 * HEAD_COLS, WIDTH), jnp.bfloat16)]


def load_rows(src, dst, first, last, sem):
    copy = pltpu.make_async_copy(src.at[first:last], dst.at[first:last], sem)
    copy.start()
    return copy


def anywhere():
    return pl.BlockSpec(memory_space=pl.ANY)


def whole():
    return pl.BlockSpec(memory_space=pltpu.VMEM)


def run(steps):
    for s in steps:
        s()


def block_of(ids, edges):
    return (ids >= edges[0]).astype(jnp.int32) + (ids >= edges[1]).astype(jnp.int32)


IN_EDGES = (3 * HEAD_COLS, 6 * HEAD_COLS)
OUT_EDGES = (HEAD_COLS, 2 * HEAD_COLS)


def block_sums(part_in_t, part_out, rows_out, first_in, first_out):
    sq_in, sq_out = part_in_t * part_in_t, part_out * part_out
    block_in = block_of(first_in + lax.broadcasted_iota(jnp.int32, (sq_in.shape[0], 1), 0), IN_EDGES)
    block_out = block_of(first_out + lax.broadcasted_iota(jnp.int32, (sq_out.shape[0], 1), 0), OUT_EDGES)
    rows_new = DECAY_RATE * rows_out + (1 - DECAY_RATE) * jnp.mean(sq_out, axis=1, keepdims=True)
    lane = lax.broadcasted_iota(jnp.int32, (1, WIDTH), 1)
    lines = [jnp.sum(jnp.where(block_in == k, sq_in, 0.0), axis=0, keepdims=True) for k in range(3)]
    lines += [jnp.sum(jnp.where(block_out == k, sq_out, 0.0), axis=0, keepdims=True) for k in range(3)]
    totals = jnp.zeros((1, WIDTH), jnp.float32)
    for k in range(3):
        total = jnp.sum(jnp.where(block_out == k, rows_new, 0.0), axis=0, keepdims=True)
        totals = jnp.where(lane == k, total, totals)
    return jnp.concatenate(lines + [totals, jnp.zeros((1, WIDTH), jnp.float32)], axis=0)


def prep_kernel(
    ids, row_source, modes, tokens, memory, segments, msegments, w_in, w_out, rel_bias, hot, sentinel,
    tok_s, mem_s, aux_s, win_sh, wout_sh, table_f, table_b, keep, mode_rows, seg_t, mseg_t,
):
    half_rows, length = tokens.shape[0], tokens.shape[1]
    groups, group, where = ids[0], ids[1], ids[2]
    win_sh[...] = w_in[...].astype(jnp.bfloat16)
    wout_sh[...] = w_out[...].astype(jnp.bfloat16)
    for source, out in ((segments, seg_t), (msegments, mseg_t)):
        out[0:half_rows, 0:length] = source[...].astype(jnp.float32)
        out[...] = out[...].T
    lane = lax.broadcasted_iota(jnp.int32, (length, 128), 1)
    spot = (lane & (HSIZE - 1)).astype(jnp.float32)

    @pl.loop(0, half_rows)
    def _(i):
        source = row_source[i * groups + group] - group * half_rows
        tok_s[i] = tokens[source]
        mem_s[i] = memory[source]
        col = jnp.sum(jnp.where(lane == source, seg_t[0:length, :], 0.0), axis=1, keepdims=True)
        mcol = jnp.sum(jnp.where(lane == source, mseg_t[0:length, :], 0.0), axis=1, keepdims=True)
        same = ((spot < SEGS) & (spot == col)) | ((spot >= SEGS) & (spot < 2 * SEGS) & (spot - SEGS == mcol))
        aux_s[i] = jnp.where(same, 1.0, 0.0).astype(jnp.bfloat16)

    mode = modes[row_source[where]]
    tables = jnp.dot(rel_bias[mode], hot[...], precision=PRECISE, preferred_element_type=jnp.float32)
    for k, table in enumerate((table_f, table_b)):
        table[...] = jnp.zeros_like(table)
        table[0:HEADS, :] = tables[:, k * 256 : (k + 1) * 256]
    mode_rows[...] = jnp.where(lax.broadcasted_iota(jnp.int32, (8, 128), 0) == mode, 1.0, 0.0)
    kept = (1 - sentinel[...]).astype(jnp.float32)
    keep[...] = jnp.broadcast_to(kept, (128, SEQ)).T


def prep_call(ids, row_source, modes, tokens, memory, segments, msegments, w_in, w_out, rel_bias, hot, sentinel):
    f32 = jnp.float32
    scalars = pl.BlockSpec(memory_space=pltpu.SMEM)
    half_rows, length = tokens.shape[0], tokens.shape[1]
    return vmem_call(
        prep_kernel,
        (
            sds(tokens.shape), sds(memory.shape), sds((half_rows, length, 128)), sds(w_in.shape),
            sds(w_out.shape), sds((16, 256), f32), sds((16, 256), f32), sds((SEQ, 128), f32), sds((8, 128), f32),
        ),
        [pltpu.VMEM((128, 128), f32), pltpu.VMEM((128, 128), f32)],
        in_specs=[scalars] * 3 + [whole()] * 9,
    )(ids, row_source, modes, tokens, memory, segments, msegments, w_in, w_out, rel_bias, hot, sentinel)


def update_kernel(
    ids, row_source, part_in_t, part_out, sums, early, back_tok, back_mem, w_in, w_out, gains, rel_bias, rows_in,
    cols_in, rows_out, cols_out, sq_gains, sq_rel,
    d_tokens, d_memory, grad_in, grad_out, grad_gains, grad_rel, new_in, new_out, new_gains, new_rel, rows_in_new,
    cols_in_new, rows_out_new, cols_out_new, sq_gains_new, sq_rel_new,
):
    half_rows = back_tok.shape[0]
    groups, group, where = ids[0], ids[1], ids[2]

    @pl.loop(0, half_rows)
    def _(i):
        source = row_source[i * groups + group] - group * half_rows
        d_tokens[source] = back_tok[i]
        d_memory[source] = back_mem[i]

    n_in, n_out = w_in.shape[0], w_out.shape[0]
    p_in = part_in_t[...]
    grad_in[...] = p_in
    in_cols = DECAY_RATE * cols_in[...] + (1 - DECAY_RATE) * jnp.mean(p_in * p_in, axis=1, keepdims=True)
    cols_in_new[...] = in_cols
    block_in = block_of(where * n_in + lax.broadcasted_iota(jnp.int32, (n_in, 1), 0), IN_EDGES)
    scale = jnp.zeros((n_in, WIDTH), jnp.float32)
    for k, count in enumerate((3 * HEAD_COLS, 3 * HEAD_COLS, 2 * FF)):
        row = DECAY_RATE * rows_in[k : k + 1, :] + (1 - DECAY_RATE) * (sums[k : k + 1, :] / count)
        rows_in_new[k : k + 1, :] = row
        scale = jnp.where(block_in == k, in_cols * (row / jnp.mean(row, axis=1, keepdims=True)), scale)
    new_in[...] = w_in[...] - STEP_SIZE * p_in * lax.rsqrt(scale)

    p_out = part_out[...]
    grad_out[...] = p_out
    out_rows = DECAY_RATE * rows_out[...] + (1 - DECAY_RATE) * jnp.mean(p_out * p_out, axis=1, keepdims=True)
    rows_out_new[...] = out_rows
    block_out = block_of(where * n_out + lax.broadcasted_iota(jnp.int32, (n_out, 1), 0), OUT_EDGES)
    scale = jnp.zeros((n_out, WIDTH), jnp.float32)
    for k, count in enumerate((HEAD_COLS, HEAD_COLS, FF)):
        col = DECAY_RATE * cols_out[k : k + 1, :] + (1 - DECAY_RATE) * (sums[3 + k : 4 + k, :] / count)
        cols_out_new[k : k + 1, :] = col
        mean = sums[6:7, k : k + 1] / count
        scale = jnp.where(block_out == k, (out_rows / mean) * col, scale)
    new_out[...] = w_out[...] - STEP_SIZE * p_out * lax.rsqrt(scale)

    g = early[0:3, :]
    grad_gains[...] = g
    sq = DECAY_RATE * sq_gains[...] + (1 - DECAY_RATE) * g * g
    sq_gains_new[...] = sq
    new_gains[...] = gains[...] - PLAIN_STEP * g * lax.rsqrt(sq)
    for k in range(MODES):
        g = early[8 : 8 + HEADS, k * 128 : k * 128 + BUCKETS]
        grad_rel[k] = g
        sq = DECAY_RATE * sq_rel[k] + (1 - DECAY_RATE) * g * g
        sq_rel_new[k] = sq
        new_rel[k] = rel_bias[k] - PLAIN_STEP * g * lax.rsqrt(sq)


def update_call(ids, row_source, *arrays):
    f32 = jnp.float32
    scalars = pl.BlockSpec(memory_space=pltpu.SMEM)
    (part_in_t, part_out, sums, early, back_tok, back_mem, w_in, w_out, gains, rel_bias) = arrays[:10]
    n_in, n_out = w_in.shape[0], w_out.shape[0]
    three = sds((3, WIDTH), f32)
    rel = sds(rel_bias.shape, f32)
    return vmem_call(
        update_kernel,
        (
            sds(back_tok.shape), sds(back_mem.shape), sds(w_in.shape, f32), sds(w_out.shape, f32), three, rel,
            sds(w_in.shape, f32), sds(w_out.shape, f32), three, rel, three, sds((n_in, 1), f32), sds((n_out, 1), f32),
            three, three, rel,
        ),
        [],
        in_specs=[scalars] * 2 + [whole()] * len(arrays),
    )(ids, row_source, *arrays)


def forward_kernel(boxed, *refs):
    n_in = 5
    ins, refs = refs[:n_in], refs[n_in:]
    (gains, table), refs = refs[:2], refs[2:]
    if boxed:
        win_sh, wout_sh, tok_s, mem_s, aux_s = ins
        (win, wout), rows_out, refs = refs[:2], refs[2:5], refs[5:]
    else:
        tok_s, mem_s, aux_s, win, wout = ins
        rows_out = None
    kept_out, kept, (tok, mem, aux), refs = refs[:9], refs[9:18], refs[18:21], refs[21:]
    (win_v, wout_v, sem, put_sem, ls), refs = refs[:5], refs[5:]
    puts = []

    def keep(src, dst):
        puts.append(pltpu.make_async_copy(src, dst, put_sem.at[len(puts)]))
        puts[-1].start()

    def hand_on(name):
        names = {"projected": (0,), "middle": (1, 2, 3), "crossed": (4, 5), "attended": (6, 7), "end": (8,)}
        for k in names.get(name, ()):
            keep(kept[k], kept_out[k])
        if boxed and name == "projected":
            keep(tok, rows_out[0])
            keep(aux, rows_out[2])
        if boxed and name == "crossed":
            keep(mem, rows_out[1])

    if not boxed:
        loads = [load_rows(win, win_v, 0, 6 * HEAD_COLS, sem.at[0]), load_rows(wout, wout_v, 0, 2 * HEAD_COLS, sem.at[1])]
        for k, (s, t) in enumerate(((tok_s, tok), (mem_s, mem), (aux_s, aux))):
            loads.append(pltpu.make_async_copy(s, t, ls.at[k]))
            loads[-1].start()
        for c in loads:
            c.wait()
        attention_forward(
            tok, mem, aux, win_v, wout_v, gains, table, *kept, step=lambda name, p: hand_on(name)
        )
        for c in puts:
            c.wait()
        return
    ss, rs = refs
    z, y, x, g = place()
    pos = SEQ // 16
    links = Links(ss, rs)
    near = [
        pltpu.make_async_copy(win_sh, rows_of(win, "i", z, y, x, g, 0, 272), ls.at[0]),
        pltpu.make_async_copy(wout_sh, rows_of(wout, "o", z, y, x, g, 0, 112), ls.at[1]),
    ]
    own = [own_rows(s, t, pos, ls.at[2 + k]) for k, (s, t) in enumerate(((tok_s, tok), (mem_s, mem), (aux_s, aux)))]
    for c in near + own:
        c.start()
    greet(all_peers())
    for c in near:
        c.wait()
    gather = Gather(links, {"i": win, "o": wout})
    slots = gather.slots()
    first_rows = row_exchange(links, (tok_s, aux_s), (tok, aux), pos)
    mem_rows = row_exchange(links, (mem_s,), (mem,), pos)
    half = len(gather.items) // 2
    now = half + 6
    queue = [[] for _ in range(len(slots))]
    for k, c in enumerate(first_rows):
        queue[8 + k // 4].append(c)
    for k, c in enumerate(mem_rows):
        queue[16 + k // 3].append(c)

    def run_gather(t):
        run(slots[t])
        for c in queue[t]:
            links.start(c)

    for t in range(now):
        run_gather(t)
    gather.arrived(0, half)
    loads = [
        load_rows(win, win_v, 0, 3 * HEAD_COLS, sem.at[0]), load_rows(wout, wout_v, 0, 2 * HEAD_COLS, sem.at[1]),
        load_rows(win, win_v, 3 * HEAD_COLS, 16 * 272, sem.at[2]),
    ]
    for c in first_rows:
        c.wait_recv()
    for c in own:
        c.wait()
    loads[0].wait()
    calls = HEADS // 2
    shares = [range(now + k, now + k + 1) for k in range(calls)]
    shares += [range(now + calls + k, now + calls + k + 1) for k in range(calls)]

    def step(name, p):
        hand_on(name)
        if name == "middle":
            gather.arrived(half, half + 4)
            more = load_rows(win, win_v, 16 * 272, 6 * HEAD_COLS, sem.at[3])
            for c in mem_rows:
                c.wait_recv()
            loads[2].wait()
            more.wait()
        if name not in ("self", "cross"):
            return
        for k in range(calls):

            @pl.when(p == k)
            def _(k=k):
                for t in shares[k + (0 if name == "self" else calls)]:
                    run_gather(t)
                if name == "self" and k == calls - 1:
                    loads[1].wait()

    attention_forward(tok, mem, aux, win_v, wout_v, gains, table, *kept, step=step)
    for t in range(now + 2 * calls, len(slots)):
        run_gather(t)
    gather.arrived(half + 4, 2 * half)
    for c in puts:
        c.wait()
    links.drain()


def forward_call(boxed, *arrays):
    f32 = jnp.float32
    dma = pltpu.SemaphoreType.DMA
    outs = (
        sds((SEQ, 3 * HEAD_COLS)), sds((SEQ, HEAD_COLS)), sds((SEQ, 128), f32), sds((SEQ, WIDTH), f32),
        sds((SEQ, HEAD_COLS)), sds((SEQ, 2 * HEAD_COLS)), sds((SEQ, HEAD_COLS)), sds((SEQ, 128), f32),
        sds((SEQ, WIDTH), f32),
    )
    rows = (sds((SEQ, WIDTH)), sds((SEQ, WIDTH)), sds((SEQ, 128)))
    scratch = [pltpu.VMEM(v.shape, v.dtype) for v in outs + rows] + WEIGHTS + [dma((4,)), dma((12,)), dma((5,))]
    specs = [anywhere()] * 5
    extra = {}
    if boxed:
        sems = 45 + 4 * 22 * len(PIECES)
        scratch = scratch + [dma((sems,)), dma((sems,))]
        outs = (sds((6 * HEAD_COLS + 2 * FF, WIDTH)), sds((2 * HEAD_COLS + FF, WIDTH))) + rows + outs
        specs = [whole()] * 2 + [anywhere()] * 3
        extra = dict(collective_id=1, has_side_effects=True)
    return pl.pallas_call(
        functools.partial(forward_kernel, boxed),
        out_shape=outs,
        scratch_shapes=scratch,
        in_specs=specs + [whole()] * 2,
        out_specs=(anywhere(),) * len(outs),
        compiler_params=pltpu.CompilerParams(vmem_limit_bytes=VMEM_BYTES, **extra),
    )(*arrays)


def ff_call(x2, cot, keep, gains, win, wout):
    f32 = jnp.float32
    step = 256
    n = FF // step
    at = lambda block, first: pl.BlockSpec((step, WIDTH), lambda c: (first + c, 0))
    full = lambda rows, cols: pl.BlockSpec((rows, cols), lambda c: (0, 0))
    gate0, down0 = 6 * HEAD_COLS // step, 2 * HEAD_COLS // step
    return vmem_call(
        ff_kernel,
        (
            sds((SEQ, WIDTH)), sds((SEQ, WIDTH), f32), sds((1, WIDTH), f32), sds(win.shape), sds(wout.shape),
        ),
        [
            pltpu.VMEM((SEQ, WIDTH), jnp.bfloat16), pltpu.VMEM((SEQ, WIDTH), jnp.bfloat16),
            pltpu.VMEM((SEQ, WIDTH), f32), pltpu.VMEM((SEQ, WIDTH), f32),
            pltpu.VMEM((2, 3, step, WIDTH), jnp.bfloat16), pltpu.SemaphoreType.DMA((2, 3)),
        ],
        grid=(n,),
        in_specs=[
            full(SEQ, WIDTH), full(SEQ, WIDTH), full(SEQ, 128), full(3, WIDTH),
            at(step, gate0), at(step, gate0 + n), at(step, down0),
        ],
        out_specs=(full(SEQ, WIDTH), full(SEQ, WIDTH), full(1, WIDTH), anywhere(), anywhere()),
    )(x2, cot, keep, gains, win, win, wout)


def rel_sums(dist, hot_dist, mode_rows):
    by_bucket = jnp.dot(dist, hot_dist, precision=PRECISE, preferred_element_type=jnp.float32)
    return jnp.concatenate([by_bucket * mode_rows[k : k + 1, :] for k in range(MODES)], axis=1)


def backward_kernel(boxed, _, __, win, wout, *refs):
    lazy, refs = refs[:12], refs[12:]
    (gains, table, hot_dist, mode_rows, gain_three, rows_out), refs = refs[:6], refs[6:]
    if boxed:
        (g_win, g_wout, part_in, part_out, sums, early, btok, bmem), refs = refs[:8], refs[8:]
        (d_mem, d_tok), refs = refs[:2], refs[2:]
    else:
        (g_win, g_wout, d_mem, d_tok, early), refs = refs[:5], refs[5:]
    (d_gains, dist), refs = refs[:2], refs[2:]
    scratch, (held, put_sem, blocks, block_sem, lazy_sem, sem), refs = refs[:4], refs[4:10], refs[10:]
    lazy_v, refs = refs[:12], refs[12:]
    fetched = []

    def fetch(k):
        array, block = BACK_BLOCKS[k]
        src = (win if array == "i" else wout).at[block * HEAD_COLS : (block + 1) * HEAD_COLS]
        fetched.append(pltpu.make_async_copy(src, blocks.at[k % 3], block_sem.at[k]))
        fetched[k].start()

    def weight(k, fn):
        fetched[k].wait()
        value = fn(blocks[k % 3])
        if k + 3 < len(BACK_BLOCKS):
            fetch(k + 3)
        return value

    loads = [pltpu.make_async_copy(s, t, lazy_sem.at[k]) for k, (s, t) in enumerate(zip(lazy, lazy_v))]
    loads[0].start()
    fetch(0)
    for c in loads[1:]:
        c.start()
    fetch(1)
    fetch(2)
    loaded = []

    def need(n):
        while len(loaded) < n:
            loads[len(loaded)].wait()
            loaded.append(True)

    puts, settled = [], []

    def settle(upto):
        while len(settled) < upto:
            puts[len(settled)].wait()
            settled.append(True)

    def emit(array, first, value):
        k = len(puts)
        settle(k - 1)
        rows = value.shape[0]
        held[k % 2, 0:rows] = value.astype(jnp.bfloat16)
        into = g_win if array == "i" else g_wout
        puts.append(pltpu.make_async_copy(held.at[k % 2, 0:rows], into.at[first : first + rows], put_sem.at[k]))
        puts[k].start()

    dist[...] = jnp.zeros_like(dist)
    step = lambda *a: None
    if boxed:
        own, got, plane, fin, line, room, early_room, ss, rs, load_sem = refs
        z, y, x, g = place()
        me = lax.axis_index("dp")
        pos = SEQ // 16
        greet(all_peers())
        work = Sums(g_win, g_wout, own, got, plane, fin, line, part_in, part_out, load_sem)
        n = len(PIECES)
        groups = (
            (0, [(3, k) for k in range(n)]),
            (6, [(2, k) for k in range(n)]),
            (12, [(1, k) for k in range(2, n)] + [(0, k) for k in range(4, n)]),
            (20, [(0, k) for k in range(4)] + [(1, k) for k in range(2)]),
        )
        slots = [[] for _ in range(20 + n + 14)]
        links, batches = [Links(ss, rs)], []
        for first, members in groups:
            batches.append(work.batch(links[-1], members))
            work.place_in(slots, first, batches[-1])
            links.append(Links(ss, rs, links[-1].count))
        back = links[-1]
        mem_copies = row_exchange(back, (d_mem,), (bmem,), pos)
        tok_copies = row_exchange(back, (d_tok,), (btok,), pos)
        kept_mem, kept_tok = own_rows(d_mem, bmem, pos, sem.at[2]), own_rows(d_tok, btok, pos, sem.at[3])
        work.begin(batches[0])
        shares = {("cross", LATE): ((0, 1), (2, 3)), ("cross", 0): ((4, 5), (6, 7), (8, 9), (10, 11))}
        shares["self", 0] = ((12, 13), (14, 15), (16,), (17,), (18,), (19,))

        def step(name, p, first, last):
            if name in ("late", "middle", "last"):
                settle(len(puts))
                if name == "middle":
                    kept_mem.start()
                work.begin(batches[("late", "middle", "last").index(name) + 1])
                return
            for k, share in enumerate(shares[name, first]):

                @pl.when(p == first + k)
                def _(share=share, k=k):
                    if name == "self":
                        for c in mem_copies[3 * k : 3 * k + 3]:
                            back.start(c)
                    for t in share:
                        run_slot(slots[t])

    g2, aux, qc, kvc, att2, lse2, mem, x1, att1, qkv, lse1, tok = lazy_v
    attention_backward(
        tok, mem, aux, gains, table, qkv, att1, lse1, x1, qc, kvc, att2, lse2, g2,
        d_mem, d_tok, d_gains, dist, *scratch, weight=weight, need=need, emit=emit, step=step,
    )
    early[...] = jnp.zeros_like(early)
    early[0:2, :] = d_gains[0:2, :]
    early[2:3, :] = gain_three[...]
    early[8:24, 0:384] = rel_sums(dist[...], hot_dist[...], mode_rows[...])
    if not boxed:
        settle(len(puts))
        return
    kept_tok.start()
    turns = total_steps(back, early, early_room)
    for k, slot in enumerate(slots[20:]):
        run_slot(slot)
        for c in tok_copies[3 * k : 3 * k + 3]:
            back.start(c)
        if k < len(turns):
            turns[k]()
    where = me * 2 + g
    sums[...] = block_sums(part_in[...], part_out[...], rows_out[...], where * 272, where * 112)
    run(total_steps(back, sums, room))
    for c in mem_copies + tok_copies:
        c.wait_recv()
    kept_mem.wait()
    kept_tok.wait()
    for each in links:
        each.drain()


def backward_call(boxed, g_win, g_wout, win, wout, lazy, *more):
    f32, bf16 = jnp.float32, jnp.bfloat16
    vm, dma = pltpu.VMEM, pltpu.SemaphoreType.DMA
    row = sds((SEQ, WIDTH))
    scratch = [vm((8, WIDTH), f32), vm((16, 384), f32)]
    scratch += [
        vm((SEQ, HEAD_COLS), bf16), vm((SEQ, 3 * HEAD_COLS), bf16), vm((2, 128, SEQ), f32), vm((2, 128, 384), f32),
        vm((2, HEAD_COLS, WIDTH), bf16), dma((9,)), vm((3, HEAD_COLS, WIDTH), bf16), dma((len(BACK_BLOCKS),)),
        dma((len(lazy),)), dma((4,)),
    ]
    scratch += [vm(v.shape, v.dtype) for v in lazy]
    outs = [sds(g_win.shape), sds(g_wout.shape)]
    if boxed:
        items, both = 4 * len(PIECES), 4 * 384
        outs += [sds((272, WIDTH), f32), sds((112, WIDTH), f32), sds((8, WIDTH), f32), sds((24, WIDTH), f32), row, row]
        specs = (anywhere(),) * 2 + (whole(),) * 4 + (anywhere(),) * 2
        scratch = [vm((SEQ, WIDTH), bf16), vm((SEQ, WIDTH), bf16)] + scratch
        scratch += [
            vm((4, both, WIDTH), bf16), vm((4, both, WIDTH), bf16), vm((2, both, WIDTH), bf16),
            vm((1, both, WIDTH), bf16), vm((6 * 384, WIDTH), bf16), vm((6, 8, WIDTH), f32), vm((6, 24, WIDTH), f32),
            dma((12 * items + 48,)), dma((12 * items + 48,)), dma((4 * items,)),
        ]
    else:
        outs += [row, row, sds((24, WIDTH), f32)]
        specs = (anywhere(),) * 2 + (whole(),) * 3
    extra = dict(collective_id=2, has_side_effects=True) if boxed else {}
    return pl.pallas_call(
        functools.partial(backward_kernel, boxed),
        out_shape=tuple(outs),
        scratch_shapes=scratch,
        in_specs=[anywhere()] * (4 + len(lazy)) + [whole()] * len(more),
        out_specs=specs,
        input_output_aliases={0: 0, 1: 1},
        compiler_params=pltpu.CompilerParams(vmem_limit_bytes=VMEM_BYTES, **extra),
    )(g_win, g_wout, win, wout, *lazy, *more)


def body(
    tokens, memory, segments, memory_segments, row_source, denoiser_modes, sentinel, cotangent, w_in, w_out,
    norm_gains, rel_bias, rows_in, cols_in, rows_out, cols_out, sq_gains, sq_rel,
):
    n_index = lax.axis_size("dp")
    n_group = lax.axis_size("group")
    my_group = lax.axis_index("group")
    my_place = lax.axis_index(("dp", "group"))
    half_rows = tokens.shape[0]
    rows_dev = cotangent.shape[0]
    assert rows_dev == 1
    boxed = n_index == 16 and n_group == 2
    ids = jnp.stack([jnp.int32(n_group), my_group, my_place])
    buckets = bucket_table(SEQ, BUCKETS)
    hot = (buckets[:256, None] == np.arange(BUCKETS)[None, :]).astype(np.float32)
    lane = np.arange(256)
    dist_f = np.where(lane <= 128, 128 - lane, 384 - lane)
    hot_t = jnp.asarray(np.concatenate([hot[dist_f], hot], axis=0).T)
    w_in_t, rel_t = w_in.T, jnp.swapaxes(rel_bias, 1, 2)
    tok_s, mem_s, aux_s, win_sh, wout_sh, table_f, table_b, keep, mode_rows = prep_call(
        ids, row_source, denoiser_modes, tokens, memory, segments, memory_segments, w_in_t, w_out, rel_t, hot_t, sentinel
    )
    if boxed:
        flat = lambda v: v.reshape(SEQ, v.shape[-1])
        win, wout, tok, mem, aux, *kept = forward_call(
            True, win_sh, wout_sh, flat(tok_s), flat(mem_s), flat(aux_s), norm_gains, table_f
        )
    else:
        win = lax.all_gather(win_sh, ("dp", "group"), axis=0, tiled=True)
        wout = lax.all_gather(wout_sh, ("dp", "group"), axis=0, tiled=True)
        tok, mem, aux = (
            lax.all_to_all(v, "dp", split_axis=0, concat_axis=0, tiled=True).reshape(SEQ, v.shape[-1])
            for v in (tok_s, mem_s, aux_s)
        )
        kept = forward_call(False, tok, mem, aux, win, wout, norm_gains, table_f)
    x2 = kept[8]
    mixed, g2, d_gain_three, g_win, g_wout = ff_call(
        x2, cotangent.reshape(SEQ, WIDTH), keep, norm_gains, win, wout
    )
    hot_dist = np.concatenate([hot, np.repeat(np.eye(BUCKETS, dtype=np.float32)[-1:], 128, axis=0)], axis=0)
    hot_dist = jnp.asarray(np.pad(hot_dist, ((0, 0), (0, 128 - BUCKETS))))
    rows_out_up = rows_out.reshape(-1, 1)
    qkv, att1, lse1, x1, qc, kvc, att2, lse2, _ = kept
    lazy = (g2, aux, qc, kvc, att2, lse2, mem, x1, att1, qkv, lse1, tok)
    result = backward_call(
        boxed, g_win, g_wout, win, wout, lazy, norm_gains, table_b, hot_dist, mode_rows, d_gain_three, rows_out_up
    )
    if boxed:
        _, _, part_in_t, part_out, sums, early, back_tok, back_mem = result
        back_tok, back_mem = back_tok.reshape(tok_s.shape), back_mem.reshape(mem_s.shape)
    else:
        g_win, g_wout, d_mem, d_tok, early = result
        back_tok, back_mem = (
            lax.all_to_all(v.reshape(tok_s.shape), "dp", split_axis=0, concat_axis=0, tiled=True)
            for v in (d_tok, d_mem)
        )
        part_in_t, part_out = (
            lax.psum_scatter(v.astype(jnp.float32), ("dp", "group"), scatter_dimension=0, tiled=True)
            for v in (g_win, g_wout)
        )
        sums = block_sums(
            part_in_t, part_out, rows_out_up, my_place * part_in_t.shape[0], my_place * part_out.shape[0]
        )
        sums, early = lax.psum((sums, early), ("dp", "group"))
    (
        d_tokens, d_memory, grad_in, grad_out, grad_gains, grad_rel, new_in, new_out, new_gains, new_rel,
        rows_in_new, cols_in_new, rows_out_new, cols_out_new, sq_gains_new, sq_rel_new,
    ) = update_call(
        ids, row_source, part_in_t, part_out, sums, early, back_tok, back_mem, w_in_t, w_out, norm_gains, rel_t,
        rows_in, cols_in.reshape(-1, 1), rows_out_up, cols_out, sq_gains, jnp.swapaxes(sq_rel, 1, 2),
    )
    grad_rel, new_rel, sq_rel_new = (jnp.swapaxes(v, 1, 2) for v in (grad_rel, new_rel, sq_rel_new))
    return (
        mixed[None], d_tokens, d_memory, grad_in.T, grad_out, grad_gains, grad_rel, new_in.T, new_out, new_gains,
        new_rel, rows_in_new, cols_in_new.reshape(-1), rows_out_new.reshape(-1), cols_out_new, sq_gains_new,
        sq_rel_new,
    )


def solution(mesh):
    both = ("dp", "group")
    row_in = P("group", "dp", None)
    seg_in = P("group", "dp")
    return jax.shard_map(
        body,
        mesh=mesh,
        in_specs=(
            row_in, row_in, seg_in, seg_in, P(), P(), P(both, None), P(both, None, None), P(None, both),
            P(both, None), P(), P(), P(), P(both), P(both), P(), P(), P(),
        ),
        out_specs=(
            P(both, None, None), row_in, row_in, P(None, both), P(both, None), P(), P(), P(None, both),
            P(both, None), P(), P(), P(), P(both), P(both), P(), P(), P(),
        ),
        check_vma=False,
    )
```

```python
import functools

import jax
import jax.numpy as jnp
import numpy as np
from jax import lax
from jax.experimental import pallas as pl
from jax.experimental.pallas import tpu as pltpu
from jax.sharding import PartitionSpec as P

HEADS = 12
HSIZE = 64
FF = 2048
BUCKETS = 32
MODES = 3
SEGS = 4
SEQ = 512
WIDTH = 768
EPSILON = 1e-06
MASKED = -1e30
DECAY_RATE = 0.9
STEP_SIZE = 0.01
PLAIN_STEP = 0.15
GELU_SCALE = 0.7978845608028654
PRECISE = lax.Precision.HIGHEST
MESH = pl.DeviceIdType.MESH
VMEM_BYTES = 60 << 20


def bucket_table(length, buckets):
    exact_span = buckets // 2
    distances = np.arange(length)
    safe_spans = np.maximum(distances, 1)
    logged = np.floor(
        np.log(safe_spans / exact_span) / np.log(128.0 / exact_span) * (buckets - exact_span)
    )
    far_bucket = np.minimum(exact_span + logged, buckets - 1)
    return np.where(distances < exact_span, distances, far_bucket).astype(np.int32)


def nt(a, b):
    return lax.dot_general(a, b, (((1,), (1,)), ((), ())), preferred_element_type=jnp.float32)


def nn(a, b):
    return lax.dot_general(a, b, (((1,), (0,)), ((), ())), preferred_element_type=jnp.float32)


def tn(a, b):
    return lax.dot_general(a, b, (((0,), (0,)), ((), ())), preferred_element_type=jnp.float32)


def inv_rms(values):
    return lax.rsqrt(jnp.mean(values * values, axis=-1, keepdims=True) + EPSILON)


def rms_back(values, gain, grad):
    inv = inv_rms(values)
    scaled = grad * gain
    along = jnp.mean(scaled * values, axis=-1, keepdims=True)
    return inv * scaled - values * (inv * inv * inv * along), jnp.sum(
        grad * (values * inv), axis=0, keepdims=True
    )


def lane_of(shape):
    return lax.broadcasted_iota(jnp.int32, shape, 1)


def ext_masks(aux, first):
    lane = lane_of(aux.shape)
    spot = lane & 63
    documents = (spot >= first) & (spot < first + SEGS)
    hot = jnp.where(documents, aux.astype(jnp.float32), 0.0)
    against = jnp.where(documents, (1.0 - aux.astype(jnp.float32)) * MASKED, 0.0)
    return hot, against


def halves(tile, ext, even):
    lane = lane_of(tile.shape)
    return jnp.where((lane < HSIZE) if even else (lane >= HSIZE), tile, ext)


def pick(first, second, lane):
    return jnp.where(lane < HSIZE, first, second)


def tile_cols(p, base=0):
    return pl.ds(pl.multiple_of(p * 128 + base, 128), 128)


def attend_pair(p, q_tile, k_tile, v_tile, k_ext, q_ext, att_ref, lse_ref, bias_of):
    lane = lane_of((SEQ, 128))
    ones = jnp.ones((SEQ, 128), jnp.bfloat16)
    outs, tops = [], []
    for even in (True, False):
        s = nt(halves(q_tile, q_ext, even), halves(k_tile, k_ext, even))
        if bias_of is None:
            top = jnp.max(s, axis=1, keepdims=True)
            e = jnp.exp(s - top).astype(jnp.bfloat16)
        else:
            near, far = bias_of(2 * p + (0 if even else 1))
            tops_of, rows_of_e = [], []
            for i in range(SEQ // 128):
                lo, hi = max(0, i - 2) * 128, (i + 1) * 128
                part = s[i * 128 : (i + 1) * 128, lo:hi]
                bias = [near[:, 128:]] if i == 0 else [near] if i == 1 else [far, near]
                part = part + (bias[0] if len(bias) == 1 else jnp.concatenate(bias, axis=1))
                tops_of.append(jnp.max(part, axis=1, keepdims=True))
                blocks = [jnp.exp(part - tops_of[-1]).astype(jnp.bfloat16)]
                if lo > 0:
                    blocks.insert(0, jnp.zeros((128, lo), jnp.bfloat16))
                if hi < SEQ:
                    blocks.append(jnp.zeros((128, SEQ - hi), jnp.bfloat16))
                rows_of_e.append(blocks[0] if len(blocks) == 1 else jnp.concatenate(blocks, axis=1))
            e = jnp.concatenate(rows_of_e, axis=0)
            top = jnp.concatenate(tops_of, axis=0)
        outs.append(nn(e, halves(v_tile, ones, even)))
        tops.append(top)
    total = pltpu.roll(pick(outs[1], outs[0], lane), HSIZE, 1)
    att_ref[:, tile_cols(p)] = (pick(outs[0], outs[1], lane) / total).astype(jnp.bfloat16)
    lse = pick(tops[0], tops[1], lane) + jnp.log(total)
    lse_ref[...] = jnp.where(
        lane == 2 * p, lse[:, 0:1], jnp.where(lane == 2 * p + 1, lse[:, HSIZE : HSIZE + 1], lse_ref[...])
    )


def forward_bias(table_ref):
    def bias_of(h):
        row = table_ref[pl.ds(h, 1), :]
        near = pltpu.roll(jnp.broadcast_to(row, (128, 256)), 0, 1, stride=1, stride_axis=0)
        lane = lax.broadcasted_iota(jnp.int32, (128, 256), 1)
        sub = lax.broadcasted_iota(jnp.int32, (128, 256), 0)
        near = jnp.where(lane - 128 > sub, MASKED, near)
        far = jnp.broadcast_to(row[:, :1], (128, 128))
        return near, far

    return bias_of


def back_bias(table_ref):
    def bias_of(h):
        row = table_ref[pl.ds(h, 1), :]
        near = pltpu.roll(jnp.broadcast_to(row, (128, 256)), 0, 1, stride=1, stride_axis=0)
        lane = lax.broadcasted_iota(jnp.int32, (128, 256), 1)
        sub = lax.broadcasted_iota(jnp.int32, (128, 256), 0)
        near = jnp.where(lane < sub, MASKED, near)
        far = jnp.broadcast_to(row[:, 128:129], (128, 128))
        return near, far

    return bias_of


def by_distance(near):
    rows = 64
    while rows >= 8:
        near = near[:rows] + pltpu.roll(near[rows:], 256 - rows, 1)
        rows //= 2
    sub = lax.broadcasted_iota(jnp.int32, (8, 256), 0)
    for bit in (4, 2, 1):
        near = jnp.where((sub & bit) != 0, pltpu.roll(near, 256 - bit, 1), near)
    return near


def split_cols(values, base, lane, count):
    rest, out = values, jnp.zeros((values.shape[0], 128), jnp.float32)
    for k in range(count):
        part = rest.astype(jnp.bfloat16).astype(jnp.float32)
        out = jnp.where((lane & 63) == base + k, part, out)
        rest = rest - part
    return out


def back_pair(p, q_tile, k_tile, v_tile, do_tile, att_tile, lse_all, hot, against, bias_of, rel_acc, dist_ref):
    lane = lane_of((SEQ, 128))
    spot = lane & 63
    ones3 = jnp.where((spot >= 8) & (spot < 11), 1.0, 0.0)
    k_ext = (hot + ones3).astype(jnp.bfloat16)
    v_ext = jnp.where((spot >= 0) & (spot < 2), 1.0, 0.0).astype(jnp.bfloat16)
    product = do_tile.astype(jnp.float32) * att_tile.astype(jnp.float32)
    dqs, dks, dvs = [], [], []
    for n, even in enumerate((True, False)):
        h = 2 * p + n
        lse = jnp.sum(jnp.where(lane == h, lse_all, 0.0), axis=1, keepdims=True)
        own = (lane < HSIZE) if even else (lane >= HSIZE)
        delta = jnp.sum(jnp.where(own, product, 0.0), axis=1, keepdims=True)
        q_ext = (against + split_cols(-lse, 8, lane, 3)).astype(jnp.bfloat16)
        d_ext = split_cols(-delta, 0, lane, 2).astype(jnp.bfloat16)
        s = nt(halves(k_tile, k_ext, even), halves(q_tile, q_ext, even))
        dp = nt(halves(v_tile, v_ext, even), halves(do_tile, d_ext, even))
        if bias_of is None:
            w = jnp.exp(s)
            ds = (w * dp).astype(jnp.bfloat16)
            w = w.astype(jnp.bfloat16)
        else:
            near, far = bias_of(h)
            w_rows, ds_rows = [], []
            for j in range(SEQ // 128):
                lo, hi = j * 128, min(SEQ, (j + 3) * 128)
                bias = near[:, :128] if hi - lo == 128 else near
                if hi - lo == 384:
                    bias = jnp.concatenate([near, far], axis=1)
                part = jnp.exp(s[lo : lo + 128, lo:hi] + bias)
                d_part = part * dp[lo : lo + 128, lo:hi]
                if j == 0:
                    rel_acc[n] = d_part
                else:
                    rel_acc[n, :, : hi - lo] += d_part
                for rows, block in ((w_rows, part), (ds_rows, d_part)):
                    blocks = [block.astype(jnp.bfloat16)]
                    if lo > 0:
                        blocks.insert(0, jnp.zeros((128, lo), jnp.bfloat16))
                    if hi < SEQ:
                        blocks.append(jnp.zeros((128, SEQ - hi), jnp.bfloat16))
                    rows.append(blocks[0] if len(blocks) == 1 else jnp.concatenate(blocks, axis=1))
            w, ds = jnp.concatenate(w_rows, axis=0), jnp.concatenate(ds_rows, axis=0)
        dvs.append(nn(w, do_tile))
        dks.append(nn(ds, q_tile))
        dqs.append(tn(k_tile, ds))
    if bias_of is not None:
        for n in range(2):
            near = by_distance(rel_acc[n, :, :256])
            dist_ref[pl.ds(2 * p + n, 1), :] = jnp.concatenate(
                [
                    jnp.sum(near, axis=0, keepdims=True),
                    jnp.sum(rel_acc[n, :, 256:], axis=0, keepdims=True),
                ],
                axis=1,
            )
    sub = lax.broadcasted_iota(jnp.int32, (128, SEQ), 0)
    dq = jnp.where(sub < HSIZE, dqs[0], dqs[1]).T * HSIZE**-0.5
    return dq, pick(dks[0], dks[1], lane), pick(dvs[0], dvs[1], lane)


HEAD_COLS = HEADS * HSIZE


def attention_forward(
    tok, mem, aux, win, wout, gains, table, qkv, att1, lse1, x1, qc, kvc, att2, lse2, x2, step
):
    x0 = tok[...].astype(jnp.float32)
    a1 = (x0 * inv_rms(x0) * gains[0:1, :]).astype(jnp.bfloat16)
    for k in range(3):
        cols = slice(k * HEAD_COLS, (k + 1) * HEAD_COLS)
        got = nt(a1, win[cols, :])
        if k == 0:
            got = got.astype(jnp.bfloat16).astype(jnp.float32) * HSIZE**-0.5
        qkv[:, cols] = got.astype(jnp.bfloat16)
    step("projected", 0)
    lse1[...] = jnp.zeros_like(lse1)
    lse2[...] = jnp.zeros_like(lse2)

    @pl.loop(0, HEADS // 2)
    def _(p):
        hot, against = ext_masks(aux[...], 0)
        attend_pair(
            p, qkv[:, tile_cols(p)], qkv[:, tile_cols(p, HEAD_COLS)], qkv[:, tile_cols(p, 2 * HEAD_COLS)],
            hot.astype(jnp.bfloat16), against.astype(jnp.bfloat16), att1, lse1, forward_bias(table),
        )
        step("self", p)

    x1[...] = tok[...].astype(jnp.float32) + nn(att1[...], wout[0:HEAD_COLS, :])
    step("middle", 0)
    a2 = (x1[...] * inv_rms(x1[...]) * gains[1:2, :]).astype(jnp.bfloat16)
    got = nt(a2, win[3 * HEAD_COLS : 4 * HEAD_COLS, :])
    qc[...] = (got.astype(jnp.bfloat16).astype(jnp.float32) * HSIZE**-0.5).astype(jnp.bfloat16)
    for k in range(2):
        kvc[:, k * HEAD_COLS : (k + 1) * HEAD_COLS] = nt(
            mem[...], win[(4 + k) * HEAD_COLS : (5 + k) * HEAD_COLS, :]
        ).astype(jnp.bfloat16)
    step("crossed", 0)

    @pl.loop(0, HEADS // 2)
    def _(p):
        _, against = ext_masks(aux[...], 0)
        hot = pltpu.roll(ext_masks(aux[...], SEGS)[0], 128 - SEGS, 1)
        attend_pair(
            p, qc[:, tile_cols(p)], kvc[:, tile_cols(p)], kvc[:, tile_cols(p, HEAD_COLS)],
            hot.astype(jnp.bfloat16), against.astype(jnp.bfloat16), att2, lse2, None,
        )
        step("cross", p)

    step("attended", 0)
    x2[...] = x1[...] + nn(att2[...], wout[HEAD_COLS : 2 * HEAD_COLS, :])
    step("end", 0)


def ff_kernel(
    x2, cot, keep, gains, w_gate, w_up, w_down, mixed, g2, d_gain, g_win, g_wout, a3, e3, acc, da3, held, sem
):
    c = pl.program_id(0)
    slot = lax.rem(c, 2)
    rows = w_gate.shape[0]
    first = pl.multiple_of(c * rows, rows)
    puts = [
        pltpu.make_async_copy(held.at[slot, 0], g_win.at[pl.ds(6 * HEAD_COLS + first, rows)], sem.at[slot, 0]),
        pltpu.make_async_copy(held.at[slot, 1], g_win.at[pl.ds(6 * HEAD_COLS + FF + first, rows)], sem.at[slot, 1]),
        pltpu.make_async_copy(held.at[slot, 2], g_wout.at[pl.ds(2 * HEAD_COLS + first, rows)], sem.at[slot, 2]),
    ]

    @pl.when(c >= 2)
    def _():
        for put in puts:
            put.wait()

    @pl.when(c == 0)
    def _():
        a3[...] = (x2[...] * inv_rms(x2[...]) * gains[2:3, :]).astype(jnp.bfloat16)
        e3[...] = (cot[...].astype(jnp.float32) * keep[:, 0:1]).astype(jnp.bfloat16)
        acc[...] = x2[...]
        da3[...] = jnp.zeros_like(da3)

    gate = nt(a3[...], w_gate[...])
    up = nt(a3[...], w_up[...])
    dh = nt(e3[...], w_down[...])
    cube = 0.044715 * gate * gate
    inner = jnp.tanh(GELU_SCALE * gate * (1.0 + cube))
    half = 0.5 * (1.0 + inner)
    gelu = gate * half
    slope = half + 0.5 * gate * (1.0 - inner * inner) * (GELU_SCALE * (1.0 + 3.0 * cube))
    hidden = (gelu * up).astype(jnp.bfloat16)
    d_gate = (dh * up * slope).astype(jnp.bfloat16)
    d_up = (dh * gelu).astype(jnp.bfloat16)
    acc[...] += nn(hidden, w_down[...])
    held[slot, 0] = tn(d_gate, a3[...]).astype(jnp.bfloat16)
    held[slot, 1] = tn(d_up, a3[...]).astype(jnp.bfloat16)
    held[slot, 2] = tn(hidden, e3[...]).astype(jnp.bfloat16)
    for put in puts:
        put.start()
    da3[...] += nn(d_gate, w_gate[...]) + nn(d_up, w_up[...])

    @pl.when(c == pl.num_programs(0) - 1)
    def _():
        mixed[...] = acc[...].astype(jnp.bfloat16)
        part, gain = rms_back(x2[...], gains[2:3, :], da3[...])
        g2[...] = cot[...].astype(jnp.float32) * keep[:, 0:1] + part
        d_gain[...] = gain
        for k in range(3):
            for other in range(2):
                pltpu.make_async_copy(held.at[other, k], g_wout.at[0:rows], sem.at[other, k]).wait()


SELF_LATE = 5
LATE = 4


BACK_BLOCKS = (("o", 1), ("i", 4), ("i", 5), ("i", 3), ("o", 0), ("i", 0), ("i", 1), ("i", 2))


def attention_backward(
    tok, mem, aux, gains, table, qkv, att1, lse1, x1, qc, kvc, att2, lse2, g2,
    d_mem, d_tok, d_gains, dist, do, dqkv, rel_acc, weight, need, emit, step,
):
    need(1)
    e2 = g2[...].astype(jnp.bfloat16)
    do[...] = weight(0, lambda w: nt(e2, w)).astype(jnp.bfloat16)
    need(8)
    emit("o", HEAD_COLS, tn(att2[...], e2))

    def cross_pairs(first, last):
        @pl.loop(first, last)
        def _(p):
            _, against = ext_masks(aux[...], 0)
            hot = pltpu.roll(ext_masks(aux[...], SEGS)[0], 128 - SEGS, 1)
            dq, dk, dv = back_pair(
                p, qc[:, tile_cols(p)], kvc[:, tile_cols(p)], kvc[:, tile_cols(p, HEAD_COLS)], do[:, tile_cols(p)],
                att2[:, tile_cols(p)], lse2[...], hot, against, None, rel_acc, dist,
            )
            dqkv[:, tile_cols(p)] = dq.astype(jnp.bfloat16)
            dqkv[:, tile_cols(p, HEAD_COLS)] = dk.astype(jnp.bfloat16)
            dqkv[:, tile_cols(p, 2 * HEAD_COLS)] = dv.astype(jnp.bfloat16)
            step("cross", p, first, last)

    late = 2 * HEAD_COLS + LATE * 128
    cross_pairs(LATE, HEADS // 2)
    emit("i", 3 * HEAD_COLS + late, tn(dqkv[:, late:], mem[...]))
    step("late", None, 0, 0)
    cross_pairs(0, LATE)
    need(12)
    a2 = (x1[...] * inv_rms(x1[...]) * gains[1:2, :]).astype(jnp.bfloat16)
    emit("i", 3 * HEAD_COLS, tn(dqkv[:, 0:HEAD_COLS], a2))
    emit("i", 4 * HEAD_COLS, tn(dqkv[:, HEAD_COLS : 2 * HEAD_COLS], mem[...]))
    step("mid", 0, 0, 0)
    emit("i", 5 * HEAD_COLS, tn(dqkv[:, 2 * HEAD_COLS : late], mem[...]))
    d_rows = weight(1, lambda w: nn(dqkv[:, HEAD_COLS : 2 * HEAD_COLS], w))
    d_rows += weight(2, lambda w: nn(dqkv[:, 2 * HEAD_COLS : 3 * HEAD_COLS], w))
    d_mem[...] = d_rows.astype(jnp.bfloat16)
    step("mid", 1, 0, 0)
    da2 = weight(3, lambda w: nn(dqkv[:, 0:HEAD_COLS], w))
    part, gain = rms_back(x1[...], gains[1:2, :], da2)
    d_gains[1:2, :] = gain
    g2[...] += part
    step("mid", 2, 0, 0)
    e1 = g2[...].astype(jnp.bfloat16)
    do[...] = weight(4, lambda w: nt(e1, w)).astype(jnp.bfloat16)
    emit("o", 0, tn(att1[...], e1))
    step("middle", None, 0, 0)

    def self_pairs(first, last):
        @pl.loop(first, last)
        def _(p):
            hot, against = ext_masks(aux[...], 0)
            dq, dk, dv = back_pair(
                p, qkv[:, tile_cols(p)], qkv[:, tile_cols(p, HEAD_COLS)], qkv[:, tile_cols(p, 2 * HEAD_COLS)],
                do[:, tile_cols(p)], att1[:, tile_cols(p)], lse1[...], hot, against, back_bias(table), rel_acc, dist,
            )
            dqkv[:, tile_cols(p)] = dq.astype(jnp.bfloat16)
            dqkv[:, tile_cols(p, HEAD_COLS)] = dk.astype(jnp.bfloat16)
            dqkv[:, tile_cols(p, 2 * HEAD_COLS)] = dv.astype(jnp.bfloat16)
            step("self", p, first, last)

    x0 = tok[...].astype(jnp.float32)
    a1 = (x0 * inv_rms(x0) * gains[0:1, :]).astype(jnp.bfloat16)
    late = 2 * HEAD_COLS + SELF_LATE * 128
    self_pairs(SELF_LATE, HEADS // 2)
    emit("i", late, tn(dqkv[:, late:], a1))
    step("self late", None, 0, 0)
    self_pairs(0, SELF_LATE)
    x0 = tok[...].astype(jnp.float32)
    a1 = (x0 * inv_rms(x0) * gains[0:1, :]).astype(jnp.bfloat16)
    for first, last in ((0, HEAD_COLS), (HEAD_COLS, 2 * HEAD_COLS), (2 * HEAD_COLS, late)):
        emit("i", first, tn(dqkv[:, first:last], a1))
    step("last", None, 0, 0)
    da1 = weight(5, lambda w: nn(dqkv[:, 0:HEAD_COLS], w))
    for k in (1, 2):
        step("end", k - 1, 0, 0)
        da1 += weight(5 + k, lambda w: nn(dqkv[:, k * HEAD_COLS : (k + 1) * HEAD_COLS], w))
    part, gain = rms_back(x0, gains[0:1, :], da1)
    d_gains[0:1, :] = gain
    d_tok[...] = (g2[...] + part).astype(jnp.bfloat16)


SHARE = {"i": 272, "o": 112}
PIECES = (
    ("i", 0, 64, 32), ("i", 64, 64, 32), ("i", 128, 64, 32), ("i", 192, 80, 48),
    ("o", 0, 64, 32), ("o", 64, 48, 16),
)


LEAD = 4


def place():
    dp = lax.axis_index("dp")
    return dp // 4, (dp // 2) % 2, dp % 2, lax.axis_index("group")


def dev(z, y, x, g):
    return ((z * 2 + y) * 2 + x, g)


def rows_of(ref, kind, zz, yy, xx, gg, lo, n):
    share = ((zz * 2 + yy) * 2 + xx) * 2 + gg
    return ref.at[pl.ds(pl.multiple_of(share * SHARE[kind] + lo, 16), n)]


class Links:
    def __init__(self, send_sem, recv_sem):
        self.send_sem, self.recv_sem, self.sends, self.recvs = send_sem, recv_sem, 0, 0

    def new_send(self):
        self.sends += 1
        assert self.sends <= self.send_sem.shape[0]
        return self.sends - 1

    def new_recv(self, n=1):
        self.recvs += n
        assert self.recvs <= self.recv_sem.shape[0]
        return self.recvs - n

    def copy(self, src, dst, device, send=None, recv=None):
        send = self.new_send() if send is None else send
        recv = self.new_recv() if recv is None else recv
        return pltpu.make_async_remote_copy(
            src_ref=src, dst_ref=dst, send_sem=self.send_sem.at[send], recv_sem=self.recv_sem.at[recv],
            device_id=device, device_id_type=MESH,
        )

    def sent(self, send, like):
        wait_bytes(self.send_sem.at[send], like)

    def arrived(self, recv, like):
        wait_bytes(self.recv_sem.at[recv], like)


def wait_bytes(sem, like):
    pltpu.make_async_copy(like, like, sem).wait()


def drain_line(links, send, like, rows):
    z = place()[0]
    for k, n in enumerate(rows):
        if n > 0:
            pl.when(z == k)(functools.partial(links.sent, send, like.at[0:n]))


def greet(peers):
    barrier = pltpu.get_barrier_semaphore()
    total = 0
    for device, cond in peers:
        if cond is None:
            pl.semaphore_signal(barrier, inc=1, device_id=device, device_id_type=MESH)
            total = total + 1
        else:

            @pl.when(cond)
            def _(device=device):
                pl.semaphore_signal(barrier, inc=1, device_id=device, device_id_type=MESH)

            total = total + cond.astype(jnp.int32)
    pl.semaphore_wait(barrier, total)


def near_peers():
    z, y, x, g = place()
    return [
        (dev(z, y, 1 - x, g), None), (dev(z, 1 - y, x, g), None), (dev(z, y, x, 1 - g), None),
        (dev(jnp.minimum(z + 1, 3), y, x, g), z < 3), (dev(jnp.maximum(z - 1, 0), y, x, g), z > 0),
    ]


def all_peers():
    z, y, x, g = place()
    me = lax.axis_index("dp")
    return [((lax.rem(me + k, 16), g), None) for k in range(1, 16)] + [(dev(z, y, x, 1 - g), None)]


class Gather:
    def __init__(self, links, arrays):
        z, y, x, g = place()
        self.links, self.items, self.arrays = links, [], arrays
        self.send = {k: links.new_send() for k in ("plane", "core", "up", "down")}
        self.groups, self.cores = ((0, 12), (12, 16), (16, 24)), []
        for first, last in self.groups:
            self.cores += [links.new_recv()] * (last - first)
        for low in (0, 2):
            nearest = jnp.clip(z, 0, 1) if low == 0 else low
            bases = [links.new_recv(2) for _ in PIECES]
            for zz in (nearest, 2 * low + 1 - nearest):
                for (kind, lo, n, half), line in zip(PIECES, bases):

                    def here(yy, xx, first, count, zz=zz, kind=kind):
                        return rows_of(arrays[kind], kind, zz, yy, xx, g, first, count)

                    c = {"go_up": (z >= zz) & (z < 3), "go_down": (z <= zz) & (z > 0), "n": n}
                    c["from_below"], c["from_above"] = z > zz, z < zz
                    c["hops"] = jnp.abs(z - zz)
                    core = self.cores[len(self.items)]

                    def add(name, ref, device, send, recv=None, c=c):
                        c[name] = links.copy(ref, ref, device, self.send[send], recv)

                    own = here(y, x, lo, n)
                    add("up", own, dev(jnp.minimum(z + 1, 3), y, x, g), "up", line + zz - low)
                    add("down", own, dev(jnp.maximum(z - 1, 0), y, x, g), "down", line + zz - low)
                    add("x", own, dev(z, y, 1 - x, g), "plane")
                    add("y", own, dev(z, 1 - y, x, g), "plane")
                    add("a", here(y, 1 - x, lo, half), dev(z, 1 - y, x, g), "plane")
                    add("b", here(1 - y, x, lo + half, n - half), dev(z, y, 1 - x, g), "plane")
                    other = dev(z, y, x, 1 - g)
                    add("p", own, other, "core", core)
                    add("px", here(y, 1 - x, lo, n), other, "core", core)
                    add("py", here(1 - y, x, lo, n), other, "core", core)
                    add("pa", here(1 - y, 1 - x, lo, half), other, "core", core)
                    add("pb", here(1 - y, 1 - x, lo + half, n - half), other, "core", core)
                    self.items.append(c)

    def along(self, c):
        pl.when(c["from_below"])(c["up"].wait_recv)
        pl.when(c["from_above"])(c["down"].wait_recv)
        pl.when(c["go_up"])(c["up"].start)
        pl.when(c["go_down"])(c["down"].start)

    def hop(self, c, h):
        pl.when(c["hops"] == h)(functools.partial(self.along, c))

    def near(self, c):
        for k in ("x", "y", "p"):
            c[k].start()

    def second(self, c):
        c["x"].wait_recv()
        c["a"].start()
        c["px"].start()
        c["y"].wait_recv()
        c["b"].start()
        c["py"].start()

    def third(self, c):
        c["a"].wait_recv()
        c["pa"].start()
        c["b"].wait_recv()
        c["pb"].start()

    def arrived(self, group):
        first, last = self.groups[group]
        rows = 4 * sum(c["n"] for c in self.items[first:last])
        self.links.arrived(self.cores[first], self.arrays["i"].at[0:rows])

    def drain(self):
        rows = sum(c["n"] for c in self.items)
        like = self.arrays["i"]
        self.links.sent(self.send["plane"], like.at[0 : 3 * rows])
        self.links.sent(self.send["core"], like.at[0 : 4 * rows])
        plane = rows // 4
        drain_line(self.links, self.send["up"], like, [plane, 2 * plane, 3 * plane, 0])
        drain_line(self.links, self.send["down"], like, [0, 3 * plane, 2 * plane, plane])

    def slots(self):
        n = len(self.items)
        half = n // 2
        lead = LEAD
        out = [[] for _ in range(n + 6)]
        for t, c in enumerate(self.items):
            out[t + 6].append(functools.partial(self.third, c))
        for t, c in enumerate(self.items):
            out[t + 3].append(functools.partial(self.second, c))
        for t, c in enumerate(self.items):
            if t < half:
                out[t].append(functools.partial(self.along, c))
            out[t].append(functools.partial(self.near, c))
        for t, c in enumerate(self.items[half:]):
            for h in range(4):
                out[half + t - lead + h].append(functools.partial(self.hop, c, h))
        return out


class Exchange:
    def __init__(self, links, src, dst, rows):
        me, g = lax.axis_index("dp"), lax.axis_index("group")
        self.links, self.send, self.recv = links, links.new_send(), links.new_recv()
        self.like, self.copies = src.at[0 : 15 * rows], []
        for k in range(1, 16):
            to = lax.rem(me + k, 16)
            there = dst.at[pl.ds(pl.multiple_of(me * rows, 16), rows)]
            here = src.at[pl.ds(pl.multiple_of(to * rows, 16), rows)]
            self.copies.append(links.copy(here, there, (to, g), self.send, self.recv))

    def arrived(self):
        self.links.arrived(self.recv, self.like)

    def drain(self):
        self.links.sent(self.send, self.like)


def own_rows(src, dst, rows, sem):
    here = pl.ds(pl.multiple_of(lax.axis_index("dp") * rows, 16), rows)
    return pltpu.make_async_copy(src.at[here], dst.at[here], sem)


class Sums:
    def __init__(self, links, win_g, wout_g, own, got, plane, fin, line, part_in, part_out, load_sem):
        self.links, self.arrays = links, {"i": win_g, "o": wout_g}
        self.own, self.got, self.plane, self.fin, self.line = own, got, plane, fin, line
        self.part_in, self.part_out, self.load_sem = part_in, part_out, load_sem
        self.loads, self.rows, self.line_rows, self.got_rows = 0, 0, 0, 0
        self.send = {k: links.new_send() for k in ("core", "plane", "up", "down")}

    def batch(self, members, got_from=None):
        z, y, x, g = place()
        self.got_rows = self.got_rows if got_from is None else got_from
        links = self.links
        items = []
        for zz, k in members:
            kind, lo, n, half = PIECES[k]
            base, rest = self.rows, n - half
            at = lambda ref, c, off, m, base=base: ref.at[c, pl.ds(base + off, m)]
            it = {"zz": zz, "z": z, "n": n, "half": half, "base": base, "kind": kind, "lo": lo}
            it["load"], it["core"], it["pair"] = [], links.new_recv(), []
            it["got"] = self.got_rows
            self.got_rows += n
            it["load_sem"] = self.load_sem.at[self.loads]
            self.loads += 1
            for c, (yy, xx) in enumerate(((y, x), (y, 1 - x), (1 - y, x), (1 - y, 1 - x))):
                ref = self.arrays[kind]
                mine = rows_of(ref, kind, zz, yy, xx, g, lo, n)
                it["load"].append(pltpu.make_async_copy(mine, at(self.own, c, 0, n), it["load_sem"]))
                theirs = rows_of(ref, kind, zz, yy, xx, 1 - g, lo, n)
                it["pair"].append(
                    links.copy(theirs, self.got.at[c, pl.ds(it["got"], n)], dev(z, y, x, 1 - g), self.send["core"], it["core"])
                )
            nx, ny = dev(z, y, 1 - x, g), dev(z, 1 - y, x, g)
            own, plane, fin, send = self.own, self.plane, self.fin, self.send["plane"]
            it["x_recv"], it["y_recv"] = links.new_recv(), links.new_recv()
            it["x1"] = [
                links.copy(at(own, c, 0, half), at(plane, s, 0, half), nx, send, it["x_recv"]) for s, c in ((0, 1), (1, 3))
            ]
            it["y1"] = [
                links.copy(at(own, c, half, rest), at(plane, s, half, rest), ny, send, it["y_recv"])
                for s, c in ((0, 2), (1, 3))
            ]
            it["y2"] = links.copy(at(own, 2, 0, half), at(fin, 0, 0, half), ny, send)
            it["x2"] = links.copy(at(own, 1, half, rest), at(fin, 0, half, rest), nx, send)
            for way, needed in (("from_below", zz > 0), ("from_above", zz < 3)):
                if needed:
                    it[way] = pl.ds(self.line_rows, n)
                    self.line_rows += n
            if zz > 0:
                up = dev(jnp.minimum(z + 1, 3), y, x, g)
                it["up"] = links.copy(at(own, 0, 0, n), self.line.at[it["from_below"]], up, self.send["up"])
            if zz < 3:
                down = dev(jnp.maximum(z - 1, 0), y, x, g)
                it["down"] = links.copy(at(own, 0, 0, n), self.line.at[it["from_above"]], down, self.send["down"])
            items.append(it)
            self.rows += n
        return items

    def begin(self, items):
        for it in items:
            for c in it["load"]:
                c.start()
            for c in it["pair"]:
                c.start()

    def drain(self):
        rows, plane = self.rows, self.rows // 4
        like = self.arrays["i"]
        self.links.sent(self.send["core"], like.at[0 : 4 * rows])
        self.links.sent(self.send["plane"], like.at[0 : 3 * rows])
        drain_line(self.links, self.send["up"], like, [3 * plane, 2 * plane, plane, 0])
        drain_line(self.links, self.send["down"], like, [0, plane, 2 * plane, 3 * plane])

    def place_in(self, slots, first, items):
        for k, it in enumerate(items):
            t = first + k
            slots[t].append((2, self.to_core, it))
            slots[t + 3].append((1, self.to_plane, it))
            slots[t + 6].append((0, self.to_line, it))
            for h in range(1, max(it["zz"], 3 - it["zz"]) + 1):
                slots[t + 6 + 2 * h].append((-h, functools.partial(self.hop, h), it))

    @staticmethod
    def add(dst, c, first, src, s, start, m):
        rows = pl.ds(first, m)
        more = src[s, pl.ds(start, m), :].astype(jnp.float32)
        dst[c, rows, :] = (dst[c, rows, :].astype(jnp.float32) + more).astype(jnp.bfloat16)

    def add_line(self, it, way):
        rows = pl.ds(it["base"], it["n"])
        more = self.line[it[way], :].astype(jnp.float32)
        self.own[0, rows, :] = (self.own[0, rows, :].astype(jnp.float32) + more).astype(jnp.bfloat16)

    def to_core(self, it):
        rows = pl.ds(it["base"], it["n"])
        wait_bytes(it["load_sem"], self.own.at[:, rows])
        self.links.arrived(it["core"], self.got.at[:, pl.ds(it["got"], it["n"])])
        for c in (3, 1, 2, 0):
            self.add(self.own, c, it["base"], self.got, c, it["got"], it["n"])
            if c == 3:
                it["x1"][1].start()
                it["y1"][1].start()
            if c == 1:
                it["x1"][0].start()
            if c == 2:
                it["y1"][0].start()

    def to_plane(self, it):
        half, rest, base = it["half"], it["n"] - it["half"], it["base"]
        low = base + half
        self.links.arrived(it["x_recv"], self.plane.at[:, pl.ds(base, half)])
        self.add(self.own, 2, base, self.plane, 1, base, half)
        it["y2"].start()
        self.links.arrived(it["y_recv"], self.plane.at[:, pl.ds(low, rest)])
        self.add(self.own, 1, low, self.plane, 1, low, rest)
        it["x2"].start()
        self.add(self.own, 0, base, self.plane, 0, base, half)
        self.add(self.own, 0, low, self.plane, 0, low, rest)

    def to_line(self, it):
        it["y2"].wait_recv()
        it["x2"].wait_recv()
        self.add(self.own, 0, it["base"], self.fin, 0, it["base"], it["n"])
        z, zz = it["z"], it["zz"]
        if zz > 0:
            pl.when(z == 0)(it["up"].start)
        if zz < 3:
            pl.when(z == 3)(it["down"].start)

    def hop(self, h, it):
        z, zz, n, base = it["z"], it["zz"], it["n"], it["base"]
        if h < zz:

            @pl.when(z == h)
            def _():
                it["up"].wait_recv()
                self.add_line(it, "from_below")
                it["up"].start()

        if h < 3 - zz:

            @pl.when(z == 3 - h)
            def _():
                it["down"].wait_recv()
                self.add_line(it, "from_above")
                it["down"].start()

        if h == max(zz, 3 - zz):

            @pl.when(z == zz)
            def _():
                total = self.own[0, pl.ds(base, n), :].astype(jnp.float32)
                if zz > 0:
                    it["up"].wait_recv()
                    total += self.line[it["from_below"], :].astype(jnp.float32)
                if zz < 3:
                    it["down"].wait_recv()
                    total += self.line[it["from_above"], :].astype(jnp.float32)
                into = self.part_in if it["kind"] == "i" else self.part_out
                into[it["lo"] : it["lo"] + n, :] = total


def run_slot(slot):
    for _, step, it in sorted(slot, key=lambda entry: entry[0]):
        step(it)


def total_steps(links, ref, room):
    z, y, x, g = place()
    here = y * 2 + x
    core = links.copy(ref, room.at[0], dev(z, y, x, 1 - g))
    plane = [
        links.copy(ref, room.at[1], dev(z, y, 1 - x, g)),
        links.copy(ref, room.at[2], dev(z, 1 - y, x, g)),
        links.copy(ref, room.at[3], dev(z, 1 - y, 1 - x, g)),
    ]
    line = [links.copy(ref, room.at[3 + k], dev(lax.rem(z + k, 4), y, x, g)) for k in (1, 2, 3)]

    def in_order(first, came_from):
        mine = ref[...]
        total = jnp.zeros_like(mine)
        for n in range(4):
            came = came_from(n)
            term = jnp.where(came == 0, mine, jnp.zeros_like(mine))
            for k in (1, 2, 3):
                term = jnp.where(came == k, room[first + k], term)
            total = total + term
        return total

    def to_plane():
        core.wait()
        ref[...] = ref[...] + room[0]
        for c in plane:
            c.start()

    def to_line():
        for c in plane:
            c.wait()
        ref[...] = in_order(0, lambda n: jnp.bitwise_xor(here, n))
        for c in line:
            c.start()

    def finish():
        for c in line:
            c.wait()
        ref[...] = in_order(3, lambda n: lax.rem(z - n + 4, 4))

    return [core.start, to_plane, to_line, finish]


def vmem_call(kernel, out_shape, scratch, **kw):
    return pl.pallas_call(
        kernel,
        out_shape=out_shape,
        scratch_shapes=scratch,
        compiler_params=pltpu.CompilerParams(vmem_limit_bytes=VMEM_BYTES),
        **kw,
    )


def sds(shape, dtype=jnp.bfloat16):
    return jax.ShapeDtypeStruct(shape, dtype)


WEIGHTS = [pltpu.VMEM((6 * HEAD_COLS, WIDTH), jnp.bfloat16), pltpu.VMEM((2 * HEAD_COLS, WIDTH), jnp.bfloat16)]


def load_rows(src, dst, first, last, sem):
    copy = pltpu.make_async_copy(src.at[first:last], dst.at[first:last], sem)
    copy.start()
    return copy


def anywhere():
    return pl.BlockSpec(memory_space=pl.ANY)


def whole():
    return pl.BlockSpec(memory_space=pltpu.VMEM)


def run(steps):
    for s in steps:
        s()


def block_of(ids, edges):
    return (ids >= edges[0]).astype(jnp.int32) + (ids >= edges[1]).astype(jnp.int32)


IN_EDGES = (3 * HEAD_COLS, 6 * HEAD_COLS)
OUT_EDGES = (HEAD_COLS, 2 * HEAD_COLS)


def block_sums(part_in_t, part_out, rows_out, first_in, first_out):
    sq_in, sq_out = part_in_t * part_in_t, part_out * part_out
    block_in = block_of(first_in + lax.broadcasted_iota(jnp.int32, (sq_in.shape[0], 1), 0), IN_EDGES)
    block_out = block_of(first_out + lax.broadcasted_iota(jnp.int32, (sq_out.shape[0], 1), 0), OUT_EDGES)
    rows_new = DECAY_RATE * rows_out + (1 - DECAY_RATE) * jnp.mean(sq_out, axis=1, keepdims=True)
    lane = lax.broadcasted_iota(jnp.int32, (1, WIDTH), 1)
    lines = [jnp.sum(jnp.where(block_in == k, sq_in, 0.0), axis=0, keepdims=True) for k in range(3)]
    lines += [jnp.sum(jnp.where(block_out == k, sq_out, 0.0), axis=0, keepdims=True) for k in range(3)]
    totals = jnp.zeros((1, WIDTH), jnp.float32)
    for k in range(3):
        total = jnp.sum(jnp.where(block_out == k, rows_new, 0.0), axis=0, keepdims=True)
        totals = jnp.where(lane == k, total, totals)
    return jnp.concatenate(lines + [totals, jnp.zeros((1, WIDTH), jnp.float32)], axis=0)


def prep_kernel(
    ids, row_source, modes, tokens, memory, segments, msegments, w_in, w_out, rel_bias, hot, sentinel,
    tok_s, mem_s, aux_s, win_sh, wout_sh, table_f, table_b, keep, mode_rows, seg_t, mseg_t,
):
    half_rows, length = tokens.shape[0], tokens.shape[1]
    groups, group, where = ids[0], ids[1], ids[2]
    win_sh[...] = w_in[...].astype(jnp.bfloat16)
    wout_sh[...] = w_out[...].astype(jnp.bfloat16)
    for source, out in ((segments, seg_t), (msegments, mseg_t)):
        out[0:half_rows, 0:length] = source[...].astype(jnp.float32)
        out[...] = out[...].T
    lane = lax.broadcasted_iota(jnp.int32, (length, 128), 1)
    spot = (lane & (HSIZE - 1)).astype(jnp.float32)

    @pl.loop(0, half_rows)
    def _(i):
        source = row_source[i * groups + group] - group * half_rows
        tok_s[i] = tokens[source]
        mem_s[i] = memory[source]
        col = jnp.sum(jnp.where(lane == source, seg_t[0:length, :], 0.0), axis=1, keepdims=True)
        mcol = jnp.sum(jnp.where(lane == source, mseg_t[0:length, :], 0.0), axis=1, keepdims=True)
        same = ((spot < SEGS) & (spot == col)) | ((spot >= SEGS) & (spot < 2 * SEGS) & (spot - SEGS == mcol))
        aux_s[i] = jnp.where(same, 1.0, 0.0).astype(jnp.bfloat16)

    mode = modes[row_source[where]]
    tables = jnp.dot(rel_bias[mode], hot[...], precision=PRECISE, preferred_element_type=jnp.float32)
    for k, table in enumerate((table_f, table_b)):
        table[...] = jnp.zeros_like(table)
        table[0:HEADS, :] = tables[:, k * 256 : (k + 1) * 256]
    mode_rows[...] = jnp.where(lax.broadcasted_iota(jnp.int32, (8, 128), 0) == mode, 1.0, 0.0)
    kept = (1 - sentinel[...]).astype(jnp.float32)
    keep[...] = jnp.broadcast_to(kept, (128, SEQ)).T


def prep_call(ids, row_source, modes, tokens, memory, segments, msegments, w_in, w_out, rel_bias, hot, sentinel):
    f32 = jnp.float32
    scalars = pl.BlockSpec(memory_space=pltpu.SMEM)
    half_rows, length = tokens.shape[0], tokens.shape[1]
    return vmem_call(
        prep_kernel,
        (
            sds(tokens.shape), sds(memory.shape), sds((half_rows, length, 128)), sds(w_in.shape),
            sds(w_out.shape), sds((16, 256), f32), sds((16, 256), f32), sds((SEQ, 128), f32), sds((8, 128), f32),
        ),
        [pltpu.VMEM((128, 128), f32), pltpu.VMEM((128, 128), f32)],
        in_specs=[scalars] * 3 + [whole()] * 9,
    )(ids, row_source, modes, tokens, memory, segments, msegments, w_in, w_out, rel_bias, hot, sentinel)


def upright(row):
    return jnp.broadcast_to(row, (128, row.shape[1])).T[:, 0:1]


def level(col):
    return jnp.broadcast_to(col, (col.shape[0], 128)).T[0:1, :]


def update_kernel(
    ids, row_source, part_in_t, part_out, sums, early, back_tok, back_mem, w_in, w_out, gains, rel_bias, rows_in,
    cols_in, rows_out, cols_out, sq_gains, sq_rel,
    d_tokens, d_memory, grad_in, grad_out, grad_gains, grad_rel, new_in, new_out, new_gains, new_rel, rows_in_new,
    cols_in_new, rows_out_new, cols_out_new, sq_gains_new, sq_rel_new,
):
    half_rows = back_tok.shape[0]
    groups, group, where = ids[0], ids[1], ids[2]

    @pl.loop(0, half_rows)
    def _(i):
        source = row_source[i * groups + group] - group * half_rows
        d_tokens[source] = back_tok[i]
        d_memory[source] = back_mem[i]

    n_in, n_out = w_in.shape[0], w_out.shape[0]
    p_in = part_in_t[...]
    grad_in[...] = p_in
    in_cols = DECAY_RATE * upright(cols_in[...]) + (1 - DECAY_RATE) * jnp.mean(p_in * p_in, axis=1, keepdims=True)
    cols_in_new[...] = level(in_cols)
    block_in = block_of(where * n_in + lax.broadcasted_iota(jnp.int32, (n_in, 1), 0), IN_EDGES)
    scale = jnp.zeros((n_in, WIDTH), jnp.float32)
    for k, count in enumerate((3 * HEAD_COLS, 3 * HEAD_COLS, 2 * FF)):
        row = DECAY_RATE * rows_in[k : k + 1, :] + (1 - DECAY_RATE) * (sums[k : k + 1, :] / count)
        rows_in_new[k : k + 1, :] = row
        scale = jnp.where(block_in == k, in_cols * (row / jnp.mean(row, axis=1, keepdims=True)), scale)
    new_in[...] = w_in[...] - STEP_SIZE * p_in * lax.rsqrt(scale)

    p_out = part_out[...]
    grad_out[...] = p_out
    out_rows = DECAY_RATE * upright(rows_out[...]) + (1 - DECAY_RATE) * jnp.mean(p_out * p_out, axis=1, keepdims=True)
    rows_out_new[...] = level(out_rows)
    block_out = block_of(where * n_out + lax.broadcasted_iota(jnp.int32, (n_out, 1), 0), OUT_EDGES)
    scale = jnp.zeros((n_out, WIDTH), jnp.float32)
    for k, count in enumerate((HEAD_COLS, HEAD_COLS, FF)):
        col = DECAY_RATE * cols_out[k : k + 1, :] + (1 - DECAY_RATE) * (sums[3 + k : 4 + k, :] / count)
        cols_out_new[k : k + 1, :] = col
        mean = sums[6:7, k : k + 1] / count
        scale = jnp.where(block_out == k, (out_rows / mean) * col, scale)
    new_out[...] = w_out[...] - STEP_SIZE * p_out * lax.rsqrt(scale)

    g = early[0:3, 0:WIDTH]
    rel = jnp.concatenate([early[:, WIDTH : WIDTH + 128], early[:, WIDTH + 128 : WIDTH + 256]], axis=0)
    grad_gains[...] = g
    sq = DECAY_RATE * sq_gains[...] + (1 - DECAY_RATE) * g * g
    sq_gains_new[...] = sq
    new_gains[...] = gains[...] - PLAIN_STEP * g * lax.rsqrt(sq)
    for k in range(MODES):
        g = rel[0:HEADS, k * BUCKETS : (k + 1) * BUCKETS]
        grad_rel[k] = g
        sq = DECAY_RATE * sq_rel[k] + (1 - DECAY_RATE) * g * g
        sq_rel_new[k] = sq
        new_rel[k] = rel_bias[k] - PLAIN_STEP * g * lax.rsqrt(sq)


def update_call(ids, row_source, *arrays):
    f32 = jnp.float32
    scalars = pl.BlockSpec(memory_space=pltpu.SMEM)
    (part_in_t, part_out, sums, early, back_tok, back_mem, w_in, w_out, gains, rel_bias) = arrays[:10]
    n_in, n_out = w_in.shape[0], w_out.shape[0]
    three = sds((3, WIDTH), f32)
    rel = sds(rel_bias.shape, f32)
    return vmem_call(
        update_kernel,
        (
            sds(back_tok.shape), sds(back_mem.shape), sds(w_in.shape, f32), sds(w_out.shape, f32), three, rel,
            sds(w_in.shape, f32), sds(w_out.shape, f32), three, rel, three, sds((1, n_in), f32), sds((1, n_out), f32),
            three, three, rel,
        ),
        [],
        in_specs=[scalars] * 2 + [whole()] * len(arrays),
    )(ids, row_source, *arrays)


ROWS_FROM = 10
TOK_RATE = 3


def forward_kernel(boxed, *refs):
    n_in = 5
    ins, refs = refs[:n_in], refs[n_in:]
    (gains, table), refs = refs[:2], refs[2:]
    if boxed:
        win_sh, wout_sh, tok_s, mem_s, aux_s = ins
        (win, wout), rows_out, refs = refs[:2], refs[2:5], refs[5:]
    else:
        tok_s, mem_s, aux_s, win, wout = ins
        rows_out = None
    kept_out, kept, (tok, mem, aux), refs = refs[:9], refs[9:18], refs[18:21], refs[21:]
    (win_v, wout_v, sem, put_sem, ls), refs = refs[:5], refs[5:]
    puts = []

    def keep(src, dst):
        puts.append(pltpu.make_async_copy(src, dst, put_sem.at[len(puts)]))
        puts[-1].start()

    def hand_on(name):
        names = {"projected": (0,), "middle": (1, 2, 3), "crossed": (4, 5), "attended": (6, 7), "end": (8,)}
        for k in names.get(name, ()):
            keep(kept[k], kept_out[k])
        if boxed and name == "projected":
            keep(tok, rows_out[0])
            keep(aux, rows_out[2])
        if boxed and name == "crossed":
            keep(mem, rows_out[1])

    if not boxed:
        loads = [load_rows(win, win_v, 0, 6 * HEAD_COLS, sem.at[0]), load_rows(wout, wout_v, 0, 2 * HEAD_COLS, sem.at[1])]
        for k, (s, t) in enumerate(((tok_s, tok), (mem_s, mem), (aux_s, aux))):
            loads.append(pltpu.make_async_copy(s, t, ls.at[k]))
            loads[-1].start()
        for c in loads:
            c.wait()
        attention_forward(
            tok, mem, aux, win_v, wout_v, gains, table, *kept, step=lambda name, p: hand_on(name)
        )
        for c in puts:
            c.wait()
        return
    ss, rs = refs
    z, y, x, g = place()
    pos = SEQ // 16
    links = Links(ss, rs)
    near = [
        pltpu.make_async_copy(win_sh, rows_of(win, "i", z, y, x, g, 0, 272), ls.at[0]),
        pltpu.make_async_copy(wout_sh, rows_of(wout, "o", z, y, x, g, 0, 112), ls.at[1]),
    ]
    own = [own_rows(s, t, pos, ls.at[2 + k]) for k, (s, t) in enumerate(((tok_s, tok), (mem_s, mem), (aux_s, aux)))]
    for c in near + own:
        c.start()
    greet(all_peers())
    for c in near:
        c.wait()
    gather = Gather(links, {"i": win, "o": wout})
    slots = gather.slots()
    tok_rows, aux_rows, mem_rows = (
        Exchange(links, s, t, pos) for s, t in ((tok_s, tok), (aux_s, aux), (mem_s, mem))
    )
    half = len(gather.items) // 2
    now = half + 6
    queue = [[] for _ in range(len(slots))]
    for k in range(15):
        queue[ROWS_FROM + k // 3] += [tok_rows.copies[k], aux_rows.copies[k]]
        queue[ROWS_FROM + 5 + k // 2].append(mem_rows.copies[k])

    def run_gather(t):
        run(slots[t])
        for c in queue[t]:
            c.start()

    for t in range(now):
        run_gather(t)
    gather.arrived(0)
    loads = [
        load_rows(win, win_v, 0, 3 * HEAD_COLS, sem.at[0]), load_rows(wout, wout_v, 0, 2 * HEAD_COLS, sem.at[1]),
        load_rows(win, win_v, 3 * HEAD_COLS, 16 * 272, sem.at[2]),
    ]
    tok_rows.arrived()
    aux_rows.arrived()
    for c in own:
        c.wait()
    loads[0].wait()
    calls = HEADS // 2
    shares = [range(now + k, now + k + 1) for k in range(calls)]
    shares += [range(now + calls + k, now + calls + k + 1) for k in range(calls)]

    def step(name, p):
        hand_on(name)
        if name == "middle":
            gather.arrived(1)
            more = load_rows(win, win_v, 16 * 272, 6 * HEAD_COLS, sem.at[3])
            mem_rows.arrived()
            loads[2].wait()
            more.wait()
        if name not in ("self", "cross"):
            return
        for k in range(calls):

            @pl.when(p == k)
            def _(k=k):
                for t in shares[k + (0 if name == "self" else calls)]:
                    run_gather(t)
                if name == "self" and k == calls - 1:
                    loads[1].wait()

    attention_forward(tok, mem, aux, win_v, wout_v, gains, table, *kept, step=step)
    for t in range(now + 2 * calls, len(slots)):
        run_gather(t)
    gather.arrived(2)
    for c in puts:
        c.wait()
    gather.drain()
    for rows in (tok_rows, aux_rows, mem_rows):
        rows.drain()


def forward_call(boxed, *arrays):
    f32 = jnp.float32
    dma = pltpu.SemaphoreType.DMA
    outs = (
        sds((SEQ, 3 * HEAD_COLS)), sds((SEQ, HEAD_COLS)), sds((SEQ, 128), f32), sds((SEQ, WIDTH), f32),
        sds((SEQ, HEAD_COLS)), sds((SEQ, 2 * HEAD_COLS)), sds((SEQ, HEAD_COLS)), sds((SEQ, 128), f32),
        sds((SEQ, WIDTH), f32),
    )
    rows = (sds((SEQ, WIDTH)), sds((SEQ, WIDTH)), sds((SEQ, 128)))
    scratch = [pltpu.VMEM(v.shape, v.dtype) for v in outs + rows] + WEIGHTS + [dma((4,)), dma((12,)), dma((5,))]
    specs = [anywhere()] * 5
    extra = {}
    if boxed:
        scratch = scratch + [dma((7,)), dma((20 * len(PIECES) + 6,))]
        outs = (sds((6 * HEAD_COLS + 2 * FF, WIDTH)), sds((2 * HEAD_COLS + FF, WIDTH))) + rows + outs
        specs = [whole()] * 2 + [anywhere()] * 3
        extra = dict(collective_id=1, has_side_effects=True)
    return pl.pallas_call(
        functools.partial(forward_kernel, boxed),
        out_shape=outs,
        scratch_shapes=scratch,
        in_specs=specs + [whole()] * 2,
        out_specs=(anywhere(),) * len(outs),
        compiler_params=pltpu.CompilerParams(vmem_limit_bytes=VMEM_BYTES, **extra),
    )(*arrays)


def ff_call(x2, cot, keep, gains, win, wout):
    f32 = jnp.float32
    step = 512
    n = FF // step
    at = lambda block, first: pl.BlockSpec((step, WIDTH), lambda c: (first + c, 0))
    full = lambda rows, cols: pl.BlockSpec((rows, cols), lambda c: (0, 0))
    gate0, down0 = 6 * HEAD_COLS // step, 2 * HEAD_COLS // step
    return vmem_call(
        ff_kernel,
        (
            sds((SEQ, WIDTH)), sds((SEQ, WIDTH), f32), sds((1, WIDTH), f32), sds(win.shape), sds(wout.shape),
        ),
        [
            pltpu.VMEM((SEQ, WIDTH), jnp.bfloat16), pltpu.VMEM((SEQ, WIDTH), jnp.bfloat16),
            pltpu.VMEM((SEQ, WIDTH), f32), pltpu.VMEM((SEQ, WIDTH), f32),
            pltpu.VMEM((2, 3, step, WIDTH), jnp.bfloat16), pltpu.SemaphoreType.DMA((2, 3)),
        ],
        grid=(n,),
        in_specs=[
            full(SEQ, WIDTH), full(SEQ, WIDTH), full(SEQ, 128), full(3, WIDTH),
            at(step, gate0), at(step, gate0 + n), at(step, down0),
        ],
        out_specs=(full(SEQ, WIDTH), full(SEQ, WIDTH), full(1, WIDTH), anywhere(), anywhere()),
    )(x2, cot, keep, gains, win, win, wout)


def rel_sums(dist, hot_dist, mode_rows):
    by_bucket = jnp.dot(dist, hot_dist, precision=PRECISE, preferred_element_type=jnp.float32)
    lane = lane_of(by_bucket.shape)
    total = jnp.zeros_like(by_bucket)
    for k in range(MODES):
        moved = pltpu.roll(by_bucket * mode_rows[k : k + 1, :], k * BUCKETS, 1)
        total = jnp.where(lane // BUCKETS == k, moved, total)
    return total


def backward_kernel(boxed, _, __, win, wout, *refs):
    lazy, refs = refs[:12], refs[12:]
    (gains, table, hot_dist, mode_rows, gain_three, rows_out), refs = refs[:6], refs[6:]
    if boxed:
        (g_win, g_wout, part_in, part_out, sums, early, btok, bmem), refs = refs[:8], refs[8:]
        (d_mem, d_tok), refs = refs[:2], refs[2:]
    else:
        (g_win, g_wout, d_mem, d_tok, early), refs = refs[:5], refs[5:]
    (d_gains, dist), refs = refs[:2], refs[2:]
    scratch, (held, put_sem, blocks, block_sem, lazy_sem, sem), refs = refs[:3], refs[3:9], refs[9:]
    lazy_v, refs = refs[:12], refs[12:]
    fetched = []

    def fetch(k):
        array, block = BACK_BLOCKS[k]
        src = (win if array == "i" else wout).at[block * HEAD_COLS : (block + 1) * HEAD_COLS]
        fetched.append(pltpu.make_async_copy(src, blocks.at[k % 3], block_sem.at[k]))
        fetched[k].start()

    def weight(k, fn):
        fetched[k].wait()
        value = fn(blocks[k % 3])
        if k + 3 < len(BACK_BLOCKS):
            fetch(k + 3)
        return value

    loads = [pltpu.make_async_copy(s, t, lazy_sem.at[k]) for k, (s, t) in enumerate(zip(lazy, lazy_v))]
    loads[0].start()
    fetch(0)
    for c in loads[1:]:
        c.start()
    fetch(1)
    fetch(2)
    loaded = []

    def need(n):
        while len(loaded) < n:
            loads[len(loaded)].wait()
            loaded.append(True)

    puts, settled = [], []

    def settle(upto):
        while len(settled) < upto:
            puts[len(settled)].wait()
            settled.append(True)

    def emit(array, first, value):
        k = len(puts)
        settle(k - 1)
        rows = value.shape[0]
        held[k % 2, 0:rows] = value.astype(jnp.bfloat16)
        into = g_win if array == "i" else g_wout
        puts.append(pltpu.make_async_copy(held.at[k % 2, 0:rows], into.at[first : first + rows], put_sem.at[k]))
        puts[k].start()

    dist[...] = jnp.zeros_like(dist)
    step = lambda *a: None
    if boxed:
        own, got, plane, fin, line, room, early_room, ss, rs, load_sem, freed = refs
        z, y, x, g = place()
        me = lax.axis_index("dp")
        pos = SEQ // 16
        greet(all_peers())
        links = Links(ss, rs)
        work = Sums(links, g_win, g_wout, own, got, plane, fin, line, part_in, part_out, load_sem)
        n = len(PIECES)
        groups = (
            (0, 0, [(3, k) for k in range(n)]),
            (6, 400, [(2, k) for k in range(n)]),
            (12, 0, [(1, k) for k in range(2, n)] + [(0, k) for k in range(4, n)]),
            (18, 400, [(1, k) for k in range(2)]),
            (20, 528, [(0, k) for k in range(4)]),
        )
        slots = [[] for _ in range(20 + n + 14)]
        batches = []
        for first, got_from, members in groups:
            batches.append(work.batch(members, got_from))
            work.place_in(slots, first, batches[-1])
        mem_rows, tok_rows = Exchange(links, d_mem, bmem, pos), Exchange(links, d_tok, btok, pos)
        kept_mem, kept_tok = own_rows(d_mem, bmem, pos, sem.at[2]), own_rows(d_tok, btok, pos, sem.at[3])
        work.begin(batches[0])
        shares = {("cross", LATE): ((0,), (1,)), ("cross", 0): ((2,), (3,), (4,), (5,))}
        shares["mid"] = ((6,), (7, 8), (9,))
        shares["self", SELF_LATE] = ((10, 11),)
        shares["self", 0] = ((12,), (13,), (14,), (15, 16), (17,))
        shares["end"] = ((18, 19), (20,))
        gates = ("late", "middle", "self late", "last")

        def step(name, p, first, last):
            if name in gates:
                settle(len(puts))
                if name == "middle":
                    kept_mem.start()
                if name in ("middle", "self late"):
                    pl.semaphore_wait(freed, 1)
                work.begin(batches[gates.index(name) + 1])
                return
            if name in ("mid", "end"):
                for t in shares[name][p]:
                    run_slot(slots[t])
                return
            for k, share in enumerate(shares[name, first]):

                @pl.when(p == first + k)
                def _(share=share, k=k):
                    if name == "self":
                        turn = k if first == 0 else 4
                        for c in mem_rows.copies[3 * turn : 3 * turn + 3] if turn < 5 and (first or k < 4) else []:
                            c.start()
                    for t in share:
                        run_slot(slots[t])
                    if n - 1 in share or 2 * n - 1 in share:
                        pl.semaphore_signal(freed, inc=1, device_id=dev(z, y, x, 1 - g), device_id_type=MESH)

    g2, aux, qc, kvc, att2, lse2, mem, x1, att1, qkv, lse1, tok = lazy_v
    attention_backward(
        tok, mem, aux, gains, table, qkv, att1, lse1, x1, qc, kvc, att2, lse2, g2,
        d_mem, d_tok, d_gains, dist, *scratch, weight=weight, need=need, emit=emit, step=step,
    )
    early[...] = jnp.zeros_like(early)
    early[0:2, 0:WIDTH] = d_gains[0:2, :]
    early[2:3, 0:WIDTH] = gain_three[...]
    rel = rel_sums(dist[...], hot_dist[...], mode_rows[...])
    early[:, WIDTH : WIDTH + 128] = rel[0:8]
    early[:, WIDTH + 128 : WIDTH + 256] = rel[8:16]
    if not boxed:
        settle(len(puts))
        return
    kept_tok.start()
    turns = total_steps(links, early, early_room)
    for k, slot in enumerate(slots[21:]):
        run_slot(slot)
        for c in tok_rows.copies[TOK_RATE * k : TOK_RATE * k + TOK_RATE]:
            c.start()
        if k % 4 == 0 and k // 4 < len(turns):
            turns[k // 4]()
    where = me * 2 + g
    sums[...] = block_sums(part_in[...], part_out[...], upright(rows_out[...]), where * 272, where * 112)
    run(total_steps(links, sums, room))
    mem_rows.arrived()
    tok_rows.arrived()
    kept_mem.wait()
    kept_tok.wait()
    work.drain()
    mem_rows.drain()
    tok_rows.drain()


def backward_call(boxed, g_win, g_wout, win, wout, lazy, *more):
    f32, bf16 = jnp.float32, jnp.bfloat16
    vm, dma = pltpu.VMEM, pltpu.SemaphoreType.DMA
    row = sds((SEQ, WIDTH))
    scratch = [vm((8, WIDTH), f32), vm((16, 384), f32)]
    scratch += [
        vm((SEQ, HEAD_COLS), bf16), vm((SEQ, 3 * HEAD_COLS), bf16), vm((2, 128, 384), f32),
        vm((2, HEAD_COLS, WIDTH), bf16), dma((10,)), vm((3, HEAD_COLS, WIDTH), bf16), dma((len(BACK_BLOCKS),)),
        dma((len(lazy),)), dma((4,)),
    ]
    scratch += [vm(v.shape, v.dtype) for v in lazy]
    outs = [sds(g_win.shape), sds(g_wout.shape)]
    if boxed:
        items, both = 4 * len(PIECES), 4 * 384
        outs += [sds((272, WIDTH), f32), sds((112, WIDTH), f32), sds((8, WIDTH), f32), sds((8, WIDTH + 256), f32), row, row]
        specs = (anywhere(),) * 2 + (whole(),) * 4 + (anywhere(),) * 2
        scratch = [vm((SEQ, WIDTH), bf16), vm((SEQ, WIDTH), bf16)] + scratch
        scratch += [
            vm((4, both, WIDTH), bf16), vm((4, 800, WIDTH), bf16), vm((2, both, WIDTH), bf16),
            vm((1, both, WIDTH), bf16), vm((6 * 384, WIDTH), bf16), vm((7, 8, WIDTH), f32), vm((7, 8, WIDTH + 256), f32),
            dma((20,)), dma((7 * items + 16,)), dma((items,)),
            pltpu.SemaphoreType.REGULAR,
        ]
    else:
        outs += [row, row, sds((8, WIDTH + 256), f32)]
        specs = (anywhere(),) * 2 + (whole(),) * 3
    extra = dict(collective_id=2, has_side_effects=True) if boxed else {}
    return pl.pallas_call(
        functools.partial(backward_kernel, boxed),
        out_shape=tuple(outs),
        scratch_shapes=scratch,
        in_specs=[anywhere()] * (4 + len(lazy)) + [whole()] * len(more),
        out_specs=specs,
        input_output_aliases={0: 0, 1: 1},
        compiler_params=pltpu.CompilerParams(vmem_limit_bytes=VMEM_BYTES, **extra),
    )(g_win, g_wout, win, wout, *lazy, *more)


def body(
    tokens, memory, segments, memory_segments, row_source, denoiser_modes, sentinel, cotangent, w_in, w_out,
    norm_gains, rel_bias, rows_in, cols_in, rows_out, cols_out, sq_gains, sq_rel,
):
    n_index = lax.axis_size("dp")
    n_group = lax.axis_size("group")
    my_group = lax.axis_index("group")
    my_place = lax.axis_index(("dp", "group"))
    half_rows = tokens.shape[0]
    rows_dev = cotangent.shape[0]
    assert rows_dev == 1
    boxed = n_index == 16 and n_group == 2
    ids = jnp.stack([jnp.int32(n_group), my_group, my_place])
    buckets = bucket_table(SEQ, BUCKETS)
    hot = (buckets[:256, None] == np.arange(BUCKETS)[None, :]).astype(np.float32)
    lane = np.arange(256)
    dist_f = np.where(lane <= 128, 128 - lane, 384 - lane)
    hot_t = jnp.asarray(np.concatenate([hot[dist_f], hot], axis=0).T)
    w_in_t, rel_t = w_in.T, jnp.swapaxes(rel_bias, 1, 2)
    tok_s, mem_s, aux_s, win_sh, wout_sh, table_f, table_b, keep, mode_rows = prep_call(
        ids, row_source, denoiser_modes, tokens, memory, segments, memory_segments, w_in_t, w_out, rel_t, hot_t, sentinel
    )
    if boxed:
        flat = lambda v: v.reshape(SEQ, v.shape[-1])
        win, wout, tok, mem, aux, *kept = forward_call(
            True, win_sh, wout_sh, flat(tok_s), flat(mem_s), flat(aux_s), norm_gains, table_f
        )
    else:
        win = lax.all_gather(win_sh, ("dp", "group"), axis=0, tiled=True)
        wout = lax.all_gather(wout_sh, ("dp", "group"), axis=0, tiled=True)
        tok, mem, aux = (
            lax.all_to_all(v, "dp", split_axis=0, concat_axis=0, tiled=True).reshape(SEQ, v.shape[-1])
            for v in (tok_s, mem_s, aux_s)
        )
        kept = forward_call(False, tok, mem, aux, win, wout, norm_gains, table_f)
    x2 = kept[8]
    mixed, g2, d_gain_three, g_win, g_wout = ff_call(
        x2, cotangent.reshape(SEQ, WIDTH), keep, norm_gains, win, wout
    )
    hot_dist = np.concatenate([hot, np.repeat(np.eye(BUCKETS, dtype=np.float32)[-1:], 128, axis=0)], axis=0)
    hot_dist = jnp.asarray(np.pad(hot_dist, ((0, 0), (0, 128 - BUCKETS))))
    rows_out_up = rows_out.reshape(1, -1)
    qkv, att1, lse1, x1, qc, kvc, att2, lse2, _ = kept
    lazy = (g2, aux, qc, kvc, att2, lse2, mem, x1, att1, qkv, lse1, tok)
    result = backward_call(
        boxed, g_win, g_wout, win, wout, lazy, norm_gains, table_b, hot_dist, mode_rows, d_gain_three, rows_out_up
    )
    if boxed:
        _, _, part_in_t, part_out, sums, early, back_tok, back_mem = result
        back_tok, back_mem = back_tok.reshape(tok_s.shape), back_mem.reshape(mem_s.shape)
    else:
        g_win, g_wout, d_mem, d_tok, early = result
        back_tok, back_mem = (
            lax.all_to_all(v.reshape(tok_s.shape), "dp", split_axis=0, concat_axis=0, tiled=True)
            for v in (d_tok, d_mem)
        )
        part_in_t, part_out = (
            lax.psum_scatter(v.astype(jnp.float32), ("dp", "group"), scatter_dimension=0, tiled=True)
            for v in (g_win, g_wout)
        )
        sums = block_sums(
            part_in_t, part_out, rows_out.reshape(-1, 1), my_place * part_in_t.shape[0], my_place * part_out.shape[0]
        )
        sums, early = lax.psum((sums, early), ("dp", "group"))
    (
        d_tokens, d_memory, grad_in, grad_out, grad_gains, grad_rel, new_in, new_out, new_gains, new_rel,
        rows_in_new, cols_in_new, rows_out_new, cols_out_new, sq_gains_new, sq_rel_new,
    ) = update_call(
        ids, row_source, part_in_t, part_out, sums, early, back_tok, back_mem, w_in_t, w_out, norm_gains, rel_t,
        rows_in, cols_in.reshape(1, -1), rows_out.reshape(1, -1), cols_out, sq_gains, jnp.swapaxes(sq_rel, 1, 2),
    )
    grad_rel, new_rel, sq_rel_new = (jnp.swapaxes(v, 1, 2) for v in (grad_rel, new_rel, sq_rel_new))
    return (
        mixed[None], d_tokens, d_memory, grad_in.T, grad_out, grad_gains, grad_rel, new_in.T, new_out, new_gains,
        new_rel, rows_in_new, cols_in_new.reshape(-1), rows_out_new.reshape(-1), cols_out_new, sq_gains_new,
        sq_rel_new,
    )


def solution(mesh):
    both = ("dp", "group")
    row_in = P("group", "dp", None)
    seg_in = P("group", "dp")
    return jax.shard_map(
        body,
        mesh=mesh,
        in_specs=(
            row_in, row_in, seg_in, seg_in, P(), P(), P(both, None), P(both, None, None), P(None, both),
            P(both, None), P(), P(), P(), P(both), P(both), P(), P(), P(),
        ),
        out_specs=(
            P(both, None, None), row_in, row_in, P(None, both), P(both, None), P(), P(), P(None, both),
            P(both, None), P(), P(), P(), P(both), P(both), P(), P(), P(),
        ),
        check_vma=False,
    )
```

```python
import functools

import jax
import jax.numpy as jnp
import numpy as np
from jax import lax
from jax.experimental import pallas as pl
from jax.experimental.pallas import tpu as pltpu
from jax.sharding import PartitionSpec as P

HEADS = 12
HSIZE = 64
FF = 2048
BUCKETS = 32
MODES = 3
SEGS = 4
SEQ = 512
WIDTH = 768
EPSILON = 1e-06
MASKED = -1e30
DECAY_RATE = 0.9
STEP_SIZE = 0.01
PLAIN_STEP = 0.15
GELU_SCALE = 0.7978845608028654
PRECISE = lax.Precision.HIGHEST
MESH = pl.DeviceIdType.MESH
VMEM_BYTES = 60 << 20


def bucket_table(length, buckets):
    exact_span = buckets // 2
    distances = np.arange(length)
    safe_spans = np.maximum(distances, 1)
    logged = np.floor(
        np.log(safe_spans / exact_span) / np.log(128.0 / exact_span) * (buckets - exact_span)
    )
    far_bucket = np.minimum(exact_span + logged, buckets - 1)
    return np.where(distances < exact_span, distances, far_bucket).astype(np.int32)


def nt(a, b):
    return lax.dot_general(a, b, (((1,), (1,)), ((), ())), preferred_element_type=jnp.float32)


def nn(a, b):
    return lax.dot_general(a, b, (((1,), (0,)), ((), ())), preferred_element_type=jnp.float32)


def tn(a, b):
    return lax.dot_general(a, b, (((0,), (0,)), ((), ())), preferred_element_type=jnp.float32)


def inv_rms(values):
    return lax.rsqrt(jnp.mean(values * values, axis=-1, keepdims=True) + EPSILON)


def rms_back(values, gain, grad):
    inv = inv_rms(values)
    scaled = grad * gain
    along = jnp.mean(scaled * values, axis=-1, keepdims=True)
    return inv * scaled - values * (inv * inv * inv * along), jnp.sum(
        grad * (values * inv), axis=0, keepdims=True
    )


def lane_of(shape):
    return lax.broadcasted_iota(jnp.int32, shape, 1)


def ext_masks(aux, first):
    lane = lane_of(aux.shape)
    spot = lane & 63
    documents = (spot >= first) & (spot < first + SEGS)
    hot = jnp.where(documents, aux.astype(jnp.float32), 0.0)
    against = jnp.where(documents, (1.0 - aux.astype(jnp.float32)) * MASKED, 0.0)
    return hot, against


def halves(tile, ext, even):
    lane = lane_of(tile.shape)
    return jnp.where((lane < HSIZE) if even else (lane >= HSIZE), tile, ext)


def pick(first, second, lane):
    return jnp.where(lane < HSIZE, first, second)


def tile_cols(p, base=0):
    return pl.ds(pl.multiple_of(p * 128 + base, 128), 128)


def attend_pair(p, q_tile, k_tile, v_tile, k_ext, q_ext, att_ref, lse_ref, bias_of):
    lane = lane_of((SEQ, 128))
    ones = jnp.ones((SEQ, 128), jnp.bfloat16)
    outs, tops = [], []
    for even in (True, False):
        s = nt(halves(q_tile, q_ext, even), halves(k_tile, k_ext, even))
        if bias_of is None:
            top = jnp.max(s, axis=1, keepdims=True)
            e = jnp.exp(s - top).astype(jnp.bfloat16)
        else:
            near, far = bias_of(2 * p + (0 if even else 1))
            tops_of, rows_of_e = [], []
            for i in range(SEQ // 128):
                lo, hi = max(0, i - 2) * 128, (i + 1) * 128
                part = s[i * 128 : (i + 1) * 128, lo:hi]
                bias = [near[:, 128:]] if i == 0 else [near] if i == 1 else [far, near]
                part = part + (bias[0] if len(bias) == 1 else jnp.concatenate(bias, axis=1))
                tops_of.append(jnp.max(part, axis=1, keepdims=True))
                blocks = [jnp.exp(part - tops_of[-1]).astype(jnp.bfloat16)]
                if lo > 0:
                    blocks.insert(0, jnp.zeros((128, lo), jnp.bfloat16))
                if hi < SEQ:
                    blocks.append(jnp.zeros((128, SEQ - hi), jnp.bfloat16))
                rows_of_e.append(blocks[0] if len(blocks) == 1 else jnp.concatenate(blocks, axis=1))
            e = jnp.concatenate(rows_of_e, axis=0)
            top = jnp.concatenate(tops_of, axis=0)
        outs.append(nn(e, halves(v_tile, ones, even)))
        tops.append(top)
    total = pltpu.roll(pick(outs[1], outs[0], lane), HSIZE, 1)
    att_ref[:, tile_cols(p)] = (pick(outs[0], outs[1], lane) / total).astype(jnp.bfloat16)
    lse = pick(tops[0], tops[1], lane) + jnp.log(total)
    lse_ref[...] = jnp.where(
        lane == 2 * p, lse[:, 0:1], jnp.where(lane == 2 * p + 1, lse[:, HSIZE : HSIZE + 1], lse_ref[...])
    )


def forward_bias(table_ref):
    def bias_of(h):
        row = table_ref[pl.ds(h, 1), :]
        near = pltpu.roll(jnp.broadcast_to(row, (128, 256)), 0, 1, stride=1, stride_axis=0)
        lane = lax.broadcasted_iota(jnp.int32, (128, 256), 1)
        sub = lax.broadcasted_iota(jnp.int32, (128, 256), 0)
        near = jnp.where(lane - 128 > sub, MASKED, near)
        far = jnp.broadcast_to(row[:, :1], (128, 128))
        return near, far

    return bias_of


def back_bias(table_ref):
    def bias_of(h):
        row = table_ref[pl.ds(h, 1), :]
        near = pltpu.roll(jnp.broadcast_to(row, (128, 256)), 0, 1, stride=1, stride_axis=0)
        lane = lax.broadcasted_iota(jnp.int32, (128, 256), 1)
        sub = lax.broadcasted_iota(jnp.int32, (128, 256), 0)
        near = jnp.where(lane < sub, MASKED, near)
        far = jnp.broadcast_to(row[:, 128:129], (128, 128))
        return near, far

    return bias_of


def by_distance(near):
    rows = 64
    while rows >= 8:
        near = near[:rows] + pltpu.roll(near[rows:], 256 - rows, 1)
        rows //= 2
    sub = lax.broadcasted_iota(jnp.int32, (8, 256), 0)
    for bit in (4, 2, 1):
        near = jnp.where((sub & bit) != 0, pltpu.roll(near, 256 - bit, 1), near)
    return near


def split_cols(values, base, lane, count):
    rest, out = values, jnp.zeros((values.shape[0], 128), jnp.float32)
    for k in range(count):
        part = rest.astype(jnp.bfloat16).astype(jnp.float32)
        out = jnp.where((lane & 63) == base + k, part, out)
        rest = rest - part
    return out


def back_pair(p, q_tile, k_tile, v_tile, do_tile, att_tile, lse_all, hot, against, bias_of, rel_acc, dist_ref):
    lane = lane_of((SEQ, 128))
    spot = lane & 63
    ones3 = jnp.where((spot >= 8) & (spot < 11), 1.0, 0.0)
    k_ext = (hot + ones3).astype(jnp.bfloat16)
    v_ext = jnp.where((spot >= 0) & (spot < 2), 1.0, 0.0).astype(jnp.bfloat16)
    product = do_tile.astype(jnp.float32) * att_tile.astype(jnp.float32)
    dqs, dks, dvs = [], [], []
    for n, even in enumerate((True, False)):
        h = 2 * p + n
        lse = jnp.sum(jnp.where(lane == h, lse_all, 0.0), axis=1, keepdims=True)
        own = (lane < HSIZE) if even else (lane >= HSIZE)
        delta = jnp.sum(jnp.where(own, product, 0.0), axis=1, keepdims=True)
        q_ext = (against + split_cols(-lse, 8, lane, 3)).astype(jnp.bfloat16)
        d_ext = split_cols(-delta, 0, lane, 2).astype(jnp.bfloat16)
        s = nt(halves(k_tile, k_ext, even), halves(q_tile, q_ext, even))
        dp = nt(halves(v_tile, v_ext, even), halves(do_tile, d_ext, even))
        if bias_of is None:
            w = jnp.exp(s)
            ds = (w * dp).astype(jnp.bfloat16)
            w = w.astype(jnp.bfloat16)
        else:
            near, far = bias_of(h)
            w_rows, ds_rows = [], []
            for j in range(SEQ // 128):
                lo, hi = j * 128, min(SEQ, (j + 3) * 128)
                bias = near[:, :128] if hi - lo == 128 else near
                if hi - lo == 384:
                    bias = jnp.concatenate([near, far], axis=1)
                part = jnp.exp(s[lo : lo + 128, lo:hi] + bias)
                d_part = part * dp[lo : lo + 128, lo:hi]
                if j == 0:
                    rel_acc[n] = d_part
                else:
                    rel_acc[n, :, : hi - lo] += d_part
                for rows, block in ((w_rows, part), (ds_rows, d_part)):
                    blocks = [block.astype(jnp.bfloat16)]
                    if lo > 0:
                        blocks.insert(0, jnp.zeros((128, lo), jnp.bfloat16))
                    if hi < SEQ:
                        blocks.append(jnp.zeros((128, SEQ - hi), jnp.bfloat16))
                    rows.append(blocks[0] if len(blocks) == 1 else jnp.concatenate(blocks, axis=1))
            w, ds = jnp.concatenate(w_rows, axis=0), jnp.concatenate(ds_rows, axis=0)
        dvs.append(nn(w, do_tile))
        dks.append(nn(ds, q_tile))
        dqs.append(tn(k_tile, ds))
    if bias_of is not None:
        for n in range(2):
            near = by_distance(rel_acc[n, :, :256])
            dist_ref[pl.ds(2 * p + n, 1), :] = jnp.concatenate(
                [
                    jnp.sum(near, axis=0, keepdims=True),
                    jnp.sum(rel_acc[n, :, 256:], axis=0, keepdims=True),
                ],
                axis=1,
            )
    sub = lax.broadcasted_iota(jnp.int32, (128, SEQ), 0)
    dq = jnp.where(sub < HSIZE, dqs[0], dqs[1]).T * HSIZE**-0.5
    return dq, pick(dks[0], dks[1], lane), pick(dvs[0], dvs[1], lane)


HEAD_COLS = HEADS * HSIZE


def attention_forward(
    tok, mem, aux, win, wout, gains, table, qkv, att1, lse1, x1, qc, kvc, att2, lse2, x2, step
):
    x0 = tok[...].astype(jnp.float32)
    a1 = (x0 * inv_rms(x0) * gains[0:1, :]).astype(jnp.bfloat16)
    for k in range(3):
        cols = slice(k * HEAD_COLS, (k + 1) * HEAD_COLS)
        got = nt(a1, win[cols, :])
        if k == 0:
            got = got.astype(jnp.bfloat16).astype(jnp.float32) * HSIZE**-0.5
        qkv[:, cols] = got.astype(jnp.bfloat16)
    step("projected", 0)
    lse1[...] = jnp.zeros_like(lse1)
    lse2[...] = jnp.zeros_like(lse2)

    @pl.loop(0, HEADS // 2)
    def _(p):
        hot, against = ext_masks(aux[...], 0)
        attend_pair(
            p, qkv[:, tile_cols(p)], qkv[:, tile_cols(p, HEAD_COLS)], qkv[:, tile_cols(p, 2 * HEAD_COLS)],
            hot.astype(jnp.bfloat16), against.astype(jnp.bfloat16), att1, lse1, forward_bias(table),
        )
        step("self", p)

    x1[...] = tok[...].astype(jnp.float32) + nn(att1[...], wout[0:HEAD_COLS, :])
    step("middle", 0)
    a2 = (x1[...] * inv_rms(x1[...]) * gains[1:2, :]).astype(jnp.bfloat16)
    got = nt(a2, win[3 * HEAD_COLS : 4 * HEAD_COLS, :])
    qc[...] = (got.astype(jnp.bfloat16).astype(jnp.float32) * HSIZE**-0.5).astype(jnp.bfloat16)
    for k in range(2):
        kvc[:, k * HEAD_COLS : (k + 1) * HEAD_COLS] = nt(
            mem[...], win[(4 + k) * HEAD_COLS : (5 + k) * HEAD_COLS, :]
        ).astype(jnp.bfloat16)
    step("crossed", 0)

    @pl.loop(0, HEADS // 2)
    def _(p):
        _, against = ext_masks(aux[...], 0)
        hot = pltpu.roll(ext_masks(aux[...], SEGS)[0], 128 - SEGS, 1)
        attend_pair(
            p, qc[:, tile_cols(p)], kvc[:, tile_cols(p)], kvc[:, tile_cols(p, HEAD_COLS)],
            hot.astype(jnp.bfloat16), against.astype(jnp.bfloat16), att2, lse2, None,
        )
        step("cross", p)

    step("attended", 0)
    x2[...] = x1[...] + nn(att2[...], wout[HEAD_COLS : 2 * HEAD_COLS, :])
    step("end", 0)


def ff_kernel(
    x2, cot, keep, gains, w_gate, w_up, w_down, mixed, g2, d_gain, g_win, g_wout, a3, e3, acc, da3, held, sem
):
    c = pl.program_id(0)
    slot = lax.rem(c, 2)
    rows = w_gate.shape[0]
    first = pl.multiple_of(c * rows, rows)
    puts = [
        pltpu.make_async_copy(held.at[slot, 0], g_win.at[pl.ds(6 * HEAD_COLS + first, rows)], sem.at[slot, 0]),
        pltpu.make_async_copy(held.at[slot, 1], g_win.at[pl.ds(6 * HEAD_COLS + FF + first, rows)], sem.at[slot, 1]),
        pltpu.make_async_copy(held.at[slot, 2], g_wout.at[pl.ds(2 * HEAD_COLS + first, rows)], sem.at[slot, 2]),
    ]

    @pl.when(c >= 2)
    def _():
        for put in puts:
            put.wait()

    @pl.when(c == 0)
    def _():
        a3[...] = (x2[...] * inv_rms(x2[...]) * gains[2:3, :]).astype(jnp.bfloat16)
        e3[...] = (cot[...].astype(jnp.float32) * keep[:, 0:1]).astype(jnp.bfloat16)
        acc[...] = x2[...]
        da3[...] = jnp.zeros_like(da3)

    gate = nt(a3[...], w_gate[...])
    up = nt(a3[...], w_up[...])
    dh = nt(e3[...], w_down[...])
    cube = 0.044715 * gate * gate
    inner = jnp.tanh(GELU_SCALE * gate * (1.0 + cube))
    half = 0.5 * (1.0 + inner)
    gelu = gate * half
    slope = half + 0.5 * gate * (1.0 - inner * inner) * (GELU_SCALE * (1.0 + 3.0 * cube))
    hidden = (gelu * up).astype(jnp.bfloat16)
    d_gate = (dh * up * slope).astype(jnp.bfloat16)
    d_up = (dh * gelu).astype(jnp.bfloat16)
    acc[...] += nn(hidden, w_down[...])
    held[slot, 0] = tn(d_gate, a3[...]).astype(jnp.bfloat16)
    held[slot, 1] = tn(d_up, a3[...]).astype(jnp.bfloat16)
    held[slot, 2] = tn(hidden, e3[...]).astype(jnp.bfloat16)
    for put in puts:
        put.start()
    da3[...] += nn(d_gate, w_gate[...]) + nn(d_up, w_up[...])

    @pl.when(c == pl.num_programs(0) - 1)
    def _():
        mixed[...] = acc[...].astype(jnp.bfloat16)
        part, gain = rms_back(x2[...], gains[2:3, :], da3[...])
        g2[...] = cot[...].astype(jnp.float32) * keep[:, 0:1] + part
        d_gain[...] = gain
        for k in range(3):
            for other in range(2):
                pltpu.make_async_copy(held.at[other, k], g_wout.at[0:rows], sem.at[other, k]).wait()


SELF_LATE = 5
LATE = 4


BACK_BLOCKS = (("o", 1), ("i", 4), ("i", 5), ("i", 3), ("o", 0), ("i", 0), ("i", 1), ("i", 2))


def attention_backward(
    tok, mem, aux, gains, table, qkv, att1, lse1, x1, qc, kvc, att2, lse2, g2,
    d_mem, d_tok, d_gains, dist, do, dqkv, rel_acc, weight, need, emit, step,
):
    need(1)
    e2 = g2[...].astype(jnp.bfloat16)
    do[...] = weight(0, lambda w: nt(e2, w)).astype(jnp.bfloat16)
    need(8)
    emit("o", HEAD_COLS, tn(att2[...], e2))

    def cross_pairs(first, last):
        @pl.loop(first, last)
        def _(p):
            _, against = ext_masks(aux[...], 0)
            hot = pltpu.roll(ext_masks(aux[...], SEGS)[0], 128 - SEGS, 1)
            dq, dk, dv = back_pair(
                p, qc[:, tile_cols(p)], kvc[:, tile_cols(p)], kvc[:, tile_cols(p, HEAD_COLS)], do[:, tile_cols(p)],
                att2[:, tile_cols(p)], lse2[...], hot, against, None, rel_acc, dist,
            )
            dqkv[:, tile_cols(p)] = dq.astype(jnp.bfloat16)
            dqkv[:, tile_cols(p, HEAD_COLS)] = dk.astype(jnp.bfloat16)
            dqkv[:, tile_cols(p, 2 * HEAD_COLS)] = dv.astype(jnp.bfloat16)
            step("cross", p, first, last)

    late = 2 * HEAD_COLS + LATE * 128
    cross_pairs(LATE, HEADS // 2)
    emit("i", 3 * HEAD_COLS + late, tn(dqkv[:, late:], mem[...]))
    step("late", None, 0, 0)
    cross_pairs(0, LATE)
    need(12)
    a2 = (x1[...] * inv_rms(x1[...]) * gains[1:2, :]).astype(jnp.bfloat16)
    emit("i", 3 * HEAD_COLS, tn(dqkv[:, 0:HEAD_COLS], a2))
    emit("i", 4 * HEAD_COLS, tn(dqkv[:, HEAD_COLS : 2 * HEAD_COLS], mem[...]))
    step("mid", 0, 0, 0)
    emit("i", 5 * HEAD_COLS, tn(dqkv[:, 2 * HEAD_COLS : late], mem[...]))
    d_rows = weight(1, lambda w: nn(dqkv[:, HEAD_COLS : 2 * HEAD_COLS], w))
    d_rows += weight(2, lambda w: nn(dqkv[:, 2 * HEAD_COLS : 3 * HEAD_COLS], w))
    d_mem[...] = d_rows.astype(jnp.bfloat16)
    step("mid", 1, 0, 0)
    da2 = weight(3, lambda w: nn(dqkv[:, 0:HEAD_COLS], w))
    part, gain = rms_back(x1[...], gains[1:2, :], da2)
    d_gains[1:2, :] = gain
    g2[...] += part
    step("mid", 2, 0, 0)
    e1 = g2[...].astype(jnp.bfloat16)
    do[...] = weight(4, lambda w: nt(e1, w)).astype(jnp.bfloat16)
    emit("o", 0, tn(att1[...], e1))
    step("middle", None, 0, 0)

    def self_pairs(first, last):
        @pl.loop(first, last)
        def _(p):
            hot, against = ext_masks(aux[...], 0)
            dq, dk, dv = back_pair(
                p, qkv[:, tile_cols(p)], qkv[:, tile_cols(p, HEAD_COLS)], qkv[:, tile_cols(p, 2 * HEAD_COLS)],
                do[:, tile_cols(p)], att1[:, tile_cols(p)], lse1[...], hot, against, back_bias(table), rel_acc, dist,
            )
            dqkv[:, tile_cols(p)] = dq.astype(jnp.bfloat16)
            dqkv[:, tile_cols(p, HEAD_COLS)] = dk.astype(jnp.bfloat16)
            dqkv[:, tile_cols(p, 2 * HEAD_COLS)] = dv.astype(jnp.bfloat16)
            step("self", p, first, last)

    x0 = tok[...].astype(jnp.float32)
    a1 = (x0 * inv_rms(x0) * gains[0:1, :]).astype(jnp.bfloat16)
    late = 2 * HEAD_COLS + SELF_LATE * 128
    self_pairs(SELF_LATE, HEADS // 2)
    emit("i", late, tn(dqkv[:, late:], a1))
    step("self late", None, 0, 0)
    self_pairs(0, SELF_LATE)
    x0 = tok[...].astype(jnp.float32)
    a1 = (x0 * inv_rms(x0) * gains[0:1, :]).astype(jnp.bfloat16)
    for first, last in ((0, HEAD_COLS), (HEAD_COLS, 2 * HEAD_COLS), (2 * HEAD_COLS, late)):
        emit("i", first, tn(dqkv[:, first:last], a1))
    step("last", None, 0, 0)
    da1 = weight(5, lambda w: nn(dqkv[:, 0:HEAD_COLS], w))
    for k in (1, 2):
        step("end", k - 1, 0, 0)
        da1 += weight(5 + k, lambda w: nn(dqkv[:, k * HEAD_COLS : (k + 1) * HEAD_COLS], w))
    part, gain = rms_back(x0, gains[0:1, :], da1)
    d_gains[0:1, :] = gain
    d_tok[...] = (g2[...] + part).astype(jnp.bfloat16)


SHARE = {"i": 272, "o": 112}
PIECES = (
    ("i", 0, 64, 32), ("i", 64, 64, 32), ("i", 128, 64, 32), ("i", 192, 80, 48),
    ("o", 0, 64, 32), ("o", 64, 48, 16),
)


UP_LEAD = (4, 3)
DOWN_LEAD = (12, 9, 6, 3)


SUM_PIECES = (
    ("i", 0, 32, 16), ("i", 32, 32, 16), ("i", 64, 64, 32), ("i", 128, 64, 32), ("i", 192, 80, 48),
    ("o", 0, 64, 32), ("o", 64, 48, 16),
)


def place():
    dp = lax.axis_index("dp")
    return dp // 4, (dp // 2) % 2, dp % 2, lax.axis_index("group")


def dev(z, y, x, g):
    return ((z * 2 + y) * 2 + x, g)


def rows_of(ref, kind, zz, yy, xx, gg, lo, n):
    share = ((zz * 2 + yy) * 2 + xx) * 2 + gg
    return ref.at[pl.ds(pl.multiple_of(share * SHARE[kind] + lo, 16), n)]


class Links:
    def __init__(self, send_sem, recv_sem):
        self.send_sem, self.recv_sem, self.sends, self.recvs = send_sem, recv_sem, 0, 0

    def new_send(self):
        self.sends += 1
        assert self.sends <= self.send_sem.shape[0]
        return self.sends - 1

    def new_recv(self, n=1):
        self.recvs += n
        assert self.recvs <= self.recv_sem.shape[0]
        return self.recvs - n

    def copy(self, src, dst, device, send=None, recv=None):
        send = self.new_send() if send is None else send
        recv = self.new_recv() if recv is None else recv
        return pltpu.make_async_remote_copy(
            src_ref=src, dst_ref=dst, send_sem=self.send_sem.at[send], recv_sem=self.recv_sem.at[recv],
            device_id=device, device_id_type=MESH,
        )

    def sent(self, send, like):
        wait_bytes(self.send_sem.at[send], like)

    def arrived(self, recv, like):
        wait_bytes(self.recv_sem.at[recv], like)


def wait_bytes(sem, like):
    pltpu.make_async_copy(like, like, sem).wait()


def drain_line(links, send, like, rows):
    z = place()[0]
    for k, n in enumerate(rows):
        if n > 0:
            pl.when(z == k)(functools.partial(links.sent, send, like.at[0:n]))


def greet(peers):
    barrier = pltpu.get_barrier_semaphore()
    total = 0
    for device, cond in peers:
        if cond is None:
            pl.semaphore_signal(barrier, inc=1, device_id=device, device_id_type=MESH)
            total = total + 1
        else:

            @pl.when(cond)
            def _(device=device):
                pl.semaphore_signal(barrier, inc=1, device_id=device, device_id_type=MESH)

            total = total + cond.astype(jnp.int32)
    pl.semaphore_wait(barrier, total)


def near_peers():
    z, y, x, g = place()
    return [
        (dev(z, y, 1 - x, g), None), (dev(z, 1 - y, x, g), None), (dev(z, y, x, 1 - g), None),
        (dev(jnp.minimum(z + 1, 3), y, x, g), z < 3), (dev(jnp.maximum(z - 1, 0), y, x, g), z > 0),
    ]


def all_peers():
    z, y, x, g = place()
    me = lax.axis_index("dp")
    return [((lax.rem(me + k, 16), g), None) for k in range(1, 16)] + [(dev(z, y, x, 1 - g), None)]


class Gather:
    def __init__(self, links, arrays):
        z, y, x, g = place()
        self.links, self.items, self.arrays = links, [], arrays
        self.send = {k: links.new_send() for k in ("plane", "core", "up", "down")}
        self.groups, self.cores = ((0, 12), (12, 16), (16, 24)), []
        for first, last in self.groups:
            self.cores += [links.new_recv()] * (last - first)
        for low in (0, 2):
            nearest = jnp.clip(z, 0, 1) if low == 0 else low
            bases = [links.new_recv(2) for _ in PIECES]
            for zz in (nearest, 2 * low + 1 - nearest):
                for (kind, lo, n, half), line in zip(PIECES, bases):

                    def here(yy, xx, first, count, zz=zz, kind=kind):
                        return rows_of(arrays[kind], kind, zz, yy, xx, g, first, count)

                    c = {"go_up": (z >= zz) & (z < 3), "go_down": (z <= zz) & (z > 0), "n": n}
                    c["from_below"], c["from_above"] = z > zz, z < zz
                    c["hops"] = jnp.abs(z - zz)
                    core = self.cores[len(self.items)]

                    def add(name, ref, device, send, recv=None, c=c):
                        c[name] = links.copy(ref, ref, device, self.send[send], recv)

                    own = here(y, x, lo, n)
                    add("up", own, dev(jnp.minimum(z + 1, 3), y, x, g), "up", line + zz - low)
                    add("down", own, dev(jnp.maximum(z - 1, 0), y, x, g), "down", line + zz - low)
                    add("x", own, dev(z, y, 1 - x, g), "plane")
                    add("y", own, dev(z, 1 - y, x, g), "plane")
                    add("a", here(y, 1 - x, lo, half), dev(z, 1 - y, x, g), "plane")
                    add("b", here(1 - y, x, lo + half, n - half), dev(z, y, 1 - x, g), "plane")
                    other = dev(z, y, x, 1 - g)
                    add("p", own, other, "core", core)
                    add("px", here(y, 1 - x, lo, n), other, "core", core)
                    add("py", here(1 - y, x, lo, n), other, "core", core)
                    add("pa", here(1 - y, 1 - x, lo, half), other, "core", core)
                    add("pb", here(1 - y, 1 - x, lo + half, n - half), other, "core", core)
                    self.items.append(c)

    def along(self, c):
        pl.when(c["from_below"])(c["up"].wait_recv)
        pl.when(c["from_above"])(c["down"].wait_recv)
        pl.when(c["go_up"])(c["up"].start)
        pl.when(c["go_down"])(c["down"].start)

    def hop(self, c, h, way, start, arrival):
        @pl.when((c["hops"] == h) & jnp.logical_not(c[arrival]))
        def _():
            if h > 0:
                c[way].wait_recv()
            pl.when(c[start])(c[way].start)

    def near(self, c):
        for k in ("x", "y", "p"):
            c[k].start()

    def second(self, c):
        c["x"].wait_recv()
        c["a"].start()
        c["px"].start()
        c["y"].wait_recv()
        c["b"].start()
        c["py"].start()

    def third(self, c):
        c["a"].wait_recv()
        c["pa"].start()
        c["b"].wait_recv()
        c["pb"].start()

    def arrived(self, group):
        first, last = self.groups[group]
        rows = 4 * sum(c["n"] for c in self.items[first:last])
        self.links.arrived(self.cores[first], self.arrays["i"].at[0:rows])

    def drain(self):
        rows = sum(c["n"] for c in self.items)
        like = self.arrays["i"]
        self.links.sent(self.send["plane"], like.at[0 : 3 * rows])
        self.links.sent(self.send["core"], like.at[0 : 4 * rows])
        plane = rows // 4
        drain_line(self.links, self.send["up"], like, [plane, 2 * plane, 3 * plane, 0])
        drain_line(self.links, self.send["down"], like, [0, 3 * plane, 2 * plane, plane])

    def slots(self):
        n = len(self.items)
        half = n // 2
        out = [[] for _ in range(n + 6)]
        for t, c in enumerate(self.items):
            out[t + 6].append(functools.partial(self.third, c))
        for t, c in enumerate(self.items):
            out[t + 3].append(functools.partial(self.second, c))
        for t, c in enumerate(self.items):
            if t < half:
                out[t].append(functools.partial(self.along, c))
            out[t].append(functools.partial(self.near, c))
        for t, c in enumerate(self.items[half:]):
            for h in range(4):
                if h < 2:
                    up = functools.partial(self.hop, c, h, "up", "go_up", "from_above")
                    out[half + t - UP_LEAD[h]].append(up)
                down = functools.partial(self.hop, c, h, "down", "go_down", "from_below")
                out[half + t - DOWN_LEAD[h]].append(down)
        return out


class Exchange:
    def __init__(self, links, src, dst, rows):
        me, g = lax.axis_index("dp"), lax.axis_index("group")
        self.links, self.send, self.recv = links, links.new_send(), links.new_recv()
        self.like, self.copies = src.at[0 : 15 * rows], []
        for k in range(1, 16):
            to = lax.rem(me + k, 16)
            there = dst.at[pl.ds(pl.multiple_of(me * rows, 16), rows)]
            here = src.at[pl.ds(pl.multiple_of(to * rows, 16), rows)]
            self.copies.append(links.copy(here, there, (to, g), self.send, self.recv))

    def arrived(self):
        self.links.arrived(self.recv, self.like)

    def drain(self):
        self.links.sent(self.send, self.like)


def own_rows(src, dst, rows, sem):
    here = pl.ds(pl.multiple_of(lax.axis_index("dp") * rows, 16), rows)
    return pltpu.make_async_copy(src.at[here], dst.at[here], sem)


class Sums:
    def __init__(self, links, win_g, wout_g, own, got, plane, fin, line, part_in, part_out, load_sem):
        self.links, self.arrays = links, {"i": win_g, "o": wout_g}
        self.own, self.got, self.plane, self.fin, self.line = own, got, plane, fin, line
        self.part_in, self.part_out, self.load_sem = part_in, part_out, load_sem
        self.loads, self.rows, self.line_rows, self.got_rows = 0, 0, 0, 0
        self.send = {k: links.new_send() for k in ("core", "plane", "up", "down")}

    def batch(self, members, got_from=None):
        z, y, x, g = place()
        self.got_rows = self.got_rows if got_from is None else got_from
        links = self.links
        items = []
        for zz, k in members:
            kind, lo, n, half = SUM_PIECES[k]
            base, rest = self.rows, n - half
            at = lambda ref, c, off, m, base=base: ref.at[c, pl.ds(base + off, m)]
            it = {"zz": zz, "z": z, "n": n, "half": half, "base": base, "kind": kind, "lo": lo}
            it["load"], it["core"], it["pair"] = [], links.new_recv(), []
            it["got"] = self.got_rows
            self.got_rows += n
            it["load_sem"] = self.load_sem.at[self.loads]
            self.loads += 1
            for c, (yy, xx) in enumerate(((y, x), (y, 1 - x), (1 - y, x), (1 - y, 1 - x))):
                ref = self.arrays[kind]
                mine = rows_of(ref, kind, zz, yy, xx, g, lo, n)
                it["load"].append(pltpu.make_async_copy(mine, at(self.own, c, 0, n), it["load_sem"]))
                theirs = rows_of(ref, kind, zz, yy, xx, 1 - g, lo, n)
                it["pair"].append(
                    links.copy(theirs, self.got.at[c, pl.ds(it["got"], n)], dev(z, y, x, 1 - g), self.send["core"], it["core"])
                )
            nx, ny = dev(z, y, 1 - x, g), dev(z, 1 - y, x, g)
            own, plane, fin, send = self.own, self.plane, self.fin, self.send["plane"]
            it["x_recv"], it["y_recv"] = links.new_recv(), links.new_recv()
            it["x1"] = [
                links.copy(at(own, c, 0, half), at(plane, s, 0, half), nx, send, it["x_recv"]) for s, c in ((0, 1), (1, 3))
            ]
            it["y1"] = [
                links.copy(at(own, c, half, rest), at(plane, s, half, rest), ny, send, it["y_recv"])
                for s, c in ((0, 2), (1, 3))
            ]
            it["y2"] = links.copy(at(own, 2, 0, half), at(fin, 0, 0, half), ny, send)
            it["x2"] = links.copy(at(own, 1, half, rest), at(fin, 0, half, rest), nx, send)
            for way, needed in (("from_below", zz > 0), ("from_above", zz < 3)):
                if needed:
                    it[way] = pl.ds(self.line_rows, n)
                    self.line_rows += n
            if zz > 0:
                up = dev(jnp.minimum(z + 1, 3), y, x, g)
                it["up"] = links.copy(at(own, 0, 0, n), self.line.at[it["from_below"]], up, self.send["up"])
            if zz < 3:
                down = dev(jnp.maximum(z - 1, 0), y, x, g)
                it["down"] = links.copy(at(own, 0, 0, n), self.line.at[it["from_above"]], down, self.send["down"])
            items.append(it)
            self.rows += n
        return items

    def begin(self, items):
        for it in items:
            for c in it["load"]:
                c.start()
            for c in it["pair"]:
                c.start()

    def drain(self):
        rows, plane = self.rows, self.rows // 4
        like = self.arrays["i"]
        self.links.sent(self.send["core"], like.at[0 : 4 * rows])
        self.links.sent(self.send["plane"], like.at[0 : 3 * rows])
        drain_line(self.links, self.send["up"], like, [3 * plane, 2 * plane, plane, 0])
        drain_line(self.links, self.send["down"], like, [0, plane, 2 * plane, 3 * plane])

    def place_in(self, slots, first, items):
        for k, it in enumerate(items):
            t = first + k
            slots[t].append((2, self.to_core, it))
            slots[t + 3].append((1, self.to_plane, it))
            slots[t + 6].append((0, self.to_line, it))
            for h in range(1, max(it["zz"], 3 - it["zz"]) + 1):
                slots[t + 6 + 2 * h].append((-h, functools.partial(self.hop, h), it))

    @staticmethod
    def add(dst, c, first, src, s, start, m):
        rows = pl.ds(first, m)
        more = src[s, pl.ds(start, m), :].astype(jnp.float32)
        dst[c, rows, :] = (dst[c, rows, :].astype(jnp.float32) + more).astype(jnp.bfloat16)

    def add_line(self, it, way):
        rows = pl.ds(it["base"], it["n"])
        more = self.line[it[way], :].astype(jnp.float32)
        self.own[0, rows, :] = (self.own[0, rows, :].astype(jnp.float32) + more).astype(jnp.bfloat16)

    def to_core(self, it):
        rows = pl.ds(it["base"], it["n"])
        wait_bytes(it["load_sem"], self.own.at[:, rows])
        self.links.arrived(it["core"], self.got.at[:, pl.ds(it["got"], it["n"])])
        for c in (3, 1, 2, 0):
            self.add(self.own, c, it["base"], self.got, c, it["got"], it["n"])
            if c == 3:
                it["x1"][1].start()
                it["y1"][1].start()
            if c == 1:
                it["x1"][0].start()
            if c == 2:
                it["y1"][0].start()

    def to_plane(self, it):
        half, rest, base = it["half"], it["n"] - it["half"], it["base"]
        low = base + half
        self.links.arrived(it["x_recv"], self.plane.at[:, pl.ds(base, half)])
        self.add(self.own, 2, base, self.plane, 1, base, half)
        it["y2"].start()
        self.links.arrived(it["y_recv"], self.plane.at[:, pl.ds(low, rest)])
        self.add(self.own, 1, low, self.plane, 1, low, rest)
        it["x2"].start()
        self.add(self.own, 0, base, self.plane, 0, base, half)
        self.add(self.own, 0, low, self.plane, 0, low, rest)

    def to_line(self, it):
        it["y2"].wait_recv()
        it["x2"].wait_recv()
        self.add(self.own, 0, it["base"], self.fin, 0, it["base"], it["n"])
        z, zz = it["z"], it["zz"]
        if zz > 0:
            pl.when(z == 0)(it["up"].start)
        if zz < 3:
            pl.when(z == 3)(it["down"].start)

    def hop(self, h, it):
        z, zz, n, base = it["z"], it["zz"], it["n"], it["base"]
        if h < zz:

            @pl.when(z == h)
            def _():
                it["up"].wait_recv()
                self.add_line(it, "from_below")
                it["up"].start()

        if h < 3 - zz:

            @pl.when(z == 3 - h)
            def _():
                it["down"].wait_recv()
                self.add_line(it, "from_above")
                it["down"].start()

        if h == max(zz, 3 - zz):

            @pl.when(z == zz)
            def _():
                total = self.own[0, pl.ds(base, n), :].astype(jnp.float32)
                if zz > 0:
                    it["up"].wait_recv()
                    total += self.line[it["from_below"], :].astype(jnp.float32)
                if zz < 3:
                    it["down"].wait_recv()
                    total += self.line[it["from_above"], :].astype(jnp.float32)
                into = self.part_in if it["kind"] == "i" else self.part_out
                into[it["lo"] : it["lo"] + n, :] = total


def run_slot(slot):
    for _, step, it in sorted(slot, key=lambda entry: entry[0]):
        step(it)


def total_steps(links, ref, room):
    z, y, x, g = place()
    here = y * 2 + x
    core = links.copy(ref, room.at[0], dev(z, y, x, 1 - g))
    plane = [
        links.copy(ref, room.at[1], dev(z, y, 1 - x, g)),
        links.copy(ref, room.at[2], dev(z, 1 - y, x, g)),
        links.copy(ref, room.at[3], dev(z, 1 - y, 1 - x, g)),
    ]
    line = [links.copy(ref, room.at[3 + k], dev(lax.rem(z + k, 4), y, x, g)) for k in (1, 2, 3)]

    def in_order(first, came_from):
        mine = ref[...]
        total = jnp.zeros_like(mine)
        for n in range(4):
            came = came_from(n)
            term = jnp.where(came == 0, mine, jnp.zeros_like(mine))
            for k in (1, 2, 3):
                term = jnp.where(came == k, room[first + k], term)
            total = total + term
        return total

    def to_plane():
        core.wait()
        ref[...] = ref[...] + room[0]
        for c in plane:
            c.start()

    def to_line():
        for c in plane:
            c.wait()
        ref[...] = in_order(0, lambda n: jnp.bitwise_xor(here, n))
        for c in line:
            c.start()

    def finish():
        for c in line:
            c.wait()
        ref[...] = in_order(3, lambda n: lax.rem(z - n + 4, 4))

    return [core.start, to_plane, to_line, finish]


def vmem_call(kernel, out_shape, scratch, **kw):
    return pl.pallas_call(
        kernel,
        out_shape=out_shape,
        scratch_shapes=scratch,
        compiler_params=pltpu.CompilerParams(vmem_limit_bytes=VMEM_BYTES),
        **kw,
    )


def sds(shape, dtype=jnp.bfloat16):
    return jax.ShapeDtypeStruct(shape, dtype)


WEIGHTS = [pltpu.VMEM((6 * HEAD_COLS, WIDTH), jnp.bfloat16), pltpu.VMEM((2 * HEAD_COLS, WIDTH), jnp.bfloat16)]


def load_rows(src, dst, first, last, sem):
    copy = pltpu.make_async_copy(src.at[first:last], dst.at[first:last], sem)
    copy.start()
    return copy


def anywhere():
    return pl.BlockSpec(memory_space=pl.ANY)


def whole():
    return pl.BlockSpec(memory_space=pltpu.VMEM)


def run(steps):
    for s in steps:
        s()


def block_of(ids, edges):
    return (ids >= edges[0]).astype(jnp.int32) + (ids >= edges[1]).astype(jnp.int32)


IN_EDGES = (3 * HEAD_COLS, 6 * HEAD_COLS)
OUT_EDGES = (HEAD_COLS, 2 * HEAD_COLS)


def block_sums(part_in_t, part_out, rows_out, first_in, first_out):
    sq_in, sq_out = part_in_t * part_in_t, part_out * part_out
    block_in = block_of(first_in + lax.broadcasted_iota(jnp.int32, (sq_in.shape[0], 1), 0), IN_EDGES)
    block_out = block_of(first_out + lax.broadcasted_iota(jnp.int32, (sq_out.shape[0], 1), 0), OUT_EDGES)
    rows_new = DECAY_RATE * rows_out + (1 - DECAY_RATE) * jnp.mean(sq_out, axis=1, keepdims=True)
    lane = lax.broadcasted_iota(jnp.int32, (1, WIDTH), 1)
    lines = [jnp.sum(jnp.where(block_in == k, sq_in, 0.0), axis=0, keepdims=True) for k in range(3)]
    lines += [jnp.sum(jnp.where(block_out == k, sq_out, 0.0), axis=0, keepdims=True) for k in range(3)]
    totals = jnp.zeros((1, WIDTH), jnp.float32)
    for k in range(3):
        total = jnp.sum(jnp.where(block_out == k, rows_new, 0.0), axis=0, keepdims=True)
        totals = jnp.where(lane == k, total, totals)
    return jnp.concatenate(lines + [totals, jnp.zeros((1, WIDTH), jnp.float32)], axis=0)


def prep_rows(group, groups, row_source, tokens, memory, segments, msegments, seg_t, mseg_t, store):
    half_rows, length = tokens.shape[0], tokens.shape[1]
    for source, out in ((segments, seg_t), (msegments, mseg_t)):
        out[...] = jnp.zeros_like(out)
        out[0:half_rows, 0:length] = source[...].astype(jnp.float32)
        out[...] = out[...].T
    lane = lax.broadcasted_iota(jnp.int32, (length, 128), 1)
    spot = (lane & (HSIZE - 1)).astype(jnp.float32)

    @pl.loop(0, half_rows)
    def _(i):
        source = lax.rem(row_source[i * groups + group], half_rows)
        col = jnp.sum(jnp.where(lane == source, seg_t[0:length, :], 0.0), axis=1, keepdims=True)
        mcol = jnp.sum(jnp.where(lane == source, mseg_t[0:length, :], 0.0), axis=1, keepdims=True)
        same = ((spot < SEGS) & (spot == col)) | ((spot >= SEGS) & (spot < 2 * SEGS) & (spot - SEGS == mcol))
        store(i, tokens[source], memory[source], jnp.where(same, 1.0, 0.0).astype(jnp.bfloat16))


def prep_tables(mode, rel_bias, hot, sentinel, table_f, table_b, keep, mode_rows):
    tables = jnp.dot(rel_bias[mode], hot[...], precision=PRECISE, preferred_element_type=jnp.float32)
    for k, table in enumerate((table_f, table_b)):
        table[...] = jnp.zeros_like(table)
        table[0:HEADS, :] = tables[:, k * 256 : (k + 1) * 256]
    mode_rows[...] = jnp.where(lax.broadcasted_iota(jnp.int32, (8, 128), 0) == mode, 1.0, 0.0)
    kept = (1 - sentinel[...]).astype(jnp.float32)
    keep[...] = jnp.broadcast_to(kept, (128, SEQ)).T


def prep_kernel(
    ids, row_source, modes, tokens, memory, segments, msegments, w_in, w_out, rel_bias, hot, sentinel,
    tok_s, mem_s, aux_s, win_sh, wout_sh, table_f, table_b, keep, mode_rows, seg_t, mseg_t,
):
    win_sh[...] = w_in[...].astype(jnp.bfloat16)
    wout_sh[...] = w_out[...].astype(jnp.bfloat16)

    def store(i, tok, mem, aux):
        tok_s[i], mem_s[i], aux_s[i] = tok, mem, aux

    prep_rows(ids[1], ids[0], row_source, tokens, memory, segments, msegments, seg_t, mseg_t, store)
    prep_tables(modes[row_source[ids[2]]], rel_bias, hot, sentinel, table_f, table_b, keep, mode_rows)


def prep_call(ids, row_source, modes, tokens, memory, segments, msegments, w_in, w_out, rel_bias, hot, sentinel):
    f32 = jnp.float32
    scalars = pl.BlockSpec(memory_space=pltpu.SMEM)
    half_rows, length = tokens.shape[0], tokens.shape[1]
    return vmem_call(
        prep_kernel,
        (
            sds(tokens.shape), sds(memory.shape), sds((half_rows, length, 128)), sds(w_in.shape),
            sds(w_out.shape), sds((16, 256), f32), sds((16, 256), f32), sds((SEQ, 128), f32), sds((8, 128), f32),
        ),
        [pltpu.VMEM((128, 128), f32), pltpu.VMEM((128, 128), f32)],
        in_specs=[scalars] * 3 + [whole()] * 9,
    )(ids, row_source, modes, tokens, memory, segments, msegments, w_in, w_out, rel_bias, hot, sentinel)


def upright(row):
    return jnp.broadcast_to(row, (128, row.shape[1])).T[:, 0:1]


def level(col):
    return jnp.broadcast_to(col, (col.shape[0], 128)).T[0:1, :]


def update_kernel(
    ids, row_source, part_in_t, part_out, sums, early, back_tok, back_mem, w_in, w_out, gains, rel_bias, rows_in,
    cols_in, rows_out, cols_out, sq_gains, sq_rel,
    d_tokens, d_memory, grad_in, grad_out, grad_gains, grad_rel, new_in, new_out, new_gains, new_rel, rows_in_new,
    cols_in_new, rows_out_new, cols_out_new, sq_gains_new, sq_rel_new,
):
    half_rows = back_tok.shape[0]
    groups, group, where = ids[0], ids[1], ids[2]

    @pl.loop(0, half_rows)
    def _(i):
        source = row_source[i * groups + group] - group * half_rows
        d_tokens[source] = back_tok[i]
        d_memory[source] = back_mem[i]

    n_in, n_out = w_in.shape[0], w_out.shape[0]
    p_in = part_in_t[...]
    grad_in[...] = p_in
    in_cols = DECAY_RATE * upright(cols_in[...].reshape(1, -1)) + (1 - DECAY_RATE) * jnp.mean(p_in * p_in, axis=1, keepdims=True)
    cols_in_new[...] = level(in_cols).reshape(-1)
    block_in = block_of(where * n_in + lax.broadcasted_iota(jnp.int32, (n_in, 1), 0), IN_EDGES)
    scale = jnp.zeros((n_in, WIDTH), jnp.float32)
    for k, count in enumerate((3 * HEAD_COLS, 3 * HEAD_COLS, 2 * FF)):
        row = DECAY_RATE * rows_in[k : k + 1, :] + (1 - DECAY_RATE) * (sums[k : k + 1, :] / count)
        rows_in_new[k : k + 1, :] = row
        scale = jnp.where(block_in == k, in_cols * (row / jnp.mean(row, axis=1, keepdims=True)), scale)
    new_in[...] = w_in[...] - STEP_SIZE * p_in * lax.rsqrt(scale)

    p_out = part_out[...]
    grad_out[...] = p_out
    out_rows = DECAY_RATE * upright(rows_out[...].reshape(1, -1)) + (1 - DECAY_RATE) * jnp.mean(p_out * p_out, axis=1, keepdims=True)
    rows_out_new[...] = level(out_rows).reshape(-1)
    block_out = block_of(where * n_out + lax.broadcasted_iota(jnp.int32, (n_out, 1), 0), OUT_EDGES)
    scale = jnp.zeros((n_out, WIDTH), jnp.float32)
    for k, count in enumerate((HEAD_COLS, HEAD_COLS, FF)):
        col = DECAY_RATE * cols_out[k : k + 1, :] + (1 - DECAY_RATE) * (sums[3 + k : 4 + k, :] / count)
        cols_out_new[k : k + 1, :] = col
        mean = sums[6:7, k : k + 1] / count
        scale = jnp.where(block_out == k, (out_rows / mean) * col, scale)
    new_out[...] = w_out[...] - STEP_SIZE * p_out * lax.rsqrt(scale)

    g = early[0:3, 0:WIDTH]
    rel = jnp.concatenate([early[:, WIDTH : WIDTH + 128], early[:, WIDTH + 128 : WIDTH + 256]], axis=0)
    grad_gains[...] = g
    sq = DECAY_RATE * sq_gains[...] + (1 - DECAY_RATE) * g * g
    sq_gains_new[...] = sq
    new_gains[...] = gains[...] - PLAIN_STEP * g * lax.rsqrt(sq)
    for k in range(MODES):
        g = rel[0:HEADS, k * BUCKETS : (k + 1) * BUCKETS]
        grad_rel[k] = g
        sq = DECAY_RATE * sq_rel[k] + (1 - DECAY_RATE) * g * g
        sq_rel_new[k] = sq
        new_rel[k] = rel_bias[k] - PLAIN_STEP * g * lax.rsqrt(sq)


def update_call(ids, row_source, *arrays):
    f32 = jnp.float32
    scalars = pl.BlockSpec(memory_space=pltpu.SMEM)
    (part_in_t, part_out, sums, early, back_tok, back_mem, w_in, w_out, gains, rel_bias) = arrays[:10]
    n_in, n_out = w_in.shape[0], w_out.shape[0]
    three = sds((3, WIDTH), f32)
    rel = sds(rel_bias.shape, f32)
    return vmem_call(
        update_kernel,
        (
            sds(back_tok.shape), sds(back_mem.shape), sds(w_in.shape, f32), sds(w_out.shape, f32), three, rel,
            sds(w_in.shape, f32), sds(w_out.shape, f32), three, rel, three, sds((n_in,), f32), sds((n_out,), f32),
            three, three, rel,
        ),
        [],
        in_specs=[scalars] * 2 + [whole()] * len(arrays),
    )(ids, row_source, *arrays)


ROWS_FROM = 10
TOK_RATE = 3


def forward_kernel(boxed, *refs):
    if boxed:
        (row_source, modes, tokens, memory, segments, msegments, w_in, w_out, rel_bias, hot, sentinel), refs = refs[:11], refs[11:]
        gains, (win, wout), rows_out, refs = refs[0], refs[1:3], refs[3:6], refs[6:]
        (table_b, keep_col, mode_rows), refs = refs[:3], refs[3:]
    else:
        (tok_s, mem_s, aux_s, win, wout, gains, table), refs = refs[:7], refs[7:]
        rows_out = None
    kept_out, kept, (tok, mem, aux), refs = refs[:9], refs[9:18], refs[18:21], refs[21:]
    (win_v, wout_v, sem, put_sem, ls), refs = refs[:5], refs[5:]
    puts = []

    def keep(src, dst):
        puts.append(pltpu.make_async_copy(src, dst, put_sem.at[len(puts)]))
        puts[-1].start()

    def hand_on(name):
        names = {"projected": (0,), "middle": (1, 2, 3), "crossed": (4, 5), "attended": (6, 7), "end": (8,)}
        for k in names.get(name, ()):
            keep(kept[k], kept_out[k])
        if boxed and name == "projected":
            keep(tok, rows_out[0])
            keep(aux, rows_out[2])
        if boxed and name == "crossed":
            keep(mem, rows_out[1])

    if not boxed:
        loads = [load_rows(win, win_v, 0, 6 * HEAD_COLS, sem.at[0]), load_rows(wout, wout_v, 0, 2 * HEAD_COLS, sem.at[1])]
        for k, (s, t) in enumerate(((tok_s, tok), (mem_s, mem), (aux_s, aux))):
            loads.append(pltpu.make_async_copy(s, t, ls.at[k]))
            loads[-1].start()
        for c in loads:
            c.wait()
        attention_forward(
            tok, mem, aux, win_v, wout_v, gains, table, *kept, step=lambda name, p: hand_on(name)
        )
        for c in puts:
            c.wait()
        return
    ss, rs, win_sh, wout_sh, tokens_v, memory_v, tok_s, mem_s, aux_s, seg_t, mseg_t, table = refs
    z, y, x, g = place()
    me = lax.axis_index("dp")
    pos = SEQ // 16
    links = Links(ss, rs)
    row_loads = [
        pltpu.make_async_copy(tokens, tokens_v, ls.at[2]), pltpu.make_async_copy(memory, memory_v, ls.at[3]),
    ]
    for c in row_loads:
        c.start()
    win_sh[...] = w_in[...].astype(jnp.bfloat16)
    wout_sh[...] = w_out[...].astype(jnp.bfloat16)
    near = [
        pltpu.make_async_copy(win_sh, rows_of(win, "i", z, y, x, g, 0, 272), ls.at[0]),
        pltpu.make_async_copy(wout_sh, rows_of(wout, "o", z, y, x, g, 0, 112), ls.at[1]),
    ]
    for c in near:
        c.start()
    greet(all_peers())
    for c in near:
        c.wait()
    gather = Gather(links, {"i": win, "o": wout})
    slots = gather.slots()
    tok_rows, aux_rows, mem_rows = (
        Exchange(links, s, t, pos) for s, t in ((tok_s, tok), (aux_s, aux), (mem_s, mem))
    )
    half = len(gather.items) // 2
    now = half + 6
    queue = [[] for _ in range(len(slots))]
    for k in range(15):
        queue[ROWS_FROM + k // 3] += [tok_rows.copies[k], aux_rows.copies[k]]
        queue[ROWS_FROM + 5 + k // 2].append(mem_rows.copies[k])

    def run_gather(t):
        run(slots[t])
        for c in queue[t]:
            c.start()

    def store(i, *values):
        here = pl.ds(pl.multiple_of(i * pos, pos), pos)
        for ref, value in zip((tok_s, mem_s, aux_s), values):
            ref[here, :] = value

    for t in range(now):
        run_gather(t)
        if t == 2:
            for c in row_loads:
                c.wait()
            prep_rows(g, 2, row_source, tokens_v, memory_v, segments, msegments, seg_t, mseg_t, store)
        if t == 4:
            prep_tables(modes[row_source[me * 2 + g]], rel_bias, hot, sentinel, table, table_b, keep_col, mode_rows)
            here = pl.ds(pl.multiple_of(me * pos, pos), pos)
            for src, dst in ((tok_s, tok), (mem_s, mem), (aux_s, aux)):
                dst[here, :] = src[here, :]
    gather.arrived(0)
    loads = [
        load_rows(win, win_v, 0, 3 * HEAD_COLS, sem.at[0]), load_rows(wout, wout_v, 0, 2 * HEAD_COLS, sem.at[1]),
        load_rows(win, win_v, 3 * HEAD_COLS, 16 * 272, sem.at[2]),
    ]
    tok_rows.arrived()
    aux_rows.arrived()
    loads[0].wait()
    calls = HEADS // 2
    shares = [range(now + k, now + k + 1) for k in range(calls)]
    shares += [range(now + calls + k, now + calls + k + 1) for k in range(calls)]

    def step(name, p):
        hand_on(name)
        if name == "middle":
            gather.arrived(1)
            more = load_rows(win, win_v, 16 * 272, 6 * HEAD_COLS, sem.at[3])
            mem_rows.arrived()
            loads[2].wait()
            more.wait()
        if name not in ("self", "cross"):
            return
        for k in range(calls):

            @pl.when(p == k)
            def _(k=k):
                for t in shares[k + (0 if name == "self" else calls)]:
                    run_gather(t)
                if name == "self" and k == calls - 1:
                    loads[1].wait()

    attention_forward(tok, mem, aux, win_v, wout_v, gains, table, *kept, step=step)
    for t in range(now + 2 * calls, len(slots)):
        run_gather(t)
    gather.arrived(2)
    for c in puts:
        c.wait()
    gather.drain()
    for rows in (tok_rows, aux_rows, mem_rows):
        rows.drain()


def forward_call(boxed, *arrays):
    f32 = jnp.float32
    dma = pltpu.SemaphoreType.DMA
    outs = (
        sds((SEQ, 3 * HEAD_COLS)), sds((SEQ, HEAD_COLS)), sds((SEQ, 128), f32), sds((SEQ, WIDTH), f32),
        sds((SEQ, HEAD_COLS)), sds((SEQ, 2 * HEAD_COLS)), sds((SEQ, HEAD_COLS)), sds((SEQ, 128), f32),
        sds((SEQ, WIDTH), f32),
    )
    rows = (sds((SEQ, WIDTH)), sds((SEQ, WIDTH)), sds((SEQ, 128)))
    scratch = [pltpu.VMEM(v.shape, v.dtype) for v in outs + rows] + WEIGHTS + [dma((4,)), dma((12,)), dma((5,))]
    specs = [anywhere()] * 5 + [whole()] * 2
    out_specs = [anywhere()] * len(outs)
    extra = {}
    if boxed:
        vm, bf16 = pltpu.VMEM, jnp.bfloat16
        scratch = scratch + [dma((7,)), dma((20 * len(PIECES) + 6,)), vm((272, WIDTH), bf16), vm((112, WIDTH), bf16)]
        scratch += [vm((16, SEQ // 16, WIDTH), bf16)] * 2 + [vm((SEQ, WIDTH), bf16)] * 2 + [vm((SEQ, 128), bf16)]
        scratch += [vm((128, 128), f32)] * 2 + [vm((16, 256), f32)]
        small = (sds((16, 256), f32), sds((SEQ, 128), f32), sds((8, 128), f32))
        outs = (sds((6 * HEAD_COLS + 2 * FF, WIDTH)), sds((2 * HEAD_COLS + FF, WIDTH))) + rows + small + outs
        scalars = pl.BlockSpec(memory_space=pltpu.SMEM)
        specs = [scalars] * 2 + [anywhere()] * 2 + [whole()] * 8
        out_specs = [anywhere()] * 5 + [whole()] * 3 + out_specs
        extra = dict(collective_id=1, has_side_effects=True)
    return pl.pallas_call(
        functools.partial(forward_kernel, boxed),
        out_shape=outs,
        scratch_shapes=scratch,
        in_specs=specs,
        out_specs=tuple(out_specs),
        compiler_params=pltpu.CompilerParams(vmem_limit_bytes=VMEM_BYTES, **extra),
    )(*arrays)


def ff_call(x2, cot, keep, gains, win, wout):
    f32 = jnp.float32
    step = 512
    n = FF // step
    at = lambda block, first: pl.BlockSpec((step, WIDTH), lambda c: (first + c, 0))
    full = lambda rows, cols: pl.BlockSpec((rows, cols), lambda c: (0, 0))
    gate0, down0 = 6 * HEAD_COLS // step, 2 * HEAD_COLS // step
    return vmem_call(
        ff_kernel,
        (
            sds((SEQ, WIDTH)), sds((SEQ, WIDTH), f32), sds((1, WIDTH), f32), sds(win.shape), sds(wout.shape),
        ),
        [
            pltpu.VMEM((SEQ, WIDTH), jnp.bfloat16), pltpu.VMEM((SEQ, WIDTH), jnp.bfloat16),
            pltpu.VMEM((SEQ, WIDTH), f32), pltpu.VMEM((SEQ, WIDTH), f32),
            pltpu.VMEM((2, 3, step, WIDTH), jnp.bfloat16), pltpu.SemaphoreType.DMA((2, 3)),
        ],
        grid=(n,),
        in_specs=[
            full(SEQ, WIDTH), full(SEQ, WIDTH), full(SEQ, 128), full(3, WIDTH),
            at(step, gate0), at(step, gate0 + n), at(step, down0),
        ],
        out_specs=(full(SEQ, WIDTH), full(SEQ, WIDTH), full(1, WIDTH), anywhere(), anywhere()),
    )(x2, cot, keep, gains, win, win, wout)


def rel_sums(dist, hot_dist, mode_rows):
    by_bucket = jnp.dot(dist, hot_dist, precision=PRECISE, preferred_element_type=jnp.float32)
    lane = lane_of(by_bucket.shape)
    total = jnp.zeros_like(by_bucket)
    for k in range(MODES):
        moved = pltpu.roll(by_bucket * mode_rows[k : k + 1, :], k * BUCKETS, 1)
        total = jnp.where(lane // BUCKETS == k, moved, total)
    return total


def backward_kernel(boxed, _, __, win, wout, *refs):
    lazy, refs = refs[:12], refs[12:]
    (gains, table, hot_dist, mode_rows, gain_three, rows_out), refs = refs[:6], refs[6:]
    if boxed:
        (g_win, g_wout, part_in, part_out, sums, early, btok, bmem), refs = refs[:8], refs[8:]
        (d_mem, d_tok), refs = refs[:2], refs[2:]
    else:
        (g_win, g_wout, d_mem, d_tok, early), refs = refs[:5], refs[5:]
    (d_gains, dist), refs = refs[:2], refs[2:]
    scratch, (held, put_sem, blocks, block_sem, lazy_sem, sem), refs = refs[:3], refs[3:9], refs[9:]
    lazy_v, refs = refs[:12], refs[12:]
    fetched = []

    def fetch(k):
        array, block = BACK_BLOCKS[k]
        src = (win if array == "i" else wout).at[block * HEAD_COLS : (block + 1) * HEAD_COLS]
        fetched.append(pltpu.make_async_copy(src, blocks.at[k % 3], block_sem.at[k]))
        fetched[k].start()

    def weight(k, fn):
        fetched[k].wait()
        value = fn(blocks[k % 3])
        if k + 3 < len(BACK_BLOCKS):
            fetch(k + 3)
        return value

    loads = [pltpu.make_async_copy(s, t, lazy_sem.at[k]) for k, (s, t) in enumerate(zip(lazy, lazy_v))]
    loads[0].start()
    fetch(0)
    for c in loads[1:]:
        c.start()
    fetch(1)
    fetch(2)
    loaded = []

    def need(n):
        while len(loaded) < n:
            loads[len(loaded)].wait()
            loaded.append(True)

    puts, settled = [], []

    def settle(upto):
        while len(settled) < upto:
            puts[len(settled)].wait()
            settled.append(True)

    def emit(array, first, value):
        k = len(puts)
        settle(k - 1)
        rows = value.shape[0]
        held[k % 2, 0:rows] = value.astype(jnp.bfloat16)
        into = g_win if array == "i" else g_wout
        puts.append(pltpu.make_async_copy(held.at[k % 2, 0:rows], into.at[first : first + rows], put_sem.at[k]))
        puts[k].start()

    dist[...] = jnp.zeros_like(dist)
    step = lambda *a: None
    if boxed:
        own, got, plane, fin, line, room, early_room, ss, rs, load_sem, freed = refs
        z, y, x, g = place()
        me = lax.axis_index("dp")
        pos = SEQ // 16
        greet(all_peers())
        links = Links(ss, rs)
        work = Sums(links, g_win, g_wout, own, got, plane, fin, line, part_in, part_out, load_sem)
        n = len(SUM_PIECES)
        groups = (
            (0, 0, [(3, k) for k in range(n)]),
            (7, 400, [(2, k) for k in range(n)]),
            (14, 0, [(1, k) for k in range(3, n)] + [(0, k) for k in range(5, n)]),
            (20, 400, [(1, k) for k in (2, 1, 0)]),
            (23, 528, [(0, k) for k in (4, 3, 2, 1, 0)]),
        )
        slots = [[] for _ in range(42)]
        batches = []
        for first, got_from, members in groups:
            batches.append(work.batch(members, got_from))
            work.place_in(slots, first, batches[-1])
        mem_rows, tok_rows = Exchange(links, d_mem, bmem, pos), Exchange(links, d_tok, btok, pos)
        kept_mem, kept_tok = own_rows(d_mem, bmem, pos, sem.at[2]), own_rows(d_tok, btok, pos, sem.at[3])
        work.begin(batches[0])
        shares = {("cross", LATE): ((0,), (1,)), ("cross", 0): ((2,), (3,), (4,), (5, 6))}
        shares["mid"] = ((7,), (8, 9), (10,))
        shares["self", SELF_LATE] = ((11, 12, 13),)
        shares["self", 0] = ((14,), (15,), (16,), (17, 18), (19, 20))
        shares["end"] = ((21, 22), (23,))
        gates = ("late", "middle", "self late", "last")

        def step(name, p, first, last):
            if name in gates:
                settle(len(puts))
                if name == "middle":
                    kept_mem.start()
                if name in ("middle", "self late"):
                    pl.semaphore_wait(freed, 1)
                work.begin(batches[gates.index(name) + 1])
                return
            if name in ("mid", "end"):
                for t in shares[name][p]:
                    run_slot(slots[t])
                return
            for k, share in enumerate(shares[name, first]):

                @pl.when(p == first + k)
                def _(share=share, k=k):
                    if name == "self":
                        turn = k if first == 0 else 4
                        for c in mem_rows.copies[3 * turn : 3 * turn + 3] if turn < 5 and (first or k < 4) else []:
                            c.start()
                    for t in share:
                        run_slot(slots[t])
                    if n - 1 in share or 2 * n - 1 in share:
                        pl.semaphore_signal(freed, inc=1, device_id=dev(z, y, x, 1 - g), device_id_type=MESH)

    g2, aux, qc, kvc, att2, lse2, mem, x1, att1, qkv, lse1, tok = lazy_v
    attention_backward(
        tok, mem, aux, gains, table, qkv, att1, lse1, x1, qc, kvc, att2, lse2, g2,
        d_mem, d_tok, d_gains, dist, *scratch, weight=weight, need=need, emit=emit, step=step,
    )
    early[...] = jnp.zeros_like(early)
    early[0:2, 0:WIDTH] = d_gains[0:2, :]
    early[2:3, 0:WIDTH] = gain_three[...]
    rel = rel_sums(dist[...], hot_dist[...], mode_rows[...])
    early[:, WIDTH : WIDTH + 128] = rel[0:8]
    early[:, WIDTH + 128 : WIDTH + 256] = rel[8:16]
    if not boxed:
        settle(len(puts))
        return
    kept_tok.start()
    turns = total_steps(links, early, early_room)
    for k, slot in enumerate(slots[24:]):
        run_slot(slot)
        for c in tok_rows.copies[TOK_RATE * k : TOK_RATE * k + TOK_RATE]:
            c.start()
        if k % 4 == 0 and k // 4 < len(turns):
            turns[k // 4]()
    where = me * 2 + g
    sums[...] = block_sums(part_in[...], part_out[...], upright(rows_out[...]), where * 272, where * 112)
    run(total_steps(links, sums, room))
    mem_rows.arrived()
    tok_rows.arrived()
    kept_mem.wait()
    kept_tok.wait()
    work.drain()
    mem_rows.drain()
    tok_rows.drain()


def backward_call(boxed, g_win, g_wout, win, wout, lazy, *more):
    f32, bf16 = jnp.float32, jnp.bfloat16
    vm, dma = pltpu.VMEM, pltpu.SemaphoreType.DMA
    row = sds((SEQ, WIDTH))
    scratch = [vm((8, WIDTH), f32), vm((16, 384), f32)]
    scratch += [
        vm((SEQ, HEAD_COLS), bf16), vm((SEQ, 3 * HEAD_COLS), bf16), vm((2, 128, 384), f32),
        vm((2, HEAD_COLS, WIDTH), bf16), dma((10,)), vm((3, HEAD_COLS, WIDTH), bf16), dma((len(BACK_BLOCKS),)),
        dma((len(lazy),)), dma((4,)),
    ]
    scratch += [vm(v.shape, v.dtype) for v in lazy]
    outs = [sds(g_win.shape), sds(g_wout.shape)]
    if boxed:
        items, both = 4 * len(SUM_PIECES), 4 * 384
        outs += [sds((272, WIDTH), f32), sds((112, WIDTH), f32), sds((8, WIDTH), f32), sds((8, WIDTH + 256), f32), row, row]
        specs = (anywhere(),) * 2 + (whole(),) * 4 + (anywhere(),) * 2
        scratch = [vm((SEQ, WIDTH), bf16), vm((SEQ, WIDTH), bf16)] + scratch
        scratch += [
            vm((4, both, WIDTH), bf16), vm((4, 800, WIDTH), bf16), vm((2, both, WIDTH), bf16),
            vm((1, both, WIDTH), bf16), vm((6 * 384, WIDTH), bf16), vm((7, 8, WIDTH), f32), vm((7, 8, WIDTH + 256), f32),
            dma((20,)), dma((7 * items + 16,)), dma((items,)),
            pltpu.SemaphoreType.REGULAR,
        ]
    else:
        outs += [row, row, sds((8, WIDTH + 256), f32)]
        specs = (anywhere(),) * 2 + (whole(),) * 3
    extra = dict(collective_id=2, has_side_effects=True) if boxed else {}
    return pl.pallas_call(
        functools.partial(backward_kernel, boxed),
        out_shape=tuple(outs),
        scratch_shapes=scratch,
        in_specs=[anywhere()] * (4 + len(lazy)) + [whole()] * len(more),
        out_specs=specs,
        input_output_aliases={0: 0, 1: 1},
        compiler_params=pltpu.CompilerParams(vmem_limit_bytes=VMEM_BYTES, **extra),
    )(g_win, g_wout, win, wout, *lazy, *more)


def body(
    tokens, memory, segments, memory_segments, row_source, denoiser_modes, sentinel, cotangent, w_in, w_out,
    norm_gains, rel_bias, rows_in, cols_in, rows_out, cols_out, sq_gains, sq_rel,
):
    n_index = lax.axis_size("dp")
    n_group = lax.axis_size("group")
    my_group = lax.axis_index("group")
    my_place = lax.axis_index(("dp", "group"))
    half_rows = tokens.shape[0]
    rows_dev = cotangent.shape[0]
    assert rows_dev == 1
    boxed = n_index == 16 and n_group == 2
    ids = jnp.stack([jnp.int32(n_group), my_group, my_place])
    buckets = bucket_table(SEQ, BUCKETS)
    hot = (buckets[:256, None] == np.arange(BUCKETS)[None, :]).astype(np.float32)
    lane = np.arange(256)
    dist_f = np.where(lane <= 128, 128 - lane, 384 - lane)
    hot_t = jnp.asarray(np.concatenate([hot[dist_f], hot], axis=0).T)
    w_in_t, rel_t = w_in.T, jnp.swapaxes(rel_bias, 1, 2)
    if boxed:
        win, wout, tok, mem, aux, table_b, keep, mode_rows, *kept = forward_call(
            True, row_source, denoiser_modes, tokens, memory, segments, memory_segments, w_in_t, w_out, rel_t, hot_t,
            sentinel, norm_gains,
        )
    else:
        tok_s, mem_s, aux_s, win_sh, wout_sh, table_f, table_b, keep, mode_rows = prep_call(
            ids, row_source, denoiser_modes, tokens, memory, segments, memory_segments, w_in_t, w_out, rel_t, hot_t,
            sentinel,
        )
        win = lax.all_gather(win_sh, ("dp", "group"), axis=0, tiled=True)
        wout = lax.all_gather(wout_sh, ("dp", "group"), axis=0, tiled=True)
        tok, mem, aux = (
            lax.all_to_all(v, "dp", split_axis=0, concat_axis=0, tiled=True).reshape(SEQ, v.shape[-1])
            for v in (tok_s, mem_s, aux_s)
        )
        kept = forward_call(False, tok, mem, aux, win, wout, norm_gains, table_f)
    x2 = kept[8]
    mixed, g2, d_gain_three, g_win, g_wout = ff_call(
        x2, cotangent.reshape(SEQ, WIDTH), keep, norm_gains, win, wout
    )
    hot_dist = np.concatenate([hot, np.repeat(np.eye(BUCKETS, dtype=np.float32)[-1:], 128, axis=0)], axis=0)
    hot_dist = jnp.asarray(np.pad(hot_dist, ((0, 0), (0, 128 - BUCKETS))))
    rows_out_up = rows_out.reshape(1, -1)
    qkv, att1, lse1, x1, qc, kvc, att2, lse2, _ = kept
    lazy = (g2, aux, qc, kvc, att2, lse2, mem, x1, att1, qkv, lse1, tok)
    result = backward_call(
        boxed, g_win, g_wout, win, wout, lazy, norm_gains, table_b, hot_dist, mode_rows, d_gain_three, rows_out_up
    )
    if boxed:
        _, _, part_in_t, part_out, sums, early, back_tok, back_mem = result
        back_tok, back_mem = back_tok.reshape(tokens.shape), back_mem.reshape(memory.shape)
    else:
        g_win, g_wout, d_mem, d_tok, early = result
        back_tok, back_mem = (
            lax.all_to_all(v.reshape(tokens.shape), "dp", split_axis=0, concat_axis=0, tiled=True)
            for v in (d_tok, d_mem)
        )
        part_in_t, part_out = (
            lax.psum_scatter(v.astype(jnp.float32), ("dp", "group"), scatter_dimension=0, tiled=True)
            for v in (g_win, g_wout)
        )
        sums = block_sums(
            part_in_t, part_out, rows_out.reshape(-1, 1), my_place * part_in_t.shape[0], my_place * part_out.shape[0]
        )
        sums, early = lax.psum((sums, early), ("dp", "group"))
    (
        d_tokens, d_memory, grad_in, grad_out, grad_gains, grad_rel, new_in, new_out, new_gains, new_rel,
        rows_in_new, cols_in_new, rows_out_new, cols_out_new, sq_gains_new, sq_rel_new,
    ) = update_call(
        ids, row_source, part_in_t, part_out, sums, early, back_tok, back_mem, w_in_t, w_out, norm_gains, rel_t,
        rows_in, cols_in, rows_out, cols_out, sq_gains, jnp.swapaxes(sq_rel, 1, 2),
    )
    grad_rel, new_rel, sq_rel_new = (jnp.swapaxes(v, 1, 2) for v in (grad_rel, new_rel, sq_rel_new))
    return (
        mixed[None], d_tokens, d_memory, grad_in.T, grad_out, grad_gains, grad_rel, new_in.T, new_out, new_gains,
        new_rel, rows_in_new, cols_in_new, rows_out_new, cols_out_new, sq_gains_new,
        sq_rel_new,
    )


def solution(mesh):
    both = ("dp", "group")
    row_in = P("group", "dp", None)
    seg_in = P("group", "dp")
    return jax.shard_map(
        body,
        mesh=mesh,
        in_specs=(
            row_in, row_in, seg_in, seg_in, P(), P(), P(both, None), P(both, None, None), P(None, both),
            P(both, None), P(), P(), P(), P(both), P(both), P(), P(), P(),
        ),
        out_specs=(
            P(both, None, None), row_in, row_in, P(None, both), P(both, None), P(), P(), P(None, both),
            P(both, None), P(), P(), P(), P(both), P(both), P(), P(), P(),
        ),
        check_vma=False,
    )
```

```python
import functools

import jax
import jax.numpy as jnp
import numpy as np
from jax import lax
from jax.experimental import pallas as pl
from jax.experimental.pallas import tpu as pltpu
from jax.sharding import PartitionSpec as P

HEADS = 12
HSIZE = 64
FF = 2048
BUCKETS = 32
MODES = 3
SEGS = 4
SEQ = 512
WIDTH = 768
EPSILON = 1e-06
MASKED = -1e30
DECAY_RATE = 0.9
STEP_SIZE = 0.01
PLAIN_STEP = 0.15
GELU_SCALE = 0.7978845608028654
PRECISE = lax.Precision.HIGHEST
MESH = pl.DeviceIdType.MESH
VMEM_BYTES = 60 << 20


def bucket_table(length, buckets):
    exact_span = buckets // 2
    distances = np.arange(length)
    safe_spans = np.maximum(distances, 1)
    logged = np.floor(
        np.log(safe_spans / exact_span) / np.log(128.0 / exact_span) * (buckets - exact_span)
    )
    far_bucket = np.minimum(exact_span + logged, buckets - 1)
    return np.where(distances < exact_span, distances, far_bucket).astype(np.int32)


def nt(a, b):
    return lax.dot_general(a, b, (((1,), (1,)), ((), ())), preferred_element_type=jnp.float32)


def nn(a, b):
    return lax.dot_general(a, b, (((1,), (0,)), ((), ())), preferred_element_type=jnp.float32)


def tn(a, b):
    return lax.dot_general(a, b, (((0,), (0,)), ((), ())), preferred_element_type=jnp.float32)


def inv_rms(values):
    return lax.rsqrt(jnp.mean(values * values, axis=-1, keepdims=True) + EPSILON)


def rms_back(values, gain, grad):
    inv = inv_rms(values)
    scaled = grad * gain
    along = jnp.mean(scaled * values, axis=-1, keepdims=True)
    return inv * scaled - values * (inv * inv * inv * along), jnp.sum(
        grad * (values * inv), axis=0, keepdims=True
    )


def lane_of(shape):
    return lax.broadcasted_iota(jnp.int32, shape, 1)


def ext_masks(aux, first):
    lane = lane_of(aux.shape)
    spot = lane & 63
    documents = (spot >= first) & (spot < first + SEGS)
    hot = jnp.where(documents, aux.astype(jnp.float32), 0.0)
    against = jnp.where(documents, (1.0 - aux.astype(jnp.float32)) * MASKED, 0.0)
    return hot, against


def halves(tile, ext, even):
    lane = lane_of(tile.shape)
    return jnp.where((lane < HSIZE) if even else (lane >= HSIZE), tile, ext)


def pick(first, second, lane):
    return jnp.where(lane < HSIZE, first, second)


def tile_cols(p, base=0):
    return pl.ds(pl.multiple_of(p * 128 + base, 128), 128)


def attend_pair(p, q_tile, k_tile, v_tile, k_ext, q_ext, att_ref, lse_ref, bias_of):
    lane = lane_of((SEQ, 128))
    ones = jnp.ones((SEQ, 128), jnp.bfloat16)
    outs, tops = [], []
    for even in (True, False):
        s = nt(halves(q_tile, q_ext, even), halves(k_tile, k_ext, even))
        if bias_of is None:
            top = jnp.max(s, axis=1, keepdims=True)
            e = jnp.exp(s - top).astype(jnp.bfloat16)
        else:
            near, far = bias_of(2 * p + (0 if even else 1))
            tops_of, rows_of_e = [], []
            for i in range(SEQ // 128):
                lo, hi = max(0, i - 2) * 128, (i + 1) * 128
                part = s[i * 128 : (i + 1) * 128, lo:hi]
                bias = [near[:, 128:]] if i == 0 else [near] if i == 1 else [far, near]
                part = part + (bias[0] if len(bias) == 1 else jnp.concatenate(bias, axis=1))
                tops_of.append(jnp.max(part, axis=1, keepdims=True))
                blocks = [jnp.exp(part - tops_of[-1]).astype(jnp.bfloat16)]
                if lo > 0:
                    blocks.insert(0, jnp.zeros((128, lo), jnp.bfloat16))
                if hi < SEQ:
                    blocks.append(jnp.zeros((128, SEQ - hi), jnp.bfloat16))
                rows_of_e.append(blocks[0] if len(blocks) == 1 else jnp.concatenate(blocks, axis=1))
            e = jnp.concatenate(rows_of_e, axis=0)
            top = jnp.concatenate(tops_of, axis=0)
        outs.append(nn(e, halves(v_tile, ones, even)))
        tops.append(top)
    total = pltpu.roll(pick(outs[1], outs[0], lane), HSIZE, 1)
    att_ref[:, tile_cols(p)] = (pick(outs[0], outs[1], lane) / total).astype(jnp.bfloat16)
    lse = pick(tops[0], tops[1], lane) + jnp.log(total)
    lse_ref[...] = jnp.where(
        lane == 2 * p, lse[:, 0:1], jnp.where(lane == 2 * p + 1, lse[:, HSIZE : HSIZE + 1], lse_ref[...])
    )


def forward_bias(table_ref):
    def bias_of(h):
        row = table_ref[pl.ds(h, 1), :]
        near = pltpu.roll(jnp.broadcast_to(row, (128, 256)), 0, 1, stride=1, stride_axis=0)
        lane = lax.broadcasted_iota(jnp.int32, (128, 256), 1)
        sub = lax.broadcasted_iota(jnp.int32, (128, 256), 0)
        near = jnp.where(lane - 128 > sub, MASKED, near)
        far = jnp.broadcast_to(row[:, :1], (128, 128))
        return near, far

    return bias_of


def back_bias(table_ref):
    def bias_of(h):
        row = table_ref[pl.ds(h, 1), :]
        near = pltpu.roll(jnp.broadcast_to(row, (128, 256)), 0, 1, stride=1, stride_axis=0)
        lane = lax.broadcasted_iota(jnp.int32, (128, 256), 1)
        sub = lax.broadcasted_iota(jnp.int32, (128, 256), 0)
        near = jnp.where(lane < sub, MASKED, near)
        far = jnp.broadcast_to(row[:, 128:129], (128, 128))
        return near, far

    return bias_of


def by_distance(near):
    rows = 64
    while rows >= 8:
        near = near[:rows] + pltpu.roll(near[rows:], 256 - rows, 1)
        rows //= 2
    sub = lax.broadcasted_iota(jnp.int32, (8, 256), 0)
    for bit in (4, 2, 1):
        near = jnp.where((sub & bit) != 0, pltpu.roll(near, 256 - bit, 1), near)
    return near


def split_cols(values, base, lane, count):
    rest, out = values, jnp.zeros((values.shape[0], 128), jnp.float32)
    for k in range(count):
        part = rest.astype(jnp.bfloat16).astype(jnp.float32)
        out = jnp.where((lane & 63) == base + k, part, out)
        rest = rest - part
    return out


def back_pair(p, q_tile, k_tile, v_tile, do_tile, att_tile, lse_all, hot, against, bias_of, rel_acc, dist_ref):
    lane = lane_of((SEQ, 128))
    spot = lane & 63
    ones3 = jnp.where((spot >= 8) & (spot < 11), 1.0, 0.0)
    k_ext = (hot + ones3).astype(jnp.bfloat16)
    v_ext = jnp.where((spot >= 0) & (spot < 2), 1.0, 0.0).astype(jnp.bfloat16)
    product = do_tile.astype(jnp.float32) * att_tile.astype(jnp.float32)
    dqs, dks, dvs = [], [], []
    for n, even in enumerate((True, False)):
        h = 2 * p + n
        lse = jnp.sum(jnp.where(lane == h, lse_all, 0.0), axis=1, keepdims=True)
        own = (lane < HSIZE) if even else (lane >= HSIZE)
        delta = jnp.sum(jnp.where(own, product, 0.0), axis=1, keepdims=True)
        q_ext = (against + split_cols(-lse, 8, lane, 3)).astype(jnp.bfloat16)
        d_ext = split_cols(-delta, 0, lane, 2).astype(jnp.bfloat16)
        s = nt(halves(k_tile, k_ext, even), halves(q_tile, q_ext, even))
        dp = nt(halves(v_tile, v_ext, even), halves(do_tile, d_ext, even))
        if bias_of is None:
            w = jnp.exp(s)
            ds = (w * dp).astype(jnp.bfloat16)
            w = w.astype(jnp.bfloat16)
        else:
            near, far = bias_of(h)
            w_rows, ds_rows = [], []
            for j in range(SEQ // 128):
                lo, hi = j * 128, min(SEQ, (j + 3) * 128)
                bias = near[:, :128] if hi - lo == 128 else near
                if hi - lo == 384:
                    bias = jnp.concatenate([near, far], axis=1)
                part = jnp.exp(s[lo : lo + 128, lo:hi] + bias)
                d_part = part * dp[lo : lo + 128, lo:hi]
                if j == 0:
                    rel_acc[n] = d_part
                else:
                    rel_acc[n, :, : hi - lo] += d_part
                for rows, block in ((w_rows, part), (ds_rows, d_part)):
                    blocks = [block.astype(jnp.bfloat16)]
                    if lo > 0:
                        blocks.insert(0, jnp.zeros((128, lo), jnp.bfloat16))
                    if hi < SEQ:
                        blocks.append(jnp.zeros((128, SEQ - hi), jnp.bfloat16))
                    rows.append(blocks[0] if len(blocks) == 1 else jnp.concatenate(blocks, axis=1))
            w, ds = jnp.concatenate(w_rows, axis=0), jnp.concatenate(ds_rows, axis=0)
        dvs.append(nn(w, do_tile))
        dks.append(nn(ds, q_tile))
        dqs.append(tn(k_tile, ds))
    if bias_of is not None:
        for n in range(2):
            near = by_distance(rel_acc[n, :, :256])
            dist_ref[pl.ds(2 * p + n, 1), :] = jnp.concatenate(
                [
                    jnp.sum(near, axis=0, keepdims=True),
                    jnp.sum(rel_acc[n, :, 256:], axis=0, keepdims=True),
                ],
                axis=1,
            )
    sub = lax.broadcasted_iota(jnp.int32, (128, SEQ), 0)
    dq = jnp.where(sub < HSIZE, dqs[0], dqs[1]).T * HSIZE**-0.5
    return dq, pick(dks[0], dks[1], lane), pick(dvs[0], dvs[1], lane)


HEAD_COLS = HEADS * HSIZE


def attention_forward(
    tok, mem, aux, win, wout, gains, table, qkv, att1, lse1, x1, qc, kvc, att2, lse2, x2, step
):
    x0 = tok[...].astype(jnp.float32)
    a1 = (x0 * inv_rms(x0) * gains[0:1, :]).astype(jnp.bfloat16)
    for k in range(3):
        cols = slice(k * HEAD_COLS, (k + 1) * HEAD_COLS)
        got = nt(a1, win[cols, :])
        if k == 0:
            got = got.astype(jnp.bfloat16).astype(jnp.float32) * HSIZE**-0.5
        qkv[:, cols] = got.astype(jnp.bfloat16)
    step("projected", 0)
    lse1[...] = jnp.zeros_like(lse1)
    lse2[...] = jnp.zeros_like(lse2)

    @pl.loop(0, HEADS // 2)
    def _(p):
        hot, against = ext_masks(aux[...], 0)
        attend_pair(
            p, qkv[:, tile_cols(p)], qkv[:, tile_cols(p, HEAD_COLS)], qkv[:, tile_cols(p, 2 * HEAD_COLS)],
            hot.astype(jnp.bfloat16), against.astype(jnp.bfloat16), att1, lse1, forward_bias(table),
        )
        step("self", p)

    x1[...] = tok[...].astype(jnp.float32) + nn(att1[...], wout[0:HEAD_COLS, :])
    step("middle", 0)
    a2 = (x1[...] * inv_rms(x1[...]) * gains[1:2, :]).astype(jnp.bfloat16)
    got = nt(a2, win[3 * HEAD_COLS : 4 * HEAD_COLS, :])
    qc[...] = (got.astype(jnp.bfloat16).astype(jnp.float32) * HSIZE**-0.5).astype(jnp.bfloat16)
    for k in range(2):
        kvc[:, k * HEAD_COLS : (k + 1) * HEAD_COLS] = nt(
            mem[...], win[(4 + k) * HEAD_COLS : (5 + k) * HEAD_COLS, :]
        ).astype(jnp.bfloat16)
    step("crossed", 0)

    @pl.loop(0, HEADS // 2)
    def _(p):
        _, against = ext_masks(aux[...], 0)
        hot = pltpu.roll(ext_masks(aux[...], SEGS)[0], 128 - SEGS, 1)
        attend_pair(
            p, qc[:, tile_cols(p)], kvc[:, tile_cols(p)], kvc[:, tile_cols(p, HEAD_COLS)],
            hot.astype(jnp.bfloat16), against.astype(jnp.bfloat16), att2, lse2, None,
        )
        step("cross", p)

    step("attended", 0)
    x2[...] = x1[...] + nn(att2[...], wout[HEAD_COLS : 2 * HEAD_COLS, :])
    step("end", 0)


def ff_kernel(
    x2, cot, keep, gains, w_gate, w_up, w_down, mixed, g2, d_gain, g_win, g_wout, a3, e3, acc, da3, held, sem
):
    c = pl.program_id(0)
    slot = lax.rem(c, 2)
    rows = w_gate.shape[0]
    first = pl.multiple_of(c * rows, rows)
    puts = [
        pltpu.make_async_copy(held.at[slot, 0], g_win.at[pl.ds(6 * HEAD_COLS + first, rows)], sem.at[slot, 0]),
        pltpu.make_async_copy(held.at[slot, 1], g_win.at[pl.ds(6 * HEAD_COLS + FF + first, rows)], sem.at[slot, 1]),
        pltpu.make_async_copy(held.at[slot, 2], g_wout.at[pl.ds(2 * HEAD_COLS + first, rows)], sem.at[slot, 2]),
    ]

    @pl.when(c >= 2)
    def _():
        for put in puts:
            put.wait()

    @pl.when(c == 0)
    def _():
        a3[...] = (x2[...] * inv_rms(x2[...]) * gains[2:3, :]).astype(jnp.bfloat16)
        e3[...] = (cot[...].astype(jnp.float32) * keep[:, 0:1]).astype(jnp.bfloat16)
        acc[...] = x2[...]
        da3[...] = jnp.zeros_like(da3)

    gate = nt(a3[...], w_gate[...])
    up = nt(a3[...], w_up[...])
    dh = nt(e3[...], w_down[...])
    cube = 0.044715 * gate * gate
    inner = jnp.tanh(GELU_SCALE * gate * (1.0 + cube))
    half = 0.5 * (1.0 + inner)
    gelu = gate * half
    slope = half + 0.5 * gate * (1.0 - inner * inner) * (GELU_SCALE * (1.0 + 3.0 * cube))
    hidden = (gelu * up).astype(jnp.bfloat16)
    d_gate = (dh * up * slope).astype(jnp.bfloat16)
    d_up = (dh * gelu).astype(jnp.bfloat16)
    acc[...] += nn(hidden, w_down[...])
    held[slot, 0] = tn(d_gate, a3[...]).astype(jnp.bfloat16)
    held[slot, 1] = tn(d_up, a3[...]).astype(jnp.bfloat16)
    held[slot, 2] = tn(hidden, e3[...]).astype(jnp.bfloat16)
    for put in puts:
        put.start()
    da3[...] += nn(d_gate, w_gate[...]) + nn(d_up, w_up[...])

    @pl.when(c == pl.num_programs(0) - 1)
    def _():
        mixed[...] = acc[...].astype(jnp.bfloat16)
        part, gain = rms_back(x2[...], gains[2:3, :], da3[...])
        g2[...] = cot[...].astype(jnp.float32) * keep[:, 0:1] + part
        d_gain[...] = gain
        for k in range(3):
            for other in range(2):
                pltpu.make_async_copy(held.at[other, k], g_wout.at[0:rows], sem.at[other, k]).wait()


SELF_LATE = 5
LATE = 4


BACK_BLOCKS = (("o", 1), ("i", 4), ("i", 5), ("i", 3), ("o", 0), ("i", 0), ("i", 1), ("i", 2))


def attention_backward(
    tok, mem, aux, gains, table, qkv, att1, lse1, x1, qc, kvc, att2, lse2, g2,
    d_mem, d_tok, d_gains, dist, do, dqkv, rel_acc, weight, need, emit, step,
):
    need(1)
    e2 = g2[...].astype(jnp.bfloat16)
    do[...] = weight(0, lambda w: nt(e2, w)).astype(jnp.bfloat16)
    need(8)
    emit("o", HEAD_COLS, tn(att2[...], e2))

    def cross_pairs(first, last):
        @pl.loop(first, last)
        def _(p):
            _, against = ext_masks(aux[...], 0)
            hot = pltpu.roll(ext_masks(aux[...], SEGS)[0], 128 - SEGS, 1)
            dq, dk, dv = back_pair(
                p, qc[:, tile_cols(p)], kvc[:, tile_cols(p)], kvc[:, tile_cols(p, HEAD_COLS)], do[:, tile_cols(p)],
                att2[:, tile_cols(p)], lse2[...], hot, against, None, rel_acc, dist,
            )
            dqkv[:, tile_cols(p)] = dq.astype(jnp.bfloat16)
            dqkv[:, tile_cols(p, HEAD_COLS)] = dk.astype(jnp.bfloat16)
            dqkv[:, tile_cols(p, 2 * HEAD_COLS)] = dv.astype(jnp.bfloat16)
            step("cross", p, first, last)

    late = 2 * HEAD_COLS + LATE * 128
    cross_pairs(LATE, HEADS // 2)
    emit("i", 3 * HEAD_COLS + late, tn(dqkv[:, late:], mem[...]))
    step("late", None, 0, 0)
    cross_pairs(0, LATE)
    need(12)
    a2 = (x1[...] * inv_rms(x1[...]) * gains[1:2, :]).astype(jnp.bfloat16)
    emit("i", 3 * HEAD_COLS, tn(dqkv[:, 0:HEAD_COLS], a2))
    emit("i", 4 * HEAD_COLS, tn(dqkv[:, HEAD_COLS : 2 * HEAD_COLS], mem[...]))
    step("mid", 0, 0, 0)
    emit("i", 5 * HEAD_COLS, tn(dqkv[:, 2 * HEAD_COLS : late], mem[...]))
    d_rows = weight(1, lambda w: nn(dqkv[:, HEAD_COLS : 2 * HEAD_COLS], w))
    d_rows += weight(2, lambda w: nn(dqkv[:, 2 * HEAD_COLS : 3 * HEAD_COLS], w))
    d_mem[...] = d_rows.astype(jnp.bfloat16)
    step("mid", 1, 0, 0)
    da2 = weight(3, lambda w: nn(dqkv[:, 0:HEAD_COLS], w))
    part, gain = rms_back(x1[...], gains[1:2, :], da2)
    d_gains[1:2, :] = gain
    g2[...] += part
    step("mid", 2, 0, 0)
    e1 = g2[...].astype(jnp.bfloat16)
    do[...] = weight(4, lambda w: nt(e1, w)).astype(jnp.bfloat16)
    emit("o", 0, tn(att1[...], e1))
    step("middle", None, 0, 0)

    def self_pairs(first, last):
        @pl.loop(first, last)
        def _(p):
            hot, against = ext_masks(aux[...], 0)
            dq, dk, dv = back_pair(
                p, qkv[:, tile_cols(p)], qkv[:, tile_cols(p, HEAD_COLS)], qkv[:, tile_cols(p, 2 * HEAD_COLS)],
                do[:, tile_cols(p)], att1[:, tile_cols(p)], lse1[...], hot, against, back_bias(table), rel_acc, dist,
            )
            dqkv[:, tile_cols(p)] = dq.astype(jnp.bfloat16)
            dqkv[:, tile_cols(p, HEAD_COLS)] = dk.astype(jnp.bfloat16)
            dqkv[:, tile_cols(p, 2 * HEAD_COLS)] = dv.astype(jnp.bfloat16)
            step("self", p, first, last)

    x0 = tok[...].astype(jnp.float32)
    a1 = (x0 * inv_rms(x0) * gains[0:1, :]).astype(jnp.bfloat16)
    late = 2 * HEAD_COLS + SELF_LATE * 128
    self_pairs(SELF_LATE, HEADS // 2)
    emit("i", late, tn(dqkv[:, late:], a1))
    step("self late", None, 0, 0)
    self_pairs(0, SELF_LATE)
    x0 = tok[...].astype(jnp.float32)
    a1 = (x0 * inv_rms(x0) * gains[0:1, :]).astype(jnp.bfloat16)
    for first, last in ((0, HEAD_COLS), (HEAD_COLS, 2 * HEAD_COLS), (2 * HEAD_COLS, late)):
        emit("i", first, tn(dqkv[:, first:last], a1))
    step("last", None, 0, 0)
    da1 = weight(5, lambda w: nn(dqkv[:, 0:HEAD_COLS], w))
    for k in (1, 2):
        step("end", k - 1, 0, 0)
        da1 += weight(5 + k, lambda w: nn(dqkv[:, k * HEAD_COLS : (k + 1) * HEAD_COLS], w))
    part, gain = rms_back(x0, gains[0:1, :], da1)
    d_gains[0:1, :] = gain
    d_tok[...] = (g2[...] + part).astype(jnp.bfloat16)


SHARE = {"i": 272, "o": 112}
PIECES = (
    ("i", 0, 64, 32), ("i", 64, 64, 32), ("i", 128, 64, 32), ("i", 192, 80, 48),
    ("o", 0, 64, 32), ("o", 64, 48, 16),
)


UP_LEAD = (4, 3)
DOWN_LEAD = (12, 9, 6, 3)


SUM_PIECES = (
    ("i", 0, 32, 16), ("i", 32, 32, 16), ("i", 64, 64, 32), ("i", 128, 64, 32), ("i", 192, 80, 48),
    ("o", 0, 64, 32), ("o", 64, 48, 16),
)


def place():
    dp = lax.axis_index("dp")
    return dp // 4, (dp // 2) % 2, dp % 2, lax.axis_index("group")


def dev(z, y, x, g):
    return ((z * 2 + y) * 2 + x, g)


def rows_of(ref, kind, zz, yy, xx, gg, lo, n):
    share = ((zz * 2 + yy) * 2 + xx) * 2 + gg
    return ref.at[pl.ds(pl.multiple_of(share * SHARE[kind] + lo, 16), n)]


class Links:
    def __init__(self, send_sem, recv_sem):
        self.send_sem, self.recv_sem, self.sends, self.recvs = send_sem, recv_sem, 0, 0

    def new_send(self):
        self.sends += 1
        assert self.sends <= self.send_sem.shape[0]
        return self.sends - 1

    def new_recv(self, n=1):
        self.recvs += n
        assert self.recvs <= self.recv_sem.shape[0]
        return self.recvs - n

    def copy(self, src, dst, device, send=None, recv=None):
        send = self.new_send() if send is None else send
        recv = self.new_recv() if recv is None else recv
        return pltpu.make_async_remote_copy(
            src_ref=src, dst_ref=dst, send_sem=self.send_sem.at[send], recv_sem=self.recv_sem.at[recv],
            device_id=device, device_id_type=MESH,
        )

    def sent(self, send, like):
        wait_bytes(self.send_sem.at[send], like)

    def arrived(self, recv, like):
        wait_bytes(self.recv_sem.at[recv], like)


def wait_bytes(sem, like):
    pltpu.make_async_copy(like, like, sem).wait()


def drain_line(links, send, like, rows):
    z = place()[0]
    for k, n in enumerate(rows):
        if n > 0:
            pl.when(z == k)(functools.partial(links.sent, send, like.at[0:n]))


def greet(peers):
    barrier = pltpu.get_barrier_semaphore()
    total = 0
    for device, cond in peers:
        if cond is None:
            pl.semaphore_signal(barrier, inc=1, device_id=device, device_id_type=MESH)
            total = total + 1
        else:

            @pl.when(cond)
            def _(device=device):
                pl.semaphore_signal(barrier, inc=1, device_id=device, device_id_type=MESH)

            total = total + cond.astype(jnp.int32)
    return total


def meet(total):
    pl.semaphore_wait(pltpu.get_barrier_semaphore(), total)


def near_peers():
    z, y, x, g = place()
    return [
        (dev(z, y, 1 - x, g), None), (dev(z, 1 - y, x, g), None), (dev(z, y, x, 1 - g), None),
        (dev(jnp.minimum(z + 1, 3), y, x, g), z < 3), (dev(jnp.maximum(z - 1, 0), y, x, g), z > 0),
    ]


def all_peers():
    z, y, x, g = place()
    me = lax.axis_index("dp")
    return [((lax.rem(me + k, 16), g), None) for k in range(1, 16)] + [(dev(z, y, x, 1 - g), None)]


class Gather:
    def __init__(self, links, arrays):
        z, y, x, g = place()
        self.links, self.items, self.arrays = links, [], arrays
        self.send = {k: links.new_send() for k in ("plane", "core", "up", "down")}
        self.groups, self.cores = ((0, 12), (12, 16), (16, 24)), []
        for first, last in self.groups:
            self.cores += [links.new_recv()] * (last - first)
        for low in (0, 2):
            nearest = jnp.clip(z, 0, 1) if low == 0 else low
            bases = [links.new_recv(2) for _ in PIECES]
            for zz in (nearest, 2 * low + 1 - nearest):
                for (kind, lo, n, half), line in zip(PIECES, bases):

                    def here(yy, xx, first, count, zz=zz, kind=kind):
                        return rows_of(arrays[kind], kind, zz, yy, xx, g, first, count)

                    c = {"go_up": (z >= zz) & (z < 3), "go_down": (z <= zz) & (z > 0), "n": n}
                    c["from_below"], c["from_above"] = z > zz, z < zz
                    c["hops"] = jnp.abs(z - zz)
                    core = self.cores[len(self.items)]

                    def add(name, ref, device, send, recv=None, c=c):
                        c[name] = links.copy(ref, ref, device, self.send[send], recv)

                    own = here(y, x, lo, n)
                    add("up", own, dev(jnp.minimum(z + 1, 3), y, x, g), "up", line + zz - low)
                    add("down", own, dev(jnp.maximum(z - 1, 0), y, x, g), "down", line + zz - low)
                    add("x", own, dev(z, y, 1 - x, g), "plane")
                    add("y", own, dev(z, 1 - y, x, g), "plane")
                    add("a", here(y, 1 - x, lo, half), dev(z, 1 - y, x, g), "plane")
                    add("b", here(1 - y, x, lo + half, n - half), dev(z, y, 1 - x, g), "plane")
                    other = dev(z, y, x, 1 - g)
                    add("p", own, other, "core", core)
                    add("px", here(y, 1 - x, lo, n), other, "core", core)
                    add("py", here(1 - y, x, lo, n), other, "core", core)
                    add("pa", here(1 - y, 1 - x, lo, half), other, "core", core)
                    add("pb", here(1 - y, 1 - x, lo + half, n - half), other, "core", core)
                    self.items.append(c)

    def along(self, c):
        pl.when(c["from_below"])(c["up"].wait_recv)
        pl.when(c["from_above"])(c["down"].wait_recv)
        pl.when(c["go_up"])(c["up"].start)
        pl.when(c["go_down"])(c["down"].start)

    def hop(self, c, h, way, start, arrival):
        @pl.when((c["hops"] == h) & jnp.logical_not(c[arrival]))
        def _():
            if h > 0:
                c[way].wait_recv()
            pl.when(c[start])(c[way].start)

    def near(self, c):
        for k in ("x", "y", "p"):
            c[k].start()

    def second(self, c):
        c["x"].wait_recv()
        c["a"].start()
        c["px"].start()
        c["y"].wait_recv()
        c["b"].start()
        c["py"].start()

    def third(self, c):
        c["a"].wait_recv()
        c["pa"].start()
        c["b"].wait_recv()
        c["pb"].start()

    def arrived(self, group):
        first, last = self.groups[group]
        rows = 4 * sum(c["n"] for c in self.items[first:last])
        self.links.arrived(self.cores[first], self.arrays["i"].at[0:rows])

    def drain(self):
        rows = sum(c["n"] for c in self.items)
        like = self.arrays["i"]
        self.links.sent(self.send["plane"], like.at[0 : 3 * rows])
        self.links.sent(self.send["core"], like.at[0 : 4 * rows])
        plane = rows // 4
        drain_line(self.links, self.send["up"], like, [plane, 2 * plane, 3 * plane, 0])
        drain_line(self.links, self.send["down"], like, [0, 3 * plane, 2 * plane, plane])

    def slots(self):
        n = len(self.items)
        half = n // 2
        out = [[] for _ in range(n + 6)]
        for t, c in enumerate(self.items):
            out[t + 6].append(functools.partial(self.third, c))
        for t, c in enumerate(self.items):
            out[t + 3].append(functools.partial(self.second, c))
        for t, c in enumerate(self.items):
            if t < half:
                out[t].append(functools.partial(self.along, c))
            out[t].append(functools.partial(self.near, c))
        for t, c in enumerate(self.items[half:]):
            for h in range(4):
                if h < 2:
                    up = functools.partial(self.hop, c, h, "up", "go_up", "from_above")
                    out[half + t - UP_LEAD[h]].append(up)
                down = functools.partial(self.hop, c, h, "down", "go_down", "from_below")
                out[half + t - DOWN_LEAD[h]].append(down)
        return out


class Exchange:
    def __init__(self, links, src, dst, rows):
        me, g = lax.axis_index("dp"), lax.axis_index("group")
        self.links, self.send, self.recv = links, links.new_send(), links.new_recv()
        self.like, self.copies = src.at[0 : 15 * rows], []
        for k in range(1, 16):
            to = lax.rem(me + k, 16)
            there = dst.at[pl.ds(pl.multiple_of(me * rows, 16), rows)]
            here = src.at[pl.ds(pl.multiple_of(to * rows, 16), rows)]
            self.copies.append(links.copy(here, there, (to, g), self.send, self.recv))

    def arrived(self):
        self.links.arrived(self.recv, self.like)

    def drain(self):
        self.links.sent(self.send, self.like)


def own_rows(src, dst, rows, sem):
    here = pl.ds(pl.multiple_of(lax.axis_index("dp") * rows, 16), rows)
    return pltpu.make_async_copy(src.at[here], dst.at[here], sem)


class Sums:
    def __init__(self, links, win_g, wout_g, own, got, plane, fin, line, part_in, part_out, load_sem):
        self.links, self.arrays = links, {"i": win_g, "o": wout_g}
        self.own, self.got, self.plane, self.fin, self.line = own, got, plane, fin, line
        self.part_in, self.part_out, self.load_sem = part_in, part_out, load_sem
        self.loads, self.rows, self.line_rows, self.got_rows = 0, 0, 0, 0
        self.send = {k: links.new_send() for k in ("core", "plane", "up", "down")}

    def batch(self, members, got_from=None):
        z, y, x, g = place()
        self.got_rows = self.got_rows if got_from is None else got_from
        links = self.links
        items = []
        for zz, k in members:
            kind, lo, n, half = SUM_PIECES[k]
            base, rest = self.rows, n - half
            at = lambda ref, c, off, m, base=base: ref.at[c, pl.ds(base + off, m)]
            it = {"zz": zz, "z": z, "n": n, "half": half, "base": base, "kind": kind, "lo": lo}
            it["load"], it["core"], it["pair"] = [], links.new_recv(), []
            it["got"] = self.got_rows
            self.got_rows += n
            it["load_sem"] = self.load_sem.at[self.loads]
            self.loads += 1
            for c, (yy, xx) in enumerate(((y, x), (y, 1 - x), (1 - y, x), (1 - y, 1 - x))):
                ref = self.arrays[kind]
                mine = rows_of(ref, kind, zz, yy, xx, g, lo, n)
                it["load"].append(pltpu.make_async_copy(mine, at(self.own, c, 0, n), it["load_sem"]))
                theirs = rows_of(ref, kind, zz, yy, xx, 1 - g, lo, n)
                it["pair"].append(
                    links.copy(theirs, self.got.at[c, pl.ds(it["got"], n)], dev(z, y, x, 1 - g), self.send["core"], it["core"])
                )
            nx, ny = dev(z, y, 1 - x, g), dev(z, 1 - y, x, g)
            own, plane, fin, send = self.own, self.plane, self.fin, self.send["plane"]
            it["x_recv"], it["y_recv"] = links.new_recv(), links.new_recv()
            it["x1"] = [
                links.copy(at(own, c, 0, half), at(plane, s, 0, half), nx, send, it["x_recv"]) for s, c in ((0, 1), (1, 3))
            ]
            it["y1"] = [
                links.copy(at(own, c, half, rest), at(plane, s, half, rest), ny, send, it["y_recv"])
                for s, c in ((0, 2), (1, 3))
            ]
            it["y2"] = links.copy(at(own, 2, 0, half), at(fin, 0, 0, half), ny, send)
            it["x2"] = links.copy(at(own, 1, half, rest), at(fin, 0, half, rest), nx, send)
            for way, needed in (("from_below", zz > 0), ("from_above", zz < 3)):
                if needed:
                    it[way] = pl.ds(self.line_rows, n)
                    self.line_rows += n
            if zz > 0:
                up = dev(jnp.minimum(z + 1, 3), y, x, g)
                it["up"] = links.copy(at(own, 0, 0, n), self.line.at[it["from_below"]], up, self.send["up"])
            if zz < 3:
                down = dev(jnp.maximum(z - 1, 0), y, x, g)
                it["down"] = links.copy(at(own, 0, 0, n), self.line.at[it["from_above"]], down, self.send["down"])
            items.append(it)
            self.rows += n
        return items

    def begin(self, items):
        for it in items:
            for c in it["load"]:
                c.start()
            for c in it["pair"]:
                c.start()

    def drain(self):
        rows, plane = self.rows, self.rows // 4
        like = self.arrays["i"]
        self.links.sent(self.send["core"], like.at[0 : 4 * rows])
        self.links.sent(self.send["plane"], like.at[0 : 3 * rows])
        drain_line(self.links, self.send["up"], like, [3 * plane, 2 * plane, plane, 0])
        drain_line(self.links, self.send["down"], like, [0, plane, 2 * plane, 3 * plane])

    def place_in(self, slots, first, items):
        for k, it in enumerate(items):
            t = first + k
            slots[t].append((2, self.to_core, it))
            slots[t + 3].append((1, self.to_plane, it))
            slots[t + 6].append((0, self.to_line, it))
            for h in range(1, max(it["zz"], 3 - it["zz"]) + 1):
                slots[t + 6 + 2 * h].append((-h, functools.partial(self.hop, h), it))

    @staticmethod
    def add(dst, c, first, src, s, start, m):
        rows = pl.ds(first, m)
        more = src[s, pl.ds(start, m), :].astype(jnp.float32)
        dst[c, rows, :] = (dst[c, rows, :].astype(jnp.float32) + more).astype(jnp.bfloat16)

    def add_line(self, it, way):
        rows = pl.ds(it["base"], it["n"])
        more = self.line[it[way], :].astype(jnp.float32)
        self.own[0, rows, :] = (self.own[0, rows, :].astype(jnp.float32) + more).astype(jnp.bfloat16)

    def to_core(self, it):
        rows = pl.ds(it["base"], it["n"])
        wait_bytes(it["load_sem"], self.own.at[:, rows])
        self.links.arrived(it["core"], self.got.at[:, pl.ds(it["got"], it["n"])])
        for c in (3, 1, 2, 0):
            self.add(self.own, c, it["base"], self.got, c, it["got"], it["n"])
            if c == 3:
                it["x1"][1].start()
                it["y1"][1].start()
            if c == 1:
                it["x1"][0].start()
            if c == 2:
                it["y1"][0].start()

    def to_plane(self, it):
        half, rest, base = it["half"], it["n"] - it["half"], it["base"]
        low = base + half
        self.links.arrived(it["x_recv"], self.plane.at[:, pl.ds(base, half)])
        self.add(self.own, 2, base, self.plane, 1, base, half)
        it["y2"].start()
        self.links.arrived(it["y_recv"], self.plane.at[:, pl.ds(low, rest)])
        self.add(self.own, 1, low, self.plane, 1, low, rest)
        it["x2"].start()
        self.add(self.own, 0, base, self.plane, 0, base, half)
        self.add(self.own, 0, low, self.plane, 0, low, rest)

    def to_line(self, it):
        it["y2"].wait_recv()
        it["x2"].wait_recv()
        self.add(self.own, 0, it["base"], self.fin, 0, it["base"], it["n"])
        z, zz = it["z"], it["zz"]
        if zz > 0:
            pl.when(z == 0)(it["up"].start)
        if zz < 3:
            pl.when(z == 3)(it["down"].start)

    def hop(self, h, it):
        z, zz, n, base = it["z"], it["zz"], it["n"], it["base"]
        if h < zz:

            @pl.when(z == h)
            def _():
                it["up"].wait_recv()
                self.add_line(it, "from_below")
                it["up"].start()

        if h < 3 - zz:

            @pl.when(z == 3 - h)
            def _():
                it["down"].wait_recv()
                self.add_line(it, "from_above")
                it["down"].start()

        if h == max(zz, 3 - zz):

            @pl.when(z == zz)
            def _():
                total = self.own[0, pl.ds(base, n), :].astype(jnp.float32)
                if zz > 0:
                    it["up"].wait_recv()
                    total += self.line[it["from_below"], :].astype(jnp.float32)
                if zz < 3:
                    it["down"].wait_recv()
                    total += self.line[it["from_above"], :].astype(jnp.float32)
                into = self.part_in if it["kind"] == "i" else self.part_out
                into[it["lo"] : it["lo"] + n, :] = total


def run_slot(slot):
    for _, step, it in sorted(slot, key=lambda entry: entry[0]):
        step(it)


def total_steps(links, ref, room):
    z, y, x, g = place()
    here = y * 2 + x
    core = links.copy(ref, room.at[0], dev(z, y, x, 1 - g))
    plane = [
        links.copy(ref, room.at[1], dev(z, y, 1 - x, g)),
        links.copy(ref, room.at[2], dev(z, 1 - y, x, g)),
        links.copy(ref, room.at[3], dev(z, 1 - y, 1 - x, g)),
    ]
    line = [links.copy(ref, room.at[3 + k], dev(lax.rem(z + k, 4), y, x, g)) for k in (1, 2, 3)]

    def in_order(first, came_from):
        mine = ref[...]
        total = jnp.zeros_like(mine)
        for n in range(4):
            came = came_from(n)
            term = jnp.where(came == 0, mine, jnp.zeros_like(mine))
            for k in (1, 2, 3):
                term = jnp.where(came == k, room[first + k], term)
            total = total + term
        return total

    def to_plane():
        core.wait()
        ref[...] = ref[...] + room[0]
        for c in plane:
            c.start()

    def to_line():
        for c in plane:
            c.wait()
        ref[...] = in_order(0, lambda n: jnp.bitwise_xor(here, n))
        for c in line:
            c.start()

    def finish():
        for c in line:
            c.wait()
        ref[...] = in_order(3, lambda n: lax.rem(z - n + 4, 4))

    return [core.start, to_plane, to_line, finish]


def vmem_call(kernel, out_shape, scratch, **kw):
    return pl.pallas_call(
        kernel,
        out_shape=out_shape,
        scratch_shapes=scratch,
        compiler_params=pltpu.CompilerParams(vmem_limit_bytes=VMEM_BYTES),
        **kw,
    )


def sds(shape, dtype=jnp.bfloat16):
    return jax.ShapeDtypeStruct(shape, dtype)


WEIGHTS = [pltpu.VMEM((6 * HEAD_COLS, WIDTH), jnp.bfloat16), pltpu.VMEM((2 * HEAD_COLS, WIDTH), jnp.bfloat16)]


def load_rows(src, dst, first, last, sem):
    copy = pltpu.make_async_copy(src.at[first:last], dst.at[first:last], sem)
    copy.start()
    return copy


def anywhere():
    return pl.BlockSpec(memory_space=pl.ANY)


def whole():
    return pl.BlockSpec(memory_space=pltpu.VMEM)


def run(steps):
    for s in steps:
        s()


def block_of(ids, edges):
    return (ids >= edges[0]).astype(jnp.int32) + (ids >= edges[1]).astype(jnp.int32)


IN_EDGES = (3 * HEAD_COLS, 6 * HEAD_COLS)
OUT_EDGES = (HEAD_COLS, 2 * HEAD_COLS)


def block_sums(part_in_t, part_out, rows_out, first_in, first_out):
    sq_in, sq_out = part_in_t * part_in_t, part_out * part_out
    block_in = block_of(first_in + lax.broadcasted_iota(jnp.int32, (sq_in.shape[0], 1), 0), IN_EDGES)
    block_out = block_of(first_out + lax.broadcasted_iota(jnp.int32, (sq_out.shape[0], 1), 0), OUT_EDGES)
    rows_new = DECAY_RATE * rows_out + (1 - DECAY_RATE) * jnp.mean(sq_out, axis=1, keepdims=True)
    lane = lax.broadcasted_iota(jnp.int32, (1, WIDTH), 1)
    lines = [jnp.sum(jnp.where(block_in == k, sq_in, 0.0), axis=0, keepdims=True) for k in range(3)]
    lines += [jnp.sum(jnp.where(block_out == k, sq_out, 0.0), axis=0, keepdims=True) for k in range(3)]
    totals = jnp.zeros((1, WIDTH), jnp.float32)
    for k in range(3):
        total = jnp.sum(jnp.where(block_out == k, rows_new, 0.0), axis=0, keepdims=True)
        totals = jnp.where(lane == k, total, totals)
    return jnp.concatenate(lines + [totals, jnp.zeros((1, WIDTH), jnp.float32)], axis=0)


def prep_rows(group, groups, row_source, tokens, memory, segments, msegments, seg_t, mseg_t, store):
    half_rows, length = tokens.shape[0], tokens.shape[1]
    for source, out in ((segments, seg_t), (msegments, mseg_t)):
        out[...] = jnp.zeros_like(out)
        out[0:half_rows, 0:length] = source[...].astype(jnp.float32)
        out[...] = out[...].T
    lane = lax.broadcasted_iota(jnp.int32, (length, 128), 1)
    spot = (lane & (HSIZE - 1)).astype(jnp.float32)

    @pl.loop(0, half_rows)
    def _(i):
        source = lax.rem(row_source[i * groups + group], half_rows)
        col = jnp.sum(jnp.where(lane == source, seg_t[0:length, :], 0.0), axis=1, keepdims=True)
        mcol = jnp.sum(jnp.where(lane == source, mseg_t[0:length, :], 0.0), axis=1, keepdims=True)
        same = ((spot < SEGS) & (spot == col)) | ((spot >= SEGS) & (spot < 2 * SEGS) & (spot - SEGS == mcol))
        store(i, tokens[source], memory[source], jnp.where(same, 1.0, 0.0).astype(jnp.bfloat16))


def prep_tables(mode, rel_bias, hot, sentinel, table_f, table_b, keep, mode_rows):
    tables = jnp.dot(rel_bias[mode], hot[...], precision=PRECISE, preferred_element_type=jnp.float32)
    for k, table in enumerate((table_f, table_b)):
        table[...] = jnp.zeros_like(table)
        table[0:HEADS, :] = tables[:, k * 256 : (k + 1) * 256]
    mode_rows[...] = jnp.where(lax.broadcasted_iota(jnp.int32, (8, 128), 0) == mode, 1.0, 0.0)
    kept = (1 - sentinel[...]).astype(jnp.float32)
    keep[...] = jnp.broadcast_to(kept, (128, SEQ)).T


def prep_kernel(
    ids, row_source, modes, tokens, memory, segments, msegments, w_in, w_out, rel_bias, hot, sentinel,
    tok_s, mem_s, aux_s, win_sh, wout_sh, table_f, table_b, keep, mode_rows, seg_t, mseg_t,
):
    win_sh[...] = w_in[...].astype(jnp.bfloat16)
    wout_sh[...] = w_out[...].astype(jnp.bfloat16)

    def store(i, tok, mem, aux):
        tok_s[i], mem_s[i], aux_s[i] = tok, mem, aux

    prep_rows(ids[1], ids[0], row_source, tokens, memory, segments, msegments, seg_t, mseg_t, store)
    prep_tables(modes[row_source[ids[2]]], rel_bias, hot, sentinel, table_f, table_b, keep, mode_rows)


def prep_call(ids, row_source, modes, tokens, memory, segments, msegments, w_in, w_out, rel_bias, hot, sentinel):
    f32 = jnp.float32
    scalars = pl.BlockSpec(memory_space=pltpu.SMEM)
    half_rows, length = tokens.shape[0], tokens.shape[1]
    return vmem_call(
        prep_kernel,
        (
            sds(tokens.shape), sds(memory.shape), sds((half_rows, length, 128)), sds(w_in.shape),
            sds(w_out.shape), sds((16, 256), f32), sds((16, 256), f32), sds((SEQ, 128), f32), sds((8, 128), f32),
        ),
        [pltpu.VMEM((128, 128), f32), pltpu.VMEM((128, 128), f32)],
        in_specs=[scalars] * 3 + [whole()] * 9,
    )(ids, row_source, modes, tokens, memory, segments, msegments, w_in, w_out, rel_bias, hot, sentinel)


def upright(row):
    return jnp.broadcast_to(row, (128, row.shape[1])).T[:, 0:1]


def level(col):
    return jnp.broadcast_to(col, (col.shape[0], 128)).T[0:1, :]


def update_kernel(
    ids, row_source, part_in_t, part_out, sums, early, back_tok, back_mem, w_in, w_out, gains, rel_bias, rows_in,
    cols_in, rows_out, cols_out, sq_gains, sq_rel,
    d_tokens, d_memory, grad_in, grad_out, grad_gains, grad_rel, new_in, new_out, new_gains, new_rel, rows_in_new,
    cols_in_new, rows_out_new, cols_out_new, sq_gains_new, sq_rel_new,
):
    half_rows = back_tok.shape[0]
    groups, group, where = ids[0], ids[1], ids[2]

    @pl.loop(0, half_rows)
    def _(i):
        source = row_source[i * groups + group] - group * half_rows
        d_tokens[source] = back_tok[i]
        d_memory[source] = back_mem[i]

    n_in, n_out = w_in.shape[0], w_out.shape[0]
    p_in = part_in_t[...]
    grad_in[...] = p_in
    in_cols = DECAY_RATE * upright(cols_in[...].reshape(1, -1)) + (1 - DECAY_RATE) * jnp.mean(p_in * p_in, axis=1, keepdims=True)
    cols_in_new[...] = level(in_cols).reshape(-1)
    block_in = block_of(where * n_in + lax.broadcasted_iota(jnp.int32, (n_in, 1), 0), IN_EDGES)
    scale = jnp.zeros((n_in, WIDTH), jnp.float32)
    for k, count in enumerate((3 * HEAD_COLS, 3 * HEAD_COLS, 2 * FF)):
        row = DECAY_RATE * rows_in[k : k + 1, :] + (1 - DECAY_RATE) * (sums[k : k + 1, :] / count)
        rows_in_new[k : k + 1, :] = row
        scale = jnp.where(block_in == k, in_cols * (row / jnp.mean(row, axis=1, keepdims=True)), scale)
    new_in[...] = w_in[...] - STEP_SIZE * p_in * lax.rsqrt(scale)

    p_out = part_out[...]
    grad_out[...] = p_out
    out_rows = DECAY_RATE * upright(rows_out[...].reshape(1, -1)) + (1 - DECAY_RATE) * jnp.mean(p_out * p_out, axis=1, keepdims=True)
    rows_out_new[...] = level(out_rows).reshape(-1)
    block_out = block_of(where * n_out + lax.broadcasted_iota(jnp.int32, (n_out, 1), 0), OUT_EDGES)
    scale = jnp.zeros((n_out, WIDTH), jnp.float32)
    for k, count in enumerate((HEAD_COLS, HEAD_COLS, FF)):
        col = DECAY_RATE * cols_out[k : k + 1, :] + (1 - DECAY_RATE) * (sums[3 + k : 4 + k, :] / count)
        cols_out_new[k : k + 1, :] = col
        mean = sums[6:7, k : k + 1] / count
        scale = jnp.where(block_out == k, (out_rows / mean) * col, scale)
    new_out[...] = w_out[...] - STEP_SIZE * p_out * lax.rsqrt(scale)

    g = early[0:3, 0:WIDTH]
    rel = jnp.concatenate([early[:, WIDTH : WIDTH + 128], early[:, WIDTH + 128 : WIDTH + 256]], axis=0)
    grad_gains[...] = g
    sq = DECAY_RATE * sq_gains[...] + (1 - DECAY_RATE) * g * g
    sq_gains_new[...] = sq
    new_gains[...] = gains[...] - PLAIN_STEP * g * lax.rsqrt(sq)
    for k in range(MODES):
        g = rel[0:HEADS, k * BUCKETS : (k + 1) * BUCKETS]
        grad_rel[k] = g
        sq = DECAY_RATE * sq_rel[k] + (1 - DECAY_RATE) * g * g
        sq_rel_new[k] = sq
        new_rel[k] = rel_bias[k] - PLAIN_STEP * g * lax.rsqrt(sq)


def update_call(ids, row_source, *arrays):
    f32 = jnp.float32
    scalars = pl.BlockSpec(memory_space=pltpu.SMEM)
    (part_in_t, part_out, sums, early, back_tok, back_mem, w_in, w_out, gains, rel_bias) = arrays[:10]
    n_in, n_out = w_in.shape[0], w_out.shape[0]
    three = sds((3, WIDTH), f32)
    rel = sds(rel_bias.shape, f32)
    return vmem_call(
        update_kernel,
        (
            sds(back_tok.shape), sds(back_mem.shape), sds(w_in.shape, f32), sds(w_out.shape, f32), three, rel,
            sds(w_in.shape, f32), sds(w_out.shape, f32), three, rel, three, sds((n_in,), f32), sds((n_out,), f32),
            three, three, rel,
        ),
        [],
        in_specs=[scalars] * 2 + [whole()] * len(arrays),
    )(ids, row_source, *arrays)


ROWS_FROM = 10
TOK_RATE = 3


def forward_kernel(boxed, *refs):
    if boxed:
        (row_source, modes, tokens, memory, segments, msegments, w_in, w_out, rel_bias, hot, sentinel), refs = refs[:11], refs[11:]
        gains, (win, wout), rows_out, refs = refs[0], refs[1:3], refs[3:6], refs[6:]
        (table_b, keep_col, mode_rows), refs = refs[:3], refs[3:]
    else:
        (tok_s, mem_s, aux_s, win, wout, gains, table), refs = refs[:7], refs[7:]
        rows_out = None
    kept_out, kept, (tok, mem, aux), refs = refs[:9], refs[9:18], refs[18:21], refs[21:]
    (win_v, wout_v, sem, put_sem, ls), refs = refs[:5], refs[5:]
    puts = []

    def keep(src, dst):
        puts.append(pltpu.make_async_copy(src, dst, put_sem.at[len(puts)]))
        puts[-1].start()

    def hand_on(name):
        names = {"projected": (0,), "middle": (1, 2, 3), "crossed": (4, 5), "attended": (6, 7), "end": (8,)}
        for k in names.get(name, ()):
            keep(kept[k], kept_out[k])
        if boxed and name == "projected":
            keep(tok, rows_out[0])
            keep(aux, rows_out[2])
        if boxed and name == "crossed":
            keep(mem, rows_out[1])

    if not boxed:
        loads = [load_rows(win, win_v, 0, 6 * HEAD_COLS, sem.at[0]), load_rows(wout, wout_v, 0, 2 * HEAD_COLS, sem.at[1])]
        for k, (s, t) in enumerate(((tok_s, tok), (mem_s, mem), (aux_s, aux))):
            loads.append(pltpu.make_async_copy(s, t, ls.at[k]))
            loads[-1].start()
        for c in loads:
            c.wait()
        attention_forward(
            tok, mem, aux, win_v, wout_v, gains, table, *kept, step=lambda name, p: hand_on(name)
        )
        for c in puts:
            c.wait()
        return
    ss, rs, win_sh, wout_sh, tokens_v, memory_v, tok_s, mem_s, aux_s, seg_t, mseg_t, table = refs
    z, y, x, g = place()
    me = lax.axis_index("dp")
    pos = SEQ // 16
    links = Links(ss, rs)
    greeted = greet(all_peers())
    row_loads = [
        pltpu.make_async_copy(tokens, tokens_v, ls.at[2]), pltpu.make_async_copy(memory, memory_v, ls.at[3]),
    ]
    for c in row_loads:
        c.start()
    win_sh[...] = w_in[...].astype(jnp.bfloat16)
    wout_sh[...] = w_out[...].astype(jnp.bfloat16)
    near = [
        pltpu.make_async_copy(win_sh, rows_of(win, "i", z, y, x, g, 0, 272), ls.at[0]),
        pltpu.make_async_copy(wout_sh, rows_of(wout, "o", z, y, x, g, 0, 112), ls.at[1]),
    ]
    for c in near:
        c.start()
    meet(greeted)
    for c in near:
        c.wait()
    gather = Gather(links, {"i": win, "o": wout})
    slots = gather.slots()
    tok_rows, aux_rows, mem_rows = (
        Exchange(links, s, t, pos) for s, t in ((tok_s, tok), (aux_s, aux), (mem_s, mem))
    )
    half = len(gather.items) // 2
    now = half + 6
    queue = [[] for _ in range(len(slots))]
    for k in range(15):
        queue[ROWS_FROM + k // 3] += [tok_rows.copies[k], aux_rows.copies[k]]
        queue[ROWS_FROM + 5 + k // 2].append(mem_rows.copies[k])

    def run_gather(t):
        run(slots[t])
        for c in queue[t]:
            c.start()

    def store(i, *values):
        here = pl.ds(pl.multiple_of(i * pos, pos), pos)
        for ref, value in zip((tok_s, mem_s, aux_s), values):
            ref[here, :] = value

    for t in range(now):
        run_gather(t)
        if t == 2:
            for c in row_loads:
                c.wait()
            prep_rows(g, 2, row_source, tokens_v, memory_v, segments, msegments, seg_t, mseg_t, store)
        if t == 4:
            prep_tables(modes[row_source[me * 2 + g]], rel_bias, hot, sentinel, table, table_b, keep_col, mode_rows)
            here = pl.ds(pl.multiple_of(me * pos, pos), pos)
            for src, dst in ((tok_s, tok), (mem_s, mem), (aux_s, aux)):
                dst[here, :] = src[here, :]
    gather.arrived(0)
    loads = [
        load_rows(win, win_v, 0, 3 * HEAD_COLS, sem.at[0]), load_rows(wout, wout_v, 0, 2 * HEAD_COLS, sem.at[1]),
        load_rows(win, win_v, 3 * HEAD_COLS, 16 * 272, sem.at[2]),
    ]
    tok_rows.arrived()
    aux_rows.arrived()
    loads[0].wait()
    calls = HEADS // 2
    shares = [range(now + k, now + k + 1) for k in range(calls)]
    shares += [range(now + calls + k, now + calls + k + 1) for k in range(calls)]

    def step(name, p):
        hand_on(name)
        if name == "middle":
            gather.arrived(1)
            more = load_rows(win, win_v, 16 * 272, 6 * HEAD_COLS, sem.at[3])
            mem_rows.arrived()
            loads[2].wait()
            more.wait()
        if name not in ("self", "cross"):
            return
        for k in range(calls):

            @pl.when(p == k)
            def _(k=k):
                for t in shares[k + (0 if name == "self" else calls)]:
                    run_gather(t)
                if name == "self" and k == calls - 1:
                    loads[1].wait()

    attention_forward(tok, mem, aux, win_v, wout_v, gains, table, *kept, step=step)
    for t in range(now + 2 * calls, len(slots)):
        run_gather(t)
    gather.arrived(2)
    for c in puts:
        c.wait()
    gather.drain()
    for rows in (tok_rows, aux_rows, mem_rows):
        rows.drain()


def forward_call(boxed, *arrays):
    f32 = jnp.float32
    dma = pltpu.SemaphoreType.DMA
    outs = (
        sds((SEQ, 3 * HEAD_COLS)), sds((SEQ, HEAD_COLS)), sds((SEQ, 128), f32), sds((SEQ, WIDTH), f32),
        sds((SEQ, HEAD_COLS)), sds((SEQ, 2 * HEAD_COLS)), sds((SEQ, HEAD_COLS)), sds((SEQ, 128), f32),
        sds((SEQ, WIDTH), f32),
    )
    rows = (sds((SEQ, WIDTH)), sds((SEQ, WIDTH)), sds((SEQ, 128)))
    scratch = [pltpu.VMEM(v.shape, v.dtype) for v in outs + rows] + WEIGHTS + [dma((4,)), dma((12,)), dma((5,))]
    specs = [anywhere()] * 5 + [whole()] * 2
    out_specs = [anywhere()] * len(outs)
    extra = {}
    if boxed:
        vm, bf16 = pltpu.VMEM, jnp.bfloat16
        scratch = scratch + [dma((7,)), dma((20 * len(PIECES) + 6,)), vm((272, WIDTH), bf16), vm((112, WIDTH), bf16)]
        scratch += [vm((16, SEQ // 16, WIDTH), bf16)] * 2 + [vm((SEQ, WIDTH), bf16)] * 2 + [vm((SEQ, 128), bf16)]
        scratch += [vm((128, 128), f32)] * 2 + [vm((16, 256), f32)]
        small = (sds((16, 256), f32), sds((SEQ, 128), f32), sds((8, 128), f32))
        outs = (sds((6 * HEAD_COLS + 2 * FF, WIDTH)), sds((2 * HEAD_COLS + FF, WIDTH))) + rows + small + outs
        scalars = pl.BlockSpec(memory_space=pltpu.SMEM)
        specs = [scalars] * 2 + [anywhere()] * 2 + [whole()] * 8
        out_specs = [anywhere()] * 5 + [whole()] * 3 + out_specs
        extra = dict(collective_id=1, has_side_effects=True)
    return pl.pallas_call(
        functools.partial(forward_kernel, boxed),
        out_shape=outs,
        scratch_shapes=scratch,
        in_specs=specs,
        out_specs=tuple(out_specs),
        compiler_params=pltpu.CompilerParams(vmem_limit_bytes=VMEM_BYTES, **extra),
    )(*arrays)


def ff_call(x2, cot, keep, gains, win, wout):
    f32 = jnp.float32
    step = 512
    n = FF // step
    at = lambda block, first: pl.BlockSpec((step, WIDTH), lambda c: (first + c, 0))
    full = lambda rows, cols: pl.BlockSpec((rows, cols), lambda c: (0, 0))
    gate0, down0 = 6 * HEAD_COLS // step, 2 * HEAD_COLS // step
    return vmem_call(
        ff_kernel,
        (
            sds((SEQ, WIDTH)), sds((SEQ, WIDTH), f32), sds((1, WIDTH), f32), sds(win.shape), sds(wout.shape),
        ),
        [
            pltpu.VMEM((SEQ, WIDTH), jnp.bfloat16), pltpu.VMEM((SEQ, WIDTH), jnp.bfloat16),
            pltpu.VMEM((SEQ, WIDTH), f32), pltpu.VMEM((SEQ, WIDTH), f32),
            pltpu.VMEM((2, 3, step, WIDTH), jnp.bfloat16), pltpu.SemaphoreType.DMA((2, 3)),
        ],
        grid=(n,),
        in_specs=[
            full(SEQ, WIDTH), full(SEQ, WIDTH), full(SEQ, 128), full(3, WIDTH),
            at(step, gate0), at(step, gate0 + n), at(step, down0),
        ],
        out_specs=(full(SEQ, WIDTH), full(SEQ, WIDTH), full(1, WIDTH), anywhere(), anywhere()),
    )(x2, cot, keep, gains, win, win, wout)


def rel_sums(dist, hot_dist, mode_rows):
    by_bucket = jnp.dot(dist, hot_dist, precision=PRECISE, preferred_element_type=jnp.float32)
    lane = lane_of(by_bucket.shape)
    total = jnp.zeros_like(by_bucket)
    for k in range(MODES):
        moved = pltpu.roll(by_bucket * mode_rows[k : k + 1, :], k * BUCKETS, 1)
        total = jnp.where(lane // BUCKETS == k, moved, total)
    return total


def backward_kernel(boxed, _, __, win, wout, *refs):
    lazy, refs = refs[:12], refs[12:]
    (gains, table, hot_dist, mode_rows, gain_three, rows_out), refs = refs[:6], refs[6:]
    if boxed:
        (g_win, g_wout, part_in, part_out, sums, early, btok, bmem), refs = refs[:8], refs[8:]
        (d_mem, d_tok), refs = refs[:2], refs[2:]
    else:
        (g_win, g_wout, d_mem, d_tok, early), refs = refs[:5], refs[5:]
    (d_gains, dist), refs = refs[:2], refs[2:]
    scratch, (held, put_sem, blocks, block_sem, lazy_sem, sem), refs = refs[:3], refs[3:9], refs[9:]
    lazy_v, refs = refs[:12], refs[12:]
    fetched = []
    greeted = greet(all_peers()) if boxed else 0

    def fetch(k):
        array, block = BACK_BLOCKS[k]
        src = (win if array == "i" else wout).at[block * HEAD_COLS : (block + 1) * HEAD_COLS]
        fetched.append(pltpu.make_async_copy(src, blocks.at[k % 3], block_sem.at[k]))
        fetched[k].start()

    def weight(k, fn):
        fetched[k].wait()
        value = fn(blocks[k % 3])
        if k + 3 < len(BACK_BLOCKS):
            fetch(k + 3)
        return value

    loads = [pltpu.make_async_copy(s, t, lazy_sem.at[k]) for k, (s, t) in enumerate(zip(lazy, lazy_v))]
    loads[0].start()
    fetch(0)
    for c in loads[1:]:
        c.start()
    fetch(1)
    fetch(2)
    loaded = []

    def need(n):
        while len(loaded) < n:
            loads[len(loaded)].wait()
            loaded.append(True)

    puts, settled = [], []

    def settle(upto):
        while len(settled) < upto:
            puts[len(settled)].wait()
            settled.append(True)

    def emit(array, first, value):
        k = len(puts)
        settle(k - 1)
        rows = value.shape[0]
        held[k % 2, 0:rows] = value.astype(jnp.bfloat16)
        into = g_win if array == "i" else g_wout
        puts.append(pltpu.make_async_copy(held.at[k % 2, 0:rows], into.at[first : first + rows], put_sem.at[k]))
        puts[k].start()

    dist[...] = jnp.zeros_like(dist)
    step = lambda *a: None
    if boxed:
        own, got, plane, fin, line, room, early_room, ss, rs, load_sem, freed = refs
        z, y, x, g = place()
        me = lax.axis_index("dp")
        pos = SEQ // 16
        meet(greeted)
        links = Links(ss, rs)
        work = Sums(links, g_win, g_wout, own, got, plane, fin, line, part_in, part_out, load_sem)
        n = len(SUM_PIECES)
        groups = (
            (0, 0, [(3, k) for k in range(n)]),
            (7, 400, [(2, k) for k in range(n)]),
            (14, 0, [(1, k) for k in range(3, n)] + [(0, k) for k in range(5, n)]),
            (20, 400, [(1, k) for k in (2, 1, 0)]),
            (23, 528, [(0, k) for k in (4, 3, 2, 1, 0)]),
        )
        slots = [[] for _ in range(42)]
        batches = []
        for first, got_from, members in groups:
            batches.append(work.batch(members, got_from))
            work.place_in(slots, first, batches[-1])
        mem_rows, tok_rows = Exchange(links, d_mem, bmem, pos), Exchange(links, d_tok, btok, pos)
        kept_mem, kept_tok = own_rows(d_mem, bmem, pos, sem.at[2]), own_rows(d_tok, btok, pos, sem.at[3])
        work.begin(batches[0])
        shares = {("cross", LATE): ((0,), (1,)), ("cross", 0): ((2,), (3,), (4,), (5, 6))}
        shares["mid"] = ((7,), (8, 9), (10,))
        shares["self", SELF_LATE] = ((11, 12, 13),)
        shares["self", 0] = ((14,), (15,), (16,), (17, 18), (19, 20))
        shares["end"] = ((21, 22), (23,))
        gates = ("late", "middle", "self late", "last")

        def step(name, p, first, last):
            if name in gates:
                settle(len(puts))
                if name == "middle":
                    kept_mem.start()
                if name in ("middle", "self late"):
                    pl.semaphore_wait(freed, 1)
                work.begin(batches[gates.index(name) + 1])
                return
            if name in ("mid", "end"):
                for t in shares[name][p]:
                    run_slot(slots[t])
                return
            for k, share in enumerate(shares[name, first]):

                @pl.when(p == first + k)
                def _(share=share, k=k):
                    if name == "self":
                        turn = k if first == 0 else 4
                        for c in mem_rows.copies[3 * turn : 3 * turn + 3] if turn < 5 and (first or k < 4) else []:
                            c.start()
                    for t in share:
                        run_slot(slots[t])
                    if n - 1 in share or 2 * n - 1 in share:
                        pl.semaphore_signal(freed, inc=1, device_id=dev(z, y, x, 1 - g), device_id_type=MESH)

    g2, aux, qc, kvc, att2, lse2, mem, x1, att1, qkv, lse1, tok = lazy_v
    attention_backward(
        tok, mem, aux, gains, table, qkv, att1, lse1, x1, qc, kvc, att2, lse2, g2,
        d_mem, d_tok, d_gains, dist, *scratch, weight=weight, need=need, emit=emit, step=step,
    )
    early[...] = jnp.zeros_like(early)
    early[0:2, 0:WIDTH] = d_gains[0:2, :]
    early[2:3, 0:WIDTH] = gain_three[...]
    rel = rel_sums(dist[...], hot_dist[...], mode_rows[...])
    early[:, WIDTH : WIDTH + 128] = rel[0:8]
    early[:, WIDTH + 128 : WIDTH + 256] = rel[8:16]
    if not boxed:
        settle(len(puts))
        return
    kept_tok.start()
    turns = total_steps(links, early, early_room)
    for k, slot in enumerate(slots[24:]):
        run_slot(slot)
        for c in tok_rows.copies[TOK_RATE * k : TOK_RATE * k + TOK_RATE]:
            c.start()
        if k % 4 == 0 and k // 4 < len(turns):
            turns[k // 4]()
    where = me * 2 + g
    sums[...] = block_sums(part_in[...], part_out[...], upright(rows_out[...]), where * 272, where * 112)
    run(total_steps(links, sums, room))
    mem_rows.arrived()
    tok_rows.arrived()
    kept_mem.wait()
    kept_tok.wait()
    work.drain()
    mem_rows.drain()
    tok_rows.drain()


def backward_call(boxed, g_win, g_wout, win, wout, lazy, *more):
    f32, bf16 = jnp.float32, jnp.bfloat16
    vm, dma = pltpu.VMEM, pltpu.SemaphoreType.DMA
    row = sds((SEQ, WIDTH))
    scratch = [vm((8, WIDTH), f32), vm((16, 384), f32)]
    scratch += [
        vm((SEQ, HEAD_COLS), bf16), vm((SEQ, 3 * HEAD_COLS), bf16), vm((2, 128, 384), f32),
        vm((2, HEAD_COLS, WIDTH), bf16), dma((10,)), vm((3, HEAD_COLS, WIDTH), bf16), dma((len(BACK_BLOCKS),)),
        dma((len(lazy),)), dma((4,)),
    ]
    scratch += [vm(v.shape, v.dtype) for v in lazy]
    outs = [sds(g_win.shape), sds(g_wout.shape)]
    if boxed:
        items, both = 4 * len(SUM_PIECES), 4 * 384
        outs += [sds((272, WIDTH), f32), sds((112, WIDTH), f32), sds((8, WIDTH), f32), sds((8, WIDTH + 256), f32), row, row]
        specs = (anywhere(),) * 2 + (whole(),) * 4 + (anywhere(),) * 2
        scratch = [vm((SEQ, WIDTH), bf16), vm((SEQ, WIDTH), bf16)] + scratch
        scratch += [
            vm((4, both, WIDTH), bf16), vm((4, 800, WIDTH), bf16), vm((2, both, WIDTH), bf16),
            vm((1, both, WIDTH), bf16), vm((6 * 384, WIDTH), bf16), vm((7, 8, WIDTH), f32), vm((7, 8, WIDTH + 256), f32),
            dma((20,)), dma((7 * items + 16,)), dma((items,)),
            pltpu.SemaphoreType.REGULAR,
        ]
    else:
        outs += [row, row, sds((8, WIDTH + 256), f32)]
        specs = (anywhere(),) * 2 + (whole(),) * 3
    extra = dict(collective_id=2, has_side_effects=True) if boxed else {}
    return pl.pallas_call(
        functools.partial(backward_kernel, boxed),
        out_shape=tuple(outs),
        scratch_shapes=scratch,
        in_specs=[anywhere()] * (4 + len(lazy)) + [whole()] * len(more),
        out_specs=specs,
        input_output_aliases={0: 0, 1: 1},
        compiler_params=pltpu.CompilerParams(vmem_limit_bytes=VMEM_BYTES, **extra),
    )(g_win, g_wout, win, wout, *lazy, *more)


def body(
    tokens, memory, segments, memory_segments, row_source, denoiser_modes, sentinel, cotangent, w_in, w_out,
    norm_gains, rel_bias, rows_in, cols_in, rows_out, cols_out, sq_gains, sq_rel,
):
    n_index = lax.axis_size("dp")
    n_group = lax.axis_size("group")
    my_group = lax.axis_index("group")
    my_place = lax.axis_index(("dp", "group"))
    half_rows = tokens.shape[0]
    rows_dev = cotangent.shape[0]
    assert rows_dev == 1
    boxed = n_index == 16 and n_group == 2
    ids = jnp.stack([jnp.int32(n_group), my_group, my_place])
    buckets = bucket_table(SEQ, BUCKETS)
    hot = (buckets[:256, None] == np.arange(BUCKETS)[None, :]).astype(np.float32)
    lane = np.arange(256)
    dist_f = np.where(lane <= 128, 128 - lane, 384 - lane)
    hot_t = jnp.asarray(np.concatenate([hot[dist_f], hot], axis=0).T)
    w_in_t, rel_t = w_in.T, jnp.swapaxes(rel_bias, 1, 2)
    if boxed:
        win, wout, tok, mem, aux, table_b, keep, mode_rows, *kept = forward_call(
            True, row_source, denoiser_modes, tokens, memory, segments, memory_segments, w_in_t, w_out, rel_t, hot_t,
            sentinel, norm_gains,
        )
    else:
        tok_s, mem_s, aux_s, win_sh, wout_sh, table_f, table_b, keep, mode_rows = prep_call(
            ids, row_source, denoiser_modes, tokens, memory, segments, memory_segments, w_in_t, w_out, rel_t, hot_t,
            sentinel,
        )
        win = lax.all_gather(win_sh, ("dp", "group"), axis=0, tiled=True)
        wout = lax.all_gather(wout_sh, ("dp", "group"), axis=0, tiled=True)
        tok, mem, aux = (
            lax.all_to_all(v, "dp", split_axis=0, concat_axis=0, tiled=True).reshape(SEQ, v.shape[-1])
            for v in (tok_s, mem_s, aux_s)
        )
        kept = forward_call(False, tok, mem, aux, win, wout, norm_gains, table_f)
    x2 = kept[8]
    mixed, g2, d_gain_three, g_win, g_wout = ff_call(
        x2, cotangent.reshape(SEQ, WIDTH), keep, norm_gains, win, wout
    )
    hot_dist = np.concatenate([hot, np.repeat(np.eye(BUCKETS, dtype=np.float32)[-1:], 128, axis=0)], axis=0)
    hot_dist = jnp.asarray(np.pad(hot_dist, ((0, 0), (0, 128 - BUCKETS))))
    rows_out_up = rows_out.reshape(1, -1)
    qkv, att1, lse1, x1, qc, kvc, att2, lse2, _ = kept
    lazy = (g2, aux, qc, kvc, att2, lse2, mem, x1, att1, qkv, lse1, tok)
    result = backward_call(
        boxed, g_win, g_wout, win, wout, lazy, norm_gains, table_b, hot_dist, mode_rows, d_gain_three, rows_out_up
    )
    if boxed:
        _, _, part_in_t, part_out, sums, early, back_tok, back_mem = result
        back_tok, back_mem = back_tok.reshape(tokens.shape), back_mem.reshape(memory.shape)
    else:
        g_win, g_wout, d_mem, d_tok, early = result
        back_tok, back_mem = (
            lax.all_to_all(v.reshape(tokens.shape), "dp", split_axis=0, concat_axis=0, tiled=True)
            for v in (d_tok, d_mem)
        )
        part_in_t, part_out = (
            lax.psum_scatter(v.astype(jnp.float32), ("dp", "group"), scatter_dimension=0, tiled=True)
            for v in (g_win, g_wout)
        )
        sums = block_sums(
            part_in_t, part_out, rows_out.reshape(-1, 1), my_place * part_in_t.shape[0], my_place * part_out.shape[0]
        )
        sums, early = lax.psum((sums, early), ("dp", "group"))
    (
        d_tokens, d_memory, grad_in, grad_out, grad_gains, grad_rel, new_in, new_out, new_gains, new_rel,
        rows_in_new, cols_in_new, rows_out_new, cols_out_new, sq_gains_new, sq_rel_new,
    ) = update_call(
        ids, row_source, part_in_t, part_out, sums, early, back_tok, back_mem, w_in_t, w_out, norm_gains, rel_t,
        rows_in, cols_in, rows_out, cols_out, sq_gains, jnp.swapaxes(sq_rel, 1, 2),
    )
    grad_rel, new_rel, sq_rel_new = (jnp.swapaxes(v, 1, 2) for v in (grad_rel, new_rel, sq_rel_new))
    return (
        mixed[None], d_tokens, d_memory, grad_in.T, grad_out, grad_gains, grad_rel, new_in.T, new_out, new_gains,
        new_rel, rows_in_new, cols_in_new, rows_out_new, cols_out_new, sq_gains_new,
        sq_rel_new,
    )


def solution(mesh):
    both = ("dp", "group")
    row_in = P("group", "dp", None)
    seg_in = P("group", "dp")
    return jax.shard_map(
        body,
        mesh=mesh,
        in_specs=(
            row_in, row_in, seg_in, seg_in, P(), P(), P(both, None), P(both, None, None), P(None, both),
            P(both, None), P(), P(), P(), P(both), P(both), P(), P(), P(),
        ),
        out_specs=(
            P(both, None, None), row_in, row_in, P(None, both), P(both, None), P(), P(), P(None, both),
            P(both, None), P(), P(), P(), P(both), P(both), P(), P(), P(),
        ),
        check_vma=False,
    )
```
